32 devices in a mesh: frame: 16 (over z, x, core), head: 2 (over y).
Axes of the slice: x: 2, y: 2, z: 4, core: 2. Of those that a mesh axis runs over, the one named last changes fastest.
Arguments:
- queries: bfloat16 [16384, 256], P(('frame', 'head')), may hold values from -8 to 8
- key_vectors: bfloat16 [16384, 256], P(('frame', 'head')), may hold values from -5 to 5
- value_vectors: bfloat16 [16384, 256], P(('frame', 'head')), may hold values from -6 to 6
- tile_lists: int32 [2, 128, 20], P('head', 'frame'), may hold values from 0 to 127, as said below
- live_slots: int32 [2, 128], P('head', 'frame'), may hold values from 2 to 20
Outputs:
- attended: bfloat16 [16384, 256], P(('frame', 'head'))
The draws below stay inside these ranges and needn't reach their ends.
Inputs may be any that keep to these rules, and one draw needn't show every extreme that they name: `tile_lists`: slot 0 of query tile t holds t; the slots below live_slots hold distinct tiles u with |u - t| <= 32; the other slots hold t.
All inputs are finite; a program needn't handle non-finite values.
Results may differ from the reference program's by a relative error of at most 0.0045.
Values may be sent and summed in bfloat16 or wider, within the bound.
No kernel may reach another device: no remote copies, remote signals or barrier semaphores. Data moves between devices by JAX's collectives and lax.ppermute only.
A program may use at most 64 MiB of HBM per device.

```python
import math
import jax
import jax.numpy as jnp
from jax import lax

TILE = 128
HEAD_DIM = 128
SEL = 20
FRAME_TILES = 28
JITTER = 4
TILES_DEV = 8
TILES = 128
TOKENS = 16384
HEADS = 2
REACH = 32


def tile_plan(key):
    span_count = 2 * REACH + 1
    offsets = jnp.arange(span_count, dtype=jnp.int32) - REACH
    pattern = jax.random.randint(jax.random.fold_in(key, 31), (HEADS, 1, 1), 0, 2)
    nearby = jnp.abs(offsets) <= JITTER
    framed = jnp.abs(jnp.abs(offsets) - FRAME_TILES) <= JITTER
    eligible = jnp.where(pattern == 1, nearby | framed, True) & (offsets != 0)
    query_tile = jnp.arange(TILES, dtype=jnp.int32)[None, :, None]
    targets = jnp.broadcast_to(query_tile + offsets, (HEADS, TILES, span_count))
    inside = eligible & (targets >= 0) & (targets < TILES)
    noise = jax.random.randint(jax.random.fold_in(key, 32), (HEADS, TILES, span_count), 0, 2 ** 20)
    ranking = noise * span_count + offsets + REACH
    middle = query_tile == TILES // 2
    ranking = jnp.where(middle & (offsets == REACH), -2, ranking)
    ranking = jnp.where(middle & (offsets == -REACH), -1, ranking)
    ranking = jnp.where(inside, ranking, 2 ** 30 + offsets + REACH)
    ordering = jnp.argsort(ranking, axis=-1, stable=True)[:, :, :SEL - 1]
    picked = jnp.take_along_axis(targets, ordering, axis=-1)
    counted = jnp.sum(inside.astype(jnp.int32), axis=-1)
    plenty = jax.random.randint(jax.random.fold_in(key, 33), (HEADS, TILES), SEL - SEL // 4, SEL + 1)
    sparse_count = jax.random.randint(jax.random.fold_in(key, 34), (HEADS, TILES), 2, SEL // 2 + 1)
    living = jnp.where(pattern[:, :, 0] == 1, sparse_count, plenty)
    living = jnp.where(middle[:, :, 0], SEL, living)
    living = jnp.minimum(living, counted + 1)
    own_tile = jnp.broadcast_to(query_tile, (HEADS, TILES, 1))
    slots_all = jnp.concatenate([own_tile, picked], axis=-1)
    slot_ids = jnp.arange(SEL, dtype=jnp.int32)
    slots_all = jnp.where(slot_ids < living[:, :, None], slots_all, query_tile)
    return (slots_all.astype(jnp.int32), living.astype(jnp.int32))


def draw_tile_lists(key, part):
    return tile_plan(key)[0]


def draw_live_slots(key, part):
    return tile_plan(key)[1]


def draw_queries(key, part):
    dimensions = (TOKENS, HEADS * HEAD_DIM)
    values_drawn = 2.0 * jnp.clip(jax.random.normal(jax.random.fold_in(key, 42), dimensions, dtype=jnp.float32), -4.0, 4.0)
    return values_drawn.astype(jnp.bfloat16)


def draw_key_vectors(key, part):
    dimensions = (TOKENS, HEADS * HEAD_DIM)
    values_drawn = jnp.clip(jax.random.normal(jax.random.fold_in(key, 44), dimensions, dtype=jnp.float32), -5.0, 5.0)
    return values_drawn.astype(jnp.bfloat16)


def steps_of(key, shape, cuts, least, high):
    gain = 1.0
    for dim, parts in cuts:
        steps = jax.random.uniform(jax.random.fold_in(jax.random.fold_in(key, 6), dim), (parts,), jnp.float32, least / len(cuts), high / len(cuts))
        gain = gain * jnp.repeat(jnp.exp(steps), shape[dim] // parts).reshape((-1,) + (1,) * (len(shape) - 1 - dim))
    return gain


def centred(stream_key, dims, deviation, bound, cuts=(), held_as=jnp.bfloat16):
    values = jax.random.normal(stream_key, dims, jnp.float32) * deviation
    if len(cuts) > 0:
        values = steps_of(stream_key, dims, cuts, -0.22, 0.18) * values
    return jnp.clip(values, min=-bound, max=bound).astype(held_as)


def setup_inputs(seed: int = 0) -> dict:
    streams_of = jax.random.split(jax.random.key(seed), 6)
    return {
        "queries": draw_queries(jax.random.fold_in(streams_of[5], 71), 0),
        "key_vectors": draw_key_vectors(jax.random.fold_in(streams_of[5], 71), 0),
        "value_vectors": centred(streams_of[2], (TOKENS, HEADS * HEAD_DIM), 1.0, 6.0, ((0, 32),)),
        "tile_lists": draw_tile_lists(jax.random.fold_in(streams_of[5], 71), 0),
        "live_slots": draw_live_slots(jax.random.fold_in(streams_of[5], 71), 0),
    }


def masked_softmax(query_tile_rows, gathered_key_block, gathered_value_block, usable):
    softmax_scale = 1.0 / math.sqrt(query_tile_rows.shape[-1])
    logit_scores = jnp.einsum('mar,mxr->max', query_tile_rows.astype(jnp.float32), gathered_key_block.astype(jnp.float32)) * softmax_scale
    logit_scores = jnp.where(usable[:, None, :], logit_scores, -jnp.inf)
    highest = lax.optimization_barrier(jnp.max(logit_scores, axis=-1, keepdims=True))
    exponent = jnp.exp(logit_scores - highest)
    denominator = lax.optimization_barrier(jnp.sum(exponent, axis=-1, keepdims=True))
    attention_weights = lax.optimization_barrier(exponent.astype(jnp.bfloat16)).astype(jnp.float32)
    weighted_sum = jnp.einsum('fve,fez->fvz', attention_weights, gathered_value_block.astype(jnp.float32))
    return (weighted_sum / denominator).astype(jnp.bfloat16)

def reference(queries, key_vectors, value_vectors, tile_lists, live_slots):
    groups = TILES // TILES_DEV
    outputs = []
    for head_index in range(HEADS):
        first_col = head_index * HEAD_DIM
        query_tile_rows = lax.slice_in_dim(queries, first_col, first_col + HEAD_DIM, axis=1).reshape(groups, TILES_DEV, TILE, HEAD_DIM)
        key_tiles = lax.slice_in_dim(key_vectors, first_col, first_col + HEAD_DIM, axis=1).reshape(TILES, TILE, HEAD_DIM)
        value_tiles = lax.slice_in_dim(value_vectors, first_col, first_col + HEAD_DIM, axis=1).reshape(TILES, TILE, HEAD_DIM)
        chosen = tile_lists[head_index].reshape(groups, TILES_DEV, SEL)
        living = live_slots[head_index].reshape(groups, TILES_DEV)

        def one_group(pieces, key_tiles=key_tiles, value_tiles=value_tiles):
            group_queries, group_ids, group_live = pieces
            gathered_key_block = key_tiles[group_ids].reshape(TILES_DEV, SEL * TILE, HEAD_DIM)
            gathered_value_block = value_tiles[group_ids].reshape(TILES_DEV, SEL * TILE, HEAD_DIM)
            slot_ids = jnp.arange(SEL, dtype=jnp.int32)
            usable = jnp.repeat(slot_ids[None, :] < group_live[:, None], TILE, axis=1)
            return masked_softmax(group_queries, gathered_key_block, gathered_value_block, usable)
        result = lax.map(one_group, (query_tile_rows, chosen, living))
        outputs.append(result.reshape(TOKENS, HEAD_DIM))
    return jnp.concatenate(outputs, axis=1)
```

```python
import functools
import math

import jax
import jax.numpy as jnp
import numpy as np
from jax import lax
from jax.experimental import pallas as pl
from jax.experimental.pallas import tpu as pltpu
from jax.sharding import PartitionSpec as P

TILE = 128
HEAD_DIM = 128
REACH = 32
PLANE = 4
DEAD = 1e30


def piece_table():
    table = np.zeros((PLANE, 2 * PLANE + 1), np.int32)
    for place in range(PLANE):
        x, core = divmod(place, 2)
        for distance in range(-PLANE, PLANE + 1):
            plane, there = divmod(place + distance, PLANE)
            same_x, same_core = there // 2 == x, there % 2 == core
            if plane == 0:
                kind = 0 if same_x else 3
            elif same_x:
                kind = 1 if plane < 0 else 2
            else:
                kind = 4
            if not same_core:
                kind = {0: 5, 1: 6, 2: 6, 3: 7, 4: 8}[kind]
            table[place, distance + PLANE] = kind
    return table


def split_kernel(heads, head_ref, q_ref, k_ref, v_ref, q_keep, kv_keep, q_send, kv_send):
    head = head_ref[0]
    tiles = q_ref.shape[0] // TILE
    for step in range(heads):
        column = lax.rem(head + step, heads) * HEAD_DIM
        columns = pl.ds(pl.multiple_of(column, HEAD_DIM), HEAD_DIM)
        q_to = q_keep if step == 0 else q_send.at[step - 1]
        kv_to = kv_keep if step == 0 else kv_send.at[step - 1]
        for tile in range(tiles):
            rows = pl.ds(tile * TILE, TILE)
            kv_to[0, tile] = k_ref[rows, columns]
            kv_to[1, tile] = v_ref[rows, columns].T
            q_to[tile] = q_ref[rows, columns]


def split_heads(head, queries, key_vectors, value_vectors, heads):
    tiles = queries.shape[0] // TILE
    dtype = queries.dtype
    tile = (TILE, HEAD_DIM)
    vmem = pl.BlockSpec(memory_space=pltpu.VMEM)
    return pl.pallas_call(
        functools.partial(split_kernel, heads),
        in_specs=[pl.BlockSpec(memory_space=pltpu.SMEM), vmem, vmem, vmem],
        out_specs=[vmem] * 4,
        out_shape=[
            jax.ShapeDtypeStruct((tiles,) + tile, dtype),
            jax.ShapeDtypeStruct((2, tiles) + tile, dtype),
            jax.ShapeDtypeStruct((heads - 1, tiles) + tile, dtype),
            jax.ShapeDtypeStruct((heads - 1, 2, tiles) + tile, dtype),
        ],
    )(head, queries, key_vectors, value_vectors)


def join_kernel(heads, head_ref, *refs):
    out_ref = refs[-1]
    for step in range(heads):
        column = lax.rem(head_ref[0] + step, heads) * HEAD_DIM
        columns = pl.ds(pl.multiple_of(column, HEAD_DIM), HEAD_DIM)
        out_ref[:, columns] = refs[step][...]


def join_heads(head, pieces):
    rows = pieces[0].shape[0]
    heads = len(pieces)
    vmem = pl.BlockSpec(memory_space=pltpu.VMEM)
    return pl.pallas_call(
        functools.partial(join_kernel, heads),
        in_specs=[pl.BlockSpec(memory_space=pltpu.SMEM)] + [vmem] * heads,
        out_specs=vmem,
        out_shape=jax.ShapeDtypeStruct((rows, heads * HEAD_DIM), pieces[0].dtype),
    )(head, *pieces)


def attend_kernel(
    heads, first, offset, head_ref, ids_ref, live_ref, q_ref, window_ref, out_ref, scores, highest
):
    tiles = q_ref.shape[0]
    slots = ids_ref.shape[1]
    part_tiles = live_ref.shape[0] // heads
    factor = math.log2(math.e) / math.sqrt(HEAD_DIM)

    def row_of(tile):
        part, inside = (tile + first) // part_tiles, lax.rem(tile + first, part_tiles)
        return lax.rem(head_ref[0] - part + heads, heads) * part_tiles + inside

    def score(tile, buffer):
        row = row_of(tile)
        queries = q_ref[tile]
        top = None
        for slot in range(slots):
            keys = window_ref[ids_ref[row, slot]]
            block = lax.dot_general(
                keys, queries, (((1,), (1,)), ((), ())), preferred_element_type=jnp.float32
            )
            scores[buffer, slot] = block
            top = block if top is None else jnp.maximum(top, block)
        highest[buffer] = jnp.max(top, axis=0, keepdims=True)

    def weigh(tile, buffer):
        row = row_of(tile)
        live = live_ref[row]
        top = highest[buffer]
        total = jnp.zeros((TILE, TILE), jnp.float32)
        out = jnp.zeros((HEAD_DIM, TILE), jnp.float32)
        for pair in range(0, slots, 2):
            weights, values = [], []
            for slot in (pair, pair + 1):
                shift = jnp.where(slot < live, top, DEAD)
                weight = jnp.exp2((scores[buffer, slot] - shift) * factor)
                total = total + weight
                weights.append(weight.astype(jnp.bfloat16))
                values.append(window_ref[ids_ref[row, slot] + offset])
            out = out + jnp.dot(
                jnp.concatenate(values, axis=1),
                jnp.concatenate(weights, axis=0),
                preferred_element_type=jnp.float32,
            )
        denominator = jnp.sum(total, axis=0, keepdims=True)
        out_ref[tile] = (out / denominator).T.astype(out_ref.dtype)

    score(0, 0)

    def step(tile, carry):
        buffer = lax.rem(tile, 2)
        score(jnp.minimum(tile + 1, tiles - 1), 1 - buffer)
        weigh(tile, buffer)
        return carry

    lax.fori_loop(0, tiles, step, 0)


def attend(head, ids, live, queries, window, heads, first, offset):
    tiles = queries.shape[0]
    slots = ids.shape[1]
    vmem = pl.BlockSpec(memory_space=pltpu.VMEM)
    smem = pl.BlockSpec(memory_space=pltpu.SMEM)
    pairs = tiles * slots * TILE * TILE
    return pl.pallas_call(
        functools.partial(attend_kernel, heads, first, offset),
        in_specs=[smem, smem, smem, vmem, vmem],
        out_specs=vmem,
        out_shape=jax.ShapeDtypeStruct(queries.shape, queries.dtype),
        scratch_shapes=[
            pltpu.VMEM((2, slots, TILE, TILE), jnp.float32),
            pltpu.VMEM((2, 1, TILE), jnp.float32),
        ],
        compiler_params=pltpu.CompilerParams(vmem_limit_bytes=32 * 2**20),
        cost_estimate=pl.CostEstimate(
            flops=4 * pairs * HEAD_DIM, bytes_accessed=window.size * 2, transcendentals=pairs
        ),
    )(head, ids, live, queries, window)


def moved(block, axis, source):
    size = lax.axis_size(axis)
    route = [(source(i), i) for i in range(size) if 0 <= source(i) < size]
    return lax.ppermute(block, axis, route)


def body(queries, key_vectors, value_vectors, tile_lists, live_slots):
    heads = lax.axis_size("head")
    frame = lax.axis_index("frame")
    head = lax.axis_index("head")
    head_ref = head[None]
    place = lax.rem(frame, PLANE)
    shard_tiles = tile_lists.shape[1]
    part_tiles = shard_tiles // heads
    assert shard_tiles * PLANE == REACH and lax.axis_size("frame") % PLANE == 0

    q_keep, kv_keep, q_send, kv_send = split_heads(
        head_ref, queries, key_vectors, value_vectors, heads
    )
    kv_parts, q_parts = [kv_keep], [q_keep]
    for step in range(1, heads):
        kv_parts.append(moved(kv_send[step - 1], "head", lambda i: (i - step) % heads))
    for step in range(1, heads):
        q_parts.append(moved(q_send[step - 1], "head", lambda i: (i - step) % heads))
    own = jnp.stack(kv_parts)

    before = moved(own, "frame", lambda i: i - PLANE)
    after = moved(own, "frame", lambda i: i + PLANE)
    across = moved(own, "frame", lambda i: i ^ 2)
    cut = heads // 2
    far_z = moved(across[:cut], "frame", lambda i: i - PLANE if i % PLANE < 2 else i + PLANE)
    far_x = moved(jnp.where(place < 2, after[cut:], before[cut:]), "frame", lambda i: i ^ 2)
    far = jnp.concatenate((far_z, far_x))
    own_core = moved(own, "frame", lambda i: i ^ 1)
    level_core = moved(jnp.where(place % 2 == 0, after, before), "frame", lambda i: i ^ 1)
    across_core = moved(across, "frame", lambda i: i ^ 1)
    far_core = moved(far, "frame", lambda i: i ^ 1)
    window = jnp.concatenate(
        (own, before, after, across, far, own_core, level_core, across_core, far_core)
    ).reshape(-1, TILE, HEAD_DIM)

    listed = tile_lists[0]
    shard = listed // shard_tiles - frame + PLANE
    kinds = jnp.asarray(piece_table())[place]
    piece = jnp.sum(
        jnp.where(shard[..., None] == jnp.arange(2 * PLANE + 1), kinds, 0), axis=-1, dtype=jnp.int32
    )
    within = lax.rem(listed, shard_tiles)
    part = lax.rem(head - within // part_tiles + heads, heads)
    ids = (piece * heads + part) * (2 * part_tiles) + lax.rem(within, part_tiles)
    live = live_slots[0]

    rest = attend(
        head_ref, ids, live, jnp.concatenate(q_parts[1:]), window, heads, part_tiles, part_tiles
    )
    pieces = [None]
    for step in range(1, heads):
        sent = rest[(step - 1) * part_tiles : step * part_tiles]
        pieces.append(moved(sent, "head", lambda i: (i + step) % heads))
    pieces[0] = attend(head_ref, ids, live, q_parts[0], window, heads, 0, part_tiles)
    return join_heads(head_ref, [p.reshape(-1, HEAD_DIM) for p in pieces])


def solution(mesh):
    placed = (
        P(("frame", "head"), None),
        P(("frame", "head"), None),
        P(("frame", "head"), None),
        P("head", "frame", None),
        P("head", "frame"),
    )
    return jax.shard_map(
        body, mesh=mesh, in_specs=placed, out_specs=P(("frame", "head"), None), check_vma=False
    )
```

```python
import functools
import math

import jax
import jax.numpy as jnp
import numpy as np
from jax import lax
from jax.experimental import pallas as pl
from jax.experimental.pallas import tpu as pltpu
from jax.sharding import PartitionSpec as P

TILE = 128
HEAD_DIM = 128
REACH = 32
PLANE = 4
GROUP = 4
PHASES = 3
FAR_OFF = 1e30
VMEM = pl.BlockSpec(memory_space=pltpu.VMEM)
SMEM = pl.BlockSpec(memory_space=pltpu.SMEM)


def part_table(heads):
    rest = heads - 1
    table = np.zeros((PLANE, 2 * PLANE + 1, heads, 2), np.int32)
    for place in range(PLANE):
        x, core = divmod(place, 2)
        for distance in range(-PLANE, PLANE + 1):
            plane, there = divmod(place + distance, PLANE)
            same_x, same_core = there // 2 == x, there % 2 == core
            for part in range(heads):
                if plane == 0 and same_x:
                    entry = 0, part + (0 if same_core else heads + 3)
                elif plane != 0 and not same_x:
                    entry = 2, part + (0 if same_core else heads)
                else:
                    kind = 0 if plane == 0 else (1 if plane < 0 else 2)
                    if not same_core:
                        kind = 3 if plane == 0 else 4
                    if part > 0:
                        entry = 1, kind * rest + part - 1
                    else:
                        entry = 0, heads + kind + (heads if kind > 2 else 0)
                table[place, distance + PLANE, part] = entry
    return table[..., 0] * 1024 + table[..., 1]


def split_kernel(heads, first, head_ref, k_ref, v_ref, q_ref, out_ref):
    for step in range(out_ref.shape[0]):
        column = lax.rem(head_ref[0] + first + step, heads) * HEAD_DIM
        columns = pl.ds(pl.multiple_of(column, HEAD_DIM), HEAD_DIM)
        for tile in range(out_ref.shape[2]):
            rows = pl.ds(tile * TILE, TILE)
            out_ref[step, 0, tile] = k_ref[rows, columns]
            out_ref[step, 1, tile] = v_ref[rows, columns].T
            out_ref[step, 2, tile] = q_ref[rows, columns].T


def split_heads(head, arrays, heads, first, count):
    tiles = arrays[0].shape[0] // TILE
    return pl.pallas_call(
        functools.partial(split_kernel, heads, first),
        in_specs=[SMEM] + [VMEM] * 3,
        out_specs=VMEM,
        out_shape=jax.ShapeDtypeStruct((count, 3, tiles, TILE, HEAD_DIM), arrays[0].dtype),
        cost_estimate=pl.CostEstimate(flops=0, bytes_accessed=1 << 24, transcendentals=0),
    )(head, *arrays)


def join_kernel(heads, head_ref, *refs):
    out_ref = refs[-1]
    for step in range(heads):
        column = lax.rem(head_ref[0] + step, heads) * HEAD_DIM
        columns = pl.ds(pl.multiple_of(column, HEAD_DIM), HEAD_DIM)
        out_ref[:, columns] = refs[step][...]


def join_heads(head, pieces):
    rows = pieces[0].shape[0]
    heads = len(pieces)
    return pl.pallas_call(
        functools.partial(join_kernel, heads),
        in_specs=[SMEM] + [VMEM] * heads,
        out_specs=VMEM,
        out_shape=jax.ShapeDtypeStruct((rows, heads * HEAD_DIM), pieces[0].dtype),
    )(head, *pieces)


def phase_kernel(heads, first, pieces, begins, ends, head_ref, ids_ref, count_ref, q_ref, *refs):
    refs = list(refs)
    state = [refs.pop(0) for _ in range(0 if begins else 3)]
    parts = [refs.pop(0) for _ in range(pieces)]
    out_ref = refs.pop(0) if ends else None
    top_ref, total_ref, sum_ref = [refs.pop(0) for _ in range(3)]
    window, scores_a, scores_b, high_a, high_b, items = refs
    tiles = q_ref.shape[0]
    part_tiles = count_ref.shape[0] // heads
    factor = math.log2(math.e) / math.sqrt(HEAD_DIM)

    at = 0
    for part in parts:
        window[at : at + part.shape[0]] = part[...]
        at += part.shape[0]
    if begins:
        top_ref[...] = jnp.full(top_ref.shape, -FAR_OFF, jnp.float32)
        total_ref[...] = jnp.zeros(total_ref.shape, jnp.float32)
        sum_ref[...] = jnp.zeros(sum_ref.shape, jnp.float32)
    else:
        for ref, old in zip((top_ref, total_ref, sum_ref), state):
            ref[...] = old[first : first + tiles]

    def put(number, tile, row, slot, live):
        items[0, number] = tile
        items[1, number] = row
        items[2, number] = slot
        items[3, number] = live

    number = jnp.int32(0)
    for tile in range(tiles):
        part, inside = divmod(tile + first, part_tiles)
        row = lax.rem(head_ref[0] - part + heads, heads) * part_tiles + inside
        count = count_ref[row]

        def add(group, number, tile=tile, row=row, count=count):
            put(number, tile, row, group * GROUP, jnp.minimum(count - group * GROUP, GROUP))
            return number + 1

        number = lax.fori_loop(0, lax.div(count + GROUP - 1, GROUP), add, number)
    put(number, 0, 0, 0, 0)
    put(number + 1, 0, 0, 0, 0)

    def score(item, scores, high):
        tile, row, first_slot = items[0, item], items[1, item], items[2, item]
        queries = q_ref[tile]
        top = None
        for slot in range(GROUP):
            keys = window[ids_ref[row, first_slot + slot]]
            block = jnp.dot(keys, queries, preferred_element_type=jnp.float32)
            scores[slot] = block
            top = block if top is None else jnp.maximum(top, block)
        high[...] = jnp.max(top, axis=0, keepdims=True)

    def weigh(item, scores, high):
        tile, row, first_slot = items[0, item], items[1, item], items[2, item]
        live = items[3, item]
        old = top_ref[tile]
        top = jnp.maximum(old, jnp.where(live > 0, high[...], -FAR_OFF))
        shrink = jnp.exp2((old - top) * factor)
        total = total_ref[tile] * shrink
        weighted = sum_ref[tile] * shrink
        for pair in range(0, GROUP, 2):
            weights, values = [], []
            for slot in (pair, pair + 1):
                shift = jnp.where(slot < live, top, FAR_OFF)
                weight = jnp.exp2((scores[slot] - shift) * factor)
                total = total + jnp.sum(weight.reshape(TILE // 8, 8, TILE), axis=0)
                weights.append(weight.astype(jnp.bfloat16))
                values.append(window[ids_ref[row, first_slot + slot] + part_tiles])
            weighted = weighted + jnp.dot(
                jnp.concatenate(values, axis=1),
                jnp.concatenate(weights, axis=0),
                preferred_element_type=jnp.float32,
            )
        top_ref[tile] = top
        total_ref[tile] = total
        sum_ref[tile] = weighted

    score(0, scores_a, high_a)

    def step(pair, carry):
        score(2 * pair + 1, scores_b, high_b)
        weigh(2 * pair, scores_a, high_a)
        score(2 * pair + 2, scores_a, high_a)
        weigh(2 * pair + 1, scores_b, high_b)
        return carry

    lax.fori_loop(0, lax.div(number + 1, 2), step, 0)
    if ends:
        for tile in range(tiles):
            total = jnp.sum(total_ref[tile], axis=0, keepdims=True)
            out_ref[tile] = (sum_ref[tile] / total).T.astype(out_ref.dtype)


def phase(head, lists, queries, state, pieces, heads, first, ends):
    ids, count = lists
    tiles = queries.shape[0]
    begins = state is None
    windows = sum(piece.shape[0] for piece in pieces)
    held = [
        jax.ShapeDtypeStruct((tiles, 1, TILE), jnp.float32),
        jax.ShapeDtypeStruct((tiles, 8, TILE), jnp.float32),
        jax.ShapeDtypeStruct((tiles, HEAD_DIM, TILE), jnp.float32),
    ]
    scratch = [
        pltpu.VMEM((windows, TILE, TILE), queries.dtype),
        pltpu.VMEM((GROUP, TILE, TILE), jnp.float32),
        pltpu.VMEM((GROUP, TILE, TILE), jnp.float32),
        pltpu.VMEM((1, TILE), jnp.float32),
        pltpu.VMEM((1, TILE), jnp.float32),
        pltpu.SMEM((4, tiles * (ids.shape[1] // GROUP + 1) + 2), jnp.int32),
    ]
    out = jax.ShapeDtypeStruct(queries.shape, queries.dtype)
    pairs = tiles * ids.shape[1] * TILE * TILE // PHASES
    return pl.pallas_call(
        functools.partial(phase_kernel, heads, first, len(pieces), begins, ends),
        in_specs=[SMEM] * 3 + [VMEM] * (1 + len(pieces) + (0 if begins else 3)),
        out_specs=VMEM if ends else [VMEM] * 3,
        out_shape=out if ends else held,
        scratch_shapes=([pltpu.VMEM(h.shape, h.dtype) for h in held] if ends else []) + scratch,
        compiler_params=pltpu.CompilerParams(vmem_limit_bytes=32 * 2**20),
        cost_estimate=pl.CostEstimate(
            flops=4 * pairs * HEAD_DIM, bytes_accessed=windows * 2**15, transcendentals=pairs
        ),
    )(head, ids, count, queries, *([] if begins else state), *pieces)


def moved(block, axis, source):
    size = lax.axis_size(axis)
    route = [(source(i), i) for i in range(size) if 0 <= source(i) < size]
    return lax.ppermute(block, axis, route)


def phase_lists(tile_lists, live_slots, frame, head, heads):
    shard_tiles, slots = tile_lists.shape
    part_tiles = shard_tiles // heads
    shard = tile_lists // shard_tiles - frame + PLANE
    within = lax.rem(tile_lists, shard_tiles)
    part = lax.rem(head - within // part_tiles + heads, heads)
    table = jnp.asarray(part_table(heads))[lax.rem(frame, PLANE)].reshape(-1)
    match = (shard * heads + part)[..., None] == jnp.arange(table.size)
    entry = jnp.sum(jnp.where(match, table, 0), axis=-1, dtype=jnp.int32)
    index = entry % 1024 * (2 * part_tiles) + lax.rem(within, part_tiles)
    order = jnp.arange(slots)
    lists = []
    for number in range(PHASES):
        member = (entry // 1024 == number) & (order < live_slots[:, None])
        before = member[:, None, :] & (order[None, :] < order[:, None])
        rank = jnp.sum(before, axis=-1, dtype=jnp.int32)
        count = jnp.sum(member, axis=-1, dtype=jnp.int32)
        wanted = jnp.where(order < count[:, None], order, 0)
        chosen = member[:, None, :] & (rank[:, None, :] == wanted[:, :, None])
        ids = jnp.sum(jnp.where(chosen, index[:, None, :], 0), axis=-1, dtype=jnp.int32)
        lists.append((ids, count))
    return lists


def body(queries, key_vectors, value_vectors, tile_lists, live_slots):
    heads = lax.axis_size("head")
    frame = lax.axis_index("frame")
    head = lax.axis_index("head")
    head_ref = head[None]
    place = lax.rem(frame, PLANE)
    shard_tiles = tile_lists.shape[1]
    part_tiles = shard_tiles // heads
    assert shard_tiles * PLANE == REACH and lax.axis_size("frame") % PLANE == 0

    arrays = key_vectors, value_vectors, queries
    send = split_heads(head_ref, arrays, heads, 1, heads - 1)
    send, arrays = lax.optimization_barrier((send, arrays))
    keep = split_heads(head_ref, arrays, heads, 0, 1)
    received = jnp.stack(
        [
            moved(send[step - 1], "head", lambda i: (i - step) % heads)
            for step in range(1, heads)
        ]
    )
    received, listed, live = lax.optimization_barrier((received, tile_lists[0], live_slots[0]))
    q_parts = jnp.concatenate((keep[:, 2], received[:, 2])).reshape(-1, HEAD_DIM, TILE)
    halves = [keep[:, :2], received[:, :2]]
    across, before, after, level = [], [], [], []
    for half in halves:
        across.append(moved(half, "frame", lambda i: i ^ 2))
        before.append(moved(half, "frame", lambda i: i - PLANE))
        after.append(moved(half, "frame", lambda i: i + PLANE))
        level.append(jnp.where(place % 2 == 0, after[-1], before[-1]))
    far = [
        moved(jnp.where(place < 2, after[0], before[0]), "frame", lambda i: i ^ 2),
        moved(across[1], "frame", lambda i: i - PLANE if i % PLANE < 2 else i + PLANE),
    ]

    def core_swap(*blocks):
        return moved(jnp.concatenate(blocks), "frame", lambda i: i ^ 1)

    def as_tiles(*blocks):
        return [block.reshape(-1, TILE, TILE) for block in blocks]

    lists = phase_lists(listed, live, frame, head, heads)
    pieces = as_tiles(
        *halves, across[0], before[0], after[0], core_swap(*halves, across[0], level[0])
    )
    pieces, arrived = lax.optimization_barrier((pieces, (across[1], before[1], after[1])))
    state = phase(head_ref, lists[0], q_parts, None, pieces, heads, 0, False)
    far, state = lax.optimization_barrier((far, state))
    pieces = as_tiles(*arrived, core_swap(across[1], level[1]))
    state = phase(head_ref, lists[1], q_parts, state, pieces, heads, 0, False)
    pieces = as_tiles(*far, core_swap(*far))
    rest = phase(
        head_ref, lists[2], q_parts[part_tiles:], state, pieces, heads, part_tiles, True
    )
    outs = [None]
    for step in range(1, heads):
        sent = rest[(step - 1) * part_tiles : step * part_tiles]
        outs.append(moved(sent, "head", lambda i: (i + step) % heads))
    outs[0] = phase(head_ref, lists[2], q_parts[:part_tiles], state, pieces, heads, 0, True)
    return join_heads(head_ref, [o.reshape(-1, HEAD_DIM) for o in outs])


def solution(mesh):
    placed = (
        P(("frame", "head"), None),
        P(("frame", "head"), None),
        P(("frame", "head"), None),
        P("head", "frame", None),
        P("head", "frame"),
    )
    return jax.shard_map(
        body, mesh=mesh, in_specs=placed, out_specs=P(("frame", "head"), None), check_vma=False
    )
```

```python
import functools
import math

import jax
import jax.numpy as jnp
import numpy as np
from jax import lax
from jax.experimental import pallas as pl
from jax.experimental.pallas import tpu as pltpu
from jax.sharding import PartitionSpec as P

TILE = 128
HEAD_DIM = 128
REACH = 32
PLANE = 4
GROUP = 4
ITEM = 8
PHASES = 3
MIB = 2**20
FAR_OFF = 1e30
VMEM = pl.BlockSpec(memory_space=pltpu.VMEM)
SMEM = pl.BlockSpec(memory_space=pltpu.SMEM)


def part_table(heads):
    table = np.zeros((PLANE, 2 * PLANE + 1, heads), np.int32)
    for place in range(PLANE):
        x, core = divmod(place, 2)
        for distance in range(-PLANE, PLANE + 1):
            plane, there = divmod(place + distance, PLANE)
            same_x, same_core = there // 2 == x, there % 2 == core
            other = 0 if same_core else 1
            if plane == 0 and same_x:
                phase, shard = 0, other
            elif plane == 0:
                phase, shard = 1, 3 + other
            elif not same_x:
                phase, shard = 2, other
            elif (plane < 0) == (core == 0):
                phase, shard = 1, other
            else:
                phase, shard = 1, 2
            table[place, distance + PLANE] = phase * 1024 + shard * heads + np.arange(heads)
    return table.reshape(-1)


def params(mib):
    return pltpu.CompilerParams(vmem_limit_bytes=mib * MIB)


def split_kernel(heads, flip, head_ref, *refs):
    count = len(flip)
    for step in range(heads):
        column = lax.rem(head_ref[0] + step, heads) * HEAD_DIM
        columns = pl.ds(pl.multiple_of(column, HEAD_DIM), HEAD_DIM)
        for which in range(count):
            for tile in range(refs[0].shape[0] // TILE):
                block = refs[which][pl.ds(tile * TILE, TILE), columns]
                block = block.T if flip[which] else block
                if step == 0:
                    refs[count][which, tile] = block
                else:
                    refs[count + 1][step - 1, which, tile] = block


def split_heads(head, arrays, flip, heads):
    tiles = arrays[0].shape[0] // TILE
    shape = (len(arrays), tiles, TILE, HEAD_DIM)
    dtype = arrays[0].dtype
    return pl.pallas_call(
        functools.partial(split_kernel, heads, flip),
        in_specs=[SMEM] + [VMEM] * len(arrays),
        out_specs=[VMEM] * 2,
        out_shape=[
            jax.ShapeDtypeStruct(shape, dtype),
            jax.ShapeDtypeStruct((heads - 1,) + shape, dtype),
        ],
        compiler_params=params(4),
    )(head, *arrays)


def join_kernel(heads, head_ref, *refs):
    out_ref = refs[-1]
    for step in range(heads):
        column = lax.rem(head_ref[0] + step, heads) * HEAD_DIM
        columns = pl.ds(pl.multiple_of(column, HEAD_DIM), HEAD_DIM)
        out_ref[:, columns] = refs[step][...]


def join_heads(head, pieces):
    rows = pieces[0].shape[0]
    heads = len(pieces)
    return pl.pallas_call(
        functools.partial(join_kernel, heads),
        in_specs=[SMEM] + [VMEM] * heads,
        out_specs=VMEM,
        out_shape=jax.ShapeDtypeStruct((rows, heads * HEAD_DIM), pieces[0].dtype),
        compiler_params=params(4),
    )(head, *pieces)


def list_kernel(heads, where_ref, lists_ref, live_ref, table_ref, numbers, *refs):
    lists, fill = refs[: PHASES + 1], refs[PHASES + 1]
    tiles = live_ref.shape[0]
    part_tiles = tiles // heads
    frame, head = where_ref[0], where_ref[1]
    base = lax.rem(frame, PLANE) * ((2 * PLANE + 1) * heads)
    for number in range(PHASES + 1):
        numbers[number] = 0
    for tile in range(tiles):
        part, inside = divmod(tile, part_tiles)
        row = lax.rem(head - part + heads, heads) * part_tiles + inside
        own = part == 0
        for number in range(PHASES):
            fill[number] = 0

        def slot_step(slot, carry, row=row, tile=tile, own=own):
            listed = lists_ref[row, slot]
            shard = lax.div(listed, tiles)
            within = listed - shard * tiles
            rank = lax.div(within, part_tiles)
            there = lax.rem(head - rank + heads, heads)
            entry = table_ref[base + (shard - frame + PLANE) * heads + there]
            phase = lax.div(entry, 1024)
            inside = within - rank * part_tiles
            place = (entry - phase * 1024) * (2 * part_tiles) + inside
            for number in range(PHASES):
                target = PHASES if own and number == PHASES - 1 else number
                first = part_tiles if target == PHASES - 1 else 0

                @pl.when(phase == number)
                def _():
                    filled = fill[number]
                    item = numbers[target]
                    ref = lists[target]

                    @pl.when(filled == 0)
                    def _():
                        ref[item * ITEM] = tile - first
                        for other in range(GROUP):
                            ref[item * ITEM + 2 + other] = place

                    ref[item * ITEM + 2 + filled] = place
                    ref[item * ITEM + 1] = filled + 1
                    full = filled == GROUP - 1
                    fill[number] = jnp.where(full, 0, filled + 1)
                    numbers[target] = jnp.where(full, item + 1, item)

            return carry

        lax.fori_loop(0, live_ref[row], slot_step, 0)
        for number in range(PHASES):
            target = PHASES if own and number == PHASES - 1 else number
            numbers[target] = numbers[target] + jnp.where(fill[number] > 0, 1, 0)
    for target in range(PHASES + 1):
        for other in range(2 * ITEM):
            lists[target][numbers[target] * ITEM + other] = 0


def work_lists(frame, head, tile_lists, live_slots, heads):
    tiles, slots = tile_lists.shape
    length = (tiles * (slots // GROUP + 1) + 2) * ITEM
    table = jnp.asarray(part_table(heads))
    return pl.pallas_call(
        functools.partial(list_kernel, heads),
        in_specs=[SMEM] * 4,
        out_specs=[SMEM] * (PHASES + 2),
        out_shape=[jax.ShapeDtypeStruct((PHASES + 1,), jnp.int32)]
        + [jax.ShapeDtypeStruct((length,), jnp.int32)] * (PHASES + 1),
        scratch_shapes=[pltpu.SMEM((PHASES,), jnp.int32)],
        compiler_params=params(4),
        cost_estimate=pl.CostEstimate(flops=0, bytes_accessed=2**22, transcendentals=0),
    )(jnp.stack((frame, head)), tile_lists, live_slots, table)


def phase_kernel(which, offset, first, pieces, begins, ends, numbers, items, q_ref, *refs):
    refs = list(refs)
    state = [refs.pop(0) for _ in range(0 if begins else 3)]
    parts = [refs.pop(0) for _ in range(pieces)]
    out_ref = refs.pop(0) if ends else None
    top_ref, total_ref, sum_ref = [refs.pop(0) for _ in range(3)]
    scores, high = refs.pop(0), refs.pop(0)
    window = refs.pop(0) if pieces > 1 else parts[0]
    tiles = q_ref.shape[0]
    factor = math.log2(math.e) / math.sqrt(HEAD_DIM)

    if pieces > 1:
        at = 0
        for part in parts:
            window[at : at + part.shape[0]] = part[...]
            at += part.shape[0]
    if begins:
        top_ref[...] = jnp.full(top_ref.shape, -FAR_OFF, jnp.float32)
        total_ref[...] = jnp.zeros(total_ref.shape, jnp.float32)
        sum_ref[...] = jnp.zeros(sum_ref.shape, jnp.float32)
    else:
        for ref, old in zip((top_ref, total_ref, sum_ref), state):
            ref[...] = old[first : first + tiles]

    def score(item):
        keys = [window[items[item * ITEM + 2 + slot]] for slot in range(GROUP)]
        block = jnp.dot(
            jnp.concatenate(keys), q_ref[items[item * ITEM]], preferred_element_type=jnp.float32
        )
        top = jnp.max(block.reshape(-1, 8, TILE), axis=0)
        return block, jnp.max(top, axis=0, keepdims=True)

    def weigh(item, block, peak):
        tile, live = items[item * ITEM], items[item * ITEM + 1]
        old = top_ref[tile]
        top = jnp.maximum(old, jnp.where(live > 0, peak, -FAR_OFF))
        shrink = jnp.exp2((old - top) * factor)
        total = total_ref[tile] * shrink
        weights, values = [], []
        for slot in range(GROUP):
            shift = jnp.where(slot < live, top, FAR_OFF)
            weight = jnp.exp2((block[slot * TILE : (slot + 1) * TILE] - shift) * factor)
            total = total + jnp.sum(weight.reshape(-1, 8, TILE), axis=0)
            weights.append(weight.astype(jnp.bfloat16))
            values.append(window[items[item * ITEM + 2 + slot] + offset])
        weighted = jnp.dot(
            jnp.concatenate(values, axis=1),
            jnp.concatenate(weights),
            preferred_element_type=jnp.float32,
        )
        top_ref[tile] = top
        total_ref[tile] = total
        sum_ref[tile] = sum_ref[tile] * shrink + weighted

    scores[...], high[...] = score(0)

    def step(pair, carry):
        here, peak_here = scores[...], high[...]
        later, peak_later = score(2 * pair + 1)
        weigh(2 * pair, here, peak_here)
        following, peak_following = score(2 * pair + 2)
        weigh(2 * pair + 1, later, peak_later)
        scores[...], high[...] = following, peak_following
        return carry

    lax.fori_loop(0, lax.div(numbers[which] + 1, 2), step, 0)
    if ends:
        for tile in range(tiles):
            total = jnp.sum(total_ref[tile], axis=0, keepdims=True)
            out_ref[tile] = (sum_ref[tile] / total).T.astype(out_ref.dtype)


def attend(lists, which, queries, state, pieces, offset, first, ends):
    tiles = queries.shape[0]
    begins = state is None
    windows = sum(piece.shape[0] for piece in pieces)
    held = [
        jax.ShapeDtypeStruct((tiles, 1, TILE), jnp.float32),
        jax.ShapeDtypeStruct((tiles, 8, TILE), jnp.float32),
        jax.ShapeDtypeStruct((tiles, HEAD_DIM, TILE), jnp.float32),
    ]
    scratch = [
        pltpu.VMEM((GROUP * TILE, TILE), jnp.float32),
        pltpu.VMEM((1, TILE), jnp.float32),
    ]
    if len(pieces) > 1:
        scratch.append(pltpu.VMEM((windows, TILE, TILE), queries.dtype))
    out = jax.ShapeDtypeStruct(queries.shape, queries.dtype)
    pairs = tiles * windows * TILE * TILE // 8
    return pl.pallas_call(
        functools.partial(phase_kernel, which, offset, first, len(pieces), begins, ends),
        in_specs=[SMEM] * 2 + [VMEM] * (1 + len(pieces) + (0 if begins else 3)),
        out_specs=VMEM if ends else [VMEM] * 3,
        out_shape=out if ends else held,
        scratch_shapes=([pltpu.VMEM(h.shape, h.dtype) for h in held] if ends else []) + scratch,
        compiler_params=params(14),
        cost_estimate=pl.CostEstimate(
            flops=4 * pairs * HEAD_DIM, bytes_accessed=windows * 2**15, transcendentals=pairs
        ),
    )(lists[0], lists[1 + which], queries, *([] if begins else state), *pieces)


def moved(block, axis, source):
    size = lax.axis_size(axis)
    route = [(source(i), i) for i in range(size) if 0 <= source(i) < size]
    return lax.ppermute(block, axis, route)


def body(queries, key_vectors, value_vectors, tile_lists, live_slots):
    heads = lax.axis_size("head")
    frame = lax.axis_index("frame")
    head = lax.axis_index("head")
    head_ref = head[None]
    place = lax.rem(frame, PLANE)
    shard_tiles = tile_lists.shape[1]
    part_tiles = shard_tiles // heads
    assert shard_tiles * PLANE == REACH and lax.axis_size("frame") % PLANE == 0

    def head_swap(blocks):
        return [
            moved(blocks[step - 1], "head", lambda i: (i - step) % heads)
            for step in range(1, heads)
        ]

    def core_swap(block):
        return moved(block, "frame", lambda i: i ^ 1)

    def tiled(block):
        return block.reshape(-1, TILE, TILE)

    keep, send = split_heads(head_ref, (key_vectors, value_vectors), (False, True), heads)
    received = jnp.concatenate([tiled(block) for block in head_swap(send)])
    lists = work_lists(frame, head, tile_lists[0], live_slots[0], heads)
    q_keep, q_send = split_heads(head_ref, (queries,), (True,), heads)
    received, lists, q_send = lax.optimization_barrier((received, lists, q_send))
    own = jnp.concatenate((tiled(keep), received))

    across = moved(own, "frame", lambda i: i ^ 2)
    chip = jnp.concatenate((own, core_swap(own)))
    level = moved(chip, "frame", lambda i: i - PLANE if i % 2 == 0 else i + PLANE)
    q_parts = jnp.concatenate([tiled(q_keep)] + [tiled(block) for block in head_swap(q_send)])

    state = attend(lists, 0, q_parts, None, [chip], part_tiles, 0, False)
    level, across, state = lax.optimization_barrier((level, across, state))
    shard = own.shape[0]
    cut = shard * 5 // 8
    far_z = moved(
        across[:cut], "frame", lambda i: i - PLANE if i % PLANE < 2 else i + PLANE
    )
    level_core = core_swap(level[shard:])
    whole = (place == 1) | (place == 2)
    far_x = moved(jnp.where(whole, level[cut:shard], level_core[cut:]), "frame", lambda i: i ^ 2)
    pieces = [level, level_core, across, core_swap(across)]
    state = attend(lists, 1, q_parts, state, pieces, part_tiles, 0, False)
    far = jnp.concatenate((far_z, far_x))
    far, state = lax.optimization_barrier((far, state))
    pieces = [far, core_swap(far)]
    rest = attend(
        lists, 2, q_parts[part_tiles:], state, pieces, part_tiles, part_tiles, True
    )
    outs = [None]
    for step in range(1, heads):
        sent = rest[(step - 1) * part_tiles : step * part_tiles]
        outs.append(moved(sent, "head", lambda i: (i + step) % heads))
    outs[0] = attend(lists, 3, q_parts[:part_tiles], state, pieces, part_tiles, 0, True)
    return join_heads(head_ref, [o.reshape(-1, HEAD_DIM) for o in outs])


def solution(mesh):
    placed = (
        P(("frame", "head"), None),
        P(("frame", "head"), None),
        P(("frame", "head"), None),
        P("head", "frame", None),
        P("head", "frame"),
    )
    return jax.shard_map(
        body, mesh=mesh, in_specs=placed, out_specs=P(("frame", "head"), None), check_vma=False
    )
```

```python
import functools
import math

import jax
import jax.numpy as jnp
import numpy as np
from jax import lax
from jax.experimental import pallas as pl
from jax.experimental.pallas import tpu as pltpu
from jax.sharding import PartitionSpec as P

TILE = 128
HEAD_DIM = 128
REACH = 32
PLANE = 4
GROUP = 4
ITEM = 8
PHASES = 2
MIB = 2**20
FAR_OFF = 1e30
VMEM = pl.BlockSpec(memory_space=pltpu.VMEM)
SMEM = pl.BlockSpec(memory_space=pltpu.SMEM)


def part_table(heads):
    rest = heads - 1
    table = np.zeros((PLANE, 2 * PLANE + 1, heads), np.int32)
    for place in range(PLANE):
        x, core = divmod(place, 2)
        for distance in range(-PLANE, PLANE + 1):
            plane, there = divmod(place + distance, PLANE)
            same_x, same_core = there // 2 == x, there % 2 == core
            for part in range(heads):
                late = part - 1
                pair = int(same_core) if part == 0 else 2 + rest * int(same_core) + late
                phase = 0
                if plane == 0 and same_x:
                    spot = pair
                elif plane == 0:
                    spot = (4 if same_core else 6) * heads + part
                elif not same_x:
                    phase, spot = 1, part + (0 if same_core else heads)
                elif (plane < 0) == (core == 0):
                    spot = 2 * heads + pair
                else:
                    spot = 5 * heads + part
                table[place, distance + PLANE, part] = phase * 1024 + spot
    return table.reshape(-1)


def params(mib):
    return pltpu.CompilerParams(vmem_limit_bytes=mib * MIB)


def split_kernel(heads, head_ref, k_ref, v_ref, q_ref, keep, send, k_in, v_in, q_in, ready):
    copies = [
        pltpu.make_async_copy(source, target, ready.at[number])
        for number, (source, target) in enumerate(((k_ref, k_in), (v_ref, v_in), (q_ref, q_in)))
    ]
    for copy in copies:
        copy.start()
    tiles = k_in.shape[0] // TILE
    for which, block_ref in enumerate((k_in, v_in, q_in)):
        copies[which].wait()
        for step in range(heads):
            column = lax.rem(head_ref[0] + step, heads) * HEAD_DIM
            columns = pl.ds(pl.multiple_of(column, HEAD_DIM), HEAD_DIM)
            for tile in range(tiles):
                block = block_ref[pl.ds(tile * TILE, TILE), columns]
                block = block if which == 0 else block.T
                if step == 0:
                    keep[which * tiles + tile] = block
                else:
                    send[step - 1, which * tiles + tile] = block


def split_heads(head, arrays, heads):
    rows, width = arrays[0].shape
    tiles = rows // TILE
    dtype = arrays[0].dtype
    return pl.pallas_call(
        functools.partial(split_kernel, heads),
        in_specs=[SMEM] + [pl.BlockSpec(memory_space=pltpu.HBM)] * 3,
        out_specs=[VMEM] * 2,
        out_shape=[
            jax.ShapeDtypeStruct((3 * tiles, TILE, HEAD_DIM), dtype),
            jax.ShapeDtypeStruct((heads - 1, 3 * tiles, TILE, HEAD_DIM), dtype),
        ],
        scratch_shapes=[pltpu.VMEM((rows, width), dtype)] * 3 + [pltpu.SemaphoreType.DMA((3,))],
        compiler_params=params(6),
    )(head, *arrays)


def join_kernel(heads, head_ref, *refs):
    out_ref = refs[-1]
    for step in range(heads):
        column = lax.rem(head_ref[0] + step, heads) * HEAD_DIM
        columns = pl.ds(pl.multiple_of(column, HEAD_DIM), HEAD_DIM)
        out_ref[:, columns] = refs[step][...]


def join_heads(head, pieces):
    rows = pieces[0].shape[0]
    heads = len(pieces)
    return pl.pallas_call(
        functools.partial(join_kernel, heads),
        in_specs=[SMEM] + [VMEM] * heads,
        out_specs=VMEM,
        out_shape=jax.ShapeDtypeStruct((rows, heads * HEAD_DIM), pieces[0].dtype),
        compiler_params=params(4),
    )(head, *pieces)


def list_kernel(heads, length, where_ref, lists_ref, live_ref, table_ref, numbers, items, fill):
    tiles = live_ref.shape[0]
    part_tiles = tiles // heads
    frame, head = where_ref[0], where_ref[1]
    base = (lax.rem(frame, PLANE) * (2 * PLANE + 1) + PLANE - frame) * heads
    for target in range(PHASES + 1):
        numbers[target] = 0
    for tile in range(tiles):
        part, inside = divmod(tile, part_tiles)
        row = ((head - part) & (heads - 1)) * part_tiles + inside
        for target in range(PHASES + 1):
            fill[target] = 0

        def slot_step(slot, carry, row=row, tile=tile, part=part):
            listed = lists_ref[row, slot]
            shard = listed >> int(math.log2(tiles))
            within = listed & (tiles - 1)
            rank = within >> int(math.log2(part_tiles))
            entry = table_ref[base + shard * heads + ((head - rank) & (heads - 1))]
            phase = entry >> 10
            place = (entry & 1023) * (2 * part_tiles) + (within & (part_tiles - 1))
            last = phase == PHASES - 1
            target = jnp.where(last, PHASES, phase) if part == 0 else phase
            inner = tile if part == 0 else jnp.where(last, tile - part_tiles, tile)
            filled, item = fill[target], numbers[target]
            at = target * length + item * ITEM
            items[at] = inner
            items[at + 1] = filled + 1
            for other in range(GROUP):
                items[at + 2 + jnp.minimum(filled + other, GROUP - 1)] = place
            full = filled == GROUP - 1
            fill[target] = jnp.where(full, 0, filled + 1)
            numbers[target] = jnp.where(full, item + 1, item)
            return carry

        lax.fori_loop(0, live_ref[row], slot_step, 0)
        for target in range(PHASES + 1):
            numbers[target] = numbers[target] + jnp.where(fill[target] > 0, 1, 0)
    for target in range(PHASES + 1):
        for other in range(3 * ITEM):
            items[target * length + numbers[target] * ITEM + other] = 0


def work_lists(frame, head, tile_lists, live_slots, heads):
    tiles, slots = tile_lists.shape
    assert tiles & (tiles - 1) == 0 and heads & (heads - 1) == 0
    length = (tiles * (slots // GROUP + 1) + 3) * ITEM
    table = jnp.asarray(part_table(heads))
    return pl.pallas_call(
        functools.partial(list_kernel, heads, length),
        in_specs=[SMEM] * 4,
        out_specs=[SMEM] * 2,
        out_shape=[
            jax.ShapeDtypeStruct((PHASES + 1,), jnp.int32),
            jax.ShapeDtypeStruct(((PHASES + 1) * length,), jnp.int32),
        ],
        scratch_shapes=[pltpu.SMEM((PHASES + 1,), jnp.int32)],
        compiler_params=params(4),
        cost_estimate=pl.CostEstimate(flops=0, bytes_accessed=0, transcendentals=0),
    )(jnp.stack((frame, head)), tile_lists, live_slots, table)


def phase_kernel(which, offset, first, begins, ends, numbers, items, q_ref, window, *refs):
    refs = list(refs)
    state = [refs.pop(0) for _ in range(0 if begins else 3)]
    out_ref = refs.pop(0) if ends else None
    top_ref, total_ref, sum_ref, scores, high, weights, shrinks = refs
    tiles = q_ref.shape[0]
    factor = math.log2(math.e) / math.sqrt(HEAD_DIM)
    base = which * (items.shape[0] // (PHASES + 1))

    if begins:
        top_ref[...] = jnp.full(top_ref.shape, -FAR_OFF, jnp.float32)
        total_ref[...] = jnp.zeros(total_ref.shape, jnp.float32)
        sum_ref[...] = jnp.zeros(sum_ref.shape, jnp.float32)
    else:
        for ref, old in zip((top_ref, total_ref, sum_ref), state):
            ref[...] = old[first : first + tiles]

    def score(item):
        at = base + item * ITEM
        keys = [window[items[at + 2 + slot]] for slot in range(GROUP)]
        block = jnp.dot(
            jnp.concatenate(keys), q_ref[items[at]], preferred_element_type=jnp.float32
        )
        top = jnp.max(block.reshape(-1, 8, TILE), axis=0)
        return block, jnp.max(top, axis=0, keepdims=True)

    def weigh(item, block, peak):
        at = base + item * ITEM
        tile, live = items[at], items[at + 1]
        old = top_ref[tile]
        top = jnp.maximum(old, jnp.where(live > 0, peak, -FAR_OFF))
        shrink = jnp.exp2((old - top) * factor)
        total = total_ref[tile] * shrink
        parts = []
        for slot in range(GROUP):
            shift = jnp.where(slot < live, top, FAR_OFF)
            weight = jnp.exp2((block[slot * TILE : (slot + 1) * TILE] - shift) * factor)
            total = total + jnp.sum(weight.reshape(-1, 8, TILE), axis=0)
            parts.append(weight.astype(jnp.bfloat16))
        top_ref[tile] = top
        total_ref[tile] = total
        return jnp.concatenate(parts), shrink

    def collect(item, weight, shrink):
        at = base + item * ITEM
        values = [window[items[at + 2 + slot] + offset] for slot in range(GROUP)]
        product = jnp.dot(
            jnp.concatenate(values, axis=1), weight, preferred_element_type=jnp.float32
        )
        sum_ref[items[at]] = sum_ref[items[at]] * shrink + product

    block, peak = score(0)
    scores[...], high[...] = score(1)
    weights[...], shrinks[...] = weigh(0, block, peak)

    def step(pair, carry):
        item = 2 * pair
        block, peak, weight, shrink = scores[...], high[...], weights[...], shrinks[...]
        block_2, peak_2 = score(item + 2)
        weight_1, shrink_1 = weigh(item + 1, block, peak)
        collect(item, weight, shrink)
        block_3, peak_3 = score(item + 3)
        weight_2, shrink_2 = weigh(item + 2, block_2, peak_2)
        collect(item + 1, weight_1, shrink_1)
        scores[...], high[...] = block_3, peak_3
        weights[...], shrinks[...] = weight_2, shrink_2
        return carry

    lax.fori_loop(0, (numbers[which] + 1) >> 1, step, 0)
    if ends:
        for tile in range(tiles):
            total = jnp.sum(total_ref[tile], axis=0, keepdims=True)
            out_ref[tile] = (sum_ref[tile] / total).T.astype(out_ref.dtype)


def attend(lists, which, queries, state, window, offset, first, ends):
    tiles = queries.shape[0]
    begins = state is None
    held = [
        jax.ShapeDtypeStruct((tiles, 1, TILE), jnp.float32),
        jax.ShapeDtypeStruct((tiles, 8, TILE), jnp.float32),
        jax.ShapeDtypeStruct((tiles, HEAD_DIM, TILE), jnp.float32),
    ]
    scratch = [
        pltpu.VMEM((GROUP * TILE, TILE), jnp.float32),
        pltpu.VMEM((1, TILE), jnp.float32),
        pltpu.VMEM((GROUP * TILE, TILE), queries.dtype),
        pltpu.VMEM((1, TILE), jnp.float32),
    ]
    out = jax.ShapeDtypeStruct(queries.shape, queries.dtype)
    return pl.pallas_call(
        functools.partial(phase_kernel, which, offset, first, begins, ends),
        in_specs=[SMEM] * 2 + [VMEM] * (2 if begins else 5),
        out_specs=VMEM if ends else [VMEM] * 3,
        out_shape=out if ends else held,
        scratch_shapes=([pltpu.VMEM(h.shape, h.dtype) for h in held] if ends else []) + scratch,
        compiler_params=params(14),
        cost_estimate=pl.CostEstimate(flops=0, bytes_accessed=0, transcendentals=0),
    )(*lists, queries, window, *([] if begins else state))


def moved(block, axis, source):
    size = lax.axis_size(axis)
    route = [(source(i), i) for i in range(size) if 0 <= source(i) < size]
    return lax.ppermute(block, axis, route)


def body(queries, key_vectors, value_vectors, tile_lists, live_slots):
    heads = lax.axis_size("head")
    frame = lax.axis_index("frame")
    head = lax.axis_index("head")
    head_ref = head[None]
    place = lax.rem(frame, PLANE)
    shard_tiles = tile_lists.shape[1]
    part_tiles = shard_tiles // heads
    assert shard_tiles * PLANE == REACH and lax.axis_size("frame") % PLANE == 0

    def core_swap(*blocks):
        return moved(jnp.concatenate(blocks), "frame", lambda i: i ^ 1)

    def along_z(pair):
        return moved(pair, "frame", lambda i: i - PLANE if i % 2 == 0 else i + PLANE)

    def along_x(block):
        return moved(block, "frame", lambda i: i ^ 2)

    size = 2 * part_tiles
    keep, send = split_heads(head_ref, (key_vectors, value_vectors, queries), heads)
    received = [
        moved(send[step - 1], "head", lambda i: (i - step) % heads) for step in range(1, heads)
    ]
    q_parts = jnp.concatenate([block[size:] for block in [keep] + received])

    early = keep[:size]
    chip_early = jnp.concatenate((core_swap(early), early))
    level_early = along_z(chip_early)
    across_early = along_x(early)

    late = jnp.concatenate([block[:size] for block in received])
    late, across_early = lax.optimization_barrier((late, across_early))
    chip_late = jnp.concatenate((core_swap(late), late))
    level_late = along_z(chip_late)
    across_late = along_x(late)

    rest = late.shape[0]
    level_core_early = core_swap(level_early[:size])
    whole = (place == 1) | (place == 2)
    far_early = along_x(jnp.where(whole, level_early[size:], level_core_early))

    listed, live, _ = lax.optimization_barrier((tile_lists[0], live_slots[0], chip_late))
    lists = work_lists(frame, head, listed, live, heads)
    level_late, across_late, lists = lax.optimization_barrier((level_late, across_late, lists))
    far_late = moved(
        across_late, "frame", lambda i: i - PLANE if i % PLANE < 2 else i + PLANE
    )
    swapped = core_swap(level_late[:rest], across_early, across_late)
    near = chip_early, chip_late, level_early, level_late, across_early, across_late
    window = jnp.concatenate(near + (level_core_early, swapped))
    state = attend(lists, 0, q_parts, None, window, part_tiles, 0, False)
    far, state = lax.optimization_barrier(((far_early, far_late), state))
    window = jnp.concatenate(far + (core_swap(*far),))
    rest = attend(lists, 1, q_parts[part_tiles:], state, window, part_tiles, part_tiles, True)
    outs = [None]
    for step in range(1, heads):
        sent = rest[(step - 1) * part_tiles : step * part_tiles]
        outs.append(moved(sent, "head", lambda i: (i + step) % heads))
    outs[0] = attend(lists, 2, q_parts[:part_tiles], state, window, part_tiles, 0, True)
    return join_heads(head_ref, [o.reshape(-1, HEAD_DIM) for o in outs])


def solution(mesh):
    placed = (
        P(("frame", "head"), None),
        P(("frame", "head"), None),
        P(("frame", "head"), None),
        P("head", "frame", None),
        P("head", "frame"),
    )
    return jax.shard_map(
        body, mesh=mesh, in_specs=placed, out_specs=P(("frame", "head"), None), check_vma=False
    )
```

```python
import functools
import math

import jax
import jax.numpy as jnp
import numpy as np
from jax import lax
from jax.experimental import pallas as pl
from jax.experimental.pallas import tpu as pltpu
from jax.sharding import PartitionSpec as P

TILE = 128
HEAD_DIM = 128
REACH = 32
PLANE = 4
GROUP = 4
ITEM = 8
PHASES = 3
MIB = 2**20
FAR_OFF = 1e30
VMEM = pl.BlockSpec(memory_space=pltpu.VMEM)
SMEM = pl.BlockSpec(memory_space=pltpu.SMEM)


def part_table(heads):
    rest = heads - 1
    table = np.zeros((PLANE, 2 * PLANE + 1, heads), np.int32)
    for place in range(PLANE):
        x, core = divmod(place, 2)
        for distance in range(-PLANE, PLANE + 1):
            plane, there = divmod(place + distance, PLANE)
            same_x, same_core = there // 2 == x, there % 2 == core
            for part in range(heads):
                late = part - 1
                first = part == 0
                pair = int(same_core) if first else 2 + rest * int(same_core) + late
                if plane == 0 and same_x:
                    phase, spot = 0, pair
                elif plane == 0 and same_core:
                    phase, spot = (0, 2 * heads + 2) if first else (1, 2 * rest + late)
                elif plane == 0:
                    phase, spot = (0, 2 * heads + 4) if first else (2, rest + late)
                elif not same_x and same_core:
                    phase, spot = 1, 3 * rest + part
                elif not same_x:
                    phase, spot = 2, 2 * rest + part
                elif (plane < 0) == (core == 0):
                    phase, spot = (0, 2 * heads + pair) if first else (1, pair - 2)
                else:
                    phase, spot = (0, 2 * heads + 3) if first else (2, late)
                table[place, distance + PLANE, part] = phase * 1024 + spot
    return table.reshape(-1)


def params(mib):
    return pltpu.CompilerParams(vmem_limit_bytes=mib * MIB)


def split_kernel(heads, flip, head_ref, *refs):
    ins, keep, send = refs[: len(flip)], refs[-2], refs[-1]
    tiles = ins[0].shape[0] // TILE
    for which, flipped in enumerate(flip):
        for step in range(heads):
            column = lax.rem(head_ref[0] + step, heads) * HEAD_DIM
            columns = pl.ds(pl.multiple_of(column, HEAD_DIM), HEAD_DIM)
            for tile in range(tiles):
                block = ins[which][pl.ds(tile * TILE, TILE), columns]
                block = block.T if flipped else block
                if step == 0:
                    keep[which * tiles + tile] = block
                else:
                    send[step - 1, which * tiles + tile] = block


def split_heads(head, arrays, flip, heads):
    tiles = len(arrays) * arrays[0].shape[0] // TILE
    dtype = arrays[0].dtype
    return pl.pallas_call(
        functools.partial(split_kernel, heads, flip),
        in_specs=[SMEM] + [VMEM] * len(arrays),
        out_specs=[VMEM] * 2,
        out_shape=[
            jax.ShapeDtypeStruct((tiles, TILE, HEAD_DIM), dtype),
            jax.ShapeDtypeStruct((heads - 1, tiles, TILE, HEAD_DIM), dtype),
        ],
        compiler_params=params(4),
    )(head, *arrays)


def join_kernel(heads, head_ref, *refs):
    out_ref = refs[-1]
    for step in range(heads):
        column = lax.rem(head_ref[0] + step, heads) * HEAD_DIM
        columns = pl.ds(pl.multiple_of(column, HEAD_DIM), HEAD_DIM)
        out_ref[:, columns] = refs[step][...]


def join_heads(head, pieces):
    rows = pieces[0].shape[0]
    heads = len(pieces)
    return pl.pallas_call(
        functools.partial(join_kernel, heads),
        in_specs=[SMEM] + [VMEM] * heads,
        out_specs=VMEM,
        out_shape=jax.ShapeDtypeStruct((rows, heads * HEAD_DIM), pieces[0].dtype),
        compiler_params=params(4),
    )(head, *pieces)


def list_kernel(heads, length, where_ref, lists_ref, live_ref, table_ref, numbers, items, fill):
    tiles = live_ref.shape[0]
    part_tiles = tiles // heads
    frame, head = where_ref[0], where_ref[1]
    base = (lax.rem(frame, PLANE) * (2 * PLANE + 1) + PLANE - frame) * heads
    for target in range(PHASES + 1):
        numbers[target] = 0
    for tile in range(tiles):
        part, inside = divmod(tile, part_tiles)
        row = ((head - part) & (heads - 1)) * part_tiles + inside
        for target in range(PHASES + 1):
            fill[target] = 0

        def slot_step(slot, carry, row=row, tile=tile, part=part):
            listed = lists_ref[row, slot]
            shard = listed >> int(math.log2(tiles))
            within = listed & (tiles - 1)
            rank = within >> int(math.log2(part_tiles))
            entry = table_ref[base + shard * heads + ((head - rank) & (heads - 1))]
            phase = entry >> 10
            place = (entry & 1023) * (2 * part_tiles) + (within & (part_tiles - 1))
            last = phase == PHASES - 1
            target = jnp.where(last, PHASES, phase) if part == 0 else phase
            inner = tile if part == 0 else jnp.where(last, tile - part_tiles, tile)
            filled, item = fill[target], numbers[target]
            at = target * length + item * ITEM
            items[at] = inner
            items[at + 1] = filled + 1
            for other in range(GROUP):
                items[at + 2 + jnp.minimum(filled + other, GROUP - 1)] = place
            full = filled == GROUP - 1
            fill[target] = jnp.where(full, 0, filled + 1)
            numbers[target] = jnp.where(full, item + 1, item)
            return carry

        lax.fori_loop(0, live_ref[row], slot_step, 0)
        for target in range(PHASES + 1):
            numbers[target] = numbers[target] + jnp.where(fill[target] > 0, 1, 0)
    for target in range(PHASES + 1):
        for other in range(3 * ITEM):
            items[target * length + numbers[target] * ITEM + other] = 0


def work_lists(frame, head, tile_lists, live_slots, heads):
    tiles, slots = tile_lists.shape
    assert tiles & (tiles - 1) == 0 and heads & (heads - 1) == 0
    length = (tiles * (slots // GROUP + 1) + 3) * ITEM
    table = jnp.asarray(part_table(heads))
    return pl.pallas_call(
        functools.partial(list_kernel, heads, length),
        in_specs=[SMEM] * 4,
        out_specs=[SMEM] * 2,
        out_shape=[
            jax.ShapeDtypeStruct((PHASES + 1,), jnp.int32),
            jax.ShapeDtypeStruct(((PHASES + 1) * length,), jnp.int32),
        ],
        scratch_shapes=[pltpu.SMEM((PHASES + 1,), jnp.int32)],
        compiler_params=params(4),
        cost_estimate=pl.CostEstimate(flops=0, bytes_accessed=0, transcendentals=0),
    )(jnp.stack((frame, head)), tile_lists, live_slots, table)


def phase_kernel(which, offset, first, pieces, begins, ends, numbers, items, q_ref, *refs):
    refs = list(refs)
    state = [refs.pop(0) for _ in range(0 if begins else 3)]
    parts = [refs.pop(0) for _ in range(pieces)]
    out_ref = refs.pop(0) if ends else None
    top_ref, total_ref, sum_ref, scores, high, weights, shrinks, window = refs
    tiles = q_ref.shape[0]
    factor = math.log2(math.e) / math.sqrt(HEAD_DIM)
    base = which * (items.shape[0] // (PHASES + 1))

    at = 0
    for part in parts:
        window[at : at + part.shape[0]] = part[...]
        at += part.shape[0]
    if begins:
        top_ref[...] = jnp.full(top_ref.shape, -FAR_OFF, jnp.float32)
        total_ref[...] = jnp.zeros(total_ref.shape, jnp.float32)
        sum_ref[...] = jnp.zeros(sum_ref.shape, jnp.float32)
    else:
        for ref, old in zip((top_ref, total_ref, sum_ref), state):
            ref[...] = old[first : first + tiles]

    def score(item):
        at = base + item * ITEM
        keys = [window[items[at + 2 + slot]] for slot in range(GROUP)]
        block = jnp.dot(
            jnp.concatenate(keys), q_ref[items[at]], preferred_element_type=jnp.float32
        )
        top = jnp.max(block.reshape(-1, 8, TILE), axis=0)
        return block, jnp.max(top, axis=0, keepdims=True)

    def weigh(item, block, peak):
        at = base + item * ITEM
        tile, live = items[at], items[at + 1]
        old = top_ref[tile]
        top = jnp.maximum(old, jnp.where(live > 0, peak, -FAR_OFF))
        shrink = jnp.exp2((old - top) * factor)
        total = total_ref[tile] * shrink
        parts = []
        for slot in range(GROUP):
            shift = jnp.where(slot < live, top, FAR_OFF)
            weight = jnp.exp2((block[slot * TILE : (slot + 1) * TILE] - shift) * factor)
            total = total + jnp.sum(weight.reshape(-1, 8, TILE), axis=0)
            parts.append(weight.astype(jnp.bfloat16))
        top_ref[tile] = top
        total_ref[tile] = total
        return jnp.concatenate(parts), shrink

    def collect(item, weight, shrink):
        at = base + item * ITEM
        values = [window[items[at + 2 + slot] + offset] for slot in range(GROUP)]
        product = jnp.dot(
            jnp.concatenate(values, axis=1), weight, preferred_element_type=jnp.float32
        )
        sum_ref[items[at]] = sum_ref[items[at]] * shrink + product

    block, peak = score(0)
    scores[...], high[...] = score(1)
    weights[...], shrinks[...] = weigh(0, block, peak)

    def step(pair, carry):
        item = 2 * pair
        block, peak, weight, shrink = scores[...], high[...], weights[...], shrinks[...]
        block_2, peak_2 = score(item + 2)
        weight_1, shrink_1 = weigh(item + 1, block, peak)
        collect(item, weight, shrink)
        block_3, peak_3 = score(item + 3)
        weight_2, shrink_2 = weigh(item + 2, block_2, peak_2)
        collect(item + 1, weight_1, shrink_1)
        scores[...], high[...] = block_3, peak_3
        weights[...], shrinks[...] = weight_2, shrink_2
        return carry

    lax.fori_loop(0, (numbers[which] + 1) >> 1, step, 0)
    if ends:
        for tile in range(tiles):
            total = jnp.sum(total_ref[tile], axis=0, keepdims=True)
            out_ref[tile] = (sum_ref[tile] / total).T.astype(out_ref.dtype)


def attend(lists, which, queries, state, pieces, offset, first, ends):
    tiles = queries.shape[0]
    begins = state is None
    held = [
        jax.ShapeDtypeStruct((tiles, 1, TILE), jnp.float32),
        jax.ShapeDtypeStruct((tiles, 8, TILE), jnp.float32),
        jax.ShapeDtypeStruct((tiles, HEAD_DIM, TILE), jnp.float32),
    ]
    scratch = [
        pltpu.VMEM((GROUP * TILE, TILE), jnp.float32),
        pltpu.VMEM((1, TILE), jnp.float32),
        pltpu.VMEM((GROUP * TILE, TILE), queries.dtype),
        pltpu.VMEM((1, TILE), jnp.float32),
        pltpu.VMEM((sum(piece.shape[0] for piece in pieces), TILE, TILE), queries.dtype),
    ]
    out = jax.ShapeDtypeStruct(queries.shape, queries.dtype)
    return pl.pallas_call(
        functools.partial(phase_kernel, which, offset, first, len(pieces), begins, ends),
        in_specs=[SMEM] * 2 + [VMEM] * (1 + len(pieces) + (0 if begins else 3)),
        out_specs=VMEM if ends else [VMEM] * 3,
        out_shape=out if ends else held,
        scratch_shapes=([pltpu.VMEM(h.shape, h.dtype) for h in held] if ends else []) + scratch,
        compiler_params=params(14),
        cost_estimate=pl.CostEstimate(flops=0, bytes_accessed=0, transcendentals=0),
    )(*lists, queries, *([] if begins else state), *pieces)


def moved(block, axis, source):
    size = lax.axis_size(axis)
    route = [(source(i), i) for i in range(size) if 0 <= source(i) < size]
    return lax.ppermute(block, axis, route)


def body(queries, key_vectors, value_vectors, tile_lists, live_slots):
    heads = lax.axis_size("head")
    frame = lax.axis_index("frame")
    head = lax.axis_index("head")
    head_ref = head[None]
    place = lax.rem(frame, PLANE)
    shard_tiles = tile_lists.shape[1]
    part_tiles = shard_tiles // heads
    assert shard_tiles * PLANE == REACH and lax.axis_size("frame") % PLANE == 0

    def core_swap(*blocks):
        return moved(jnp.concatenate(blocks), "frame", lambda i: i ^ 1)

    def along_z(pair):
        return moved(pair, "frame", lambda i: i - PLANE if i % 2 == 0 else i + PLANE)

    def along_x(block):
        return moved(block, "frame", lambda i: i ^ 2)

    def head_swap(blocks):
        return [
            moved(blocks[step - 1], "head", lambda i: (i - step) % heads)
            for step in range(1, heads)
        ]

    size = 2 * part_tiles
    early, send = split_heads(head_ref, (key_vectors, value_vectors), (False, True), heads)
    chip_early = jnp.concatenate((core_swap(early), early))
    level_early = along_z(chip_early)
    across_early = along_x(early)

    late, across_early = lax.optimization_barrier(
        (jnp.concatenate(head_swap(send)), across_early)
    )
    chip_late = jnp.concatenate((core_swap(late), late))
    level_late = along_z(chip_late)
    across_late = along_x(late)

    listed, live, queries, _ = lax.optimization_barrier(
        (tile_lists[0], live_slots[0], queries, chip_late)
    )
    q_keep, q_send = split_heads(head_ref, (queries,), (True,), heads)
    q_parts = jnp.concatenate([q_keep] + head_swap(q_send))
    lists = work_lists(frame, head, listed, live, heads)

    level_early, across_early, _ = lax.optimization_barrier(
        (level_early, across_early, chip_late)
    )
    swapped = core_swap(level_early[:size], across_early)
    whole = (place == 1) | (place == 2)
    far_early = along_x(jnp.where(whole, level_early[size:], swapped[:size]))
    far_late = moved(
        across_late, "frame", lambda i: i - PLANE if i % PLANE < 2 else i + PLANE
    )
    pieces = [chip_early, chip_late, level_early, across_early, swapped]
    state = attend(lists, 0, q_parts, None, pieces, part_tiles, 0, False)

    pieces, state = lax.optimization_barrier(
        ([level_late, across_late, far_early, far_late], state)
    )
    swapped = core_swap(level_late[: late.shape[0]], *pieces[1:])
    state = attend(lists, 1, q_parts, state, pieces, part_tiles, 0, False)
    rest = attend(lists, 2, q_parts[part_tiles:], state, [swapped], part_tiles, part_tiles, True)
    outs = [None]
    for step in range(1, heads):
        sent = rest[(step - 1) * part_tiles : step * part_tiles]
        outs.append(moved(sent, "head", lambda i: (i + step) % heads))
    outs[0] = attend(lists, 3, q_parts[:part_tiles], state, [swapped], part_tiles, 0, True)
    return join_heads(head_ref, [o.reshape(-1, HEAD_DIM) for o in outs])


def solution(mesh):
    placed = (
        P(("frame", "head"), None),
        P(("frame", "head"), None),
        P(("frame", "head"), None),
        P("head", "frame", None),
        P("head", "frame"),
    )
    return jax.shard_map(
        body, mesh=mesh, in_specs=placed, out_specs=P(("frame", "head"), None), check_vma=False
    )
```

```python
import functools
import math

import jax
import jax.numpy as jnp
import numpy as np
from jax import lax
from jax.experimental import pallas as pl
from jax.experimental.pallas import tpu as pltpu
from jax.sharding import PartitionSpec as P

TILE = 128
HEAD_DIM = 128
REACH = 32
PLANE = 4
GROUP = 4
PHASES = 2
MIB = 2**20
FAR_OFF = 1e30
VMEM = pl.BlockSpec(memory_space=pltpu.VMEM)
SMEM = pl.BlockSpec(memory_space=pltpu.SMEM)


def part_table(heads, part_tiles):
    rest = heads - 1
    table = np.zeros((PLANE, 2 * PLANE + 1, heads), np.int32)
    for place in range(PLANE):
        x, core = divmod(place, 2)
        for distance in range(-PLANE, PLANE + 1):
            plane, there = divmod(place + distance, PLANE)
            same_x, same_core = there // 2 == x, there % 2 == core
            for part in range(heads):
                late = part - 1
                first = part == 0
                pair = int(same_core) if first else 2 + rest * int(same_core) + late
                phase, swaps = 0, 5 * heads
                if plane == 0 and same_x:
                    spot = pair
                elif plane == 0 and same_core:
                    spot = 4 * heads + part
                elif plane == 0:
                    spot = swaps + (1 if first else 2 + rest + late)
                elif not same_x:
                    pair = int(there % 2 == x)
                    phase, spot = 1, pair if first else 2 + rest * pair + late
                elif (plane < 0) == (core == 0):
                    spot = 2 * heads + pair
                else:
                    spot = swaps + (0 if first else 2 + late)
                table[place, distance + PLANE, part] = phase + 4 * (2 * part_tiles * spot)
    return table.reshape(-1)


def params(mib):
    return pltpu.CompilerParams(vmem_limit_bytes=mib * MIB)


def split_kernel(heads, flip, head_ref, *refs):
    ins, keep, send = refs[: len(flip)], refs[-2], refs[-1]
    tiles = ins[0].shape[0] // TILE
    for which, flipped in enumerate(flip):
        for step in range(heads):
            column = lax.rem(head_ref[0] + step, heads) * HEAD_DIM
            columns = pl.ds(pl.multiple_of(column, HEAD_DIM), HEAD_DIM)
            for tile in range(tiles):
                block = ins[which][pl.ds(tile * TILE, TILE), columns]
                block = block.T if flipped else block
                if step == 0:
                    keep[which * tiles + tile] = block
                else:
                    send[step - 1, which * tiles + tile] = block


def split_heads(head, arrays, flip, heads):
    tiles = len(arrays) * arrays[0].shape[0] // TILE
    dtype = arrays[0].dtype
    return pl.pallas_call(
        functools.partial(split_kernel, heads, flip),
        in_specs=[SMEM] + [VMEM] * len(arrays),
        out_specs=[VMEM] * 2,
        out_shape=[
            jax.ShapeDtypeStruct((tiles, TILE, HEAD_DIM), dtype),
            jax.ShapeDtypeStruct((heads - 1, tiles, TILE, HEAD_DIM), dtype),
        ],
        compiler_params=params(4),
    )(head, *arrays)


def join_kernel(heads, head_ref, *refs):
    out_ref = refs[-1]
    for step in range(heads):
        column = lax.rem(head_ref[0] + step, heads) * HEAD_DIM
        columns = pl.ds(pl.multiple_of(column, HEAD_DIM), HEAD_DIM)
        out_ref[:, columns] = refs[step][...]


def join_heads(head, pieces):
    rows = pieces[0].shape[0]
    heads = len(pieces)
    return pl.pallas_call(
        functools.partial(join_kernel, heads),
        in_specs=[SMEM] + [VMEM] * heads,
        out_specs=VMEM,
        out_shape=jax.ShapeDtypeStruct((rows, heads * HEAD_DIM), pieces[0].dtype),
        compiler_params=params(4),
    )(head, *pieces)


def list_kernel(heads, length, where_ref, lists_ref, live_ref, table_ref, ends, metas, places):
    tiles = live_ref.shape[0]
    part_tiles = tiles // heads
    frame, head = where_ref[0], where_ref[1]
    base = (lax.rem(frame, PLANE) * (2 * PLANE + 1) + PLANE - frame) * heads
    targets = range(PHASES + 1)
    for target in targets:
        ends[target] = target * length
    for tile in range(tiles):
        part, inside = divmod(tile, part_tiles)
        row = ((head - part) & (heads - 1)) * part_tiles + inside

        def slot_step(slot, carry, row=row, tile=tile, part=part):
            listed = lists_ref[row, slot]
            within = listed & (tiles - 1)
            rank = within >> int(math.log2(part_tiles))
            shard = listed >> int(math.log2(tiles))
            entry = table_ref[base + shard * heads + ((head - rank) & (heads - 1))]
            phase = entry & 3
            last = phase == PHASES - 1
            target = jnp.where(last, PHASES, phase) if part == 0 else phase
            inner = tile if part == 0 else jnp.where(last, tile - part_tiles, tile)
            at = ends[target]
            places[at] = (entry >> 2) + (within & (part_tiles - 1))
            metas[at >> 2] = inner * 8 + (at & (GROUP - 1))
            ends[target] = at + 1
            return carry

        lax.fori_loop(0, live_ref[row], slot_step, 0)
        for target in targets:
            at = ends[target]
            up = (at + GROUP - 1) & -GROUP
            filler = places[jnp.maximum(at - 1, 0)]
            for other in range(GROUP - 1):
                places[jnp.where(at + other < up, at + other, (PHASES + 1) * length)] = filler
            ends[target] = up
    for target in targets:
        for item in range(3):
            metas[(ends[target] >> 2) + item] = -1
            for slot in range(GROUP):
                places[ends[target] + item * GROUP + slot] = 0
        ends[target] = (ends[target] - target * length) >> 2


def work_lists(frame, head, tile_lists, live_slots, heads):
    tiles, slots = tile_lists.shape
    assert tiles & (tiles - 1) == 0 and heads & (heads - 1) == 0 and GROUP == 4
    length = (tiles * (slots // GROUP + 1) + 3) * GROUP
    total = (PHASES + 1) * length
    table = jnp.asarray(part_table(heads, tiles // heads))
    return pl.pallas_call(
        functools.partial(list_kernel, heads, length),
        in_specs=[SMEM] * 4,
        out_specs=[SMEM] * 3,
        out_shape=[
            jax.ShapeDtypeStruct((PHASES + 1,), jnp.int32),
            jax.ShapeDtypeStruct((total // GROUP,), jnp.int32),
            jax.ShapeDtypeStruct((total + 1,), jnp.int32),
        ],
        compiler_params=params(4),
        cost_estimate=pl.CostEstimate(flops=0, bytes_accessed=0, transcendentals=0),
    )(jnp.stack((frame, head)), tile_lists, live_slots, table)


def phase_kernel(which, offset, first, pieces, begins, ends, numbers, metas, places, q_ref, *refs):
    refs = list(refs)
    state = [refs.pop(0) for _ in range(0 if begins else 3)]
    parts = [refs.pop(0) for _ in range(pieces)]
    out_ref = refs.pop(0) if ends else None
    top_ref, total_ref, sum_ref, scores, high, weights, shrinks, window = refs
    tiles = q_ref.shape[0]
    factor = math.log2(math.e) / math.sqrt(HEAD_DIM)
    base = which * (metas.shape[0] // (PHASES + 1))

    at = 0
    for part in parts:
        window[at : at + part.shape[0]] = part[...]
        at += part.shape[0]
    if begins:
        top_ref[...] = jnp.full(top_ref.shape, -FAR_OFF, jnp.float32)
        total_ref[...] = jnp.zeros(total_ref.shape, jnp.float32)
        sum_ref[...] = jnp.zeros(sum_ref.shape, jnp.float32)
    else:
        for ref, old in zip((top_ref, total_ref, sum_ref), state):
            ref[...] = old[first : first + tiles]

    def score(item):
        at = base + item
        keys = [window[places[at * GROUP + slot]] for slot in range(GROUP)]
        tile = jnp.maximum(metas[at] >> 3, 0)
        block = jnp.dot(jnp.concatenate(keys), q_ref[tile], preferred_element_type=jnp.float32)
        top = jnp.max(block.reshape(-1, 8, TILE), axis=0)
        return block, jnp.max(top, axis=0, keepdims=True)

    def weigh(item, block, peak):
        meta = metas[base + item]
        tile, last = jnp.maximum(meta >> 3, 0), jnp.where(meta < 0, -1, meta & 7)
        old = top_ref[tile]
        top = jnp.maximum(old, jnp.where(meta < 0, -FAR_OFF, peak))
        shrink = jnp.exp2((old - top) * factor)
        total = total_ref[tile] * shrink
        parts = []
        for slot in range(GROUP):
            shift = jnp.where(slot <= last, top, FAR_OFF)
            weight = jnp.exp2((block[slot * TILE : (slot + 1) * TILE] - shift) * factor)
            total = total + jnp.sum(weight.reshape(-1, 8, TILE), axis=0)
            parts.append(weight.astype(jnp.bfloat16))
        top_ref[tile] = top
        total_ref[tile] = total
        return jnp.concatenate(parts), shrink

    def collect(item, weight, shrink):
        at = base + item
        tile = jnp.maximum(metas[at] >> 3, 0)
        values = [window[places[at * GROUP + slot] + offset] for slot in range(GROUP)]
        product = jnp.dot(
            jnp.concatenate(values, axis=1), weight, preferred_element_type=jnp.float32
        )
        sum_ref[tile] = sum_ref[tile] * shrink + product

    block, peak = score(0)
    scores[...], high[...] = score(1)
    weights[...], shrinks[...] = weigh(0, block, peak)

    def step(pair, carry):
        item = 2 * pair
        block, peak, weight, shrink = scores[...], high[...], weights[...], shrinks[...]
        block_2, peak_2 = score(item + 2)
        weight_1, shrink_1 = weigh(item + 1, block, peak)
        collect(item, weight, shrink)
        block_3, peak_3 = score(item + 3)
        weight_2, shrink_2 = weigh(item + 2, block_2, peak_2)
        collect(item + 1, weight_1, shrink_1)
        scores[...], high[...] = block_3, peak_3
        weights[...], shrinks[...] = weight_2, shrink_2
        return carry

    lax.fori_loop(0, (numbers[which] + 1) >> 1, step, 0)
    if ends:
        for tile in range(tiles):
            total = jnp.sum(total_ref[tile], axis=0, keepdims=True)
            out_ref[tile] = (sum_ref[tile] / total).T.astype(out_ref.dtype)


def attend(lists, which, queries, state, pieces, offset, first, ends):
    tiles = queries.shape[0]
    begins = state is None
    held = [
        jax.ShapeDtypeStruct((tiles, 1, TILE), jnp.float32),
        jax.ShapeDtypeStruct((tiles, 8, TILE), jnp.float32),
        jax.ShapeDtypeStruct((tiles, HEAD_DIM, TILE), jnp.float32),
    ]
    scratch = [
        pltpu.VMEM((GROUP * TILE, TILE), jnp.float32),
        pltpu.VMEM((1, TILE), jnp.float32),
        pltpu.VMEM((GROUP * TILE, TILE), queries.dtype),
        pltpu.VMEM((1, TILE), jnp.float32),
        pltpu.VMEM((sum(piece.shape[0] for piece in pieces), TILE, TILE), queries.dtype),
    ]
    out = jax.ShapeDtypeStruct(queries.shape, queries.dtype)
    return pl.pallas_call(
        functools.partial(phase_kernel, which, offset, first, len(pieces), begins, ends),
        in_specs=[SMEM] * 3 + [VMEM] * (1 + len(pieces) + (0 if begins else 3)),
        out_specs=VMEM if ends else [VMEM] * 3,
        out_shape=out if ends else held,
        scratch_shapes=([pltpu.VMEM(h.shape, h.dtype) for h in held] if ends else []) + scratch,
        compiler_params=params(8),
        cost_estimate=pl.CostEstimate(flops=0, bytes_accessed=0, transcendentals=0),
    )(*lists, queries, *([] if begins else state), *pieces)


def moved(block, axis, source):
    size = lax.axis_size(axis)
    route = [(source(i), i) for i in range(size) if 0 <= source(i) < size]
    return lax.ppermute(block, axis, route)


def body(queries, key_vectors, value_vectors, tile_lists, live_slots):
    heads = lax.axis_size("head")
    frame = lax.axis_index("frame")
    head = lax.axis_index("head")
    head_ref = head[None]
    place = lax.rem(frame, PLANE)
    shard_tiles = tile_lists.shape[1]
    part_tiles = shard_tiles // heads
    assert shard_tiles * PLANE == REACH and lax.axis_size("frame") % PLANE == 0

    def core_swap(*blocks):
        return moved(jnp.concatenate(blocks), "frame", lambda i: i ^ 1)

    def along_z(pair):
        return moved(pair, "frame", lambda i: i - PLANE if i % 2 == 0 else i + PLANE)

    def along_x(block):
        return moved(block, "frame", lambda i: i ^ 2)

    def head_swap(blocks):
        return [
            moved(blocks[step - 1], "head", lambda i: (i - step) % heads)
            for step in range(1, heads)
        ]

    size = 2 * part_tiles
    early, send = split_heads(head_ref, (key_vectors, value_vectors), (False, True), heads)
    chip_early = jnp.concatenate((core_swap(early), early))
    level_early = along_z(chip_early)
    across_early = along_x(early)

    lists = work_lists(frame, head, tile_lists[0], live_slots[0], heads)
    late, across_early, lists = lax.optimization_barrier(
        (jnp.concatenate(head_swap(send)), across_early, lists)
    )
    chip_late = jnp.concatenate((core_swap(late), late))
    level_late = along_z(chip_late)
    across_late = along_x(late)

    level_early, across_early, _ = lax.optimization_barrier(
        (level_early, across_early, chip_late)
    )
    swapped_early = core_swap(level_early[:size], across_early)
    queries, swapped_early = lax.optimization_barrier((queries, swapped_early))
    q_keep, q_send = split_heads(head_ref, (queries,), (True,), heads)
    q_parts = jnp.concatenate([q_keep] + head_swap(q_send))

    def exchanged(pair):
        return moved(pair, "frame", lambda i: {1: i + 1, 2: i - 1}.get(i % PLANE, -1))

    def handed(pair):
        other = moved(pair, "frame", lambda i: {0: i + 1, 3: i - 1}.get(i % PLANE, -1))
        return jnp.where((place == 1) | (place == 2), pair, other)

    far_early = exchanged(level_early)
    level_late, across_late, q_parts, far_early = lax.optimization_barrier(
        (level_late, across_late, q_parts, far_early)
    )
    far_late = exchanged(level_late)
    swapped_late = core_swap(level_late[: late.shape[0]], across_late)
    pieces = [chip_early, chip_late, level_early, level_late, across_early, across_late]
    pieces += [swapped_early, swapped_late]
    state = attend(lists, 0, q_parts, None, pieces, part_tiles, 0, False)

    far_late, state = lax.optimization_barrier((far_late, state))
    pieces = [handed(far_early), handed(far_late)]
    rest = attend(lists, 1, q_parts[part_tiles:], state, pieces, part_tiles, part_tiles, True)
    outs = [None]
    for step in range(1, heads):
        sent = rest[(step - 1) * part_tiles : step * part_tiles]
        outs.append(moved(sent, "head", lambda i: (i + step) % heads))
    outs[0] = attend(lists, 2, q_parts[:part_tiles], state, pieces, part_tiles, 0, True)
    return join_heads(head_ref, [o.reshape(-1, HEAD_DIM) for o in outs])


def solution(mesh):
    placed = (
        P(("frame", "head"), None),
        P(("frame", "head"), None),
        P(("frame", "head"), None),
        P("head", "frame", None),
        P("head", "frame"),
    )
    return jax.shard_map(
        body, mesh=mesh, in_specs=placed, out_specs=P(("frame", "head"), None), check_vma=False
    )
```

```python
import functools
import math

import jax
import jax.numpy as jnp
import numpy as np
from jax import lax
from jax.experimental import pallas as pl
from jax.experimental.pallas import tpu as pltpu
from jax.sharding import PartitionSpec as P

TILE = 128
HEAD_DIM = 128
REACH = 32
PLANE = 4
GROUP = 4
LISTS = 3
FAR_OFF = 1e30
FACTOR = math.log2(math.e) / math.sqrt(HEAD_DIM)
VMEM = pl.BlockSpec(memory_space=pltpu.VMEM)
SMEM = pl.BlockSpec(memory_space=pltpu.SMEM)


def shard_table():
    table = np.zeros((PLANE, 2 * PLANE + 1), np.int32)
    for place in range(PLANE):
        x, core = divmod(place, 2)
        for distance in range(-PLANE, PLANE + 1):
            plane, there = divmod(place + distance, PLANE)
            same_x, same_core = there // 2 == x, there % 2 == core
            phase = 0
            if plane == 0:
                spot = int(same_core) if same_x else (4 if same_core else 5)
            elif not same_x:
                phase, spot = 1, 1 if same_core else 2
            elif (plane < 0) == (core == 0):
                spot = 2 + int(same_core)
            else:
                phase, spot = 1, 0
            table[place, distance + PLANE] = phase + 4 * spot
    return table.reshape(-1)


def params(mib):
    return pltpu.CompilerParams(vmem_limit_bytes=mib * 2**20)


def cost():
    return pl.CostEstimate(flops=0, bytes_accessed=0, transcendentals=0)


def tile_kernel(heads, flip, *refs):
    out_ref = refs[-1]
    tiles = refs[0].shape[0] // TILE
    for head in range(heads):
        for which, flipped in enumerate(flip):
            for tile in range(tiles):
                block = refs[which][
                    tile * TILE : (tile + 1) * TILE, head * HEAD_DIM : (head + 1) * HEAD_DIM
                ]
                out_ref[(head * len(flip) + which) * tiles + tile] = block.T if flipped else block


def as_tiles(arrays, flip):
    rows, width = arrays[0].shape
    heads = width // HEAD_DIM
    count = len(arrays) * heads * rows // TILE
    return pl.pallas_call(
        functools.partial(tile_kernel, heads, flip),
        in_specs=[VMEM] * len(arrays),
        out_specs=VMEM,
        out_shape=jax.ShapeDtypeStruct((count, TILE, HEAD_DIM), arrays[0].dtype),
        compiler_params=params(4),
    )(*arrays)


def list_kernel(heads, length, where_ref, lists_ref, live_ref, table_ref, ends, metas, places):
    tiles = live_ref.shape[0]
    part_tiles = tiles // heads
    frame, head = where_ref[0], where_ref[1]
    base = lax.rem(frame, PLANE) * (2 * PLANE + 1) + PLANE - frame
    targets = range(LISTS * heads)
    for target in targets:
        ends[target] = target * length
    for row in range(tiles):
        part, inner = divmod(row, part_tiles)

        def slot_step(slot, carry, row=row, part=part, inner=inner):
            listed = lists_ref[row, slot]
            within = listed & (tiles - 1)
            rank = within >> int(math.log2(part_tiles))
            entry = table_ref[base + (listed >> int(math.log2(tiles)))]
            step = (rank - head) & (heads - 1)
            turn = (rank - part) & (heads - 1)
            phase = entry & 3
            query = (turn * heads + head) * part_tiles + inner
            other = (phase == 1) & (turn > 0)
            query = jnp.where(other, query - heads * part_tiles, query)
            target = step * LISTS + jnp.where((phase == 1) & (turn == 0), 2, phase)
            at = ends[target]
            places[at] = (entry >> 2) * (2 * tiles) + (
                head * (2 * part_tiles) + (within & (part_tiles - 1))
            )
            metas[at >> 2] = query * 8 + (at & (GROUP - 1))
            ends[target] = at + 1
            return carry

        lax.fori_loop(0, live_ref[row], slot_step, 0)
        for target in targets:
            at = ends[target]
            up = (at + GROUP - 1) & -GROUP
            filler = places[jnp.maximum(at - 1, 0)]
            for other in range(GROUP - 1):
                spare = LISTS * heads * length
                places[jnp.where(at + other < up, at + other, spare)] = filler
            ends[target] = up
    for target in targets:
        ends[target] = (ends[target] - target * length) >> 2


def work_lists(frame, head, tile_lists, live_slots, heads):
    tiles, slots = tile_lists.shape
    assert tiles & (tiles - 1) == 0 and heads & (heads - 1) == 0 and GROUP == 4
    length = tiles * (slots // GROUP + 1) * GROUP
    total = LISTS * heads * length
    ends, metas, places = pl.pallas_call(
        functools.partial(list_kernel, heads, length),
        in_specs=[SMEM] * 4,
        out_specs=[SMEM] * 3,
        out_shape=[
            jax.ShapeDtypeStruct((LISTS * heads,), jnp.int32),
            jax.ShapeDtypeStruct((total // GROUP,), jnp.int32),
            jax.ShapeDtypeStruct((total + 1,), jnp.int32),
        ],
        compiler_params=params(4),
        cost_estimate=cost(),
    )(jnp.stack((frame, head)), tile_lists, live_slots, jnp.asarray(shard_table()))
    arrays = ends, metas, places[:total]
    return jnp.concatenate([array.reshape(heads, -1) for array in arrays], axis=1)


def phase_kernel(which, offset, first, pieces, begins, ends, lists, q_ref, *refs):
    refs = list(refs)
    state = [refs.pop(0) for _ in range(0 if begins else 3)]
    parts = [refs.pop(0) for _ in range(pieces)]
    out_ref, stats_ref = [refs.pop(0) for _ in range(2)] if ends else [None] * 2
    top_ref, total_ref, sum_ref, scores, high, weights, shrinks, window = refs
    tiles = q_ref.shape[0]
    heads, width = lists.shape
    length = (width - LISTS) // (LISTS * (GROUP + 1))

    at = 0
    for part in parts:
        window[at : at + part.shape[0]] = part[...]
        at += part.shape[0]
    if begins:
        top_ref[...] = jnp.full(top_ref.shape, -FAR_OFF, jnp.float32)
        total_ref[...] = jnp.zeros(total_ref.shape, jnp.float32)
        sum_ref[...] = jnp.zeros(sum_ref.shape, jnp.float32)
    else:
        for ref, old in zip((top_ref, total_ref, sum_ref), state):
            ref[...] = old[first : first + tiles]

    starts = [jnp.int32(0)]
    for head in range(heads):
        starts.append(starts[-1] + lists[head, which])

    def item_of(item):
        row, index = jnp.int32(0), item
        for head in range(1, heads):
            row = jnp.where(item >= starts[head], head, row)
            index = jnp.where(item >= starts[head], item - starts[head], index)
        real = item < starts[heads]
        row, index = jnp.where(real, row, 0), jnp.where(real, index, 0)
        meta = lists[row, LISTS + which * length + index]
        at = LISTS * (1 + length) + (which * length + index) * GROUP
        tile = jnp.where(real, meta >> 3, 0)
        spots = [jnp.where(real, lists[row, at + slot], 0) for slot in range(GROUP)]
        return tile, jnp.where(real, meta & 7, -1), spots

    def score(item):
        tile, _, spots = item_of(item)
        keys = jnp.concatenate([window[spot] for spot in spots])
        block = jnp.dot(keys, q_ref[tile], preferred_element_type=jnp.float32)
        top = jnp.max(block.reshape(-1, 8, TILE), axis=0)
        return block, jnp.max(top, axis=0, keepdims=True)

    def weigh(item, block, peak):
        tile, last, _ = item_of(item)
        old = top_ref[tile]
        top = jnp.maximum(old, jnp.where(last < 0, -FAR_OFF, peak))
        shrink = jnp.exp2((old - top) * FACTOR)
        total = total_ref[tile] * shrink
        parts = []
        for slot in range(GROUP):
            shift = jnp.where(slot <= last, top, FAR_OFF)
            weight = jnp.exp2((block[slot * TILE : (slot + 1) * TILE] - shift) * FACTOR)
            total = total + jnp.sum(weight.reshape(-1, 8, TILE), axis=0)
            parts.append(weight.astype(jnp.bfloat16))
        top_ref[tile] = top
        total_ref[tile] = total
        return jnp.concatenate(parts), shrink

    def collect(item, weight, shrink):
        tile, _, spots = item_of(item)
        values = jnp.concatenate([window[spot + offset] for spot in spots], axis=1)
        product = jnp.dot(values, weight, preferred_element_type=jnp.float32)
        sum_ref[tile] = sum_ref[tile] * shrink + product

    block, peak = score(0)
    scores[...], high[...] = score(1)
    weights[...], shrinks[...] = weigh(0, block, peak)

    def step(pair, carry):
        item = 2 * pair
        block, peak, weight, shrink = scores[...], high[...], weights[...], shrinks[...]
        block_2, peak_2 = score(item + 2)
        weight_1, shrink_1 = weigh(item + 1, block, peak)
        collect(item, weight, shrink)
        block_3, peak_3 = score(item + 3)
        weight_2, shrink_2 = weigh(item + 2, block_2, peak_2)
        collect(item + 1, weight_1, shrink_1)
        scores[...], high[...] = block_3, peak_3
        weights[...], shrinks[...] = weight_2, shrink_2
        return carry

    lax.fori_loop(0, (starts[heads] + 1) >> 1, step, 0)
    if ends:
        for tile in range(tiles):
            total = jnp.sum(total_ref[tile], axis=0, keepdims=True)
            share = jnp.where(total > 0, 1.0 / jnp.where(total > 0, total, 1.0), 0.0)
            out_ref[tile] = (sum_ref[tile] * share).astype(out_ref.dtype)
            stats_ref[tile, 0:1] = total
            stats_ref[tile, 1:2] = top_ref[tile]


def attend(lists, which, queries, state, pieces, offset, first, ends):
    tiles = queries.shape[0]
    begins = state is None
    held = [
        jax.ShapeDtypeStruct((tiles, 1, TILE), jnp.float32),
        jax.ShapeDtypeStruct((tiles, 8, TILE), jnp.float32),
        jax.ShapeDtypeStruct((tiles, HEAD_DIM, TILE), jnp.float32),
    ]
    scratch = [
        pltpu.VMEM((GROUP * TILE, TILE), jnp.float32),
        pltpu.VMEM((1, TILE), jnp.float32),
        pltpu.VMEM((GROUP * TILE, TILE), queries.dtype),
        pltpu.VMEM((1, TILE), jnp.float32),
        pltpu.VMEM((sum(piece.shape[0] for piece in pieces), TILE, TILE), queries.dtype),
    ]
    if ends:
        scratch = [pltpu.VMEM(array.shape, array.dtype) for array in held] + scratch
        held = [
            jax.ShapeDtypeStruct((tiles, HEAD_DIM, TILE), queries.dtype),
            jax.ShapeDtypeStruct((tiles, 2, TILE), jnp.float32),
        ]
    return pl.pallas_call(
        functools.partial(phase_kernel, which, offset, first, len(pieces), begins, ends),
        in_specs=[SMEM] + [VMEM] * (1 + len(pieces) + (0 if begins else 3)),
        out_specs=[VMEM] * len(held),
        out_shape=held,
        scratch_shapes=scratch,
        compiler_params=params(10),
        cost_estimate=cost(),
    )(lists, queries, *([] if begins else state), *pieces)


def merge_kernel(count, *refs):
    out_ref = refs[-1]
    values, stats = [refs[first : 2 * count : 2] for first in range(2)]
    tiles = values[0].shape[0]
    part_tiles = out_ref.shape[0] // TILE
    for tile in range(tiles):
        top = stats[0][tile, 1:2]
        for ref in stats[1:]:
            top = jnp.maximum(top, ref[tile, 1:2])
        shares = [ref[tile, 0:1] * jnp.exp2((ref[tile, 1:2] - top) * FACTOR) for ref in stats]
        whole = sum(shares[1:], shares[0])
        out = jnp.zeros((HEAD_DIM, TILE), jnp.float32)
        for value, share in zip(values, shares):
            out = out + value[tile].astype(jnp.float32) * (share / whole)
        head, inner = divmod(tile, part_tiles)
        out_ref[
            inner * TILE : (inner + 1) * TILE, head * HEAD_DIM : (head + 1) * HEAD_DIM
        ] = out.T.astype(out_ref.dtype)


def merge(parts, rows, heads):
    flat = [array for part in parts for array in part]
    return pl.pallas_call(
        functools.partial(merge_kernel, len(parts)),
        in_specs=[VMEM] * len(flat),
        out_specs=VMEM,
        out_shape=jax.ShapeDtypeStruct((rows, heads * HEAD_DIM), flat[0].dtype),
        compiler_params=params(6),
    )(*flat)


def moved(block, axis, source):
    size = lax.axis_size(axis)
    route = [(source(i), i) for i in range(size) if 0 <= source(i) < size]
    return lax.ppermute(block, axis, route)


def body(queries, key_vectors, value_vectors, tile_lists, live_slots):
    heads = lax.axis_size("head")
    frame = lax.axis_index("frame")
    head = lax.axis_index("head")
    shard_tiles = tile_lists.shape[1]
    part_tiles = shard_tiles // heads
    assert shard_tiles * PLANE == REACH and lax.axis_size("frame") % PLANE == 0

    def from_head(block, step):
        return moved(block, "head", lambda i: (i - step) % heads)

    def core_swap(block):
        return moved(block, "frame", lambda i: i ^ 1)

    own = as_tiles((key_vectors, value_vectors), (False, True))
    size = own.shape[0]
    across = moved(own, "frame", lambda i: i ^ 2)
    chip = jnp.concatenate((core_swap(own), own))
    level = moved(chip, "frame", lambda i: i - PLANE if i % 2 == 0 else i + PLANE)

    lists = work_lists(frame, head, tile_lists[0], live_slots[0], heads)
    q_own = as_tiles((queries,), (True,))
    q_parts = [q_own] + [from_head(q_own, step) for step in range(1, heads)]
    lists = [lists[:1]] + [from_head(lists[step : step + 1], step) for step in range(1, heads)]
    by_head = jnp.concatenate(lists)
    q_all = jnp.concatenate(q_parts)

    far = moved(across, "frame", lambda i: i - PLANE if i % PLANE < 2 else i + PLANE)
    level_core = core_swap(level[:size])
    pieces = [chip, level, across, core_swap(across)]
    state = attend(by_head, 0, q_all, None, pieces, part_tiles, 0, False)
    far, state = lax.optimization_barrier((far, state))
    pieces = [level_core, far, core_swap(far)]
    rest = attend(by_head, 1, q_all[shard_tiles:], state, pieces, part_tiles, shard_tiles, True)
    parts = [None]
    for step in range(1, heads):
        cut = slice((step - 1) * shard_tiles, step * shard_tiles)
        parts.append([from_head(array[cut], -step) for array in rest])
    parts[0] = attend(by_head, 2, q_all[:shard_tiles], state, pieces, part_tiles, 0, True)
    return merge(parts, queries.shape[0], heads)


def solution(mesh):
    placed = (
        P(("frame", "head"), None),
        P(("frame", "head"), None),
        P(("frame", "head"), None),
        P("head", "frame", None),
        P("head", "frame"),
    )
    return jax.shard_map(
        body, mesh=mesh, in_specs=placed, out_specs=P(("frame", "head"), None), check_vma=False
    )
```

```python
import functools
import math

import jax
import jax.numpy as jnp
import numpy as np
from jax import lax
from jax.experimental import pallas as pl
from jax.experimental.pallas import tpu as pltpu
from jax.sharding import PartitionSpec as P

TILE = 128
HEAD_DIM = 128
REACH = 32
PLANE = 4
GROUP = 4
LISTS = 3
FAR_OFF = 1e30
FACTOR = math.log2(math.e) / math.sqrt(HEAD_DIM)
VMEM = pl.BlockSpec(memory_space=pltpu.VMEM)
SMEM = pl.BlockSpec(memory_space=pltpu.SMEM)


def shard_table():
    table = np.zeros((PLANE, 2 * PLANE + 1), np.int32)
    for place in range(PLANE):
        x, core = divmod(place, 2)
        for distance in range(-PLANE, PLANE + 1):
            plane, there = divmod(place + distance, PLANE)
            same_x, same_core = there // 2 == x, there % 2 == core
            phase = 0
            if plane == 0:
                spot = int(same_core) if same_x else (4 if same_core else 5)
            elif not same_x:
                phase, spot = 1, 1 if same_core else 2
            elif (plane < 0) == (core == 0):
                spot = 2 + int(same_core)
            else:
                phase, spot = 1, 0
            table[place, distance + PLANE] = phase + 4 * spot
    return table.reshape(-1)


def params(mib):
    return pltpu.CompilerParams(vmem_limit_bytes=mib * 2**20)


def cost():
    return pl.CostEstimate(flops=0, bytes_accessed=0, transcendentals=0)


def tile_kernel(heads, flip, *refs):
    out_ref = refs[-1]
    tiles = refs[0].shape[0] // TILE
    for head in range(heads):
        for which, flipped in enumerate(flip):
            for tile in range(tiles):
                block = refs[which][
                    tile * TILE : (tile + 1) * TILE, head * HEAD_DIM : (head + 1) * HEAD_DIM
                ]
                out_ref[(head * len(flip) + which) * tiles + tile] = block.T if flipped else block


def as_tiles(arrays, flip):
    rows, width = arrays[0].shape
    heads = width // HEAD_DIM
    count = len(arrays) * heads * rows // TILE
    return pl.pallas_call(
        functools.partial(tile_kernel, heads, flip),
        in_specs=[VMEM] * len(arrays),
        out_specs=VMEM,
        out_shape=jax.ShapeDtypeStruct((count, TILE, HEAD_DIM), arrays[0].dtype),
        compiler_params=params(4),
    )(*arrays)


def list_kernel(heads, length, where_ref, lists_ref, live_ref, table_ref, ends, metas, places):
    tiles = live_ref.shape[0]
    part_tiles = tiles // heads
    frame, head = where_ref[0], where_ref[1]
    base = lax.rem(frame, PLANE) * (2 * PLANE + 1) + PLANE - frame
    targets = range(LISTS * heads)
    for target in targets:
        ends[target] = target * length
    for row in range(tiles):
        part, inner = divmod(row, part_tiles)

        def slot_step(slot, carry, row=row, part=part, inner=inner):
            listed = lists_ref[row, slot]
            within = listed & (tiles - 1)
            rank = within >> int(math.log2(part_tiles))
            entry = table_ref[base + (listed >> int(math.log2(tiles)))]
            step = (rank - head) & (heads - 1)
            turn = (rank - part) & (heads - 1)
            phase = entry & 3
            query = (turn * heads + head) * part_tiles + inner
            other = (phase == 1) & (turn > 0)
            query = jnp.where(other, query - heads * part_tiles, query)
            target = step * LISTS + jnp.where((phase == 1) & (turn == 0), 2, phase)
            at = ends[target]
            places[at] = (entry >> 2) * (2 * tiles) + (
                head * (2 * part_tiles) + (within & (part_tiles - 1))
            )
            metas[at >> 2] = query * 8 + (at & (GROUP - 1))
            ends[target] = at + 1
            return carry

        lax.fori_loop(0, live_ref[row], slot_step, 0)
        for target in targets:
            at = ends[target]
            up = (at + GROUP - 1) & -GROUP
            filler = places[jnp.maximum(at - 1, 0)]
            for other in range(GROUP - 1):
                spare = LISTS * heads * length
                places[jnp.where(at + other < up, at + other, spare)] = filler
            ends[target] = up
    for target in targets:
        ends[target] = (ends[target] - target * length) >> 2


def work_lists(frame, head, tile_lists, live_slots, heads):
    tiles, slots = tile_lists.shape
    assert tiles & (tiles - 1) == 0 and heads & (heads - 1) == 0 and GROUP == 4
    length = tiles * (slots // GROUP + 1) * GROUP
    total = LISTS * heads * length
    ends, metas, places = pl.pallas_call(
        functools.partial(list_kernel, heads, length),
        in_specs=[SMEM] * 4,
        out_specs=[SMEM] * 3,
        out_shape=[
            jax.ShapeDtypeStruct((LISTS * heads,), jnp.int32),
            jax.ShapeDtypeStruct((total // GROUP,), jnp.int32),
            jax.ShapeDtypeStruct((total + 1,), jnp.int32),
        ],
        compiler_params=params(4),
        cost_estimate=cost(),
    )(jnp.stack((frame, head)), tile_lists, live_slots, jnp.asarray(shard_table()))
    arrays = ends, metas, places[:total]
    return jnp.concatenate([array.reshape(heads, -1) for array in arrays], axis=1)


def packed(numbers):
    rows = -(-numbers.shape[0] // TILE)
    numbers = jnp.pad(numbers, (0, rows * TILE - numbers.shape[0])).reshape(rows, TILE)
    digits = jnp.concatenate((numbers & 255, numbers >> 8)).astype(jnp.bfloat16)
    return jnp.pad(digits, ((0, -2 * rows % 16), (0, 0)))


def unpacked(block, count):
    rows = -(-count // TILE)
    digits = block.astype(jnp.int32)
    return (digits[:rows] + digits[rows : 2 * rows] * 256).reshape(-1)[:count]


def phase_kernel(which, offset, first, pieces, begins, ends, lists, q_ref, *refs):
    refs = list(refs)
    state = [refs.pop(0) for _ in range(0 if begins else 3)]
    parts = [refs.pop(0) for _ in range(pieces)]
    out_ref, stats_ref = [refs.pop(0) for _ in range(2)] if ends else [None] * 2
    top_ref, total_ref, sum_ref, scores, high, weights, shrinks = refs[:7]
    window = refs[7] if pieces > 1 else parts[0]
    tiles = q_ref.shape[0]
    heads, width = lists.shape
    length = (width - LISTS) // (LISTS * (GROUP + 1))

    at = 0
    for part in parts if pieces > 1 else ():
        window[at : at + part.shape[0]] = part[...]
        at += part.shape[0]
    if begins:
        top_ref[...] = jnp.full(top_ref.shape, -FAR_OFF, jnp.float32)
        total_ref[...] = jnp.zeros(total_ref.shape, jnp.float32)
        sum_ref[...] = jnp.zeros(sum_ref.shape, jnp.float32)
    else:
        for ref, old in zip((top_ref, total_ref, sum_ref), state):
            ref[...] = old[first : first + tiles]

    starts = [jnp.int32(0)]
    for head in range(heads):
        starts.append(starts[-1] + lists[head, which])

    def item_of(item):
        row, index = jnp.int32(0), item
        for head in range(1, heads):
            row = jnp.where(item >= starts[head], head, row)
            index = jnp.where(item >= starts[head], item - starts[head], index)
        real = item < starts[heads]
        row, index = jnp.where(real, row, 0), jnp.where(real, index, 0)
        meta = lists[row, LISTS + which * length + index]
        at = LISTS * (1 + length) + (which * length + index) * GROUP
        tile = jnp.where(real, meta >> 3, 0)
        spots = [jnp.where(real, lists[row, at + slot], 0) for slot in range(GROUP)]
        return tile, jnp.where(real, meta & 7, -1), spots

    def score(entry):
        tile, _, spots = entry
        keys = jnp.concatenate([window[spot] for spot in spots])
        block = jnp.dot(keys, q_ref[tile], preferred_element_type=jnp.float32)
        top = jnp.max(block.reshape(-1, 8, TILE), axis=0)
        return block, jnp.max(top, axis=0, keepdims=True)

    def weigh(entry, block, peak):
        tile, last, _ = entry
        old = top_ref[tile]
        top = jnp.maximum(old, jnp.where(last < 0, -FAR_OFF, peak))
        shrink = jnp.exp2((old - top) * FACTOR)
        total = total_ref[tile] * shrink
        parts = []
        for slot in range(GROUP):
            shift = jnp.where(slot <= last, top, FAR_OFF)
            weight = jnp.exp2((block[slot * TILE : (slot + 1) * TILE] - shift) * FACTOR)
            total = total + jnp.sum(weight.reshape(-1, 8, TILE), axis=0)
            parts.append(weight.astype(jnp.bfloat16))
        top_ref[tile] = top
        total_ref[tile] = total
        return jnp.concatenate(parts), shrink

    def collect(entry, weight, shrink):
        tile, _, spots = entry
        values = jnp.concatenate([window[spot + offset] for spot in spots], axis=1)
        product = jnp.dot(values, weight, preferred_element_type=jnp.float32)
        sum_ref[tile] = sum_ref[tile] * shrink + product

    entry, entry_1 = item_of(0), item_of(1)
    block, peak = score(entry)
    scores[...], high[...] = score(entry_1)
    weights[...], shrinks[...] = weigh(entry, block, peak)

    def step(pair, entries):
        entry, entry_1 = entries
        entry_2, entry_3 = item_of(2 * pair + 2), item_of(2 * pair + 3)
        block, peak, weight, shrink = scores[...], high[...], weights[...], shrinks[...]
        block_2, peak_2 = score(entry_2)
        weight_1, shrink_1 = weigh(entry_1, block, peak)
        collect(entry, weight, shrink)
        block_3, peak_3 = score(entry_3)
        weight_2, shrink_2 = weigh(entry_2, block_2, peak_2)
        collect(entry_1, weight_1, shrink_1)
        scores[...], high[...] = block_3, peak_3
        weights[...], shrinks[...] = weight_2, shrink_2
        return entry_2, entry_3

    lax.fori_loop(0, (starts[heads] + 1) >> 1, step, (entry, entry_1))
    if ends:
        for tile in range(tiles):
            total = jnp.sum(total_ref[tile], axis=0, keepdims=True)
            share = jnp.where(total > 0, 1.0 / jnp.where(total > 0, total, 1.0), 0.0)
            out_ref[tile] = (sum_ref[tile] * share).astype(out_ref.dtype)
            stats_ref[tile, 0:1] = total
            stats_ref[tile, 1:2] = top_ref[tile]


def attend(lists, which, queries, state, pieces, offset, first, ends):
    tiles = queries.shape[0]
    begins = state is None
    held = [
        jax.ShapeDtypeStruct((tiles, 1, TILE), jnp.float32),
        jax.ShapeDtypeStruct((tiles, 8, TILE), jnp.float32),
        jax.ShapeDtypeStruct((tiles, HEAD_DIM, TILE), jnp.float32),
    ]
    scratch = [
        pltpu.VMEM((GROUP * TILE, TILE), jnp.float32),
        pltpu.VMEM((1, TILE), jnp.float32),
        pltpu.VMEM((GROUP * TILE, TILE), queries.dtype),
        pltpu.VMEM((1, TILE), jnp.float32),
    ]
    if len(pieces) > 1:
        rows = sum(piece.shape[0] for piece in pieces)
        scratch.append(pltpu.VMEM((rows, TILE, TILE), queries.dtype))
    if ends:
        scratch = [pltpu.VMEM(array.shape, array.dtype) for array in held] + scratch
        held = [
            jax.ShapeDtypeStruct((tiles, HEAD_DIM, TILE), queries.dtype),
            jax.ShapeDtypeStruct((tiles, 2, TILE), jnp.float32),
        ]
    return pl.pallas_call(
        functools.partial(phase_kernel, which, offset, first, len(pieces), begins, ends),
        in_specs=[SMEM] + [VMEM] * (1 + len(pieces) + (0 if begins else 3)),
        out_specs=[VMEM] * len(held),
        out_shape=held,
        scratch_shapes=scratch,
        compiler_params=params(10),
        cost_estimate=cost(),
    )(lists, queries, *([] if begins else state), *pieces)


def merge_kernel(count, *refs):
    out_ref = refs[-1]
    values, stats = [refs[first : 2 * count : 2] for first in range(2)]
    tiles = values[0].shape[0]
    part_tiles = out_ref.shape[0] // TILE
    for tile in range(tiles):
        top = stats[0][tile, 1:2]
        for ref in stats[1:]:
            top = jnp.maximum(top, ref[tile, 1:2])
        shares = [ref[tile, 0:1] * jnp.exp2((ref[tile, 1:2] - top) * FACTOR) for ref in stats]
        whole = sum(shares[1:], shares[0])
        out = jnp.zeros((HEAD_DIM, TILE), jnp.float32)
        for value, share in zip(values, shares):
            out = out + value[tile].astype(jnp.float32) * (share / whole)
        head, inner = divmod(tile, part_tiles)
        out_ref[
            inner * TILE : (inner + 1) * TILE, head * HEAD_DIM : (head + 1) * HEAD_DIM
        ] = out.T.astype(out_ref.dtype)


def merge(parts, rows, heads):
    flat = [array for part in parts for array in part]
    return pl.pallas_call(
        functools.partial(merge_kernel, len(parts)),
        in_specs=[VMEM] * len(flat),
        out_specs=VMEM,
        out_shape=jax.ShapeDtypeStruct((rows, heads * HEAD_DIM), flat[0].dtype),
        compiler_params=params(6),
    )(*flat)


def moved(block, axis, source):
    size = lax.axis_size(axis)
    route = [(source(i), i) for i in range(size) if 0 <= source(i) < size]
    return lax.ppermute(block, axis, route)


def body(queries, key_vectors, value_vectors, tile_lists, live_slots):
    heads = lax.axis_size("head")
    frame = lax.axis_index("frame")
    head = lax.axis_index("head")
    shard_tiles = tile_lists.shape[1]
    part_tiles = shard_tiles // heads
    assert shard_tiles * PLANE == REACH and lax.axis_size("frame") % PLANE == 0

    def from_head(block, step):
        return moved(block, "head", lambda i: (i - step) % heads)

    def core_swap(block):
        return moved(block, "frame", lambda i: i ^ 1)

    own = as_tiles((key_vectors, value_vectors), (False, True))
    size = own.shape[0]
    across = moved(own, "frame", lambda i: i ^ 2)
    chip = jnp.concatenate((core_swap(own), own))
    level = moved(chip, "frame", lambda i: i - PLANE if i % 2 == 0 else i + PLANE)

    listed, live, _ = lax.optimization_barrier((tile_lists[0], live_slots[0], chip))
    lists = work_lists(frame, head, listed, live, heads)
    q_own = as_tiles((queries,), (True,))
    q_parts, by_head = [q_own], [lists[:1]]
    for step in range(1, heads):
        block = from_head(jnp.concatenate((q_own.reshape(-1, TILE), packed(lists[step]))), step)
        block, _ = lax.optimization_barrier((block, level))
        q_rows = shard_tiles * TILE
        q_parts.append(block[:q_rows].reshape(q_own.shape))
        by_head.append(unpacked(block[q_rows:], lists.shape[1])[None])
    q_all, by_head = jnp.concatenate(q_parts), jnp.concatenate(by_head)

    cut = size * 5 // 8
    far_z = moved(across[:cut], "frame", lambda i: i - PLANE if i % PLANE < 2 else i + PLANE)
    pair = jnp.concatenate((level[cut:size], level[size + cut :]))
    pair = moved(pair, "frame", lambda i: {1: i + 1, 2: i - 1}.get(i % PLANE, -1))
    level_core = core_swap(level[:size])
    pieces = [chip, level, across, core_swap(across)]
    state = attend(by_head, 0, q_all, None, pieces, part_tiles, 0, False)
    far_z, pair, level_core, state = lax.optimization_barrier((far_z, pair, level_core, state))
    swapped_z = core_swap(far_z)
    handed = moved(pair, "frame", lambda i: {0: i + 1, 3: i - 1}.get(i % PLANE, -1))
    place = lax.rem(frame, PLANE)
    middle = (place == 1) | (place == 2)
    half = size - cut
    own_x = jnp.where(middle, pair[:half], handed[half:])
    other_x = jnp.where(middle, pair[half:], handed[:half])
    pieces = [level_core, far_z, own_x, swapped_z, other_x]
    rest = attend(by_head, 1, q_all[shard_tiles:], state, pieces, part_tiles, shard_tiles, True)
    parts = [None]
    for step in range(1, heads):
        cut = slice((step - 1) * shard_tiles, step * shard_tiles)
        parts.append([from_head(array[cut], -step) for array in rest])
    parts[0] = attend(by_head, 2, q_all[:shard_tiles], state, pieces, part_tiles, 0, True)
    return merge(parts, queries.shape[0], heads)


def solution(mesh):
    placed = (
        P(("frame", "head"), None),
        P(("frame", "head"), None),
        P(("frame", "head"), None),
        P("head", "frame", None),
        P("head", "frame"),
    )
    return jax.shard_map(
        body, mesh=mesh, in_specs=placed, out_specs=P(("frame", "head"), None), check_vma=False
    )
```

```python
import functools
import math

import jax
import jax.numpy as jnp
import numpy as np
from jax import lax
from jax.experimental import pallas as pl
from jax.experimental.pallas import tpu as pltpu
from jax.sharding import PartitionSpec as P

TILE = 128
HEAD_DIM = 128
REACH = 32
PLANE = 4
GROUP = 4
LISTS = 3
FAR_OFF = 1e30
FACTOR = math.log2(math.e) / math.sqrt(HEAD_DIM)
VMEM = pl.BlockSpec(memory_space=pltpu.VMEM)
SMEM = pl.BlockSpec(memory_space=pltpu.SMEM)


def shard_table(size):
    half = size // 2
    table = np.zeros((PLANE, 2 * PLANE + 1, 2), np.int32)
    for place in range(PLANE):
        x, core = divmod(place, 2)
        for distance in range(-PLANE, PLANE + 1):
            plane, there = divmod(place + distance, PLANE)
            same_x, same_core = there // 2 == x, there % 2 == core
            phase = 0
            if plane == 0:
                first = size * (int(same_core) if same_x else (4 if same_core else 5))
            elif not same_x:
                phase, first = 1, half * (0 if same_core else 3)
            elif (plane < 0) == (core == 0):
                first = size * (2 + int(same_core))
            else:
                first = size * 6
            table[place, distance + PLANE] = phase + 4 * first, phase + 4 * (first + half)
            if phase == 1:
                pair = 1 if x != core else 4
                table[place, distance + PLANE, 1] = 1 + 4 * half * (pair + int(there % 2 == x))
    return table.reshape(-1)


def params(mib):
    return pltpu.CompilerParams(vmem_limit_bytes=mib * 2**20)


def cost():
    return pl.CostEstimate(flops=0, bytes_accessed=0, transcendentals=0)


def tile_kernel(heads, flip, *refs):
    out_ref = refs[-1]
    tiles = refs[0].shape[0] // TILE
    for head in range(heads):
        for which, flipped in enumerate(flip):
            for tile in range(tiles):
                block = refs[which][
                    tile * TILE : (tile + 1) * TILE, head * HEAD_DIM : (head + 1) * HEAD_DIM
                ]
                out_ref[(head * len(flip) + which) * tiles + tile] = block.T if flipped else block


def as_tiles(arrays, flip):
    rows, width = arrays[0].shape
    heads = width // HEAD_DIM
    count = len(arrays) * heads * rows // TILE
    return pl.pallas_call(
        functools.partial(tile_kernel, heads, flip),
        in_specs=[VMEM] * len(arrays),
        out_specs=VMEM,
        out_shape=jax.ShapeDtypeStruct((count, TILE, HEAD_DIM), arrays[0].dtype),
        compiler_params=params(4),
    )(*arrays)


def list_kernel(heads, length, where_ref, lists_ref, live_ref, table_ref, ends, metas, places):
    tiles = live_ref.shape[0]
    part_tiles = tiles // heads
    frame, head = where_ref[0], where_ref[1]
    base = (lax.rem(frame, PLANE) * (2 * PLANE + 1) + PLANE - frame) * 2
    base = base + jnp.where(head < heads // 2, 0, 1)
    inner_head = (head & (heads // 2 - 1)) * (2 * part_tiles)
    targets = range(LISTS * heads)
    for target in targets:
        ends[target] = target * length
    for row in range(tiles):
        part, inner = divmod(row, part_tiles)

        def slot_step(slot, carry, row=row, part=part, inner=inner):
            listed = lists_ref[row, slot]
            within = listed & (tiles - 1)
            rank = within >> int(math.log2(part_tiles))
            entry = table_ref[base + 2 * (listed >> int(math.log2(tiles)))]
            step = (rank - head) & (heads - 1)
            turn = (rank - part) & (heads - 1)
            phase = entry & 3
            query = (turn * heads + head) * part_tiles + inner
            other = (phase == 1) & (turn > 0)
            query = jnp.where(other, query - heads * part_tiles, query)
            target = step * LISTS + jnp.where((phase == 1) & (turn == 0), 2, phase)
            at = ends[target]
            places[at] = (entry >> 2) + inner_head + (within & (part_tiles - 1))
            metas[at >> 2] = query * 8 + (at & (GROUP - 1))
            ends[target] = at + 1
            return carry

        lax.fori_loop(0, live_ref[row], slot_step, 0)
        for target in targets:
            at = ends[target]
            up = (at + GROUP - 1) & -GROUP
            filler = places[jnp.maximum(at - 1, 0)]
            for other in range(GROUP - 1):
                spare = LISTS * heads * length
                places[jnp.where(at + other < up, at + other, spare)] = filler
            ends[target] = up
    for target in targets:
        ends[target] = (ends[target] - target * length) >> 2


def work_lists(frame, head, tile_lists, live_slots, heads):
    tiles, slots = tile_lists.shape
    assert tiles & (tiles - 1) == 0 and heads & (heads - 1) == 0 and GROUP == 4
    length = tiles * (slots // GROUP + 1) * GROUP
    total = LISTS * heads * length
    ends, metas, places = pl.pallas_call(
        functools.partial(list_kernel, heads, length),
        in_specs=[SMEM] * 4,
        out_specs=[SMEM] * 3,
        out_shape=[
            jax.ShapeDtypeStruct((LISTS * heads,), jnp.int32),
            jax.ShapeDtypeStruct((total // GROUP,), jnp.int32),
            jax.ShapeDtypeStruct((total + 1,), jnp.int32),
        ],
        compiler_params=params(4),
        cost_estimate=cost(),
    )(jnp.stack((frame, head)), tile_lists, live_slots, jnp.asarray(shard_table(2 * tiles)))
    arrays = ends, metas, places[:total]
    return jnp.concatenate([array.reshape(heads, -1) for array in arrays], axis=1)


def packed(numbers):
    rows = -(-numbers.shape[0] // TILE)
    numbers = jnp.pad(numbers, (0, rows * TILE - numbers.shape[0])).reshape(rows, TILE)
    digits = jnp.concatenate((numbers & 255, numbers >> 8)).astype(jnp.bfloat16)
    return jnp.pad(digits, ((0, -2 * rows % 16), (0, 0)))


def unpacked(block, count):
    rows = -(-count // TILE)
    digits = block.astype(jnp.int32)
    return (digits[:rows] + digits[rows : 2 * rows] * 256).reshape(-1)[:count]


def phase_kernel(which, offset, first, pieces, begins, ends, lists, q_ref, *refs):
    refs = list(refs)
    state = [refs.pop(0) for _ in range(0 if begins else 3)]
    parts = [refs.pop(0) for _ in range(pieces)]
    out_ref, stats_ref = [refs.pop(0) for _ in range(2)] if ends else [None] * 2
    top_ref, total_ref, sum_ref, scores, high, weights, shrinks = refs[:7]
    window = refs[7] if pieces > 1 else parts[0]
    tiles = q_ref.shape[0]
    heads, width = lists.shape
    length = (width - LISTS) // (LISTS * (GROUP + 1))

    at = 0
    for part in parts if pieces > 1 else ():
        window[at : at + part.shape[0]] = part[...]
        at += part.shape[0]
    if begins:
        top_ref[...] = jnp.full(top_ref.shape, -FAR_OFF, jnp.float32)
        total_ref[...] = jnp.zeros(total_ref.shape, jnp.float32)
        sum_ref[...] = jnp.zeros(sum_ref.shape, jnp.float32)
    else:
        for ref, old in zip((top_ref, total_ref, sum_ref), state):
            ref[...] = old[first : first + tiles]

    starts = [jnp.int32(0)]
    for head in range(heads):
        starts.append(starts[-1] + lists[head, which])

    def item_of(item):
        row, index = jnp.int32(0), item
        for head in range(1, heads):
            row = jnp.where(item >= starts[head], head, row)
            index = jnp.where(item >= starts[head], item - starts[head], index)
        real = item < starts[heads]
        row, index = jnp.where(real, row, 0), jnp.where(real, index, 0)
        meta = lists[row, LISTS + which * length + index]
        at = LISTS * (1 + length) + (which * length + index) * GROUP
        tile = jnp.where(real, meta >> 3, 0)
        spots = [jnp.where(real, lists[row, at + slot], 0) for slot in range(GROUP)]
        return tile, jnp.where(real, meta & 7, -1), spots

    def score(entry):
        tile, _, spots = entry
        keys = jnp.concatenate([window[spot] for spot in spots])
        block = jnp.dot(keys, q_ref[tile], preferred_element_type=jnp.float32)
        top = jnp.max(block.reshape(-1, 8, TILE), axis=0)
        return block, jnp.max(top, axis=0, keepdims=True)

    def weigh(entry, block, peak):
        tile, last, _ = entry
        old = top_ref[tile]
        top = jnp.maximum(old, jnp.where(last < 0, -FAR_OFF, peak))
        shrink = jnp.exp2((old - top) * FACTOR)
        total = total_ref[tile] * shrink
        parts = []
        for slot in range(GROUP):
            shift = jnp.where(slot <= last, top, FAR_OFF)
            weight = jnp.exp2((block[slot * TILE : (slot + 1) * TILE] - shift) * FACTOR)
            total = total + jnp.sum(weight.reshape(-1, 8, TILE), axis=0)
            parts.append(weight.astype(jnp.bfloat16))
        top_ref[tile] = top
        total_ref[tile] = total
        return jnp.concatenate(parts), shrink

    def collect(entry, weight, shrink):
        tile, _, spots = entry
        values = jnp.concatenate([window[spot + offset] for spot in spots], axis=1)
        product = jnp.dot(values, weight, preferred_element_type=jnp.float32)
        sum_ref[tile] = sum_ref[tile] * shrink + product

    entry, entry_1 = item_of(0), item_of(1)
    block, peak = score(entry)
    scores[...], high[...] = score(entry_1)
    weights[...], shrinks[...] = weigh(entry, block, peak)

    def step(pair, entries):
        entry, entry_1 = entries
        entry_2, entry_3 = item_of(2 * pair + 2), item_of(2 * pair + 3)
        block, peak, weight, shrink = scores[...], high[...], weights[...], shrinks[...]
        block_2, peak_2 = score(entry_2)
        weight_1, shrink_1 = weigh(entry_1, block, peak)
        collect(entry, weight, shrink)
        block_3, peak_3 = score(entry_3)
        weight_2, shrink_2 = weigh(entry_2, block_2, peak_2)
        collect(entry_1, weight_1, shrink_1)
        scores[...], high[...] = block_3, peak_3
        weights[...], shrinks[...] = weight_2, shrink_2
        return entry_2, entry_3

    lax.fori_loop(0, (starts[heads] + 1) >> 1, step, (entry, entry_1))
    if ends:
        for tile in range(tiles):
            total = jnp.sum(total_ref[tile], axis=0, keepdims=True)
            share = jnp.where(total > 0, 1.0 / jnp.where(total > 0, total, 1.0), 0.0)
            out_ref[tile] = (sum_ref[tile] * share).astype(out_ref.dtype)
            stats_ref[tile, 0:1] = total
            stats_ref[tile, 1:2] = top_ref[tile]


def attend(lists, which, queries, state, pieces, offset, first, ends):
    tiles = queries.shape[0]
    begins = state is None
    held = [
        jax.ShapeDtypeStruct((tiles, 1, TILE), jnp.float32),
        jax.ShapeDtypeStruct((tiles, 8, TILE), jnp.float32),
        jax.ShapeDtypeStruct((tiles, HEAD_DIM, TILE), jnp.float32),
    ]
    scratch = [
        pltpu.VMEM((GROUP * TILE, TILE), jnp.float32),
        pltpu.VMEM((1, TILE), jnp.float32),
        pltpu.VMEM((GROUP * TILE, TILE), queries.dtype),
        pltpu.VMEM((1, TILE), jnp.float32),
    ]
    if len(pieces) > 1:
        rows = sum(piece.shape[0] for piece in pieces)
        scratch.append(pltpu.VMEM((rows, TILE, TILE), queries.dtype))
    if ends:
        scratch = [pltpu.VMEM(array.shape, array.dtype) for array in held] + scratch
        held = [
            jax.ShapeDtypeStruct((tiles, HEAD_DIM, TILE), queries.dtype),
            jax.ShapeDtypeStruct((tiles, 2, TILE), jnp.float32),
        ]
    return pl.pallas_call(
        functools.partial(phase_kernel, which, offset, first, len(pieces), begins, ends),
        in_specs=[SMEM] + [VMEM] * (1 + len(pieces) + (0 if begins else 3)),
        out_specs=[VMEM] * len(held),
        out_shape=held,
        scratch_shapes=scratch,
        compiler_params=params(10),
        cost_estimate=cost(),
    )(lists, queries, *([] if begins else state), *pieces)


def merge_kernel(count, *refs):
    out_ref = refs[-1]
    values, stats = [refs[first : 2 * count : 2] for first in range(2)]
    tiles = values[0].shape[0]
    part_tiles = out_ref.shape[0] // TILE
    for tile in range(tiles):
        top = stats[0][tile, 1:2]
        for ref in stats[1:]:
            top = jnp.maximum(top, ref[tile, 1:2])
        shares = [ref[tile, 0:1] * jnp.exp2((ref[tile, 1:2] - top) * FACTOR) for ref in stats]
        whole = sum(shares[1:], shares[0])
        out = jnp.zeros((HEAD_DIM, TILE), jnp.float32)
        for value, share in zip(values, shares):
            out = out + value[tile].astype(jnp.float32) * (share / whole)
        head, inner = divmod(tile, part_tiles)
        out_ref[
            inner * TILE : (inner + 1) * TILE, head * HEAD_DIM : (head + 1) * HEAD_DIM
        ] = out.T.astype(out_ref.dtype)


def merge(parts, rows, heads):
    flat = [array for part in parts for array in part]
    return pl.pallas_call(
        functools.partial(merge_kernel, len(parts)),
        in_specs=[VMEM] * len(flat),
        out_specs=VMEM,
        out_shape=jax.ShapeDtypeStruct((rows, heads * HEAD_DIM), flat[0].dtype),
        compiler_params=params(6),
    )(*flat)


def moved(block, axis, source):
    size = lax.axis_size(axis)
    route = [(source(i), i) for i in range(size) if 0 <= source(i) < size]
    return lax.ppermute(block, axis, route)


def body(queries, key_vectors, value_vectors, tile_lists, live_slots):
    heads = lax.axis_size("head")
    frame = lax.axis_index("frame")
    head = lax.axis_index("head")
    shard_tiles = tile_lists.shape[1]
    part_tiles = shard_tiles // heads
    assert shard_tiles * PLANE == REACH and lax.axis_size("frame") % PLANE == 0

    def from_head(block, step):
        return moved(block, "head", lambda i: (i - step) % heads)

    def core_swap(block):
        return moved(block, "frame", lambda i: i ^ 1)

    own = as_tiles((key_vectors, value_vectors), (False, True))
    size = own.shape[0]
    across = moved(own, "frame", lambda i: i ^ 2)
    chip = jnp.concatenate((core_swap(own), own))
    level = moved(chip, "frame", lambda i: i - PLANE if i % 2 == 0 else i + PLANE)

    listed, live, _ = lax.optimization_barrier((tile_lists[0], live_slots[0], chip))
    lists = work_lists(frame, head, listed, live, heads)
    q_own = as_tiles((queries,), (True,))
    q_parts, by_head = [q_own], [lists[:1]]
    for step in range(1, heads):
        block = from_head(jnp.concatenate((q_own.reshape(-1, TILE), packed(lists[step]))), step)
        block, _ = lax.optimization_barrier((block, level))
        q_rows = shard_tiles * TILE
        q_parts.append(block[:q_rows].reshape(q_own.shape))
        by_head.append(unpacked(block[q_rows:], lists.shape[1])[None])
    q_all, by_head = jnp.concatenate(q_parts), jnp.concatenate(by_head)

    half = size // 2
    far_z = moved(across[:half], "frame", lambda i: i - PLANE if i % PLANE < 2 else i + PLANE)
    pair = jnp.concatenate((level[half:size], level[size + half :]))
    pair = moved(pair, "frame", lambda i: {1: i + 1, 2: i - 1}.get(i % PLANE, -1))
    pieces = [chip, level, across, core_swap(across), core_swap(level[:size])]
    state = attend(by_head, 0, q_all, None, pieces, part_tiles, 0, False)
    far_z, pair, state = lax.optimization_barrier((far_z, pair, state))
    pieces = [far_z, pair, core_swap(jnp.concatenate((far_z, pair)))]
    rest = attend(by_head, 1, q_all[shard_tiles:], state, pieces, part_tiles, shard_tiles, True)
    parts = [None]
    for step in range(1, heads):
        cut = slice((step - 1) * shard_tiles, step * shard_tiles)
        parts.append([from_head(array[cut], -step) for array in rest])
    parts[0] = attend(by_head, 2, q_all[:shard_tiles], state, pieces, part_tiles, 0, True)
    return merge(parts, queries.shape[0], heads)


def solution(mesh):
    placed = (
        P(("frame", "head"), None),
        P(("frame", "head"), None),
        P(("frame", "head"), None),
        P("head", "frame", None),
        P("head", "frame"),
    )
    return jax.shard_map(
        body, mesh=mesh, in_specs=placed, out_specs=P(("frame", "head"), None), check_vma=False
    )
```

```python
import functools
import math

import jax
import jax.numpy as jnp
import numpy as np
from jax import lax
from jax.experimental import pallas as pl
from jax.experimental.pallas import tpu as pltpu
from jax.sharding import PartitionSpec as P

TILE = 128
HEAD_DIM = 128
REACH = 32
PLANE = 4
GROUP = 4
LISTS = 3
FAR_OFF = 1e30
FACTOR = math.log2(math.e) / math.sqrt(HEAD_DIM)
VMEM = pl.BlockSpec(memory_space=pltpu.VMEM)
SMEM = pl.BlockSpec(memory_space=pltpu.SMEM)


def shard_table(size, cut):
    table = np.zeros((PLANE, 2 * PLANE + 1, 2), np.int32)
    for place in range(PLANE):
        x, core = divmod(place, 2)
        for distance in range(-PLANE, PLANE + 1):
            plane, there = divmod(place + distance, PLANE)
            same_x, same_core = there // 2 == x, there % 2 == core
            phase = 0
            if plane == 0:
                first = second = size * (int(same_core) if same_x else (4 if same_core else 5))
            elif not same_x:
                swapped = 2 * size - cut
                phase, first = 1, 0 if same_core else swapped
                second = (0 if x != core else swapped) + int(there % 2 == x) * (size - cut)
            elif (plane < 0) == (core == 0):
                first = second = size * (2 + int(same_core))
            else:
                first = second = size * 6
            table[place, distance + PLANE] = phase + 4 * first, phase + 4 * second
    return table.reshape(-1)


def cut_of(size):
    return size * 5 // 8


def params(mib):
    return pltpu.CompilerParams(vmem_limit_bytes=mib * 2**20)


def cost():
    return pl.CostEstimate(flops=0, bytes_accessed=0, transcendentals=0)


def tile_kernel(heads, flip, *refs):
    out_ref = refs[-1]
    tiles = refs[0].shape[0] // TILE
    for head in range(heads):
        for which, flipped in enumerate(flip):
            for tile in range(tiles):
                block = refs[which][
                    tile * TILE : (tile + 1) * TILE, head * HEAD_DIM : (head + 1) * HEAD_DIM
                ]
                at = (tile * heads + head) * len(flip) + which
                out_ref[at] = block.T if flipped else block


def as_tiles(arrays, flip):
    rows, width = arrays[0].shape
    heads = width // HEAD_DIM
    count = len(arrays) * heads * rows // TILE
    return pl.pallas_call(
        functools.partial(tile_kernel, heads, flip),
        in_specs=[VMEM] * len(arrays),
        out_specs=VMEM,
        out_shape=jax.ShapeDtypeStruct((count, TILE, HEAD_DIM), arrays[0].dtype),
        compiler_params=params(4),
    )(*arrays)


def list_kernel(heads, length, where_ref, lists_ref, live_ref, table_ref, ends, metas, places):
    tiles = live_ref.shape[0]
    part_tiles = tiles // heads
    frame, head = where_ref[0], where_ref[1]
    base = (lax.rem(frame, PLANE) * (2 * PLANE + 1) + PLANE - frame) * 2
    targets = range(LISTS * heads)
    for target in targets:
        ends[target] = target * length
    for row in range(tiles):
        part, inner = divmod(row, part_tiles)

        def slot_step(slot, carry, row=row, part=part, inner=inner):
            listed = lists_ref[row, slot]
            within = listed & (tiles - 1)
            rank = within >> int(math.log2(part_tiles))
            spot = ((within & (part_tiles - 1)) * heads + head) * 2
            side = jnp.where(spot < cut_of(2 * tiles), 0, 1)
            entry = table_ref[base + 2 * (listed >> int(math.log2(tiles))) + side]
            step = (rank - head) & (heads - 1)
            turn = (rank - part) & (heads - 1)
            phase = entry & 3
            query = (turn * part_tiles + inner) * heads + head
            other = (phase == 1) & (turn > 0)
            query = jnp.where(other, query - heads * part_tiles, query)
            target = step * LISTS + jnp.where((phase == 1) & (turn == 0), 2, phase)
            at = ends[target]
            places[at] = (entry >> 2) + spot
            metas[at >> 2] = query * 8 + (at & (GROUP - 1))
            ends[target] = at + 1
            return carry

        lax.fori_loop(0, live_ref[row], slot_step, 0)
        for target in targets:
            at = ends[target]
            up = (at + GROUP - 1) & -GROUP
            filler = places[jnp.maximum(at - 1, 0)]
            for other in range(GROUP - 1):
                spare = LISTS * heads * length
                places[jnp.where(at + other < up, at + other, spare)] = filler
            ends[target] = up
    for target in targets:
        ends[target] = (ends[target] - target * length) >> 2


def work_lists(frame, head, tile_lists, live_slots, heads):
    tiles, slots = tile_lists.shape
    assert tiles & (tiles - 1) == 0 and heads & (heads - 1) == 0 and GROUP == 4
    length = tiles * (slots // GROUP + 1) * GROUP
    total = LISTS * heads * length
    ends, metas, places = pl.pallas_call(
        functools.partial(list_kernel, heads, length),
        in_specs=[SMEM] * 4,
        out_specs=[SMEM] * 3,
        out_shape=[
            jax.ShapeDtypeStruct((LISTS * heads,), jnp.int32),
            jax.ShapeDtypeStruct((total // GROUP,), jnp.int32),
            jax.ShapeDtypeStruct((total + 1,), jnp.int32),
        ],
        compiler_params=params(4),
        cost_estimate=cost(),
    )(jnp.stack((frame, head)), tile_lists, live_slots, jnp.asarray(shard_table(2 * tiles, cut_of(2 * tiles))))
    arrays = ends, metas, places[:total]
    return jnp.concatenate([array.reshape(heads, -1) for array in arrays], axis=1)


def packed(numbers):
    rows = -(-numbers.shape[0] // TILE)
    numbers = jnp.pad(numbers, (0, rows * TILE - numbers.shape[0])).reshape(rows, TILE)
    digits = jnp.concatenate((numbers & 255, numbers >> 8)).astype(jnp.bfloat16)
    return jnp.pad(digits, ((0, -2 * rows % 16), (0, 0)))


def unpacked(block, count):
    rows = -(-count // TILE)
    digits = block.astype(jnp.int32)
    return (digits[:rows] + digits[rows : 2 * rows] * 256).reshape(-1)[:count]


def phase_kernel(which, first, pieces, begins, ends, lists, q_ref, *refs):
    refs = list(refs)
    state = [refs.pop(0) for _ in range(0 if begins else 3)]
    parts = [refs.pop(0) for _ in range(pieces)]
    out_ref, stats_ref = [refs.pop(0) for _ in range(2)] if ends else [None] * 2
    top_ref, total_ref, sum_ref, scores, high, weights, shrinks = refs[:7]
    window = refs[7] if pieces > 1 else parts[0]
    tiles = q_ref.shape[0]
    heads, width = lists.shape
    length = (width - LISTS) // (LISTS * (GROUP + 1))

    at = 0
    for part in parts if pieces > 1 else ():
        window[at : at + part.shape[0]] = part[...]
        at += part.shape[0]
    if begins:
        top_ref[...] = jnp.full(top_ref.shape, -FAR_OFF, jnp.float32)
        total_ref[...] = jnp.zeros(total_ref.shape, jnp.float32)
        sum_ref[...] = jnp.zeros(sum_ref.shape, jnp.float32)
    else:
        for ref, old in zip((top_ref, total_ref, sum_ref), state):
            ref[...] = old[first : first + tiles]

    starts = [jnp.int32(0)]
    for head in range(heads):
        starts.append(starts[-1] + lists[head, which])

    def item_of(item):
        row, index = jnp.int32(0), item
        for head in range(1, heads):
            row = jnp.where(item >= starts[head], head, row)
            index = jnp.where(item >= starts[head], item - starts[head], index)
        real = item < starts[heads]
        row, index = jnp.where(real, row, 0), jnp.where(real, index, 0)
        meta = lists[row, LISTS + which * length + index]
        at = LISTS * (1 + length) + (which * length + index) * GROUP
        tile = jnp.where(real, meta >> 3, 0)
        spots = [jnp.where(real, lists[row, at + slot], 0) for slot in range(GROUP)]
        return tile, jnp.where(real, meta & 7, -1), spots

    def score(entry):
        tile, _, spots = entry
        keys = jnp.concatenate([window[spot] for spot in spots])
        block = jnp.dot(keys, q_ref[tile], preferred_element_type=jnp.float32)
        top = jnp.max(block.reshape(-1, 8, TILE), axis=0)
        return block, jnp.max(top, axis=0, keepdims=True)

    def weigh(entry, block, peak):
        tile, last, _ = entry
        old = top_ref[tile]
        top = jnp.maximum(old, jnp.where(last < 0, -FAR_OFF, peak))
        shrink = jnp.exp2((old - top) * FACTOR)
        total = total_ref[tile] * shrink
        parts = []
        for slot in range(GROUP):
            shift = jnp.where(slot <= last, top, FAR_OFF)
            weight = jnp.exp2((block[slot * TILE : (slot + 1) * TILE] - shift) * FACTOR)
            total = total + jnp.sum(weight.reshape(-1, 8, TILE), axis=0)
            parts.append(weight.astype(jnp.bfloat16))
        top_ref[tile] = top
        total_ref[tile] = total
        return jnp.concatenate(parts), shrink

    def collect(entry, weight, shrink):
        tile, _, spots = entry
        values = jnp.concatenate([window[spot + 1] for spot in spots], axis=1)
        product = jnp.dot(values, weight, preferred_element_type=jnp.float32)
        sum_ref[tile] = sum_ref[tile] * shrink + product

    entry, entry_1 = item_of(0), item_of(1)
    block, peak = score(entry)
    scores[...], high[...] = score(entry_1)
    weights[...], shrinks[...] = weigh(entry, block, peak)

    def step(pair, entries):
        entry, entry_1 = entries
        entry_2, entry_3 = item_of(2 * pair + 2), item_of(2 * pair + 3)
        block, peak, weight, shrink = scores[...], high[...], weights[...], shrinks[...]
        block_2, peak_2 = score(entry_2)
        weight_1, shrink_1 = weigh(entry_1, block, peak)
        collect(entry, weight, shrink)
        block_3, peak_3 = score(entry_3)
        weight_2, shrink_2 = weigh(entry_2, block_2, peak_2)
        collect(entry_1, weight_1, shrink_1)
        scores[...], high[...] = block_3, peak_3
        weights[...], shrinks[...] = weight_2, shrink_2
        return entry_2, entry_3

    lax.fori_loop(0, (starts[heads] + 1) >> 1, step, (entry, entry_1))
    if ends:
        for tile in range(tiles):
            total = jnp.sum(total_ref[tile], axis=0, keepdims=True)
            share = jnp.where(total > 0, 1.0 / jnp.where(total > 0, total, 1.0), 0.0)
            out_ref[tile] = (sum_ref[tile] * share).astype(out_ref.dtype)
            stats_ref[tile, 0:1] = total
            stats_ref[tile, 1:2] = top_ref[tile]


def attend(lists, which, queries, state, pieces, first, ends):
    tiles = queries.shape[0]
    begins = state is None
    held = [
        jax.ShapeDtypeStruct((tiles, 1, TILE), jnp.float32),
        jax.ShapeDtypeStruct((tiles, 8, TILE), jnp.float32),
        jax.ShapeDtypeStruct((tiles, HEAD_DIM, TILE), jnp.float32),
    ]
    scratch = [
        pltpu.VMEM((GROUP * TILE, TILE), jnp.float32),
        pltpu.VMEM((1, TILE), jnp.float32),
        pltpu.VMEM((GROUP * TILE, TILE), queries.dtype),
        pltpu.VMEM((1, TILE), jnp.float32),
    ]
    if len(pieces) > 1:
        rows = sum(piece.shape[0] for piece in pieces)
        scratch.append(pltpu.VMEM((rows, TILE, TILE), queries.dtype))
    if ends:
        scratch = [pltpu.VMEM(array.shape, array.dtype) for array in held] + scratch
        held = [
            jax.ShapeDtypeStruct((tiles, HEAD_DIM, TILE), queries.dtype),
            jax.ShapeDtypeStruct((tiles, 2, TILE), jnp.float32),
        ]
    return pl.pallas_call(
        functools.partial(phase_kernel, which, first, len(pieces), begins, ends),
        in_specs=[SMEM] + [VMEM] * (1 + len(pieces) + (0 if begins else 3)),
        out_specs=[VMEM] * len(held),
        out_shape=held,
        scratch_shapes=scratch,
        compiler_params=params(10),
        cost_estimate=cost(),
    )(lists, queries, *([] if begins else state), *pieces)


def merge_kernel(count, *refs):
    out_ref = refs[-1]
    values, stats = [refs[first : 2 * count : 2] for first in range(2)]
    tiles = values[0].shape[0]
    heads = out_ref.shape[1] // HEAD_DIM
    for tile in range(tiles):
        top = stats[0][tile, 1:2]
        for ref in stats[1:]:
            top = jnp.maximum(top, ref[tile, 1:2])
        shares = [ref[tile, 0:1] * jnp.exp2((ref[tile, 1:2] - top) * FACTOR) for ref in stats]
        whole = sum(shares[1:], shares[0])
        out = jnp.zeros((HEAD_DIM, TILE), jnp.float32)
        for value, share in zip(values, shares):
            out = out + value[tile].astype(jnp.float32) * (share / whole)
        inner, head = divmod(tile, heads)
        out_ref[
            inner * TILE : (inner + 1) * TILE, head * HEAD_DIM : (head + 1) * HEAD_DIM
        ] = out.T.astype(out_ref.dtype)


def merge(parts, rows, heads):
    flat = [array for part in parts for array in part]
    return pl.pallas_call(
        functools.partial(merge_kernel, len(parts)),
        in_specs=[VMEM] * len(flat),
        out_specs=VMEM,
        out_shape=jax.ShapeDtypeStruct((rows, heads * HEAD_DIM), flat[0].dtype),
        compiler_params=params(6),
    )(*flat)


def moved(block, axis, source):
    size = lax.axis_size(axis)
    route = [(source(i), i) for i in range(size) if 0 <= source(i) < size]
    return lax.ppermute(block, axis, route)


def body(queries, key_vectors, value_vectors, tile_lists, live_slots):
    heads = lax.axis_size("head")
    frame = lax.axis_index("frame")
    head = lax.axis_index("head")
    shard_tiles = tile_lists.shape[1]
    assert shard_tiles * PLANE == REACH and lax.axis_size("frame") % PLANE == 0

    def from_head(block, step):
        return moved(block, "head", lambda i: (i - step) % heads)

    def core_swap(block):
        return moved(block, "frame", lambda i: i ^ 1)

    own = as_tiles((key_vectors, value_vectors), (False, True))
    size = own.shape[0]
    across = moved(own, "frame", lambda i: i ^ 2)
    chip = jnp.concatenate((core_swap(own), own))
    level = moved(chip, "frame", lambda i: i - PLANE if i % 2 == 0 else i + PLANE)

    listed, live, _ = lax.optimization_barrier((tile_lists[0], live_slots[0], chip))
    lists = work_lists(frame, head, listed, live, heads)
    q_own = as_tiles((queries,), (True,))
    q_parts, by_head = [q_own], [lists[:1]]
    for step in range(1, heads):
        block = from_head(jnp.concatenate((q_own.reshape(-1, TILE), packed(lists[step]))), step)
        block, _ = lax.optimization_barrier((block, level))
        q_rows = shard_tiles * TILE
        q_parts.append(block[:q_rows].reshape(q_own.shape))
        by_head.append(unpacked(block[q_rows:], lists.shape[1])[None])
    q_all, by_head = jnp.concatenate(q_parts), jnp.concatenate(by_head)

    cut = cut_of(size)
    far_z = moved(across[:cut], "frame", lambda i: i - PLANE if i % PLANE < 2 else i + PLANE)
    pair = jnp.concatenate((level[cut:size], level[size + cut :]))
    pair = moved(pair, "frame", lambda i: {1: i + 1, 2: i - 1}.get(i % PLANE, -1))
    pieces = [chip, level, across, core_swap(across), core_swap(level[:size])]
    state = attend(by_head, 0, q_all, None, pieces, 0, False)
    far_z, pair, state = lax.optimization_barrier((far_z, pair, state))
    pieces = [far_z, pair, core_swap(jnp.concatenate((far_z, pair)))]
    rest = attend(by_head, 1, q_all[shard_tiles:], state, pieces, shard_tiles, True)
    parts = [None]
    for step in range(1, heads):
        cut = slice((step - 1) * shard_tiles, step * shard_tiles)
        parts.append([from_head(array[cut], -step) for array in rest])
    parts[0] = attend(by_head, 2, q_all[:shard_tiles], state, pieces, 0, True)
    return merge(parts, queries.shape[0], heads)


def solution(mesh):
    placed = (
        P(("frame", "head"), None),
        P(("frame", "head"), None),
        P(("frame", "head"), None),
        P("head", "frame", None),
        P("head", "frame"),
    )
    return jax.shard_map(
        body, mesh=mesh, in_specs=placed, out_specs=P(("frame", "head"), None), check_vma=False
    )
```

```python
import functools
import math

import jax
import jax.numpy as jnp
import numpy as np
from jax import lax
from jax.experimental import pallas as pl
from jax.experimental.pallas import tpu as pltpu
from jax.sharding import PartitionSpec as P

TILE = 128
HEAD_DIM = 128
REACH = 32
PLANE = 4
GROUP = 4
LISTS = 4
FAR_OFF = 1e30
FACTOR = math.log2(math.e) / math.sqrt(HEAD_DIM)
VMEM = pl.BlockSpec(memory_space=pltpu.VMEM)
SMEM = pl.BlockSpec(memory_space=pltpu.SMEM)


def shard_table(size, cut):
    table = np.zeros((PLANE, 2 * PLANE + 1, 2), np.int32)
    for place in range(PLANE):
        x, core = divmod(place, 2)
        for distance in range(-PLANE, PLANE + 1):
            plane, there = divmod(place + distance, PLANE)
            same_x, same_core = there // 2 == x, there % 2 == core
            phase = 0
            if plane == 0:
                first = second = size * (int(same_core) if same_x else (4 if same_core else 5))
            elif not same_x:
                swapped = 2 * size - cut
                phase, first = 1, 0 if same_core else swapped
                second = (0 if x != core else swapped) + int(there % 2 == x) * (size - cut)
            elif (plane < 0) == (core == 0):
                first = second = size * (2 + int(same_core))
            else:
                first = second = size * 6
            table[place, distance + PLANE] = phase + 4 * first, phase + 4 * second
    return table.reshape(-1)


def cut_of(size):
    return size * 3 // 4


def params(mib):
    return pltpu.CompilerParams(vmem_limit_bytes=mib * 2**20)


def cost():
    return pl.CostEstimate(flops=0, bytes_accessed=0, transcendentals=0)


def tile_kernel(heads, flip, *refs):
    out_ref = refs[-1]
    tiles = refs[0].shape[0] // TILE
    for head in range(heads):
        for which, flipped in enumerate(flip):
            for tile in range(tiles):
                block = refs[which][
                    tile * TILE : (tile + 1) * TILE, head * HEAD_DIM : (head + 1) * HEAD_DIM
                ]
                at = (tile * heads + head) * len(flip) + which
                out_ref[at] = block.T if flipped else block


def as_tiles(arrays, flip):
    rows, width = arrays[0].shape
    heads = width // HEAD_DIM
    count = len(arrays) * heads * rows // TILE
    return pl.pallas_call(
        functools.partial(tile_kernel, heads, flip),
        in_specs=[VMEM] * len(arrays),
        out_specs=VMEM,
        out_shape=jax.ShapeDtypeStruct((count, TILE, HEAD_DIM), arrays[0].dtype),
        compiler_params=params(4),
    )(*arrays)


def list_kernel(heads, length, where_ref, lists_ref, live_ref, table_ref, ends, metas, places):
    tiles = live_ref.shape[0]
    part_tiles = tiles // heads
    frame, head = where_ref[0], where_ref[1]
    base = (lax.rem(frame, PLANE) * (2 * PLANE + 1) + PLANE - frame) * 2
    targets = range(LISTS * heads)
    for target in targets:
        ends[target] = target * length
    for row in range(tiles):
        part, inner = divmod(row, part_tiles)

        def slot_step(slot, carry, row=row, part=part, inner=inner):
            listed = lists_ref[row, slot]
            within = listed & (tiles - 1)
            rank = within >> int(math.log2(part_tiles))
            spot = ((within & (part_tiles - 1)) * heads + head) * 2
            side = jnp.where(spot < cut_of(2 * tiles), 0, 1)
            entry = table_ref[base + 2 * (listed >> int(math.log2(tiles))) + side]
            step = (rank - head) & (heads - 1)
            turn = (rank - part) & (heads - 1)
            own = turn == 0
            query = (turn * part_tiles + inner) * heads + head
            query = jnp.where(own, query, query - heads * part_tiles)
            target = step * LISTS + 2 * (entry & 3) + jnp.where(own, 1, 0)
            at = ends[target]
            places[at] = (entry >> 2) + spot
            metas[at >> 2] = query * 8 + (at & (GROUP - 1))
            ends[target] = at + 1
            return carry

        lax.fori_loop(0, live_ref[row], slot_step, 0)
        for target in targets:
            at = ends[target]
            up = (at + GROUP - 1) & -GROUP
            filler = places[jnp.maximum(at - 1, 0)]
            for other in range(GROUP - 1):
                spare = LISTS * heads * length
                places[jnp.where(at + other < up, at + other, spare)] = filler
            ends[target] = up
    for target in targets:
        ends[target] = (ends[target] - target * length) >> 2


def work_lists(frame, head, tile_lists, live_slots, heads):
    tiles, slots = tile_lists.shape
    assert tiles & (tiles - 1) == 0 and heads & (heads - 1) == 0 and GROUP == 4
    length = tiles * (slots // GROUP + 1) * GROUP
    total = LISTS * heads * length
    ends, metas, places = pl.pallas_call(
        functools.partial(list_kernel, heads, length),
        in_specs=[SMEM] * 4,
        out_specs=[SMEM] * 3,
        out_shape=[
            jax.ShapeDtypeStruct((LISTS * heads,), jnp.int32),
            jax.ShapeDtypeStruct((total // GROUP,), jnp.int32),
            jax.ShapeDtypeStruct((total + 1,), jnp.int32),
        ],
        compiler_params=params(4),
        cost_estimate=cost(),
    )(jnp.stack((frame, head)), tile_lists, live_slots, jnp.asarray(shard_table(2 * tiles, cut_of(2 * tiles))))
    arrays = ends, metas, places[:total]
    return jnp.concatenate([array.reshape(heads, -1) for array in arrays], axis=1)


def packed(numbers):
    rows = -(-numbers.shape[0] // TILE)
    numbers = jnp.pad(numbers, (0, rows * TILE - numbers.shape[0])).reshape(rows, TILE)
    digits = jnp.concatenate((numbers & 255, numbers >> 8)).astype(jnp.bfloat16)
    return jnp.pad(digits, ((0, -2 * rows % 16), (0, 0)))


def unpacked(block, count):
    rows = -(-count // TILE)
    digits = block.astype(jnp.int32)
    return (digits[:rows] + digits[rows : 2 * rows] * 256).reshape(-1)[:count]


def phase_kernel(which, pieces, begins, ends, lists, q_ref, *refs):
    refs = list(refs)
    state = [refs.pop(0) for _ in range(0 if begins else 3)]
    parts = [refs.pop(0) for _ in range(pieces)]
    out_ref, stats_ref = [refs.pop(0) for _ in range(2)] if ends else [None] * 2
    top_ref, total_ref, sum_ref, scores, high, weights, shrinks = refs[:7]
    window = refs[7] if pieces > 1 else parts[0]
    tiles = q_ref.shape[0]
    heads, width = lists.shape
    length = (width - LISTS) // (LISTS * (GROUP + 1))

    at = 0
    for part in parts if pieces > 1 else ():
        window[at : at + part.shape[0]] = part[...]
        at += part.shape[0]
    if begins:
        top_ref[...] = jnp.full(top_ref.shape, -FAR_OFF, jnp.float32)
        total_ref[...] = jnp.zeros(total_ref.shape, jnp.float32)
        sum_ref[...] = jnp.zeros(sum_ref.shape, jnp.float32)
    else:
        for ref, old in zip((top_ref, total_ref, sum_ref), state):
            ref[...] = old[...]

    starts = [jnp.int32(0)]
    for head in range(heads):
        starts.append(starts[-1] + lists[head, which])

    def item_of(item):
        row, index = jnp.int32(0), item
        for head in range(1, heads):
            row = jnp.where(item >= starts[head], head, row)
            index = jnp.where(item >= starts[head], item - starts[head], index)
        real = item < starts[heads]
        row, index = jnp.where(real, row, 0), jnp.where(real, index, 0)
        meta = lists[row, LISTS + which * length + index]
        at = LISTS * (1 + length) + (which * length + index) * GROUP
        tile = jnp.where(real, meta >> 3, 0)
        spots = [jnp.where(real, lists[row, at + slot], 0) for slot in range(GROUP)]
        return tile, jnp.where(real, meta & 7, -1), spots

    def score(entry):
        tile, _, spots = entry
        keys = jnp.concatenate([window[spot] for spot in spots])
        block = jnp.dot(keys, q_ref[tile], preferred_element_type=jnp.float32)
        top = jnp.max(block.reshape(-1, 8, TILE), axis=0)
        return block, jnp.max(top, axis=0, keepdims=True)

    def weigh(entry, block, peak):
        tile, last, _ = entry
        old = top_ref[tile]
        top = jnp.maximum(old, jnp.where(last < 0, -FAR_OFF, peak))
        shrink = jnp.exp2((old - top) * FACTOR)
        total = total_ref[tile] * shrink
        parts = []
        for slot in range(GROUP):
            shift = jnp.where(slot <= last, top, FAR_OFF)
            weight = jnp.exp2((block[slot * TILE : (slot + 1) * TILE] - shift) * FACTOR)
            total = total + jnp.sum(weight.reshape(-1, 8, TILE), axis=0)
            parts.append(weight.astype(jnp.bfloat16))
        top_ref[tile] = top
        total_ref[tile] = total
        return jnp.concatenate(parts), shrink

    def collect(entry, weight, shrink):
        tile, _, spots = entry
        values = jnp.concatenate([window[spot + 1] for spot in spots], axis=1)
        product = jnp.dot(values, weight, preferred_element_type=jnp.float32)
        sum_ref[tile] = sum_ref[tile] * shrink + product

    entry, entry_1 = item_of(0), item_of(1)
    block, peak = score(entry)
    scores[...], high[...] = score(entry_1)
    weights[...], shrinks[...] = weigh(entry, block, peak)

    def step(pair, entries):
        entry, entry_1 = entries
        entry_2, entry_3 = item_of(2 * pair + 2), item_of(2 * pair + 3)
        block, peak, weight, shrink = scores[...], high[...], weights[...], shrinks[...]
        block_2, peak_2 = score(entry_2)
        weight_1, shrink_1 = weigh(entry_1, block, peak)
        collect(entry, weight, shrink)
        block_3, peak_3 = score(entry_3)
        weight_2, shrink_2 = weigh(entry_2, block_2, peak_2)
        collect(entry_1, weight_1, shrink_1)
        scores[...], high[...] = block_3, peak_3
        weights[...], shrinks[...] = weight_2, shrink_2
        return entry_2, entry_3

    lax.fori_loop(0, (starts[heads] + 1) >> 1, step, (entry, entry_1))
    if ends:
        for tile in range(tiles):
            total = jnp.sum(total_ref[tile], axis=0, keepdims=True)
            share = jnp.where(total > 0, 1.0 / jnp.where(total > 0, total, 1.0), 0.0)
            out_ref[tile] = (sum_ref[tile] * share).astype(out_ref.dtype)
            stats_ref[tile, 0:1] = total
            stats_ref[tile, 1:2] = top_ref[tile]


def attend(lists, which, queries, state, pieces, ends):
    tiles = queries.shape[0]
    begins = state is None
    held = [
        jax.ShapeDtypeStruct((tiles, 1, TILE), jnp.float32),
        jax.ShapeDtypeStruct((tiles, 8, TILE), jnp.float32),
        jax.ShapeDtypeStruct((tiles, HEAD_DIM, TILE), jnp.float32),
    ]
    scratch = [
        pltpu.VMEM((GROUP * TILE, TILE), jnp.float32),
        pltpu.VMEM((1, TILE), jnp.float32),
        pltpu.VMEM((GROUP * TILE, TILE), queries.dtype),
        pltpu.VMEM((1, TILE), jnp.float32),
    ]
    if len(pieces) > 1:
        rows = sum(piece.shape[0] for piece in pieces)
        scratch.append(pltpu.VMEM((rows, TILE, TILE), queries.dtype))
    if ends:
        scratch = [pltpu.VMEM(array.shape, array.dtype) for array in held] + scratch
        held = [
            jax.ShapeDtypeStruct((tiles, HEAD_DIM, TILE), queries.dtype),
            jax.ShapeDtypeStruct((tiles, 2, TILE), jnp.float32),
        ]
    return pl.pallas_call(
        functools.partial(phase_kernel, which, len(pieces), begins, ends),
        in_specs=[SMEM] + [VMEM] * (1 + len(pieces) + (0 if begins else 3)),
        out_specs=[VMEM] * len(held),
        out_shape=held,
        scratch_shapes=scratch,
        compiler_params=params(10),
        cost_estimate=cost(),
    )(lists, queries, *([] if begins else state), *pieces)


def merge_kernel(count, *refs):
    out_ref = refs[-1]
    values, stats = [refs[first : 2 * count : 2] for first in range(2)]
    tiles = values[0].shape[0]
    heads = out_ref.shape[1] // HEAD_DIM
    for tile in range(tiles):
        top = stats[0][tile, 1:2]
        for ref in stats[1:]:
            top = jnp.maximum(top, ref[tile, 1:2])
        shares = [ref[tile, 0:1] * jnp.exp2((ref[tile, 1:2] - top) * FACTOR) for ref in stats]
        whole = sum(shares[1:], shares[0])
        out = jnp.zeros((HEAD_DIM, TILE), jnp.float32)
        for value, share in zip(values, shares):
            out = out + value[tile].astype(jnp.float32) * (share / whole)
        inner, head = divmod(tile, heads)
        out_ref[
            inner * TILE : (inner + 1) * TILE, head * HEAD_DIM : (head + 1) * HEAD_DIM
        ] = out.T.astype(out_ref.dtype)


def merge(parts, rows, heads):
    flat = [array for part in parts for array in part]
    return pl.pallas_call(
        functools.partial(merge_kernel, len(parts)),
        in_specs=[VMEM] * len(flat),
        out_specs=VMEM,
        out_shape=jax.ShapeDtypeStruct((rows, heads * HEAD_DIM), flat[0].dtype),
        compiler_params=params(6),
    )(*flat)


def moved(block, axis, source):
    size = lax.axis_size(axis)
    route = [(source(i), i) for i in range(size) if 0 <= source(i) < size]
    return lax.ppermute(block, axis, route)


def body(queries, key_vectors, value_vectors, tile_lists, live_slots):
    heads = lax.axis_size("head")
    frame = lax.axis_index("frame")
    head = lax.axis_index("head")
    shard_tiles = tile_lists.shape[1]
    assert shard_tiles * PLANE == REACH and lax.axis_size("frame") % PLANE == 0

    def from_head(block, step):
        return moved(block, "head", lambda i: (i - step) % heads)

    def core_swap(block):
        return moved(block, "frame", lambda i: i ^ 1)

    own = as_tiles((key_vectors, value_vectors), (False, True))
    size = own.shape[0]
    cut = cut_of(size)
    across = moved(own, "frame", lambda i: i ^ 2)
    chip = jnp.concatenate((core_swap(own), own))
    level = moved(chip, "frame", lambda i: i - PLANE if i % 2 == 0 else i + PLANE)

    listed, live, _ = lax.optimization_barrier((tile_lists[0], live_slots[0], chip))
    lists = work_lists(frame, head, listed, live, heads)
    q_own = as_tiles((queries,), (True,))
    blocks = [
        from_head(jnp.concatenate((q_own.reshape(-1, TILE), packed(lists[step]))), step)
        for step in range(1, heads)
    ]
    blocks, _ = lax.optimization_barrier((blocks, level))
    q_parts, by_head = [], [lists[:1]]
    for block in blocks:
        q_rows = shard_tiles * TILE
        q_parts.append(block[:q_rows].reshape(q_own.shape))
        by_head.append(unpacked(block[q_rows:], lists.shape[1])[None])
    q_rest, by_head = jnp.concatenate(q_parts), jnp.concatenate(by_head)

    far_z = moved(across[:cut], "frame", lambda i: i - PLANE if i % PLANE < 2 else i + PLANE)
    pair = jnp.concatenate((level[cut:size], level[size + cut :]))
    pair = moved(pair, "frame", lambda i: {1: i + 1, 2: i - 1}.get(i % PLANE, -1))
    near = [chip, level, across, core_swap(across), core_swap(level[:size])]
    state = attend(by_head, 0, q_rest, None, near, False)
    far_z, pair, state = lax.optimization_barrier((far_z, pair, state))
    far = [far_z, pair, core_swap(jnp.concatenate((far_z, pair)))]
    rest = attend(by_head, 2, q_rest, state, far, True)
    parts = [None]
    for step in range(1, heads):
        cut = slice((step - 1) * shard_tiles, step * shard_tiles)
        parts.append([from_head(array[cut], -step) for array in rest])
    q_own, _ = lax.optimization_barrier((q_own, rest))
    state = attend(by_head, 1, q_own, None, near, False)
    parts[0] = attend(by_head, 3, q_own, state, far, True)
    return merge(parts, queries.shape[0], heads)


def solution(mesh):
    placed = (
        P(("frame", "head"), None),
        P(("frame", "head"), None),
        P(("frame", "head"), None),
        P("head", "frame", None),
        P("head", "frame"),
    )
    return jax.shard_map(
        body, mesh=mesh, in_specs=placed, out_specs=P(("frame", "head"), None), check_vma=False
    )
```

```python
import functools
import math

import jax
import jax.numpy as jnp
import numpy as np
from jax import lax
from jax.experimental import pallas as pl
from jax.experimental.pallas import tpu as pltpu
from jax.sharding import PartitionSpec as P

TILE = 128
HEAD_DIM = 128
REACH = 32
PLANE = 4
GROUP = 4
LISTS = 4
FAR_OFF = 1e30
FACTOR = math.log2(math.e) / math.sqrt(HEAD_DIM)
VMEM = pl.BlockSpec(memory_space=pltpu.VMEM)
SMEM = pl.BlockSpec(memory_space=pltpu.SMEM)


def shard_table(size, cut):
    table = np.zeros((PLANE, 2 * PLANE + 1, 2), np.int32)
    for place in range(PLANE):
        x, core = divmod(place, 2)
        for distance in range(-PLANE, PLANE + 1):
            plane, there = divmod(place + distance, PLANE)
            same_x, same_core = there // 2 == x, there % 2 == core
            phase = 0
            if plane == 0:
                first = second = size * (int(same_core) if same_x else (4 if same_core else 5))
            elif not same_x:
                swapped = 2 * size - cut
                phase, first = 1, 0 if same_core else swapped
                second = (0 if x == core else swapped) + int(there % 2 == x) * (size - cut)
            elif (plane < 0) == (core == 0):
                first = second = size * (2 + int(same_core))
            else:
                first = second = size * 6
            table[place, distance + PLANE] = phase + 4 * first, phase + 4 * second
    return table.reshape(-1)


def cut_of(size):
    return size * 5 // 8


def params(mib):
    return pltpu.CompilerParams(vmem_limit_bytes=mib * 2**20)


def cost():
    return pl.CostEstimate(flops=0, bytes_accessed=0, transcendentals=0)


def tile_kernel(heads, flip, *refs):
    out_ref = refs[-1]
    tiles = refs[0].shape[0] // TILE
    for head in range(heads):
        for which, flipped in enumerate(flip):
            for tile in range(tiles):
                block = refs[which][
                    tile * TILE : (tile + 1) * TILE, head * HEAD_DIM : (head + 1) * HEAD_DIM
                ]
                at = (tile * heads + head) * len(flip) + which
                out_ref[at] = block.T if flipped else block


def as_tiles(arrays, flip):
    rows, width = arrays[0].shape
    heads = width // HEAD_DIM
    count = len(arrays) * heads * rows // TILE
    return pl.pallas_call(
        functools.partial(tile_kernel, heads, flip),
        in_specs=[VMEM] * len(arrays),
        out_specs=VMEM,
        out_shape=jax.ShapeDtypeStruct((count, TILE, HEAD_DIM), arrays[0].dtype),
        compiler_params=params(4),
    )(*arrays)


def list_kernel(heads, length, where_ref, lists_ref, live_ref, table_ref, ends, metas, places):
    tiles = live_ref.shape[0]
    part_tiles = tiles // heads
    frame, head = where_ref[0], where_ref[1]
    base = (lax.rem(frame, PLANE) * (2 * PLANE + 1) + PLANE - frame) * 2
    targets = range(LISTS * heads)
    for target in targets:
        ends[target] = target * length
    for row in range(tiles):
        part, inner = divmod(row, part_tiles)

        def slot_step(slot, carry, row=row, part=part, inner=inner):
            listed = lists_ref[row, slot]
            within = listed & (tiles - 1)
            rank = within >> int(math.log2(part_tiles))
            spot = ((within & (part_tiles - 1)) * heads + head) * 2
            side = jnp.where(spot < cut_of(2 * tiles), 0, 1)
            entry = table_ref[base + 2 * (listed >> int(math.log2(tiles))) + side]
            step = (rank - head) & (heads - 1)
            turn = (rank - part) & (heads - 1)
            own = turn == 0
            query = (turn * part_tiles + inner) * heads + head
            query = jnp.where(own, query, query - heads * part_tiles)
            target = step * LISTS + 2 * (entry & 3) + jnp.where(own, 1, 0)
            at = ends[target]
            places[at] = (entry >> 2) + spot
            metas[at >> 2] = query * 8 + (at & (GROUP - 1))
            ends[target] = at + 1
            return carry

        lax.fori_loop(0, live_ref[row], slot_step, 0)
        for target in targets:
            at = ends[target]
            up = (at + GROUP - 1) & -GROUP
            filler = places[jnp.maximum(at - 1, 0)]
            for other in range(GROUP - 1):
                spare = LISTS * heads * length
                places[jnp.where(at + other < up, at + other, spare)] = filler
            ends[target] = up
    for target in targets:
        ends[target] = (ends[target] - target * length) >> 2


def work_lists(frame, head, tile_lists, live_slots, heads):
    tiles, slots = tile_lists.shape
    assert tiles & (tiles - 1) == 0 and heads & (heads - 1) == 0 and GROUP == 4
    length = tiles * (slots // GROUP + 1) * GROUP
    total = LISTS * heads * length
    ends, metas, places = pl.pallas_call(
        functools.partial(list_kernel, heads, length),
        in_specs=[SMEM] * 4,
        out_specs=[SMEM] * 3,
        out_shape=[
            jax.ShapeDtypeStruct((LISTS * heads,), jnp.int32),
            jax.ShapeDtypeStruct((total // GROUP,), jnp.int32),
            jax.ShapeDtypeStruct((total + 1,), jnp.int32),
        ],
        compiler_params=params(4),
        cost_estimate=cost(),
    )(jnp.stack((frame, head)), tile_lists, live_slots, jnp.asarray(shard_table(2 * tiles, cut_of(2 * tiles))))
    arrays = ends, metas, places[:total]
    return jnp.concatenate([array.reshape(heads, -1) for array in arrays], axis=1)


def packed(numbers):
    rows = -(-numbers.shape[0] // TILE)
    numbers = jnp.pad(numbers, (0, rows * TILE - numbers.shape[0])).reshape(rows, TILE)
    digits = jnp.concatenate((numbers & 255, numbers >> 8)).astype(jnp.bfloat16)
    return jnp.pad(digits, ((0, -2 * rows % 16), (0, 0)))


def unpacked(block, count):
    rows = -(-count // TILE)
    digits = block.astype(jnp.int32)
    return (digits[:rows] + digits[rows : 2 * rows] * 256).reshape(-1)[:count]


def phase_kernel(which, pieces, begins, ends, lists, q_ref, *refs):
    refs = list(refs)
    state = [refs.pop(0) for _ in range(0 if begins else 3)]
    parts = [refs.pop(0) for _ in range(pieces)]
    out_ref, stats_ref = [refs.pop(0) for _ in range(2)] if ends else [None] * 2
    top_ref, total_ref, sum_ref, scores, high, weights, shrinks = refs[:7]
    window = refs[7] if pieces > 1 else parts[0]
    tiles = q_ref.shape[0]
    heads, width = lists.shape
    length = (width - LISTS) // (LISTS * (GROUP + 1))

    at = 0
    for part in parts if pieces > 1 else ():
        window[at : at + part.shape[0]] = part[...]
        at += part.shape[0]
    if begins:
        top_ref[...] = jnp.full(top_ref.shape, -FAR_OFF, jnp.float32)
        total_ref[...] = jnp.zeros(total_ref.shape, jnp.float32)
        sum_ref[...] = jnp.zeros(sum_ref.shape, jnp.float32)
    else:
        for ref, old in zip((top_ref, total_ref, sum_ref), state):
            ref[...] = old[...]

    starts = [jnp.int32(0)]
    for head in range(heads):
        starts.append(starts[-1] + lists[head, which])

    def item_of(item):
        row, index = jnp.int32(0), item
        for head in range(1, heads):
            row = jnp.where(item >= starts[head], head, row)
            index = jnp.where(item >= starts[head], item - starts[head], index)
        real = item < starts[heads]
        row, index = jnp.where(real, row, 0), jnp.where(real, index, 0)
        meta = lists[row, LISTS + which * length + index]
        at = LISTS * (1 + length) + (which * length + index) * GROUP
        tile = jnp.where(real, meta >> 3, 0)
        spots = [jnp.where(real, lists[row, at + slot], 0) for slot in range(GROUP)]
        return tile, jnp.where(real, meta & 7, -1), spots

    def score(entry):
        tile, _, spots = entry
        keys = jnp.concatenate([window[spot] for spot in spots])
        block = jnp.dot(keys, q_ref[tile], preferred_element_type=jnp.float32)
        top = jnp.max(block.reshape(-1, 8, TILE), axis=0)
        return block, jnp.max(top, axis=0, keepdims=True)

    def weigh(entry, block, peak):
        tile, last, _ = entry
        old = top_ref[tile]
        top = jnp.maximum(old, jnp.where(last < 0, -FAR_OFF, peak))
        shrink = jnp.exp2((old - top) * FACTOR)
        total = total_ref[tile] * shrink
        parts = []
        for slot in range(GROUP):
            shift = jnp.where(slot <= last, top, FAR_OFF)
            weight = jnp.exp2((block[slot * TILE : (slot + 1) * TILE] - shift) * FACTOR)
            total = total + jnp.sum(weight.reshape(-1, 8, TILE), axis=0)
            parts.append(weight.astype(jnp.bfloat16))
        top_ref[tile] = top
        total_ref[tile] = total
        return jnp.concatenate(parts), shrink

    def collect(entry, weight, shrink):
        tile, _, spots = entry
        values = jnp.concatenate([window[spot + 1] for spot in spots], axis=1)
        product = jnp.dot(values, weight, preferred_element_type=jnp.float32)
        sum_ref[tile] = sum_ref[tile] * shrink + product

    entry, entry_1 = item_of(0), item_of(1)
    block, peak = score(entry)
    scores[...], high[...] = score(entry_1)
    weights[...], shrinks[...] = weigh(entry, block, peak)

    def step(pair, entries):
        entry, entry_1 = entries
        entry_2, entry_3 = item_of(2 * pair + 2), item_of(2 * pair + 3)
        block, peak, weight, shrink = scores[...], high[...], weights[...], shrinks[...]
        block_2, peak_2 = score(entry_2)
        weight_1, shrink_1 = weigh(entry_1, block, peak)
        collect(entry, weight, shrink)
        block_3, peak_3 = score(entry_3)
        weight_2, shrink_2 = weigh(entry_2, block_2, peak_2)
        collect(entry_1, weight_1, shrink_1)
        scores[...], high[...] = block_3, peak_3
        weights[...], shrinks[...] = weight_2, shrink_2
        return entry_2, entry_3

    lax.fori_loop(0, (starts[heads] + 1) >> 1, step, (entry, entry_1))
    if ends:
        for tile in range(tiles):
            total = jnp.sum(total_ref[tile], axis=0, keepdims=True)
            share = jnp.where(total > 0, 1.0 / jnp.where(total > 0, total, 1.0), 0.0)
            out_ref[tile] = (sum_ref[tile] * share).astype(out_ref.dtype)
            stats_ref[tile, 0:1] = total
            stats_ref[tile, 1:2] = top_ref[tile]


def attend(lists, which, queries, state, pieces, ends):
    tiles = queries.shape[0]
    begins = state is None
    held = [
        jax.ShapeDtypeStruct((tiles, 1, TILE), jnp.float32),
        jax.ShapeDtypeStruct((tiles, 8, TILE), jnp.float32),
        jax.ShapeDtypeStruct((tiles, HEAD_DIM, TILE), jnp.float32),
    ]
    scratch = [
        pltpu.VMEM((GROUP * TILE, TILE), jnp.float32),
        pltpu.VMEM((1, TILE), jnp.float32),
        pltpu.VMEM((GROUP * TILE, TILE), queries.dtype),
        pltpu.VMEM((1, TILE), jnp.float32),
    ]
    if len(pieces) > 1:
        rows = sum(piece.shape[0] for piece in pieces)
        scratch.append(pltpu.VMEM((rows, TILE, TILE), queries.dtype))
    if ends:
        scratch = [pltpu.VMEM(array.shape, array.dtype) for array in held] + scratch
        held = [
            jax.ShapeDtypeStruct((tiles, HEAD_DIM, TILE), queries.dtype),
            jax.ShapeDtypeStruct((tiles, 2, TILE), jnp.float32),
        ]
    return pl.pallas_call(
        functools.partial(phase_kernel, which, len(pieces), begins, ends),
        in_specs=[SMEM] + [VMEM] * (1 + len(pieces) + (0 if begins else 3)),
        out_specs=[VMEM] * len(held),
        out_shape=held,
        scratch_shapes=scratch,
        compiler_params=params(10),
        cost_estimate=cost(),
    )(lists, queries, *([] if begins else state), *pieces)


def merge_kernel(count, *refs):
    out_ref = refs[-1]
    values, stats = [refs[first : 2 * count : 2] for first in range(2)]
    tiles = values[0].shape[0]
    heads = out_ref.shape[1] // HEAD_DIM
    for tile in range(tiles):
        top = stats[0][tile, 1:2]
        for ref in stats[1:]:
            top = jnp.maximum(top, ref[tile, 1:2])
        shares = [ref[tile, 0:1] * jnp.exp2((ref[tile, 1:2] - top) * FACTOR) for ref in stats]
        whole = sum(shares[1:], shares[0])
        out = jnp.zeros((HEAD_DIM, TILE), jnp.float32)
        for value, share in zip(values, shares):
            out = out + value[tile].astype(jnp.float32) * (share / whole)
        inner, head = divmod(tile, heads)
        out_ref[
            inner * TILE : (inner + 1) * TILE, head * HEAD_DIM : (head + 1) * HEAD_DIM
        ] = out.T.astype(out_ref.dtype)


def merge(parts, rows, heads):
    flat = [array for part in parts for array in part]
    return pl.pallas_call(
        functools.partial(merge_kernel, len(parts)),
        in_specs=[VMEM] * len(flat),
        out_specs=VMEM,
        out_shape=jax.ShapeDtypeStruct((rows, heads * HEAD_DIM), flat[0].dtype),
        compiler_params=params(6),
    )(*flat)


def moved(block, axis, source):
    size = lax.axis_size(axis)
    route = [(source(i), i) for i in range(size) if 0 <= source(i) < size]
    return lax.ppermute(block, axis, route)


def body(queries, key_vectors, value_vectors, tile_lists, live_slots):
    heads = lax.axis_size("head")
    frame = lax.axis_index("frame")
    head = lax.axis_index("head")
    shard_tiles = tile_lists.shape[1]
    assert shard_tiles * PLANE == REACH and lax.axis_size("frame") % PLANE == 0

    def from_head(block, step):
        return moved(block, "head", lambda i: (i - step) % heads)

    def core_swap(block):
        return moved(block, "frame", lambda i: i ^ 1)

    own = as_tiles((key_vectors, value_vectors), (False, True))
    size = own.shape[0]
    cut = cut_of(size)
    across = moved(own, "frame", lambda i: i ^ 2)
    chip = jnp.concatenate((core_swap(own), own))
    level = moved(chip, "frame", lambda i: i - PLANE if i % 2 == 0 else i + PLANE)

    listed, live, _ = lax.optimization_barrier((tile_lists[0], live_slots[0], chip))
    lists = work_lists(frame, head, listed, live, heads)
    q_own = as_tiles((queries,), (True,))
    blocks = [
        from_head(jnp.concatenate((q_own.reshape(-1, TILE), packed(lists[step]))), step)
        for step in range(1, heads)
    ]
    blocks, _ = lax.optimization_barrier((blocks, level))
    q_parts, by_head = [], [lists[:1]]
    for block in blocks:
        q_rows = shard_tiles * TILE
        q_parts.append(block[:q_rows].reshape(q_own.shape))
        by_head.append(unpacked(block[q_rows:], lists.shape[1])[None])
    q_rest, by_head = jnp.concatenate(q_parts), jnp.concatenate(by_head)

    far_z = moved(across[:cut], "frame", lambda i: i - PLANE if i % PLANE < 2 else i + PLANE)
    pair = jnp.concatenate((level[cut:size], level[size + cut :]))
    pair = moved(pair, "frame", lambda i: {0: i + 2, 3: i - 2}.get(i % PLANE, -1))
    near = [chip, level, across, core_swap(across), core_swap(level[:size])]
    state = attend(by_head, 0, q_rest, None, near, False)
    far_z, pair, state = lax.optimization_barrier((far_z, pair, state))
    far = [far_z, pair, core_swap(jnp.concatenate((far_z, pair)))]
    rest = attend(by_head, 2, q_rest, state, far, True)
    parts = [None]
    for step in range(1, heads):
        cut = slice((step - 1) * shard_tiles, step * shard_tiles)
        parts.append([from_head(array[cut], -step) for array in rest])
    q_own, _ = lax.optimization_barrier((q_own, rest))
    state = attend(by_head, 1, q_own, None, near, False)
    parts[0] = attend(by_head, 3, q_own, state, far, True)
    return merge(parts, queries.shape[0], heads)


def solution(mesh):
    placed = (
        P(("frame", "head"), None),
        P(("frame", "head"), None),
        P(("frame", "head"), None),
        P("head", "frame", None),
        P("head", "frame"),
    )
    return jax.shard_map(
        body, mesh=mesh, in_specs=placed, out_specs=P(("frame", "head"), None), check_vma=False
    )
```

```python
import functools
import math

import jax
import jax.numpy as jnp
import numpy as np
from jax import lax
from jax.experimental import pallas as pl
from jax.experimental.pallas import tpu as pltpu
from jax.sharding import PartitionSpec as P

TILE = 128
HEAD_DIM = 128
REACH = 32
PLANE = 4
GROUP = 4
LISTS = 4
FAR_OFF = 1e30
FACTOR = math.log2(math.e) / math.sqrt(HEAD_DIM)
VMEM = pl.BlockSpec(memory_space=pltpu.VMEM)
SMEM = pl.BlockSpec(memory_space=pltpu.SMEM)


def shard_table():
    table = np.zeros((PLANE, 2 * PLANE + 1), np.int32)
    for place in range(PLANE):
        x, core = divmod(place, 2)
        for distance in range(-PLANE, PLANE + 1):
            plane, there = divmod(place + distance, PLANE)
            same_x, same_core = there // 2 == x, there % 2 == core
            phase = 0
            if plane == 0:
                spot = int(same_core) if same_x else (4 if same_core else 5)
            elif not same_x:
                phase, spot = 1, 0 if same_core else 1
            elif (plane < 0) == (core == 0):
                spot = 2 + int(same_core)
            else:
                spot = 6
            table[place, distance + PLANE] = phase + 4 * spot
    return table.reshape(-1)


def params(mib):
    return pltpu.CompilerParams(vmem_limit_bytes=mib * 2**20)


def cost():
    return pl.CostEstimate(flops=0, bytes_accessed=0, transcendentals=0)


def tile_kernel(heads, flip, *refs):
    out_ref = refs[-1]
    tiles = refs[0].shape[0] // TILE
    for head in range(heads):
        for which, flipped in enumerate(flip):
            for tile in range(tiles):
                block = refs[which][
                    tile * TILE : (tile + 1) * TILE, head * HEAD_DIM : (head + 1) * HEAD_DIM
                ]
                at = (tile * heads + head) * len(flip) + which
                out_ref[at] = block.T if flipped else block


def as_tiles(arrays, flip):
    rows, width = arrays[0].shape
    heads = width // HEAD_DIM
    count = len(arrays) * heads * rows // TILE
    return pl.pallas_call(
        functools.partial(tile_kernel, heads, flip),
        in_specs=[VMEM] * len(arrays),
        out_specs=VMEM,
        out_shape=jax.ShapeDtypeStruct((count, TILE, HEAD_DIM), arrays[0].dtype),
        compiler_params=params(4),
    )(*arrays)


def list_kernel(heads, length, where_ref, lists_ref, live_ref, table_ref, ends, metas, places):
    tiles = live_ref.shape[0]
    part_tiles = tiles // heads
    frame, head = where_ref[0], where_ref[1]
    base = lax.rem(frame, PLANE) * (2 * PLANE + 1) + PLANE - frame
    targets = range(LISTS * heads)
    for target in targets:
        ends[target] = target * length
    for row in range(tiles):
        part, inner = divmod(row, part_tiles)

        def slot_step(slot, carry, row=row, part=part, inner=inner):
            listed = lists_ref[row, slot]
            within = listed & (tiles - 1)
            rank = within >> int(math.log2(part_tiles))
            spot = ((within & (part_tiles - 1)) * heads + head) * 2
            entry = table_ref[base + (listed >> int(math.log2(tiles)))]
            step = (rank - head) & (heads - 1)
            turn = (rank - part) & (heads - 1)
            own = turn == 0
            query = (turn * part_tiles + inner) * heads + head
            query = jnp.where(own, query, query - heads * part_tiles)
            target = step * LISTS + 2 * (entry & 3) + jnp.where(own, 1, 0)
            at = ends[target]
            places[at] = (entry >> 2) * (2 * tiles) + spot
            metas[at >> 2] = query * 8 + (at & (GROUP - 1))
            ends[target] = at + 1
            return carry

        lax.fori_loop(0, live_ref[row], slot_step, 0)
        for target in targets:
            at = ends[target]
            up = (at + GROUP - 1) & -GROUP
            filler = places[jnp.maximum(at - 1, 0)]
            for other in range(GROUP - 1):
                spare = LISTS * heads * length
                places[jnp.where(at + other < up, at + other, spare)] = filler
            ends[target] = up
    for target in targets:
        ends[target] = (ends[target] - target * length) >> 2


def work_lists(frame, head, tile_lists, live_slots, heads):
    tiles, slots = tile_lists.shape
    assert tiles & (tiles - 1) == 0 and heads & (heads - 1) == 0 and GROUP == 4
    length = tiles * (slots // GROUP + 1) * GROUP
    total = LISTS * heads * length
    ends, metas, places = pl.pallas_call(
        functools.partial(list_kernel, heads, length),
        in_specs=[SMEM] * 4,
        out_specs=[SMEM] * 3,
        out_shape=[
            jax.ShapeDtypeStruct((LISTS * heads,), jnp.int32),
            jax.ShapeDtypeStruct((total // GROUP,), jnp.int32),
            jax.ShapeDtypeStruct((total + 1,), jnp.int32),
        ],
        compiler_params=params(4),
        cost_estimate=cost(),
    )(jnp.stack((frame, head)), tile_lists, live_slots, jnp.asarray(shard_table()))
    arrays = ends, metas, places[:total]
    return jnp.concatenate([array.reshape(heads, -1) for array in arrays], axis=1)


def packed(numbers):
    rows = -(-numbers.shape[0] // TILE)
    numbers = jnp.pad(numbers, (0, rows * TILE - numbers.shape[0])).reshape(rows, TILE)
    digits = jnp.concatenate((numbers & 255, numbers >> 8)).astype(jnp.bfloat16)
    return jnp.pad(digits, ((0, -2 * rows % 16), (0, 0)))


def unpacked(block, count):
    rows = -(-count // TILE)
    digits = block.astype(jnp.int32)
    return (digits[:rows] + digits[rows : 2 * rows] * 256).reshape(-1)[:count]


def phase_kernel(which, pieces, begins, ends, lists, q_ref, *refs):
    refs = list(refs)
    state = [refs.pop(0) for _ in range(0 if begins else 3)]
    parts = [refs.pop(0) for _ in range(pieces)]
    out_ref, stats_ref = [refs.pop(0) for _ in range(2)] if ends else [None] * 2
    top_ref, total_ref, sum_ref, scores, high, weights, shrinks = refs[:7]
    window = refs[7] if pieces > 1 else parts[0]
    tiles = q_ref.shape[0]
    heads, width = lists.shape
    length = (width - LISTS) // (LISTS * (GROUP + 1))

    at = 0
    for part in parts if pieces > 1 else ():
        window[at : at + part.shape[0]] = part[...]
        at += part.shape[0]
    if begins:
        top_ref[...] = jnp.full(top_ref.shape, -FAR_OFF, jnp.float32)
        total_ref[...] = jnp.zeros(total_ref.shape, jnp.float32)
        sum_ref[...] = jnp.zeros(sum_ref.shape, jnp.float32)
    else:
        for ref, old in zip((top_ref, total_ref, sum_ref), state):
            ref[...] = old[...]

    starts = [jnp.int32(0)]
    for head in range(heads):
        starts.append(starts[-1] + lists[head, which])

    def item_of(item):
        row, index = jnp.int32(0), item
        for head in range(1, heads):
            row = jnp.where(item >= starts[head], head, row)
            index = jnp.where(item >= starts[head], item - starts[head], index)
        real = item < starts[heads]
        row, index = jnp.where(real, row, 0), jnp.where(real, index, 0)
        meta = lists[row, LISTS + which * length + index]
        at = LISTS * (1 + length) + (which * length + index) * GROUP
        tile = jnp.where(real, meta >> 3, 0)
        spots = [jnp.where(real, lists[row, at + slot], 0) for slot in range(GROUP)]
        return tile, jnp.where(real, meta & 7, -1), spots

    def score(entry):
        tile, _, spots = entry
        keys = jnp.concatenate([window[spot] for spot in spots])
        block = jnp.dot(keys, q_ref[tile], preferred_element_type=jnp.float32)
        top = jnp.max(block.reshape(-1, 8, TILE), axis=0)
        return block, jnp.max(top, axis=0, keepdims=True)

    def weigh(entry, block, peak):
        tile, last, _ = entry
        old = top_ref[tile]
        top = jnp.maximum(old, jnp.where(last < 0, -FAR_OFF, peak))
        shrink = jnp.exp2((old - top) * FACTOR)
        total = total_ref[tile] * shrink
        parts = []
        for slot in range(GROUP):
            shift = jnp.where(slot <= last, top, FAR_OFF)
            weight = jnp.exp2((block[slot * TILE : (slot + 1) * TILE] - shift) * FACTOR)
            total = total + jnp.sum(weight.reshape(-1, 8, TILE), axis=0)
            parts.append(weight.astype(jnp.bfloat16))
        top_ref[tile] = top
        total_ref[tile] = total
        return jnp.concatenate(parts), shrink

    def collect(entry, weight, shrink):
        tile, _, spots = entry
        values = jnp.concatenate([window[spot + 1] for spot in spots], axis=1)
        product = jnp.dot(values, weight, preferred_element_type=jnp.float32)
        sum_ref[tile] = sum_ref[tile] * shrink + product

    entry, entry_1 = item_of(0), item_of(1)
    block, peak = score(entry)
    scores[...], high[...] = score(entry_1)
    weights[...], shrinks[...] = weigh(entry, block, peak)

    def step(pair, entries):
        entry, entry_1 = entries
        entry_2, entry_3 = item_of(2 * pair + 2), item_of(2 * pair + 3)
        block, peak, weight, shrink = scores[...], high[...], weights[...], shrinks[...]
        block_2, peak_2 = score(entry_2)
        weight_1, shrink_1 = weigh(entry_1, block, peak)
        collect(entry, weight, shrink)
        block_3, peak_3 = score(entry_3)
        weight_2, shrink_2 = weigh(entry_2, block_2, peak_2)
        collect(entry_1, weight_1, shrink_1)
        scores[...], high[...] = block_3, peak_3
        weights[...], shrinks[...] = weight_2, shrink_2
        return entry_2, entry_3

    lax.fori_loop(0, (starts[heads] + 1) >> 1, step, (entry, entry_1))
    if ends:
        for tile in range(tiles):
            total = jnp.sum(total_ref[tile], axis=0, keepdims=True)
            share = jnp.where(total > 0, 1.0 / jnp.where(total > 0, total, 1.0), 0.0)
            out_ref[tile] = (sum_ref[tile] * share).astype(out_ref.dtype)
            stats_ref[tile, 0:1] = total
            stats_ref[tile, 1:2] = top_ref[tile]


def attend(lists, which, queries, state, pieces, ends):
    tiles = queries.shape[0]
    begins = state is None
    held = [
        jax.ShapeDtypeStruct((tiles, 1, TILE), jnp.float32),
        jax.ShapeDtypeStruct((tiles, 8, TILE), jnp.float32),
        jax.ShapeDtypeStruct((tiles, HEAD_DIM, TILE), jnp.float32),
    ]
    scratch = [
        pltpu.VMEM((GROUP * TILE, TILE), jnp.float32),
        pltpu.VMEM((1, TILE), jnp.float32),
        pltpu.VMEM((GROUP * TILE, TILE), queries.dtype),
        pltpu.VMEM((1, TILE), jnp.float32),
    ]
    if len(pieces) > 1:
        rows = sum(piece.shape[0] for piece in pieces)
        scratch.append(pltpu.VMEM((rows, TILE, TILE), queries.dtype))
    if ends:
        scratch = [pltpu.VMEM(array.shape, array.dtype) for array in held] + scratch
        held = [
            jax.ShapeDtypeStruct((tiles, HEAD_DIM, TILE), queries.dtype),
            jax.ShapeDtypeStruct((tiles, 2, TILE), jnp.float32),
        ]
    return pl.pallas_call(
        functools.partial(phase_kernel, which, len(pieces), begins, ends),
        in_specs=[SMEM] + [VMEM] * (1 + len(pieces) + (0 if begins else 3)),
        out_specs=[VMEM] * len(held),
        out_shape=held,
        scratch_shapes=scratch,
        compiler_params=params(10),
        cost_estimate=cost(),
    )(lists, queries, *([] if begins else state), *pieces)


def merge_kernel(count, *refs):
    out_ref = refs[-1]
    values, stats = [refs[first : 2 * count : 2] for first in range(2)]
    tiles = values[0].shape[0]
    heads = out_ref.shape[1] // HEAD_DIM
    for tile in range(tiles):
        top = stats[0][tile, 1:2]
        for ref in stats[1:]:
            top = jnp.maximum(top, ref[tile, 1:2])
        shares = [ref[tile, 0:1] * jnp.exp2((ref[tile, 1:2] - top) * FACTOR) for ref in stats]
        whole = sum(shares[1:], shares[0])
        out = jnp.zeros((HEAD_DIM, TILE), jnp.float32)
        for value, share in zip(values, shares):
            out = out + value[tile].astype(jnp.float32) * (share / whole)
        inner, head = divmod(tile, heads)
        out_ref[
            inner * TILE : (inner + 1) * TILE, head * HEAD_DIM : (head + 1) * HEAD_DIM
        ] = out.T.astype(out_ref.dtype)


def merge(parts, rows, heads):
    flat = [array for part in parts for array in part]
    return pl.pallas_call(
        functools.partial(merge_kernel, len(parts)),
        in_specs=[VMEM] * len(flat),
        out_specs=VMEM,
        out_shape=jax.ShapeDtypeStruct((rows, heads * HEAD_DIM), flat[0].dtype),
        compiler_params=params(6),
    )(*flat)


def moved(block, axis, source):
    size = lax.axis_size(axis)
    route = [(source(i), i) for i in range(size) if 0 <= source(i) < size]
    return lax.ppermute(block, axis, route)


def body(queries, key_vectors, value_vectors, tile_lists, live_slots):
    heads = lax.axis_size("head")
    frame = lax.axis_index("frame")
    head = lax.axis_index("head")
    shard_tiles = tile_lists.shape[1]
    assert shard_tiles * PLANE == REACH and lax.axis_size("frame") % PLANE == 0

    def from_head(block, step):
        return moved(block, "head", lambda i: (i - step) % heads)

    def core_swap(block):
        return moved(block, "frame", lambda i: i ^ 1)

    own = as_tiles((key_vectors, value_vectors), (False, True))
    size = own.shape[0]
    cut = size * 5 // 8
    across = moved(own, "frame", lambda i: i ^ 2)
    chip = jnp.concatenate((core_swap(own), own))
    level = moved(chip, "frame", lambda i: i - PLANE if i % 2 == 0 else i + PLANE)

    listed, live, _ = lax.optimization_barrier((tile_lists[0], live_slots[0], chip))
    lists = work_lists(frame, head, listed, live, heads)
    q_own = as_tiles((queries,), (True,))
    blocks = [
        from_head(jnp.concatenate((q_own.reshape(-1, TILE), packed(lists[step]))), step)
        for step in range(1, heads)
    ]
    blocks, _ = lax.optimization_barrier((blocks, level))
    q_parts, by_head = [], [lists[:1]]
    for block in blocks:
        q_rows = shard_tiles * TILE
        q_parts.append(block[:q_rows].reshape(q_own.shape))
        by_head.append(unpacked(block[q_rows:], lists.shape[1])[None])
    q_rest, by_head = jnp.concatenate(q_parts), jnp.concatenate(by_head)

    far_z = moved(across[:cut], "frame", lambda i: i - PLANE if i % PLANE < 2 else i + PLANE)
    straight = moved(own[cut:], "frame", lambda i: i - 2 if i % PLANE < 2 else i + 2)
    near = [chip, level, across, core_swap(across), core_swap(level[:size])]
    state = attend(by_head, 0, q_rest, None, near, False)
    far_z, straight, state = lax.optimization_barrier((far_z, straight, state))
    far = jnp.concatenate((far_z, straight))
    far = [far, core_swap(far)]
    rest = attend(by_head, 2, q_rest, state, far, True)
    parts = [None]
    for step in range(1, heads):
        cut = slice((step - 1) * shard_tiles, step * shard_tiles)
        parts.append([from_head(array[cut], -step) for array in rest])
    q_own, _ = lax.optimization_barrier((q_own, rest))
    state = attend(by_head, 1, q_own, None, near, False)
    parts[0] = attend(by_head, 3, q_own, state, far, True)
    return merge(parts, queries.shape[0], heads)


def solution(mesh):
    placed = (
        P(("frame", "head"), None),
        P(("frame", "head"), None),
        P(("frame", "head"), None),
        P("head", "frame", None),
        P("head", "frame"),
    )
    return jax.shard_map(
        body, mesh=mesh, in_specs=placed, out_specs=P(("frame", "head"), None), check_vma=False
    )
```

```python
import functools
import math

import jax
import jax.numpy as jnp
import numpy as np
from jax import lax
from jax.experimental import pallas as pl
from jax.experimental.pallas import tpu as pltpu
from jax.sharding import PartitionSpec as P

TILE = 128
HEAD_DIM = 128
REACH = 32
PLANE = 4
GROUPS = 4, 4, 2
LISTS = 6
ROWS = 6
FAR_OFF = 1e30
FACTOR = math.log2(math.e) / math.sqrt(HEAD_DIM)
VMEM = pl.BlockSpec(memory_space=pltpu.VMEM)
SMEM = pl.BlockSpec(memory_space=pltpu.SMEM)


def shard_table():
    table = np.zeros((PLANE, 2 * PLANE + 1), np.int32)
    for place in range(PLANE):
        x, core = divmod(place, 2)
        for distance in range(-PLANE, PLANE + 1):
            plane, there = divmod(place + distance, PLANE)
            same_x, same_core = there // 2 == x, there % 2 == core
            if plane == 0:
                phase, spot = 0, int(same_core) if same_x else (2 if same_core else 3)
            elif not same_x:
                phase, spot = 2, 0 if same_core else 1
            elif (plane < 0) == (core == 0):
                phase, spot = 1, 4 + int(same_core)
            else:
                phase, spot = 1, 6
            table[place, distance + PLANE] = phase + 4 * spot
    return table.reshape(-1)


def params(mib):
    return pltpu.CompilerParams(vmem_limit_bytes=mib * 2**20)


def cost():
    return pl.CostEstimate(flops=0, bytes_accessed=0, transcendentals=0)


def tile_kernel(heads, flip, *refs):
    out_ref = refs[-1]
    tiles = refs[0].shape[0] // TILE
    for head in range(heads):
        for which, flipped in enumerate(flip):
            for tile in range(tiles):
                block = refs[which][
                    tile * TILE : (tile + 1) * TILE, head * HEAD_DIM : (head + 1) * HEAD_DIM
                ]
                at = (tile * heads + head) * len(flip) + which
                out_ref[at] = block.T if flipped else block


def as_tiles(arrays, flip):
    rows, width = arrays[0].shape
    heads = width // HEAD_DIM
    count = len(arrays) * heads * rows // TILE
    return pl.pallas_call(
        functools.partial(tile_kernel, heads, flip),
        in_specs=[VMEM] * len(arrays),
        out_specs=VMEM,
        out_shape=jax.ShapeDtypeStruct((count, TILE, HEAD_DIM), arrays[0].dtype),
        compiler_params=params(4),
    )(*arrays)


def list_kernel(heads, length, where_ref, lists_ref, live_ref, table_ref, ends, metas, places):
    tiles = live_ref.shape[0]
    part_tiles = tiles // heads
    frame, head = where_ref[0], where_ref[1]
    base = lax.rem(frame, PLANE) * (2 * PLANE + 1) + PLANE - frame
    width = max(GROUPS)
    targets = [(target, GROUPS[target % LISTS // 2]) for target in range(LISTS * heads)]
    for target, _ in targets:
        ends[target] = 0
    for row in range(tiles):
        part, inner = divmod(row, part_tiles)

        def slot_step(slot, carry, row=row, part=part, inner=inner):
            listed = lists_ref[row, slot]
            within = listed & (tiles - 1)
            rank = within >> int(math.log2(part_tiles))
            spot = ((within & (part_tiles - 1)) * heads + head) * 2
            entry = table_ref[base + (listed >> int(math.log2(tiles)))]
            step = (rank - head) & (heads - 1)
            turn = (rank - part) & (heads - 1)
            own = turn == 0
            query = (turn * part_tiles + inner) * heads + head
            query = jnp.where(own, query, query - heads * part_tiles)
            phase = entry & 3
            target = step * LISTS + 2 * phase + jnp.where(own, 1, 0)
            small = phase == len(GROUPS) - 1
            at = ends[target]
            item = at >> jnp.where(small, 1, 2)
            places[target * (length * width) + at] = (entry >> 2) * (2 * tiles) + spot
            metas[target * length + item] = query * 8 + (at & jnp.where(small, 1, 3))
            ends[target] = at + 1
            return carry

        lax.fori_loop(0, live_ref[row], slot_step, 0)
        for target, group in targets:
            at = ends[target]
            up = (at + group - 1) & -group
            first = target * (length * width)
            filler = places[first + jnp.maximum(at - 1, 0)]
            for other in range(group - 1):
                spare = LISTS * heads * length * width
                places[jnp.where(at + other < up, first + at + other, spare)] = filler
            ends[target] = up
    for target, group in targets:
        ends[target] = ends[target] // group


def work_lists(frame, head, tile_lists, live_slots, heads):
    tiles, slots = tile_lists.shape
    assert tiles & (tiles - 1) == 0 and heads & (heads - 1) == 0 and GROUPS == (4, 4, 2)
    assert slots <= 4 * (ROWS - 1) and 2 * tiles // heads <= 2 * (ROWS - 1)
    length = tiles * ROWS
    total = LISTS * heads * length
    ends, metas, places = pl.pallas_call(
        functools.partial(list_kernel, heads, length),
        in_specs=[SMEM] * 4,
        out_specs=[SMEM] * 3,
        out_shape=[
            jax.ShapeDtypeStruct((LISTS * heads,), jnp.int32),
            jax.ShapeDtypeStruct((total,), jnp.int32),
            jax.ShapeDtypeStruct((total * max(GROUPS) + 1,), jnp.int32),
        ],
        compiler_params=params(4),
        cost_estimate=cost(),
    )(jnp.stack((frame, head)), tile_lists, live_slots, jnp.asarray(shard_table()))
    arrays = ends, metas, places[: total * max(GROUPS)]
    return jnp.concatenate([array.reshape(heads, -1) for array in arrays], axis=1)


def packed(numbers):
    rows = -(-numbers.shape[0] // TILE)
    numbers = jnp.pad(numbers, (0, rows * TILE - numbers.shape[0])).reshape(rows, TILE)
    digits = jnp.concatenate((numbers & 255, numbers >> 8)).astype(jnp.bfloat16)
    return jnp.pad(digits, ((0, -2 * rows % 16), (0, 0)))


def unpacked(block, count):
    rows = -(-count // TILE)
    digits = block.astype(jnp.int32)
    return (digits[:rows] + digits[rows : 2 * rows] * 256).reshape(-1)[:count]


def phase_kernel(whiches, shift, pieces, begins, ends, lists, q_ref, *refs):
    refs = list(refs)
    state = [refs.pop(0) for _ in range(0 if begins else 3)]
    parts = [refs.pop(0) for _ in range(pieces)]
    out_ref, stats_ref = [refs.pop(0) for _ in range(2)] if ends else [None] * 2
    top_ref, total_ref, sum_ref, scores, high, weights, shrinks = refs[:7]
    window = refs[7] if pieces > 1 else parts[0]
    tiles = q_ref.shape[0]
    heads, width = lists.shape
    length = (width - LISTS) // (LISTS * (max(GROUPS) + 1))
    group = GROUPS[whiches[0] // 2]

    at = 0
    for part in parts if pieces > 1 else ():
        window[at : at + part.shape[0]] = part[...]
        at += part.shape[0]
    if begins:
        top_ref[...] = jnp.full(top_ref.shape, -FAR_OFF, jnp.float32)
        total_ref[...] = jnp.zeros(total_ref.shape, jnp.float32)
        sum_ref[...] = jnp.zeros(sum_ref.shape, jnp.float32)
    else:
        for ref, old in zip((top_ref, total_ref, sum_ref), state):
            ref[...] = old[...]

    blocks = [(which, head) for which in whiches for head in range(heads)]
    starts = [jnp.int32(0)]
    for which, head in blocks:
        starts.append(starts[-1] + lists[head, which])

    def item_of(item):
        row, which, index = jnp.int32(0), jnp.int32(blocks[0][0]), item
        for number in range(1, len(blocks)):
            later = item >= starts[number]
            row = jnp.where(later, blocks[number][1], row)
            which = jnp.where(later, blocks[number][0], which)
            index = jnp.where(later, item - starts[number], index)
        real = item < starts[-1]
        row, index = jnp.where(real, row, 0), jnp.where(real, index, 0)
        meta = lists[row, LISTS + which * length + index]
        at = LISTS * (1 + length) + which * (length * max(GROUPS)) + index * group
        tile = jnp.where(real, meta >> 3, 0)
        spots = [jnp.where(real, lists[row, at + slot] - shift, 0) for slot in range(group)]
        return tile, jnp.where(real, meta & 7, -1), spots

    def score(entry):
        tile, _, spots = entry
        keys = jnp.concatenate([window[spot] for spot in spots])
        block = jnp.dot(keys, q_ref[tile], preferred_element_type=jnp.float32)
        top = jnp.max(block.reshape(-1, 8, TILE), axis=0)
        return block, jnp.max(top, axis=0, keepdims=True)

    def weigh(entry, block, peak):
        tile, last, _ = entry
        old = top_ref[tile]
        top = jnp.maximum(old, jnp.where(last < 0, -FAR_OFF, peak))
        shrink = jnp.exp2((old - top) * FACTOR)
        total = total_ref[tile] * shrink
        parts = []
        for slot in range(group):
            level = jnp.where(slot <= last, top, FAR_OFF)
            weight = jnp.exp2((block[slot * TILE : (slot + 1) * TILE] - level) * FACTOR)
            total = total + jnp.sum(weight.reshape(-1, 8, TILE), axis=0)
            parts.append(weight.astype(jnp.bfloat16))
        top_ref[tile] = top
        total_ref[tile] = total
        return jnp.concatenate(parts), shrink

    def collect(entry, weight, shrink):
        tile, _, spots = entry
        values = jnp.concatenate([window[spot + 1] for spot in spots], axis=1)
        product = jnp.dot(values, weight, preferred_element_type=jnp.float32)
        sum_ref[tile] = sum_ref[tile] * shrink + product

    entry, entry_1 = item_of(0), item_of(1)
    block, peak = score(entry)
    scores[...], high[...] = score(entry_1)
    weights[...], shrinks[...] = weigh(entry, block, peak)

    def step(pair, entries):
        entry, entry_1 = entries
        entry_2, entry_3 = item_of(2 * pair + 2), item_of(2 * pair + 3)
        block, peak, weight, shrink = scores[...], high[...], weights[...], shrinks[...]
        block_2, peak_2 = score(entry_2)
        weight_1, shrink_1 = weigh(entry_1, block, peak)
        collect(entry, weight, shrink)
        block_3, peak_3 = score(entry_3)
        weight_2, shrink_2 = weigh(entry_2, block_2, peak_2)
        collect(entry_1, weight_1, shrink_1)
        scores[...], high[...] = block_3, peak_3
        weights[...], shrinks[...] = weight_2, shrink_2
        return entry_2, entry_3

    lax.fori_loop(0, (starts[-1] + 1) >> 1, step, (entry, entry_1))
    if ends:
        for tile in range(tiles):
            total = jnp.sum(total_ref[tile], axis=0, keepdims=True)
            share = jnp.where(total > 0, 1.0 / jnp.where(total > 0, total, 1.0), 0.0)
            out_ref[tile] = (sum_ref[tile] * share).astype(out_ref.dtype)
            stats_ref[tile, 0:1] = total
            stats_ref[tile, 1:2] = top_ref[tile]


def attend(lists, whiches, shift, queries, state, pieces, ends):
    tiles = queries.shape[0]
    begins = state is None
    held = [
        jax.ShapeDtypeStruct((tiles, 1, TILE), jnp.float32),
        jax.ShapeDtypeStruct((tiles, 8, TILE), jnp.float32),
        jax.ShapeDtypeStruct((tiles, HEAD_DIM, TILE), jnp.float32),
    ]
    rows = GROUPS[whiches[0] // 2] * TILE
    scratch = [
        pltpu.VMEM((rows, TILE), jnp.float32),
        pltpu.VMEM((1, TILE), jnp.float32),
        pltpu.VMEM((rows, TILE), queries.dtype),
        pltpu.VMEM((1, TILE), jnp.float32),
    ]
    if len(pieces) > 1:
        count = sum(piece.shape[0] for piece in pieces)
        scratch.append(pltpu.VMEM((count, TILE, TILE), queries.dtype))
    if ends:
        scratch = [pltpu.VMEM(array.shape, array.dtype) for array in held] + scratch
        held = [
            jax.ShapeDtypeStruct((tiles, HEAD_DIM, TILE), queries.dtype),
            jax.ShapeDtypeStruct((tiles, 2, TILE), jnp.float32),
        ]
    return pl.pallas_call(
        functools.partial(phase_kernel, whiches, shift, len(pieces), begins, ends),
        in_specs=[SMEM] + [VMEM] * (1 + len(pieces) + (0 if begins else 3)),
        out_specs=[VMEM] * len(held),
        out_shape=held,
        scratch_shapes=scratch,
        compiler_params=params(10),
        cost_estimate=cost(),
    )(lists, queries, *([] if begins else state), *pieces)


def merge_kernel(count, *refs):
    out_ref = refs[-1]
    values, stats = [refs[first : 2 * count : 2] for first in range(2)]
    tiles = values[0].shape[0]
    heads = out_ref.shape[1] // HEAD_DIM
    for tile in range(tiles):
        top = stats[0][tile, 1:2]
        for ref in stats[1:]:
            top = jnp.maximum(top, ref[tile, 1:2])
        shares = [ref[tile, 0:1] * jnp.exp2((ref[tile, 1:2] - top) * FACTOR) for ref in stats]
        whole = sum(shares[1:], shares[0])
        out = jnp.zeros((HEAD_DIM, TILE), jnp.float32)
        for value, share in zip(values, shares):
            out = out + value[tile].astype(jnp.float32) * (share / whole)
        inner, head = divmod(tile, heads)
        out_ref[
            inner * TILE : (inner + 1) * TILE, head * HEAD_DIM : (head + 1) * HEAD_DIM
        ] = out.T.astype(out_ref.dtype)


def merge(parts, rows, heads):
    flat = [array for part in parts for array in part]
    return pl.pallas_call(
        functools.partial(merge_kernel, len(parts)),
        in_specs=[VMEM] * len(flat),
        out_specs=VMEM,
        out_shape=jax.ShapeDtypeStruct((rows, heads * HEAD_DIM), flat[0].dtype),
        compiler_params=params(6),
    )(*flat)


def moved(block, axis, source):
    size = lax.axis_size(axis)
    route = [(source(i), i) for i in range(size) if 0 <= source(i) < size]
    return lax.ppermute(block, axis, route)


def body(queries, key_vectors, value_vectors, tile_lists, live_slots):
    heads = lax.axis_size("head")
    frame = lax.axis_index("frame")
    head = lax.axis_index("head")
    shard_tiles = tile_lists.shape[1]
    assert shard_tiles * PLANE == REACH and lax.axis_size("frame") % PLANE == 0

    def from_head(block, step):
        return moved(block, "head", lambda i: (i - step) % heads)

    def core_swap(block):
        return moved(block, "frame", lambda i: i ^ 1)

    own = as_tiles((key_vectors, value_vectors), (False, True))
    size = own.shape[0]
    cut = size // 2
    across = moved(own, "frame", lambda i: i ^ 2)
    chip = jnp.concatenate((core_swap(own), own))
    level = moved(chip, "frame", lambda i: i - PLANE if i % 2 == 0 else i + PLANE)

    listed, live, _ = lax.optimization_barrier((tile_lists[0], live_slots[0], chip))
    lists = work_lists(frame, head, listed, live, heads)
    q_own = as_tiles((queries,), (True,))
    blocks = [
        from_head(jnp.concatenate((q_own.reshape(-1, TILE), packed(lists[step]))), step)
        for step in range(1, heads)
    ]
    blocks, _ = lax.optimization_barrier((blocks, level))
    q_parts, by_head = [], [lists[:1]]
    for block in blocks:
        q_rows = shard_tiles * TILE
        q_parts.append(block[:q_rows].reshape(q_own.shape))
        by_head.append(unpacked(block[q_rows:], lists.shape[1])[None])
    q_rest, by_head = jnp.concatenate(q_parts), jnp.concatenate(by_head)

    far_z = moved(across[:cut], "frame", lambda i: i - PLANE if i % PLANE < 2 else i + PLANE)
    straight = moved(own[cut:], "frame", lambda i: i - 2 if i % PLANE < 2 else i + 2)
    plane = [chip, across, core_swap(across)]
    state = attend(by_head, (0,), 0, q_rest, None, plane, False)
    level_core, state = lax.optimization_barrier((core_swap(level[:size]), state))
    planes = [level, level_core]
    state = attend(by_head, (2,), 4 * size, q_rest, state, planes, False)
    far_z, straight, state = lax.optimization_barrier((far_z, straight, state))
    far = jnp.concatenate((far_z, straight))
    far = [far, core_swap(far)]
    rest = attend(by_head, (4,), 0, q_rest, state, far, True)
    parts = [None]
    for step in range(1, heads):
        cut = slice((step - 1) * shard_tiles, step * shard_tiles)
        parts.append([from_head(array[cut], -step) for array in rest])
    q_own, _ = lax.optimization_barrier((q_own, rest))
    state = attend(by_head, (1, 3), 0, q_own, None, plane + planes, False)
    parts[0] = attend(by_head, (5,), 0, q_own, state, far, True)
    return merge(parts, queries.shape[0], heads)


def solution(mesh):
    placed = (
        P(("frame", "head"), None),
        P(("frame", "head"), None),
        P(("frame", "head"), None),
        P("head", "frame", None),
        P("head", "frame"),
    )
    return jax.shard_map(
        body, mesh=mesh, in_specs=placed, out_specs=P(("frame", "head"), None), check_vma=False
    )
```

```python
import functools
import math

import jax
import jax.numpy as jnp
import numpy as np
from jax import lax
from jax.experimental import pallas as pl
from jax.experimental.pallas import tpu as pltpu
from jax.sharding import PartitionSpec as P

TILE = 128
HEAD_DIM = 128
REACH = 32
PLANE = 4
GROUP = 4
LISTS = 4
FAR_OFF = 1e30
FACTOR = math.log2(math.e) / math.sqrt(HEAD_DIM)
VMEM = pl.BlockSpec(memory_space=pltpu.VMEM)
SMEM = pl.BlockSpec(memory_space=pltpu.SMEM)


def shard_table():
    table = np.zeros((PLANE, 2 * PLANE + 1), np.int32)
    for place in range(PLANE):
        x, core = divmod(place, 2)
        for distance in range(-PLANE, PLANE + 1):
            plane, there = divmod(place + distance, PLANE)
            same_x, same_core = there // 2 == x, there % 2 == core
            phase = 0
            if plane == 0:
                spot = int(same_core) if same_x else (4 if same_core else 5)
            elif not same_x:
                phase, spot = 1, 0 if same_core else 1
            elif (plane < 0) == (core == 0):
                spot = 2 + int(same_core)
            else:
                spot = 6
            table[place, distance + PLANE] = phase + 4 * spot
    return table.reshape(-1)


def params(mib):
    return pltpu.CompilerParams(vmem_limit_bytes=mib * 2**20)


def cost():
    return pl.CostEstimate(flops=0, bytes_accessed=0, transcendentals=0)


def tile_kernel(heads, flip, *refs):
    out_ref = refs[-1]
    tiles = refs[0].shape[0] // TILE
    for head in range(heads):
        for which, flipped in enumerate(flip):
            for tile in range(tiles):
                block = refs[which][
                    tile * TILE : (tile + 1) * TILE, head * HEAD_DIM : (head + 1) * HEAD_DIM
                ]
                at = (tile * heads + head) * len(flip) + which
                out_ref[at] = block.T if flipped else block


def as_tiles(arrays, flip):
    rows, width = arrays[0].shape
    heads = width // HEAD_DIM
    count = len(arrays) * heads * rows // TILE
    return pl.pallas_call(
        functools.partial(tile_kernel, heads, flip),
        in_specs=[VMEM] * len(arrays),
        out_specs=VMEM,
        out_shape=jax.ShapeDtypeStruct((count, TILE, HEAD_DIM), arrays[0].dtype),
        compiler_params=params(4),
    )(*arrays)


def list_kernel(heads, length, where_ref, lists_ref, live_ref, table_ref, ends, metas, places):
    tiles = live_ref.shape[0]
    part_tiles = tiles // heads
    frame, head = where_ref[0], where_ref[1]
    base = lax.rem(frame, PLANE) * (2 * PLANE + 1) + PLANE - frame
    targets = range(LISTS * heads)
    for target in targets:
        ends[target] = target * length
    for row in range(tiles):
        part, inner = divmod(row, part_tiles)

        def slot_step(slot, carry, row=row, part=part, inner=inner):
            listed = lists_ref[row, slot]
            within = listed & (tiles - 1)
            rank = within >> int(math.log2(part_tiles))
            spot = ((within & (part_tiles - 1)) * heads + head) * 2
            entry = table_ref[base + (listed >> int(math.log2(tiles)))]
            step = (rank - head) & (heads - 1)
            turn = (rank - part) & (heads - 1)
            own = turn == 0
            query = (turn * part_tiles + inner) * heads + head
            query = jnp.where(own, query, query - heads * part_tiles)
            target = step * LISTS + 2 * (entry & 3) + jnp.where(own, 1, 0)
            at = ends[target]
            places[at] = (entry >> 2) * (2 * tiles) + spot
            metas[at >> 2] = query * 8 + (at & (GROUP - 1))
            ends[target] = at + 1
            return carry

        lax.fori_loop(0, live_ref[row], slot_step, 0)
        for target in targets:
            at = ends[target]
            up = (at + GROUP - 1) & -GROUP
            filler = places[jnp.maximum(at - 1, 0)]
            for other in range(GROUP - 1):
                spare = LISTS * heads * length
                places[jnp.where(at + other < up, at + other, spare)] = filler
            ends[target] = up
    for target in targets:
        ends[target] = (ends[target] - target * length) >> 2


def work_lists(frame, head, tile_lists, live_slots, heads):
    tiles, slots = tile_lists.shape
    assert tiles & (tiles - 1) == 0 and heads & (heads - 1) == 0 and GROUP == 4
    length = tiles * (slots // GROUP + 1) * GROUP
    total = LISTS * heads * length
    ends, metas, places = pl.pallas_call(
        functools.partial(list_kernel, heads, length),
        in_specs=[SMEM] * 4,
        out_specs=[SMEM] * 3,
        out_shape=[
            jax.ShapeDtypeStruct((LISTS * heads,), jnp.int32),
            jax.ShapeDtypeStruct((total // GROUP,), jnp.int32),
            jax.ShapeDtypeStruct((total + 1,), jnp.int32),
        ],
        compiler_params=params(4),
        cost_estimate=cost(),
    )(jnp.stack((frame, head)), tile_lists, live_slots, jnp.asarray(shard_table()))
    arrays = ends, metas, places[:total]
    return jnp.concatenate([array.reshape(heads, -1) for array in arrays], axis=1)


def packed(numbers):
    rows = -(-numbers.shape[0] // TILE)
    numbers = jnp.pad(numbers, (0, rows * TILE - numbers.shape[0])).reshape(rows, TILE)
    digits = jnp.concatenate((numbers & 255, numbers >> 8)).astype(jnp.bfloat16)
    return jnp.pad(digits, ((0, -2 * rows % 16), (0, 0)))


def unpacked(block, count):
    rows = -(-count // TILE)
    digits = block.astype(jnp.int32)
    return (digits[:rows] + digits[rows : 2 * rows] * 256).reshape(-1)[:count]


def phase_kernel(which, pieces, begins, ends, lists, q_ref, *refs):
    refs = list(refs)
    state = [refs.pop(0) for _ in range(0 if begins else 3)]
    parts = [refs.pop(0) for _ in range(pieces)]
    out_ref, stats_ref = [refs.pop(0) for _ in range(2)] if ends else [None] * 2
    top_ref, total_ref, sum_ref, scores, high, weights, shrinks = refs[:7]
    window = refs[7] if pieces > 1 else parts[0]
    tiles = q_ref.shape[0]
    heads, width = lists.shape
    length = (width - LISTS) // (LISTS * (GROUP + 1))

    at = 0
    for part in parts if pieces > 1 else ():
        window[at : at + part.shape[0]] = part[...]
        at += part.shape[0]
    if begins:
        top_ref[...] = jnp.full(top_ref.shape, -FAR_OFF, jnp.float32)
        total_ref[...] = jnp.zeros(total_ref.shape, jnp.float32)
        sum_ref[...] = jnp.zeros(sum_ref.shape, jnp.float32)
    else:
        for ref, old in zip((top_ref, total_ref, sum_ref), state):
            ref[...] = old[...]

    starts = [jnp.int32(0)]
    for head in range(heads):
        starts.append(starts[-1] + lists[head, which])

    def item_of(item):
        row, index = jnp.int32(0), item
        for head in range(1, heads):
            row = jnp.where(item >= starts[head], head, row)
            index = jnp.where(item >= starts[head], item - starts[head], index)
        real = item < starts[heads]
        row, index = jnp.where(real, row, 0), jnp.where(real, index, 0)
        meta = lists[row, LISTS + which * length + index]
        at = LISTS * (1 + length) + (which * length + index) * GROUP
        tile = jnp.where(real, meta >> 3, 0)
        spots = [jnp.where(real, lists[row, at + slot], 0) for slot in range(GROUP)]
        return tile, jnp.where(real, meta & 7, -1), spots

    def score(entry):
        tile, _, spots = entry
        keys = jnp.concatenate([window[spot] for spot in spots])
        block = jnp.dot(keys, q_ref[tile], preferred_element_type=jnp.float32)
        top = jnp.max(block.reshape(-1, 8, TILE), axis=0)
        return block, jnp.max(top, axis=0, keepdims=True)

    def weigh(entry, block, peak):
        tile, last, _ = entry
        old = top_ref[tile]
        top = jnp.maximum(old, jnp.where(last < 0, -FAR_OFF, peak))
        shrink = jnp.exp2((old - top) * FACTOR)
        total = total_ref[tile] * shrink
        parts = []
        for slot in range(GROUP):
            shift = jnp.where(slot <= last, top, FAR_OFF)
            weight = jnp.exp2((block[slot * TILE : (slot + 1) * TILE] - shift) * FACTOR)
            total = total + jnp.sum(weight.reshape(-1, 8, TILE), axis=0)
            parts.append(weight.astype(jnp.bfloat16))
        top_ref[tile] = top
        total_ref[tile] = total
        return jnp.concatenate(parts), shrink

    def collect(entry, weight, shrink):
        tile, _, spots = entry
        values = jnp.concatenate([window[spot + 1] for spot in spots], axis=1)
        product = jnp.dot(values, weight, preferred_element_type=jnp.float32)
        sum_ref[tile] = sum_ref[tile] * shrink + product

    def store_scores(pair):
        for number, (block, peak) in enumerate(pair):
            scores[number], high[number] = block, peak

    def store_weights(pair):
        for number, (weight, shrink) in enumerate(pair):
            weights[number], shrinks[number] = weight, shrink

    ahead = [item_of(0), item_of(1)]
    second = [item_of(2), item_of(3)]
    first = [score(entry) for entry in ahead]
    store_scores([score(entry) for entry in second])
    store_weights([weigh(entry, *made) for entry, made in zip(ahead, first)])

    def step(pair, entries):
        collected, weighed = entries[:2], entries[2:]
        scored = [item_of(2 * pair + 4), item_of(2 * pair + 5)]
        made = [(scores[number], high[number]) for number in range(2)]
        formed = [(weights[number], shrinks[number]) for number in range(2)]
        blocks = [score(entry) for entry in scored]
        following = [weigh(entry, *item) for entry, item in zip(weighed, made)]
        for entry, item in zip(collected, formed):
            collect(entry, *item)
        store_scores(blocks)
        store_weights(following)
        return tuple(weighed) + tuple(scored)

    lax.fori_loop(0, (starts[heads] + 1) >> 1, step, tuple(ahead + second))
    if ends:
        for tile in range(tiles):
            total = jnp.sum(total_ref[tile], axis=0, keepdims=True)
            share = jnp.where(total > 0, 1.0 / jnp.where(total > 0, total, 1.0), 0.0)
            out_ref[tile] = (sum_ref[tile] * share).astype(out_ref.dtype)
            stats_ref[tile, 0:1] = total
            stats_ref[tile, 1:2] = top_ref[tile]


def attend(lists, which, queries, state, pieces, ends):
    tiles = queries.shape[0]
    begins = state is None
    held = [
        jax.ShapeDtypeStruct((tiles, 1, TILE), jnp.float32),
        jax.ShapeDtypeStruct((tiles, 8, TILE), jnp.float32),
        jax.ShapeDtypeStruct((tiles, HEAD_DIM, TILE), jnp.float32),
    ]
    scratch = [
        pltpu.VMEM((2, GROUP * TILE, TILE), jnp.float32),
        pltpu.VMEM((2, 1, TILE), jnp.float32),
        pltpu.VMEM((2, GROUP * TILE, TILE), queries.dtype),
        pltpu.VMEM((2, 1, TILE), jnp.float32),
    ]
    if len(pieces) > 1:
        rows = sum(piece.shape[0] for piece in pieces)
        scratch.append(pltpu.VMEM((rows, TILE, TILE), queries.dtype))
    if ends:
        scratch = [pltpu.VMEM(array.shape, array.dtype) for array in held] + scratch
        held = [
            jax.ShapeDtypeStruct((tiles, HEAD_DIM, TILE), queries.dtype),
            jax.ShapeDtypeStruct((tiles, 2, TILE), jnp.float32),
        ]
    return pl.pallas_call(
        functools.partial(phase_kernel, which, len(pieces), begins, ends),
        in_specs=[SMEM] + [VMEM] * (1 + len(pieces) + (0 if begins else 3)),
        out_specs=[VMEM] * len(held),
        out_shape=held,
        scratch_shapes=scratch,
        compiler_params=params(10),
        cost_estimate=cost(),
    )(lists, queries, *([] if begins else state), *pieces)


def merge_kernel(count, *refs):
    out_ref = refs[-1]
    values, stats = [refs[first : 2 * count : 2] for first in range(2)]
    tiles = values[0].shape[0]
    heads = out_ref.shape[1] // HEAD_DIM
    for tile in range(tiles):
        top = stats[0][tile, 1:2]
        for ref in stats[1:]:
            top = jnp.maximum(top, ref[tile, 1:2])
        shares = [ref[tile, 0:1] * jnp.exp2((ref[tile, 1:2] - top) * FACTOR) for ref in stats]
        whole = sum(shares[1:], shares[0])
        out = jnp.zeros((HEAD_DIM, TILE), jnp.float32)
        for value, share in zip(values, shares):
            out = out + value[tile].astype(jnp.float32) * (share / whole)
        inner, head = divmod(tile, heads)
        out_ref[
            inner * TILE : (inner + 1) * TILE, head * HEAD_DIM : (head + 1) * HEAD_DIM
        ] = out.T.astype(out_ref.dtype)


def merge(parts, rows, heads):
    flat = [array for part in parts for array in part]
    return pl.pallas_call(
        functools.partial(merge_kernel, len(parts)),
        in_specs=[VMEM] * len(flat),
        out_specs=VMEM,
        out_shape=jax.ShapeDtypeStruct((rows, heads * HEAD_DIM), flat[0].dtype),
        compiler_params=params(6),
    )(*flat)


def moved(block, axis, source):
    size = lax.axis_size(axis)
    route = [(source(i), i) for i in range(size) if 0 <= source(i) < size]
    return lax.ppermute(block, axis, route)


def body(queries, key_vectors, value_vectors, tile_lists, live_slots):
    heads = lax.axis_size("head")
    frame = lax.axis_index("frame")
    head = lax.axis_index("head")
    shard_tiles = tile_lists.shape[1]
    assert shard_tiles * PLANE == REACH and lax.axis_size("frame") % PLANE == 0

    def from_head(block, step):
        return moved(block, "head", lambda i: (i - step) % heads)

    def core_swap(block):
        return moved(block, "frame", lambda i: i ^ 1)

    own = as_tiles((key_vectors, value_vectors), (False, True))
    size = own.shape[0]
    cut = size // 2
    across = moved(own, "frame", lambda i: i ^ 2)
    chip = jnp.concatenate((core_swap(own), own))
    level = moved(chip, "frame", lambda i: i - PLANE if i % 2 == 0 else i + PLANE)

    listed, live, _ = lax.optimization_barrier((tile_lists[0], live_slots[0], chip))
    lists = work_lists(frame, head, listed, live, heads)
    q_own = as_tiles((queries,), (True,))
    blocks = [
        from_head(jnp.concatenate((q_own.reshape(-1, TILE), packed(lists[step]))), step)
        for step in range(1, heads)
    ]
    blocks, _ = lax.optimization_barrier((blocks, level))
    q_parts, by_head = [], [lists[:1]]
    for block in blocks:
        q_rows = shard_tiles * TILE
        q_parts.append(block[:q_rows].reshape(q_own.shape))
        by_head.append(unpacked(block[q_rows:], lists.shape[1])[None])
    q_rest, by_head = jnp.concatenate(q_parts), jnp.concatenate(by_head)

    far_z = moved(across[:cut], "frame", lambda i: i - PLANE if i % PLANE < 2 else i + PLANE)
    straight = moved(own[cut:], "frame", lambda i: i - 2 if i % PLANE < 2 else i + 2)
    near = [chip, level, across, core_swap(across), core_swap(level[:size])]
    state = attend(by_head, 0, q_rest, None, near, False)
    far_z, straight, state = lax.optimization_barrier((far_z, straight, state))
    far = jnp.concatenate((far_z, straight))
    far = [far, core_swap(far)]
    rest = attend(by_head, 2, q_rest, state, far, True)
    parts = [None]
    for step in range(1, heads):
        cut = slice((step - 1) * shard_tiles, step * shard_tiles)
        parts.append([from_head(array[cut], -step) for array in rest])
    q_own, _ = lax.optimization_barrier((q_own, rest))
    state = attend(by_head, 1, q_own, None, near, False)
    parts[0] = attend(by_head, 3, q_own, state, far, True)
    return merge(parts, queries.shape[0], heads)


def solution(mesh):
    placed = (
        P(("frame", "head"), None),
        P(("frame", "head"), None),
        P(("frame", "head"), None),
        P("head", "frame", None),
        P("head", "frame"),
    )
    return jax.shard_map(
        body, mesh=mesh, in_specs=placed, out_specs=P(("frame", "head"), None), check_vma=False
    )
```

```python
import functools
import math

import jax
import jax.numpy as jnp
import numpy as np
from jax import lax
from jax.experimental import pallas as pl
from jax.experimental.pallas import tpu as pltpu
from jax.sharding import PartitionSpec as P

TILE = 128
HEAD_DIM = 128
REACH = 32
PLANE = 4
GROUP = 4
LISTS = 4
FAR_OFF = 1e30
FACTOR = math.log2(math.e) / math.sqrt(HEAD_DIM)
VMEM = pl.BlockSpec(memory_space=pltpu.VMEM)
SMEM = pl.BlockSpec(memory_space=pltpu.SMEM)


def shard_table():
    table = np.zeros((PLANE, 2 * PLANE + 1), np.int32)
    for place in range(PLANE):
        x, core = divmod(place, 2)
        for distance in range(-PLANE, PLANE + 1):
            plane, there = divmod(place + distance, PLANE)
            same_x, same_core = there // 2 == x, there % 2 == core
            phase = 0
            if plane == 0:
                spot = int(same_core) if same_x else (4 if same_core else 5)
            elif not same_x:
                phase, spot = 1, 0 if same_core else 1
            elif (plane < 0) == (core == 0):
                spot = 2 + int(same_core)
            else:
                spot = 6
            table[place, distance + PLANE] = phase + 4 * spot
    return table.reshape(-1)


def params(mib):
    return pltpu.CompilerParams(vmem_limit_bytes=mib * 2**20)


def cost():
    return pl.CostEstimate(flops=0, bytes_accessed=0, transcendentals=0)


def tile_kernel(heads, flip, *refs):
    out_ref = refs[-1]
    tiles = refs[0].shape[0] // TILE
    for head in range(heads):
        for which, flipped in enumerate(flip):
            for tile in range(tiles):
                block = refs[which][
                    tile * TILE : (tile + 1) * TILE, head * HEAD_DIM : (head + 1) * HEAD_DIM
                ]
                at = (tile * heads + head) * len(flip) + which
                out_ref[at] = block.T if flipped else block


def as_tiles(arrays, flip):
    rows, width = arrays[0].shape
    heads = width // HEAD_DIM
    count = len(arrays) * heads * rows // TILE
    return pl.pallas_call(
        functools.partial(tile_kernel, heads, flip),
        in_specs=[VMEM] * len(arrays),
        out_specs=VMEM,
        out_shape=jax.ShapeDtypeStruct((count, TILE, HEAD_DIM), arrays[0].dtype),
        compiler_params=params(4),
    )(*arrays)


def list_kernel(length, codes_ref, live_ref, ends, metas, places):
    tiles = live_ref.shape[0]
    lists = ends.shape[0]
    for target in range(lists):
        ends[target] = target * length
    for row in range(tiles):

        def slot_step(slot, carry, row=row):
            code = codes_ref[row, slot]
            target = (code >> 8) & 255
            at = ends[target]
            places[at] = code & 255
            metas[at >> 2] = (code >> 16) + (at & (GROUP - 1))
            ends[target] = at + 1
            return carry

        lax.fori_loop(0, live_ref[row], slot_step, 0)
        for target in range(lists):
            at = ends[target]
            up = (at + GROUP - 1) & -GROUP
            filler = places[jnp.maximum(at - 1, 0)]
            for other in range(GROUP - 1):
                places[jnp.where(at + other < up, at + other, lists * length)] = filler
            ends[target] = up
    for target in range(lists):
        ends[target] = (ends[target] - target * length) >> 2


def work_lists(frame, head, tile_lists, live_slots, heads):
    tiles, slots = tile_lists.shape
    part_tiles = tiles // heads
    assert tiles & (tiles - 1) == 0 and heads & (heads - 1) == 0 and GROUP == 4
    within = tile_lists & (tiles - 1)
    rank = within >> int(math.log2(part_tiles))
    spot = ((within & (part_tiles - 1)) * heads + head) * 2
    table = shard_table()
    key = lax.rem(frame, PLANE) * (2 * PLANE + 1) + PLANE - frame
    key = (tile_lists >> int(math.log2(tiles))) + key
    hit = key[..., None] == jnp.arange(table.size, dtype=jnp.int32)
    entry = jnp.sum(jnp.where(hit, jnp.asarray(table), 0), axis=-1, dtype=jnp.int32)
    row = jnp.arange(tiles, dtype=jnp.int32)[:, None]
    turn = (rank - (row >> int(math.log2(part_tiles)))) & (heads - 1)
    query = (turn * part_tiles + (row & (part_tiles - 1))) * heads + head
    query = jnp.where(turn == 0, query, query - heads * part_tiles)
    step = (rank - head) & (heads - 1)
    target = step * LISTS + 2 * (entry & 3) + jnp.where(turn == 0, 1, 0)
    place = (entry >> 2) * (2 * tiles) + spot
    codes = place + target * 256 + query * (8 * 65536)
    length = tiles * (slots // GROUP + 1) * GROUP
    total = LISTS * heads * length
    ends, metas, places = pl.pallas_call(
        functools.partial(list_kernel, length),
        in_specs=[SMEM] * 2,
        out_specs=[SMEM] * 3,
        out_shape=[
            jax.ShapeDtypeStruct((LISTS * heads,), jnp.int32),
            jax.ShapeDtypeStruct((total // GROUP,), jnp.int32),
            jax.ShapeDtypeStruct((total + 1,), jnp.int32),
        ],
        compiler_params=params(4),
        cost_estimate=cost(),
    )(codes, live_slots)
    arrays = ends, metas, places[:total]
    return jnp.concatenate([array.reshape(heads, -1) for array in arrays], axis=1)


def packed(numbers):
    rows = -(-numbers.shape[0] // TILE)
    numbers = jnp.pad(numbers, (0, rows * TILE - numbers.shape[0])).reshape(rows, TILE)
    digits = jnp.concatenate((numbers & 255, numbers >> 8)).astype(jnp.bfloat16)
    return jnp.pad(digits, ((0, -2 * rows % 16), (0, 0)))


def unpacked(block, count):
    rows = -(-count // TILE)
    digits = block.astype(jnp.int32)
    return (digits[:rows] + digits[rows : 2 * rows] * 256).reshape(-1)[:count]


def phase_kernel(which, pieces, begins, ends, lists, q_ref, *refs):
    refs = list(refs)
    state = [refs.pop(0) for _ in range(0 if begins else 3)]
    parts = [refs.pop(0) for _ in range(pieces)]
    out_ref, stats_ref = [refs.pop(0) for _ in range(2)] if ends else [None] * 2
    top_ref, total_ref, sum_ref, scores, high, weights, shrinks = refs[:7]
    window = refs[7] if pieces > 1 else parts[0]
    tiles = q_ref.shape[0]
    heads, width = lists.shape
    length = (width - LISTS) // (LISTS * (GROUP + 1))

    at = 0
    for part in parts if pieces > 1 else ():
        window[at : at + part.shape[0]] = part[...]
        at += part.shape[0]
    if begins:
        top_ref[...] = jnp.full(top_ref.shape, -FAR_OFF, jnp.float32)
        total_ref[...] = jnp.zeros(total_ref.shape, jnp.float32)
        sum_ref[...] = jnp.zeros(sum_ref.shape, jnp.float32)
    else:
        for ref, old in zip((top_ref, total_ref, sum_ref), state):
            ref[...] = old[...]

    starts = [jnp.int32(0)]
    for head in range(heads):
        starts.append(starts[-1] + lists[head, which])

    def item_of(item):
        row, index = jnp.int32(0), item
        for head in range(1, heads):
            row = jnp.where(item >= starts[head], head, row)
            index = jnp.where(item >= starts[head], item - starts[head], index)
        real = item < starts[heads]
        row, index = jnp.where(real, row, 0), jnp.where(real, index, 0)
        meta = lists[row, LISTS + which * length + index]
        at = LISTS * (1 + length) + (which * length + index) * GROUP
        tile = jnp.where(real, meta >> 3, 0)
        spots = [jnp.where(real, lists[row, at + slot], 0) for slot in range(GROUP)]
        return tile, jnp.where(real, meta & 7, -1), spots

    def score(entry):
        tile, _, spots = entry
        keys = jnp.concatenate([window[spot] for spot in spots])
        block = jnp.dot(keys, q_ref[tile], preferred_element_type=jnp.float32)
        top = jnp.max(block.reshape(-1, 8, TILE), axis=0)
        return block, jnp.max(top, axis=0, keepdims=True)

    def weigh(entry, block, peak):
        tile, last, _ = entry
        old = top_ref[tile]
        top = jnp.maximum(old, jnp.where(last < 0, -FAR_OFF, peak))
        shrink = jnp.exp2((old - top) * FACTOR)
        total = total_ref[tile] * shrink
        parts = []
        for slot in range(GROUP):
            shift = jnp.where(slot <= last, top, FAR_OFF)
            weight = jnp.exp2((block[slot * TILE : (slot + 1) * TILE] - shift) * FACTOR)
            total = total + jnp.sum(weight.reshape(-1, 8, TILE), axis=0)
            parts.append(weight.astype(jnp.bfloat16))
        top_ref[tile] = top
        total_ref[tile] = total
        return jnp.concatenate(parts), shrink

    def collect(entry, weight, shrink):
        tile, _, spots = entry
        values = jnp.concatenate([window[spot + 1] for spot in spots], axis=1)
        product = jnp.dot(values, weight, preferred_element_type=jnp.float32)
        sum_ref[tile] = sum_ref[tile] * shrink + product

    def store_scores(pair):
        for number, (block, peak) in enumerate(pair):
            scores[number], high[number] = block, peak

    def store_weights(pair):
        for number, (weight, shrink) in enumerate(pair):
            weights[number], shrinks[number] = weight, shrink

    ahead = [item_of(0), item_of(1)]
    second = [item_of(2), item_of(3)]
    first = [score(entry) for entry in ahead]
    store_scores([score(entry) for entry in second])
    store_weights([weigh(entry, *made) for entry, made in zip(ahead, first)])

    def step(pair, entries):
        collected, weighed = entries[:2], entries[2:]
        scored = [item_of(2 * pair + 4), item_of(2 * pair + 5)]
        made = [(scores[number], high[number]) for number in range(2)]
        formed = [(weights[number], shrinks[number]) for number in range(2)]
        blocks = [score(entry) for entry in scored]
        following = [weigh(entry, *item) for entry, item in zip(weighed, made)]
        for entry, item in zip(collected, formed):
            collect(entry, *item)
        store_scores(blocks)
        store_weights(following)
        return tuple(weighed) + tuple(scored)

    lax.fori_loop(0, (starts[heads] + 1) >> 1, step, tuple(ahead + second))
    if ends:
        for tile in range(tiles):
            total = jnp.sum(total_ref[tile], axis=0, keepdims=True)
            share = jnp.where(total > 0, 1.0 / jnp.where(total > 0, total, 1.0), 0.0)
            out_ref[tile] = (sum_ref[tile] * share).astype(out_ref.dtype)
            stats_ref[tile, 0:1] = total
            stats_ref[tile, 1:2] = top_ref[tile]


def attend(lists, which, queries, state, pieces, ends):
    tiles = queries.shape[0]
    begins = state is None
    held = [
        jax.ShapeDtypeStruct((tiles, 1, TILE), jnp.float32),
        jax.ShapeDtypeStruct((tiles, 8, TILE), jnp.float32),
        jax.ShapeDtypeStruct((tiles, HEAD_DIM, TILE), jnp.float32),
    ]
    scratch = [
        pltpu.VMEM((2, GROUP * TILE, TILE), jnp.float32),
        pltpu.VMEM((2, 1, TILE), jnp.float32),
        pltpu.VMEM((2, GROUP * TILE, TILE), queries.dtype),
        pltpu.VMEM((2, 1, TILE), jnp.float32),
    ]
    if len(pieces) > 1:
        rows = sum(piece.shape[0] for piece in pieces)
        scratch.append(pltpu.VMEM((rows, TILE, TILE), queries.dtype))
    if ends:
        scratch = [pltpu.VMEM(array.shape, array.dtype) for array in held] + scratch
        held = [
            jax.ShapeDtypeStruct((tiles, HEAD_DIM, TILE), queries.dtype),
            jax.ShapeDtypeStruct((tiles, 2, TILE), jnp.float32),
        ]
    return pl.pallas_call(
        functools.partial(phase_kernel, which, len(pieces), begins, ends),
        in_specs=[SMEM] + [VMEM] * (1 + len(pieces) + (0 if begins else 3)),
        out_specs=[VMEM] * len(held),
        out_shape=held,
        scratch_shapes=scratch,
        compiler_params=params(10),
        cost_estimate=cost(),
    )(lists, queries, *([] if begins else state), *pieces)


def merge_kernel(count, *refs):
    out_ref = refs[-1]
    values, stats = [refs[first : 2 * count : 2] for first in range(2)]
    tiles = values[0].shape[0]
    heads = out_ref.shape[1] // HEAD_DIM
    for tile in range(tiles):
        top = stats[0][tile, 1:2]
        for ref in stats[1:]:
            top = jnp.maximum(top, ref[tile, 1:2])
        shares = [ref[tile, 0:1] * jnp.exp2((ref[tile, 1:2] - top) * FACTOR) for ref in stats]
        whole = sum(shares[1:], shares[0])
        out = jnp.zeros((HEAD_DIM, TILE), jnp.float32)
        for value, share in zip(values, shares):
            out = out + value[tile].astype(jnp.float32) * (share / whole)
        inner, head = divmod(tile, heads)
        out_ref[
            inner * TILE : (inner + 1) * TILE, head * HEAD_DIM : (head + 1) * HEAD_DIM
        ] = out.T.astype(out_ref.dtype)


def merge(parts, rows, heads):
    flat = [array for part in parts for array in part]
    return pl.pallas_call(
        functools.partial(merge_kernel, len(parts)),
        in_specs=[VMEM] * len(flat),
        out_specs=VMEM,
        out_shape=jax.ShapeDtypeStruct((rows, heads * HEAD_DIM), flat[0].dtype),
        compiler_params=params(6),
    )(*flat)


def moved(block, axis, source):
    size = lax.axis_size(axis)
    route = [(source(i), i) for i in range(size) if 0 <= source(i) < size]
    return lax.ppermute(block, axis, route)


def body(queries, key_vectors, value_vectors, tile_lists, live_slots):
    heads = lax.axis_size("head")
    frame = lax.axis_index("frame")
    head = lax.axis_index("head")
    shard_tiles = tile_lists.shape[1]
    assert shard_tiles * PLANE == REACH and lax.axis_size("frame") % PLANE == 0

    def from_head(block, step):
        return moved(block, "head", lambda i: (i - step) % heads)

    def core_swap(block):
        return moved(block, "frame", lambda i: i ^ 1)

    own = as_tiles((key_vectors, value_vectors), (False, True))
    size = own.shape[0]
    cut = size * 5 // 8
    across = moved(own, "frame", lambda i: i ^ 2)
    chip = jnp.concatenate((core_swap(own), own))
    level = moved(chip, "frame", lambda i: i - PLANE if i % 2 == 0 else i + PLANE)

    listed, live, _ = lax.optimization_barrier((tile_lists[0], live_slots[0], chip))
    lists = work_lists(frame, head, listed, live, heads)
    q_own = as_tiles((queries,), (True,))
    blocks = [
        from_head(jnp.concatenate((q_own.reshape(-1, TILE), packed(lists[step]))), step)
        for step in range(1, heads)
    ]
    blocks, _ = lax.optimization_barrier((blocks, level))
    q_parts, by_head = [], [lists[:1]]
    for block in blocks:
        q_rows = shard_tiles * TILE
        q_parts.append(block[:q_rows].reshape(q_own.shape))
        by_head.append(unpacked(block[q_rows:], lists.shape[1])[None])
    q_rest, by_head = jnp.concatenate(q_parts), jnp.concatenate(by_head)

    far_z = moved(across[:cut], "frame", lambda i: i - PLANE if i % PLANE < 2 else i + PLANE)
    straight = moved(own[cut:], "frame", lambda i: i - 2 if i % PLANE < 2 else i + 2)
    near = [chip, level, across, core_swap(across), core_swap(level[:size])]
    state = attend(by_head, 0, q_rest, None, near, False)
    far_z, straight, state = lax.optimization_barrier((far_z, straight, state))
    far = jnp.concatenate((far_z, straight))
    far = [far, core_swap(far)]
    rest = attend(by_head, 2, q_rest, state, far, True)
    parts = [None]
    for step in range(1, heads):
        cut = slice((step - 1) * shard_tiles, step * shard_tiles)
        parts.append([from_head(array[cut], -step) for array in rest])
    q_own, _ = lax.optimization_barrier((q_own, rest))
    state = attend(by_head, 1, q_own, None, near, False)
    parts[0] = attend(by_head, 3, q_own, state, far, True)
    return merge(parts, queries.shape[0], heads)


def solution(mesh):
    placed = (
        P(("frame", "head"), None),
        P(("frame", "head"), None),
        P(("frame", "head"), None),
        P("head", "frame", None),
        P("head", "frame"),
    )
    return jax.shard_map(
        body, mesh=mesh, in_specs=placed, out_specs=P(("frame", "head"), None), check_vma=False
    )
```

```python
import functools
import math

import jax
import jax.numpy as jnp
import numpy as np
from jax import lax
from jax.experimental import pallas as pl
from jax.experimental.pallas import tpu as pltpu
from jax.sharding import PartitionSpec as P

TILE = 128
HEAD_DIM = 128
REACH = 32
PLANE = 4
GROUP = 4
LISTS = 4
FAR_OFF = 1e30
FACTOR = math.log2(math.e) / math.sqrt(HEAD_DIM)
VMEM = pl.BlockSpec(memory_space=pltpu.VMEM)
SMEM = pl.BlockSpec(memory_space=pltpu.SMEM)


def shard_table():
    table = np.zeros((PLANE, 2 * PLANE + 1), np.int32)
    for place in range(PLANE):
        x, core = divmod(place, 2)
        for distance in range(-PLANE, PLANE + 1):
            plane, there = divmod(place + distance, PLANE)
            same_x, same_core = there // 2 == x, there % 2 == core
            phase = 0
            if plane == 0:
                spot = int(same_core) if same_x else (4 if same_core else 5)
            elif not same_x:
                phase, spot = 1, 0 if same_core else 1
            elif (plane < 0) == (core == 0):
                spot = 2 + int(same_core)
            else:
                spot = 6
            table[place, distance + PLANE] = phase + 4 * spot
    return table.reshape(-1)


def params(mib):
    return pltpu.CompilerParams(vmem_limit_bytes=mib * 2**20)


def cost():
    return pl.CostEstimate(flops=0, bytes_accessed=0, transcendentals=0)


def tile_kernel(heads, flip, *refs):
    out_ref = refs[-1]
    tiles = refs[0].shape[0] // TILE
    for head in range(heads):
        for which, flipped in enumerate(flip):
            for tile in range(tiles):
                block = refs[which][
                    tile * TILE : (tile + 1) * TILE, head * HEAD_DIM : (head + 1) * HEAD_DIM
                ]
                at = (tile * heads + head) * len(flip) + which
                out_ref[at] = block.T if flipped else block


def as_tiles(arrays, flip):
    rows, width = arrays[0].shape
    heads = width // HEAD_DIM
    count = len(arrays) * heads * rows // TILE
    return pl.pallas_call(
        functools.partial(tile_kernel, heads, flip),
        in_specs=[VMEM] * len(arrays),
        out_specs=VMEM,
        out_shape=jax.ShapeDtypeStruct((count, TILE, HEAD_DIM), arrays[0].dtype),
        compiler_params=params(4),
    )(*arrays)


def list_kernel(length, codes_ref, live_ref, ends, metas, places):
    tiles = live_ref.shape[0]
    lists = ends.shape[0]
    for target in range(lists):
        ends[target] = target * length
    for row in range(tiles):

        def slot_step(slot, carry, row=row):
            code = codes_ref[row, slot]
            target = (code >> 8) & 255
            at = ends[target]
            places[at] = code & 255
            metas[at >> 2] = (code >> 16) + (at & (GROUP - 1))
            ends[target] = at + 1
            return carry

        lax.fori_loop(0, live_ref[row], slot_step, 0)
        for target in range(lists):
            at = ends[target]
            up = (at + GROUP - 1) & -GROUP
            filler = places[jnp.maximum(at - 1, 0)]
            for other in range(GROUP - 1):
                places[jnp.where(at + other < up, at + other, lists * length)] = filler
            ends[target] = up
    for target in range(lists):
        ends[target] = (ends[target] - target * length) >> 2


def work_lists(frame, head, tile_lists, live_slots, heads):
    tiles, slots = tile_lists.shape
    part_tiles = tiles // heads
    assert tiles & (tiles - 1) == 0 and heads & (heads - 1) == 0 and GROUP == 4
    within = tile_lists & (tiles - 1)
    rank = within >> int(math.log2(part_tiles))
    spot = ((within & (part_tiles - 1)) * heads + head) * 2
    table = shard_table()
    key = lax.rem(frame, PLANE) * (2 * PLANE + 1) + PLANE - frame
    key = (tile_lists >> int(math.log2(tiles))) + key
    hit = key[..., None] == jnp.arange(table.size, dtype=jnp.int32)
    entry = jnp.sum(jnp.where(hit, jnp.asarray(table), 0), axis=-1, dtype=jnp.int32)
    row = jnp.arange(tiles, dtype=jnp.int32)[:, None]
    turn = (rank - (row >> int(math.log2(part_tiles)))) & (heads - 1)
    query = (turn * part_tiles + (row & (part_tiles - 1))) * heads + head
    query = jnp.where(turn == 0, query, query - heads * part_tiles)
    step = (rank - head) & (heads - 1)
    target = step * LISTS + 2 * (entry & 3) + jnp.where(turn == 0, 1, 0)
    place = (entry >> 2) * (2 * tiles) + spot
    codes = place + target * 256 + query * (8 * 65536)
    length = max(part_tiles, tiles - part_tiles) * -(-slots // GROUP) * GROUP
    total = LISTS * heads * length
    ends, metas, places = pl.pallas_call(
        functools.partial(list_kernel, length),
        in_specs=[SMEM] * 2,
        out_specs=[SMEM] * 3,
        out_shape=[
            jax.ShapeDtypeStruct((LISTS * heads,), jnp.int32),
            jax.ShapeDtypeStruct((total // GROUP,), jnp.int32),
            jax.ShapeDtypeStruct((total + 1,), jnp.int32),
        ],
        compiler_params=params(4),
        cost_estimate=cost(),
    )(codes, live_slots)
    arrays = ends, metas, places[:total]
    return jnp.concatenate([array.reshape(heads, -1) for array in arrays], axis=1)


def packed(numbers):
    rows = -(-numbers.shape[0] // TILE)
    numbers = jnp.pad(numbers, (0, rows * TILE - numbers.shape[0])).reshape(rows, TILE)
    digits = jnp.concatenate((numbers & 255, numbers >> 8)).astype(jnp.bfloat16)
    return jnp.pad(digits, ((0, -2 * rows % 16), (0, 0)))


def unpacked(block, count):
    rows = -(-count // TILE)
    digits = block.astype(jnp.int32)
    return (digits[:rows] + digits[rows : 2 * rows] * 256).reshape(-1)[:count]


def phase_kernel(which, pieces, begins, ends, lists, q_ref, *refs):
    refs = list(refs)
    state = [refs.pop(0) for _ in range(0 if begins else 3)]
    parts = [refs.pop(0) for _ in range(pieces)]
    out_ref, stats_ref = [refs.pop(0) for _ in range(2)] if ends else [None] * 2
    top_ref, total_ref, sum_ref, scores, high, weights, shrinks = refs[:7]
    window = refs[7] if pieces > 1 else parts[0]
    tiles = q_ref.shape[0]
    heads, width = lists.shape
    length = (width - LISTS) // (LISTS * (GROUP + 1))

    at = 0
    for part in parts if pieces > 1 else ():
        window[at : at + part.shape[0]] = part[...]
        at += part.shape[0]
    if begins:
        top_ref[...] = jnp.full(top_ref.shape, -FAR_OFF, jnp.float32)
        total_ref[...] = jnp.zeros(total_ref.shape, jnp.float32)
        sum_ref[...] = jnp.zeros(sum_ref.shape, jnp.float32)
    else:
        for ref, old in zip((top_ref, total_ref, sum_ref), state):
            ref[...] = old[...]

    starts = [jnp.int32(0)]
    for head in range(heads):
        starts.append(starts[-1] + lists[head, which])

    def item_of(item):
        row, index = jnp.int32(0), item
        for head in range(1, heads):
            row = jnp.where(item >= starts[head], head, row)
            index = jnp.where(item >= starts[head], item - starts[head], index)
        real = item < starts[heads]
        row, index = jnp.where(real, row, 0), jnp.where(real, index, 0)
        meta = lists[row, LISTS + which * length + index]
        at = LISTS * (1 + length) + (which * length + index) * GROUP
        tile = jnp.where(real, meta >> 3, 0)
        spots = [jnp.where(real, lists[row, at + slot], 0) for slot in range(GROUP)]
        return tile, jnp.where(real, meta & 7, -1), spots

    def score(entry):
        tile, _, spots = entry
        keys = jnp.concatenate([window[spot] for spot in spots])
        block = jnp.dot(keys, q_ref[tile], preferred_element_type=jnp.float32)
        top = jnp.max(block.reshape(-1, 8, TILE), axis=0)
        return block, jnp.max(top, axis=0, keepdims=True)

    def weigh(entry, block, peak):
        tile, last, _ = entry
        old = top_ref[tile]
        top = jnp.maximum(old, jnp.where(last < 0, -FAR_OFF, peak))
        shrink = jnp.exp2((old - top) * FACTOR)
        total = total_ref[tile] * shrink
        parts = []
        for slot in range(GROUP):
            shift = jnp.where(slot <= last, top, FAR_OFF)
            weight = jnp.exp2((block[slot * TILE : (slot + 1) * TILE] - shift) * FACTOR)
            total = total + jnp.sum(weight.reshape(-1, 8, TILE), axis=0)
            parts.append(weight.astype(jnp.bfloat16))
        top_ref[tile] = top
        total_ref[tile] = total
        return jnp.concatenate(parts), shrink

    def collect(entry, weight, shrink):
        tile, _, spots = entry
        values = jnp.concatenate([window[spot + 1] for spot in spots], axis=1)
        product = jnp.dot(values, weight, preferred_element_type=jnp.float32)
        sum_ref[tile] = sum_ref[tile] * shrink + product

    def store_scores(pair):
        for number, (block, peak) in enumerate(pair):
            scores[number], high[number] = block, peak

    def store_weights(pair):
        for number, (weight, shrink) in enumerate(pair):
            weights[number], shrinks[number] = weight, shrink

    ahead = [item_of(0), item_of(1)]
    second = [item_of(2), item_of(3)]
    first = [score(entry) for entry in ahead]
    store_scores([score(entry) for entry in second])
    store_weights([weigh(entry, *made) for entry, made in zip(ahead, first)])

    def step(pair, entries):
        collected, weighed = entries[:2], entries[2:]
        scored = [item_of(2 * pair + 4), item_of(2 * pair + 5)]
        made = [(scores[number], high[number]) for number in range(2)]
        formed = [(weights[number], shrinks[number]) for number in range(2)]
        blocks = [score(entry) for entry in scored]
        following = [weigh(entry, *item) for entry, item in zip(weighed, made)]
        for entry, item in zip(collected, formed):
            collect(entry, *item)
        store_scores(blocks)
        store_weights(following)
        return tuple(weighed) + tuple(scored)

    lax.fori_loop(0, (starts[heads] + 1) >> 1, step, tuple(ahead + second))
    if ends:
        for tile in range(tiles):
            total = jnp.sum(total_ref[tile], axis=0, keepdims=True)
            share = jnp.where(total > 0, 1.0 / jnp.where(total > 0, total, 1.0), 0.0)
            out_ref[tile] = (sum_ref[tile] * share).astype(out_ref.dtype)
            stats_ref[tile, 0:1] = total
            stats_ref[tile, 1:2] = top_ref[tile]


def attend(lists, which, queries, state, pieces, ends):
    tiles = queries.shape[0]
    begins = state is None
    held = [
        jax.ShapeDtypeStruct((tiles, 1, TILE), jnp.float32),
        jax.ShapeDtypeStruct((tiles, 8, TILE), jnp.float32),
        jax.ShapeDtypeStruct((tiles, HEAD_DIM, TILE), jnp.float32),
    ]
    scratch = [
        pltpu.VMEM((2, GROUP * TILE, TILE), jnp.float32),
        pltpu.VMEM((2, 1, TILE), jnp.float32),
        pltpu.VMEM((2, GROUP * TILE, TILE), queries.dtype),
        pltpu.VMEM((2, 1, TILE), jnp.float32),
    ]
    if len(pieces) > 1:
        rows = sum(piece.shape[0] for piece in pieces)
        scratch.append(pltpu.VMEM((rows, TILE, TILE), queries.dtype))
    if ends:
        scratch = [pltpu.VMEM(array.shape, array.dtype) for array in held] + scratch
        held = [
            jax.ShapeDtypeStruct((tiles, HEAD_DIM, TILE), queries.dtype),
            jax.ShapeDtypeStruct((tiles, 2, TILE), jnp.float32),
        ]
    return pl.pallas_call(
        functools.partial(phase_kernel, which, len(pieces), begins, ends),
        in_specs=[SMEM] + [VMEM] * (1 + len(pieces) + (0 if begins else 3)),
        out_specs=[VMEM] * len(held),
        out_shape=held,
        scratch_shapes=scratch,
        compiler_params=params(10),
        cost_estimate=cost(),
    )(lists, queries, *([] if begins else state), *pieces)


def merge_kernel(count, *refs):
    out_ref = refs[-1]
    values, stats = [refs[first : 2 * count : 2] for first in range(2)]
    tiles = values[0].shape[0]
    heads = out_ref.shape[1] // HEAD_DIM
    for tile in range(tiles):
        top = stats[0][tile, 1:2]
        for ref in stats[1:]:
            top = jnp.maximum(top, ref[tile, 1:2])
        shares = [ref[tile, 0:1] * jnp.exp2((ref[tile, 1:2] - top) * FACTOR) for ref in stats]
        whole = sum(shares[1:], shares[0])
        out = jnp.zeros((HEAD_DIM, TILE), jnp.float32)
        for value, share in zip(values, shares):
            out = out + value[tile].astype(jnp.float32) * (share / whole)
        inner, head = divmod(tile, heads)
        out_ref[
            inner * TILE : (inner + 1) * TILE, head * HEAD_DIM : (head + 1) * HEAD_DIM
        ] = out.T.astype(out_ref.dtype)


def merge(parts, rows, heads):
    flat = [array for part in parts for array in part]
    return pl.pallas_call(
        functools.partial(merge_kernel, len(parts)),
        in_specs=[VMEM] * len(flat),
        out_specs=VMEM,
        out_shape=jax.ShapeDtypeStruct((rows, heads * HEAD_DIM), flat[0].dtype),
        compiler_params=params(6),
    )(*flat)


def moved(block, axis, source):
    size = lax.axis_size(axis)
    route = [(source(i), i) for i in range(size) if 0 <= source(i) < size]
    return lax.ppermute(block, axis, route)


def body(queries, key_vectors, value_vectors, tile_lists, live_slots):
    heads = lax.axis_size("head")
    frame = lax.axis_index("frame")
    head = lax.axis_index("head")
    shard_tiles = tile_lists.shape[1]
    assert shard_tiles * PLANE == REACH and lax.axis_size("frame") % PLANE == 0

    def from_head(block, step):
        return moved(block, "head", lambda i: (i - step) % heads)

    def core_swap(block):
        return moved(block, "frame", lambda i: i ^ 1)

    own = as_tiles((key_vectors, value_vectors), (False, True))
    size = own.shape[0]
    cut = size * 9 // 16
    across = moved(own, "frame", lambda i: i ^ 2)
    chip = jnp.concatenate((core_swap(own), own))
    level = moved(chip, "frame", lambda i: i - PLANE if i % 2 == 0 else i + PLANE)

    listed, live, _ = lax.optimization_barrier((tile_lists[0], live_slots[0], chip))
    lists = work_lists(frame, head, listed, live, heads)
    q_own = as_tiles((queries,), (True,))
    blocks = [
        from_head(jnp.concatenate((q_own.reshape(-1, TILE), packed(lists[step]))), step)
        for step in range(1, heads)
    ]
    blocks, _ = lax.optimization_barrier((blocks, level))
    q_parts, by_head = [], [lists[:1]]
    for block in blocks:
        q_rows = shard_tiles * TILE
        q_parts.append(block[:q_rows].reshape(q_own.shape))
        by_head.append(unpacked(block[q_rows:], lists.shape[1])[None])
    q_rest, by_head = jnp.concatenate(q_parts), jnp.concatenate(by_head)

    far_z = moved(across[:cut], "frame", lambda i: i - PLANE if i % PLANE < 2 else i + PLANE)
    straight = moved(own[cut:], "frame", lambda i: i - 2 if i % PLANE < 2 else i + 2)
    near = [chip, level, across, core_swap(across), core_swap(level[:size])]
    state = attend(by_head, 0, q_rest, None, near, False)
    straight, state = lax.optimization_barrier((straight, state))
    swapped = core_swap(straight)
    far_z, swapped = lax.optimization_barrier((far_z, swapped))
    far = [far_z, straight, core_swap(far_z), swapped]
    rest = attend(by_head, 2, q_rest, state, far, True)
    parts = [None]
    for step in range(1, heads):
        cut = slice((step - 1) * shard_tiles, step * shard_tiles)
        parts.append([from_head(array[cut], -step) for array in rest])
    q_own, _ = lax.optimization_barrier((q_own, rest))
    state = attend(by_head, 1, q_own, None, near, False)
    parts[0] = attend(by_head, 3, q_own, state, far, True)
    return merge(parts, queries.shape[0], heads)


def solution(mesh):
    placed = (
        P(("frame", "head"), None),
        P(("frame", "head"), None),
        P(("frame", "head"), None),
        P("head", "frame", None),
        P("head", "frame"),
    )
    return jax.shard_map(
        body, mesh=mesh, in_specs=placed, out_specs=P(("frame", "head"), None), check_vma=False
    )
```

```python
import functools
import math

import jax
import jax.numpy as jnp
import numpy as np
from jax import lax
from jax.experimental import pallas as pl
from jax.experimental.pallas import tpu as pltpu
from jax.sharding import PartitionSpec as P

TILE = 128
HEAD_DIM = 128
REACH = 32
PLANE = 4
GROUP = 4
LISTS = 4
FAR_OFF = 1e30
FACTOR = math.log2(math.e) / math.sqrt(HEAD_DIM)
VMEM = pl.BlockSpec(memory_space=pltpu.VMEM)
SMEM = pl.BlockSpec(memory_space=pltpu.SMEM)


def shard_table():
    table = np.zeros((PLANE, 2 * PLANE + 1), np.int32)
    for place in range(PLANE):
        x, core = divmod(place, 2)
        for distance in range(-PLANE, PLANE + 1):
            plane, there = divmod(place + distance, PLANE)
            same_x, same_core = there // 2 == x, there % 2 == core
            phase = 0
            if plane == 0:
                spot = int(same_core) if same_x else (4 if same_core else 5)
            elif not same_x:
                phase, spot = 1, 0 if same_core else 1
            elif (plane < 0) == (core == 0):
                spot = 2 + int(same_core)
            else:
                spot = 6
            table[place, distance + PLANE] = phase + 4 * spot
    return table.reshape(-1)


def params(mib):
    return pltpu.CompilerParams(vmem_limit_bytes=mib * 2**20)


def cost():
    return pl.CostEstimate(flops=0, bytes_accessed=0, transcendentals=0)


def tile_kernel(heads, flip, *refs):
    out_ref = refs[-1]
    tiles = refs[0].shape[0] // TILE
    for head in range(heads):
        for which, flipped in enumerate(flip):
            for tile in range(tiles):
                block = refs[which][
                    tile * TILE : (tile + 1) * TILE, head * HEAD_DIM : (head + 1) * HEAD_DIM
                ]
                at = (tile * heads + head) * len(flip) + which
                out_ref[at] = block.T if flipped else block


def as_tiles(arrays, flip):
    rows, width = arrays[0].shape
    heads = width // HEAD_DIM
    count = len(arrays) * heads * rows // TILE
    return pl.pallas_call(
        functools.partial(tile_kernel, heads, flip),
        in_specs=[VMEM] * len(arrays),
        out_specs=VMEM,
        out_shape=jax.ShapeDtypeStruct((count, TILE, HEAD_DIM), arrays[0].dtype),
        compiler_params=params(4),
    )(*arrays)


def list_kernel(length, codes_ref, live_ref, ends, metas, places):
    tiles = live_ref.shape[0]
    lists = ends.shape[0]
    for target in range(lists):
        ends[target] = target * length
    for row in range(tiles):

        def slot_step(slot, carry, row=row):
            code = codes_ref[row, slot]
            target = (code >> 8) & 255
            at = ends[target]
            places[at] = code & 255
            metas[at >> 2] = (code >> 16) + (at & (GROUP - 1))
            ends[target] = at + 1
            return carry

        lax.fori_loop(0, live_ref[row], slot_step, 0)
        for target in range(lists):
            at = ends[target]
            up = (at + GROUP - 1) & -GROUP
            filler = places[jnp.maximum(at - 1, 0)]
            for other in range(GROUP - 1):
                places[jnp.where(at + other < up, at + other, lists * length)] = filler
            ends[target] = up
    for target in range(lists):
        ends[target] = (ends[target] - target * length) >> 2


def work_lists(frame, head, tile_lists, live_slots, heads):
    tiles, slots = tile_lists.shape
    part_tiles = tiles // heads
    assert tiles & (tiles - 1) == 0 and heads & (heads - 1) == 0 and GROUP == 4
    within = tile_lists & (tiles - 1)
    rank = within >> int(math.log2(part_tiles))
    spot = ((within & (part_tiles - 1)) * heads + head) * 2
    table = shard_table()
    key = lax.rem(frame, PLANE) * (2 * PLANE + 1) + PLANE - frame
    key = (tile_lists >> int(math.log2(tiles))) + key
    hit = key[..., None] == jnp.arange(table.size, dtype=jnp.int32)
    entry = jnp.sum(jnp.where(hit, jnp.asarray(table), 0), axis=-1, dtype=jnp.int32)
    row = jnp.arange(tiles, dtype=jnp.int32)[:, None]
    turn = (rank - (row >> int(math.log2(part_tiles)))) & (heads - 1)
    query = (turn * part_tiles + (row & (part_tiles - 1))) * heads + head
    query = jnp.where(turn == 0, query, query - heads * part_tiles)
    step = (rank - head) & (heads - 1)
    target = step * LISTS + 2 * (entry & 3) + jnp.where(turn == 0, 1, 0)
    place = (entry >> 2) * (2 * tiles) + spot
    codes = place + target * 256 + query * (8 * 65536)
    length = max(part_tiles, tiles - part_tiles) * -(-slots // GROUP) * GROUP
    total = LISTS * heads * length
    ends, metas, places = pl.pallas_call(
        functools.partial(list_kernel, length),
        in_specs=[SMEM] * 2,
        out_specs=[SMEM] * 3,
        out_shape=[
            jax.ShapeDtypeStruct((LISTS * heads,), jnp.int32),
            jax.ShapeDtypeStruct((total // GROUP,), jnp.int32),
            jax.ShapeDtypeStruct((total + 1,), jnp.int32),
        ],
        compiler_params=params(4),
        cost_estimate=cost(),
    )(codes, live_slots)
    arrays = ends, metas, places[:total]
    return jnp.concatenate([array.reshape(heads, -1) for array in arrays], axis=1)


def packed(numbers):
    rows = -(-numbers.shape[0] // TILE)
    numbers = jnp.pad(numbers, (0, rows * TILE - numbers.shape[0])).reshape(rows, TILE)
    digits = jnp.concatenate((numbers & 255, numbers >> 8)).astype(jnp.bfloat16)
    return jnp.pad(digits, ((0, -2 * rows % 16), (0, 0)))


def unpacked(block, count):
    rows = -(-count // TILE)
    digits = block.astype(jnp.int32)
    return (digits[:rows] + digits[rows : 2 * rows] * 256).reshape(-1)[:count]


def phase_kernel(which, pieces, begins, ends, lists, q_ref, *refs):
    refs = list(refs)
    state = [refs.pop(0) for _ in range(0 if begins else 3)]
    parts = [refs.pop(0) for _ in range(pieces)]
    out_ref, stats_ref = [refs.pop(0) for _ in range(2)] if ends else [None] * 2
    top_ref, total_ref, sum_ref, scores, high, weights, shrinks = refs[:7]
    window = refs[7] if pieces > 1 else parts[0]
    tiles = q_ref.shape[0]
    heads, width = lists.shape
    length = (width - LISTS) // (LISTS * (GROUP + 1))

    at = 0
    for part in parts if pieces > 1 else ():
        window[at : at + part.shape[0]] = part[...]
        at += part.shape[0]
    if begins:
        top_ref[...] = jnp.full(top_ref.shape, -FAR_OFF, jnp.float32)
        total_ref[...] = jnp.zeros(total_ref.shape, jnp.float32)
        sum_ref[...] = jnp.zeros(sum_ref.shape, jnp.float32)
    else:
        for ref, old in zip((top_ref, total_ref, sum_ref), state):
            ref[...] = old[...]

    starts = [jnp.int32(0)]
    for head in range(heads):
        starts.append(starts[-1] + lists[head, which])

    def item_of(item):
        row, index = jnp.int32(0), item
        for head in range(1, heads):
            row = jnp.where(item >= starts[head], head, row)
            index = jnp.where(item >= starts[head], item - starts[head], index)
        real = item < starts[heads]
        row, index = jnp.where(real, row, 0), jnp.where(real, index, 0)
        meta = lists[row, LISTS + which * length + index]
        at = LISTS * (1 + length) + (which * length + index) * GROUP
        tile = jnp.where(real, meta >> 3, 0)
        spots = [jnp.where(real, lists[row, at + slot], 0) for slot in range(GROUP)]
        return tile, jnp.where(real, meta & 7, -1), spots

    def score(entry):
        tile, _, spots = entry
        keys = jnp.concatenate([window[spot] for spot in spots])
        block = jnp.dot(keys, q_ref[tile], preferred_element_type=jnp.float32)
        top = jnp.max(block.reshape(-1, 8, TILE), axis=0)
        return block, jnp.max(top, axis=0, keepdims=True)

    def weigh(entry, block, peak):
        tile, last, _ = entry
        old = top_ref[tile]
        top = jnp.maximum(old, jnp.where(last < 0, -FAR_OFF, peak))
        shrink = jnp.exp2((old - top) * FACTOR)
        total = total_ref[tile] * shrink
        parts = []
        for slot in range(GROUP):
            shift = jnp.where(slot <= last, top, FAR_OFF)
            weight = jnp.exp2((block[slot * TILE : (slot + 1) * TILE] - shift) * FACTOR)
            total = total + jnp.sum(weight.reshape(-1, 8, TILE), axis=0)
            parts.append(weight.astype(jnp.bfloat16))
        top_ref[tile] = top
        total_ref[tile] = total
        return jnp.concatenate(parts), shrink

    def collect(entry, weight, shrink):
        tile, _, spots = entry
        values = jnp.concatenate([window[spot + 1] for spot in spots], axis=1)
        product = jnp.dot(values, weight, preferred_element_type=jnp.float32)
        sum_ref[tile] = sum_ref[tile] * shrink + product

    def store_scores(pair):
        for number, (block, peak) in enumerate(pair):
            scores[number], high[number] = block, peak

    def store_weights(pair):
        for number, (weight, shrink) in enumerate(pair):
            weights[number], shrinks[number] = weight, shrink

    ahead = [item_of(0), item_of(1)]
    second = [item_of(2), item_of(3)]
    first = [score(entry) for entry in ahead]
    store_scores([score(entry) for entry in second])
    store_weights([weigh(entry, *made) for entry, made in zip(ahead, first)])

    def step(pair, entries):
        collected, weighed = entries[:2], entries[2:]
        scored = [item_of(2 * pair + 4), item_of(2 * pair + 5)]
        made = [(scores[number], high[number]) for number in range(2)]
        formed = [(weights[number], shrinks[number]) for number in range(2)]
        blocks = [score(entry) for entry in scored]
        following = [weigh(entry, *item) for entry, item in zip(weighed, made)]
        for entry, item in zip(collected, formed):
            collect(entry, *item)
        store_scores(blocks)
        store_weights(following)
        return tuple(weighed) + tuple(scored)

    lax.fori_loop(0, (starts[heads] + 1) >> 1, step, tuple(ahead + second))
    if ends:
        for tile in range(tiles):
            total = jnp.sum(total_ref[tile], axis=0, keepdims=True)
            share = jnp.where(total > 0, 1.0 / jnp.where(total > 0, total, 1.0), 0.0)
            out_ref[tile] = (sum_ref[tile] * share).astype(out_ref.dtype)
            stats_ref[tile, 0:1] = total
            stats_ref[tile, 1:2] = top_ref[tile]


def attend(lists, which, queries, state, pieces, ends):
    tiles = queries.shape[0]
    begins = state is None
    held = [
        jax.ShapeDtypeStruct((tiles, 1, TILE), jnp.float32),
        jax.ShapeDtypeStruct((tiles, 8, TILE), jnp.float32),
        jax.ShapeDtypeStruct((tiles, HEAD_DIM, TILE), jnp.float32),
    ]
    scratch = [
        pltpu.VMEM((2, GROUP * TILE, TILE), jnp.float32),
        pltpu.VMEM((2, 1, TILE), jnp.float32),
        pltpu.VMEM((2, GROUP * TILE, TILE), queries.dtype),
        pltpu.VMEM((2, 1, TILE), jnp.float32),
    ]
    if len(pieces) > 1:
        rows = sum(piece.shape[0] for piece in pieces)
        scratch.append(pltpu.VMEM((rows, TILE, TILE), queries.dtype))
    if ends:
        scratch = [pltpu.VMEM(array.shape, array.dtype) for array in held] + scratch
        held = [
            jax.ShapeDtypeStruct((tiles, HEAD_DIM, TILE), queries.dtype),
            jax.ShapeDtypeStruct((tiles, 2, TILE), jnp.float32),
        ]
    return pl.pallas_call(
        functools.partial(phase_kernel, which, len(pieces), begins, ends),
        in_specs=[SMEM] + [VMEM] * (1 + len(pieces) + (0 if begins else 3)),
        out_specs=[VMEM] * len(held),
        out_shape=held,
        scratch_shapes=scratch,
        compiler_params=params(10),
        cost_estimate=cost(),
    )(lists, queries, *([] if begins else state), *pieces)


def merge_kernel(count, *refs):
    out_ref = refs[-1]
    values, stats = [refs[first : 2 * count : 2] for first in range(2)]
    tiles = values[0].shape[0]
    heads = out_ref.shape[1] // HEAD_DIM
    for tile in range(tiles):
        top = stats[0][tile, 1:2]
        for ref in stats[1:]:
            top = jnp.maximum(top, ref[tile, 1:2])
        shares = [ref[tile, 0:1] * jnp.exp2((ref[tile, 1:2] - top) * FACTOR) for ref in stats]
        whole = sum(shares[1:], shares[0])
        out = jnp.zeros((HEAD_DIM, TILE), jnp.float32)
        for value, share in zip(values, shares):
            out = out + value[tile].astype(jnp.float32) * (share / whole)
        inner, head = divmod(tile, heads)
        out_ref[
            inner * TILE : (inner + 1) * TILE, head * HEAD_DIM : (head + 1) * HEAD_DIM
        ] = out.T.astype(out_ref.dtype)


def merge(parts, rows, heads):
    flat = [array for part in parts for array in part]
    return pl.pallas_call(
        functools.partial(merge_kernel, len(parts)),
        in_specs=[VMEM] * len(flat),
        out_specs=VMEM,
        out_shape=jax.ShapeDtypeStruct((rows, heads * HEAD_DIM), flat[0].dtype),
        compiler_params=params(6),
    )(*flat)


def moved(block, axis, source):
    size = lax.axis_size(axis)
    route = [(source(i), i) for i in range(size) if 0 <= source(i) < size]
    return lax.ppermute(block, axis, route)


def body(queries, key_vectors, value_vectors, tile_lists, live_slots):
    heads = lax.axis_size("head")
    frame = lax.axis_index("frame")
    head = lax.axis_index("head")
    shard_tiles = tile_lists.shape[1]
    assert shard_tiles * PLANE == REACH and lax.axis_size("frame") % PLANE == 0

    def from_head(block, step):
        return moved(block, "head", lambda i: (i - step) % heads)

    def core_swap(block):
        return moved(block, "frame", lambda i: i ^ 1)

    own = as_tiles((key_vectors, value_vectors), (False, True))
    size = own.shape[0]
    cut = size * 9 // 16
    across = moved(own, "frame", lambda i: i ^ 2)
    chip = jnp.concatenate((core_swap(own), own))
    level = moved(chip, "frame", lambda i: i - PLANE if i % 2 == 0 else i + PLANE)

    listed, live, _ = lax.optimization_barrier((tile_lists[0], live_slots[0], chip))
    lists = work_lists(frame, head, listed, live, heads)
    q_own = as_tiles((queries,), (True,))
    blocks = [
        from_head(jnp.concatenate((q_own.reshape(-1, TILE), packed(lists[step]))), step)
        for step in range(1, heads)
    ]
    blocks, _ = lax.optimization_barrier((blocks, level))
    q_parts, by_head = [], [lists[:1]]
    for block in blocks:
        q_rows = shard_tiles * TILE
        q_parts.append(block[:q_rows].reshape(q_own.shape))
        by_head.append(unpacked(block[q_rows:], lists.shape[1])[None])
    q_rest, by_head = jnp.concatenate(q_parts), jnp.concatenate(by_head)

    far_z = moved(across[:cut], "frame", lambda i: i - PLANE if i % PLANE < 2 else i + PLANE)
    straight = moved(own[cut:], "frame", lambda i: i - 2 if i % PLANE < 2 else i + 2)
    near = [chip, level, across, core_swap(across), core_swap(level[:size])]
    state = attend(by_head, 0, q_rest, None, near, False)
    far_z, straight, state = lax.optimization_barrier((far_z, straight, state))
    far = jnp.concatenate((far_z, straight))
    far = [far, core_swap(far)]
    rest = attend(by_head, 2, q_rest, state, far, True)
    parts = [None]
    for step in range(1, heads):
        cut = slice((step - 1) * shard_tiles, step * shard_tiles)
        parts.append([from_head(array[cut], -step) for array in rest])
    q_own, _ = lax.optimization_barrier((q_own, rest))
    state = attend(by_head, 1, q_own, None, near, False)
    parts[0] = attend(by_head, 3, q_own, state, far, True)
    return merge(parts, queries.shape[0], heads)


def solution(mesh):
    placed = (
        P(("frame", "head"), None),
        P(("frame", "head"), None),
        P(("frame", "head"), None),
        P("head", "frame", None),
        P("head", "frame"),
    )
    return jax.shard_map(
        body, mesh=mesh, in_specs=placed, out_specs=P(("frame", "head"), None), check_vma=False
    )
```

```python
import functools
import math

import jax
import jax.numpy as jnp
import numpy as np
from jax import lax
from jax.experimental import pallas as pl
from jax.experimental.pallas import tpu as pltpu
from jax.sharding import PartitionSpec as P

TILE = 128
HEAD_DIM = 128
REACH = 32
PLANE = 4
GROUP = 4
LISTS = 4
FAR_OFF = 1e30
FACTOR = math.log2(math.e) / math.sqrt(HEAD_DIM)
VMEM = pl.BlockSpec(memory_space=pltpu.VMEM)
SMEM = pl.BlockSpec(memory_space=pltpu.SMEM)


def shard_table():
    table = np.zeros((PLANE, 2 * PLANE + 1), np.int32)
    for place in range(PLANE):
        x, core = divmod(place, 2)
        for distance in range(-PLANE, PLANE + 1):
            plane, there = divmod(place + distance, PLANE)
            same_x, same_core = there // 2 == x, there % 2 == core
            phase = 0
            if plane == 0:
                spot = int(same_core) if same_x else (4 if same_core else 5)
            elif not same_x:
                phase, spot = 1, 0 if same_core else 1
            elif (plane < 0) == (core == 0):
                spot = 2 + int(same_core)
            else:
                spot = 6
            table[place, distance + PLANE] = phase + 4 * spot
    return table.reshape(-1)


def params(mib):
    return pltpu.CompilerParams(vmem_limit_bytes=mib * 2**20)


def cost():
    return pl.CostEstimate(flops=0, bytes_accessed=0, transcendentals=0)


def tile_kernel(heads, flip, *refs):
    out_ref = refs[-1]
    tiles = refs[0].shape[0] // TILE
    for head in range(heads):
        for which, flipped in enumerate(flip):
            for tile in range(tiles):
                block = refs[which][
                    tile * TILE : (tile + 1) * TILE, head * HEAD_DIM : (head + 1) * HEAD_DIM
                ]
                at = (tile * heads + head) * len(flip) + which
                out_ref[at] = block.T if flipped else block


def as_tiles(arrays, flip):
    rows, width = arrays[0].shape
    heads = width // HEAD_DIM
    count = len(arrays) * heads * rows // TILE
    return pl.pallas_call(
        functools.partial(tile_kernel, heads, flip),
        in_specs=[VMEM] * len(arrays),
        out_specs=VMEM,
        out_shape=jax.ShapeDtypeStruct((count, TILE, HEAD_DIM), arrays[0].dtype),
        compiler_params=params(4),
    )(*arrays)


def list_kernel(length, codes_ref, live_ref, ends, metas, places):
    tiles = live_ref.shape[0]
    lists = ends.shape[0]
    for target in range(lists):
        ends[target] = target * length
    for row in range(tiles):

        def slot_step(slot, carry, row=row):
            code = codes_ref[row, slot]
            target = (code >> 8) & 255
            at = ends[target]
            places[at] = code & 255
            metas[at >> 2] = (code >> 16) + (at & (GROUP - 1))
            ends[target] = at + 1
            return carry

        lax.fori_loop(0, live_ref[row], slot_step, 0)
        for target in range(lists):
            at = ends[target]
            up = (at + GROUP - 1) & -GROUP
            filler = places[jnp.maximum(at - 1, 0)]
            for other in range(GROUP - 1):
                places[jnp.where(at + other < up, at + other, lists * length)] = filler
            ends[target] = up
    for target in range(lists):
        ends[target] = (ends[target] - target * length) >> 2


def work_lists(frame, head, tile_lists, live_slots, heads):
    tiles, slots = tile_lists.shape
    part_tiles = tiles // heads
    assert tiles & (tiles - 1) == 0 and heads & (heads - 1) == 0 and GROUP == 4
    within = tile_lists & (tiles - 1)
    rank = within >> int(math.log2(part_tiles))
    spot = ((within & (part_tiles - 1)) * heads + head) * 2
    table = shard_table()
    key = lax.rem(frame, PLANE) * (2 * PLANE + 1) + PLANE - frame
    key = (tile_lists >> int(math.log2(tiles))) + key
    hit = key[..., None] == jnp.arange(table.size, dtype=jnp.int32)
    entry = jnp.sum(jnp.where(hit, jnp.asarray(table), 0), axis=-1, dtype=jnp.int32)
    row = jnp.arange(tiles, dtype=jnp.int32)[:, None]
    turn = (rank - (row >> int(math.log2(part_tiles)))) & (heads - 1)
    query = (turn * part_tiles + (row & (part_tiles - 1))) * heads + head
    query = jnp.where(turn == 0, query, query - heads * part_tiles)
    step = (rank - head) & (heads - 1)
    target = step * LISTS + 2 * (entry & 3) + jnp.where(turn == 0, 1, 0)
    place = (entry >> 2) * (2 * tiles) + spot
    codes = place + target * 256 + query * (8 * 65536)
    length = max(part_tiles, tiles - part_tiles) * -(-slots // GROUP) * GROUP
    total = LISTS * heads * length
    ends, metas, places = pl.pallas_call(
        functools.partial(list_kernel, length),
        in_specs=[SMEM] * 2,
        out_specs=[SMEM] * 3,
        out_shape=[
            jax.ShapeDtypeStruct((LISTS * heads,), jnp.int32),
            jax.ShapeDtypeStruct((total // GROUP,), jnp.int32),
            jax.ShapeDtypeStruct((total + 1,), jnp.int32),
        ],
        compiler_params=params(4),
        cost_estimate=cost(),
    )(codes, live_slots)
    arrays = ends, metas, places[:total]
    return jnp.concatenate([array.reshape(heads, -1) for array in arrays], axis=1)


def packed(numbers):
    rows = -(-numbers.shape[0] // TILE)
    numbers = jnp.pad(numbers, (0, rows * TILE - numbers.shape[0])).reshape(rows, TILE)
    digits = jnp.concatenate((numbers & 255, numbers >> 8)).astype(jnp.bfloat16)
    return jnp.pad(digits, ((0, -2 * rows % 16), (0, 0)))


def unpacked(block, count):
    rows = -(-count // TILE)
    digits = block.astype(jnp.int32)
    return (digits[:rows] + digits[rows : 2 * rows] * 256).reshape(-1)[:count]


def phase_kernel(which, pieces, begins, ends, lists, q_ref, *refs):
    refs = list(refs)
    state = [refs.pop(0) for _ in range(0 if begins else 3)]
    parts = [refs.pop(0) for _ in range(pieces)]
    out_ref, stats_ref = [refs.pop(0) for _ in range(2)] if ends else [None] * 2
    top_ref, total_ref, sum_ref, window = refs[:4]
    scores, high, weights, shrinks = refs[4:] if begins else [None] * 4
    tiles = q_ref.shape[0]
    heads, width = lists.shape
    length = (width - LISTS) // (LISTS * (GROUP + 1))

    at = 0
    for part in parts:
        window[at : at + part.shape[0]] = part[...]
        at += part.shape[0]
    if begins:
        top_ref[...] = jnp.full(top_ref.shape, -FAR_OFF, jnp.float32)
        total_ref[...] = jnp.zeros(total_ref.shape, jnp.float32)
        sum_ref[...] = jnp.zeros(sum_ref.shape, jnp.float32)
    else:
        for ref, old in zip((top_ref, total_ref, sum_ref), state):
            ref[...] = old[...]

    starts = [jnp.int32(0)]
    for head in range(heads):
        starts.append(starts[-1] + lists[head, which])

    def item_of(item):
        row, index = jnp.int32(0), item
        for head in range(1, heads):
            row = jnp.where(item >= starts[head], head, row)
            index = jnp.where(item >= starts[head], item - starts[head], index)
        real = item < starts[heads]
        row, index = jnp.where(real, row, 0), jnp.where(real, index, 0)
        meta = lists[row, LISTS + which * length + index]
        at = LISTS * (1 + length) + (which * length + index) * GROUP
        tile = jnp.where(real, meta >> 3, 0)
        spots = [jnp.where(real, lists[row, at + slot], 0) for slot in range(GROUP)]
        return tile, jnp.where(real, meta & 7, -1), spots

    def score(entry):
        tile, _, spots = entry
        keys = jnp.concatenate([window[spot] for spot in spots])
        block = jnp.dot(keys, q_ref[tile], preferred_element_type=jnp.float32)
        top = jnp.max(block.reshape(-1, 8, TILE), axis=0)
        return block, jnp.max(top, axis=0, keepdims=True)

    def weigh(entry, block, peak):
        tile, last, _ = entry
        old = top_ref[tile]
        top = jnp.maximum(old, jnp.where(last < 0, -FAR_OFF, peak))
        shrink = jnp.exp2((old - top) * FACTOR)
        total = total_ref[tile] * shrink
        parts = []
        for slot in range(GROUP):
            shift = jnp.where(slot <= last, top, FAR_OFF)
            weight = jnp.exp2((block[slot * TILE : (slot + 1) * TILE] - shift) * FACTOR)
            total = total + jnp.sum(weight.reshape(-1, 8, TILE), axis=0)
            parts.append(weight.astype(jnp.bfloat16))
        top_ref[tile] = top
        total_ref[tile] = total
        return jnp.concatenate(parts), shrink

    def collect(entry, weight, shrink):
        tile, _, spots = entry
        values = jnp.concatenate([window[spot + 1] for spot in spots], axis=1)
        product = jnp.dot(values, weight, preferred_element_type=jnp.float32)
        sum_ref[tile] = sum_ref[tile] * shrink + product

    if ends:

        def whole_step(four, carry):
            entries = [item_of(4 * four + number) for number in range(4)]
            made = [score(entry) for entry in entries]
            formed = [weigh(entry, *item) for entry, item in zip(entries, made)]
            for entry, item in zip(entries, formed):
                collect(entry, *item)
            return carry

        lax.fori_loop(0, (starts[heads] + 3) >> 2, whole_step, 0)
    else:

        def store_scores(pair):
            for number, (block, peak) in enumerate(pair):
                scores[number], high[number] = block, peak

        def store_weights(pair):
            for number, (weight, shrink) in enumerate(pair):
                weights[number], shrinks[number] = weight, shrink

        ahead = [item_of(0), item_of(1)]
        second = [item_of(2), item_of(3)]
        first = [score(entry) for entry in ahead]
        store_scores([score(entry) for entry in second])
        store_weights([weigh(entry, *made) for entry, made in zip(ahead, first)])

        def step(pair, entries):
            collected, weighed = entries[:2], entries[2:]
            scored = [item_of(2 * pair + 4), item_of(2 * pair + 5)]
            made = [(scores[number], high[number]) for number in range(2)]
            formed = [(weights[number], shrinks[number]) for number in range(2)]
            blocks = [score(entry) for entry in scored]
            following = [weigh(entry, *item) for entry, item in zip(weighed, made)]
            for entry, item in zip(collected, formed):
                collect(entry, *item)
            store_scores(blocks)
            store_weights(following)
            return tuple(weighed) + tuple(scored)

        lax.fori_loop(0, (starts[heads] + 1) >> 1, step, tuple(ahead + second))

    if ends:
        for tile in range(tiles):
            total = jnp.sum(total_ref[tile], axis=0, keepdims=True)
            share = jnp.where(total > 0, 1.0 / jnp.where(total > 0, total, 1.0), 0.0)
            out_ref[tile] = (sum_ref[tile] * share).astype(out_ref.dtype)
            stats_ref[tile, 0:1] = total
            stats_ref[tile, 1:2] = top_ref[tile]


def attend(lists, which, queries, state, pieces, ends):
    tiles = queries.shape[0]
    begins = state is None
    held = [
        jax.ShapeDtypeStruct((tiles, 1, TILE), jnp.float32),
        jax.ShapeDtypeStruct((tiles, 8, TILE), jnp.float32),
        jax.ShapeDtypeStruct((tiles, HEAD_DIM, TILE), jnp.float32),
    ]
    rows = sum(piece.shape[0] for piece in pieces)
    scratch = [pltpu.VMEM((rows, TILE, TILE), queries.dtype)]
    if begins:
        scratch += [
            pltpu.VMEM((2, GROUP * TILE, TILE), jnp.float32),
            pltpu.VMEM((2, 1, TILE), jnp.float32),
            pltpu.VMEM((2, GROUP * TILE, TILE), queries.dtype),
            pltpu.VMEM((2, 1, TILE), jnp.float32),
        ]
    if ends:
        scratch = [pltpu.VMEM(array.shape, array.dtype) for array in held] + scratch
        held = [
            jax.ShapeDtypeStruct((tiles, HEAD_DIM, TILE), queries.dtype),
            jax.ShapeDtypeStruct((tiles, 2, TILE), jnp.float32),
        ]
    return pl.pallas_call(
        functools.partial(phase_kernel, which, len(pieces), begins, ends),
        in_specs=[SMEM] + [VMEM] * (1 + len(pieces) + (0 if begins else 3)),
        out_specs=[VMEM] * len(held),
        out_shape=held,
        scratch_shapes=scratch,
        compiler_params=params(10),
        cost_estimate=cost(),
    )(lists, queries, *([] if begins else state), *pieces)


def merge_kernel(count, *refs):
    out_ref = refs[-1]
    values, stats = [refs[first : 2 * count : 2] for first in range(2)]
    tiles = values[0].shape[0]
    heads = out_ref.shape[1] // HEAD_DIM
    for tile in range(tiles):
        top = stats[0][tile, 1:2]
        for ref in stats[1:]:
            top = jnp.maximum(top, ref[tile, 1:2])
        shares = [ref[tile, 0:1] * jnp.exp2((ref[tile, 1:2] - top) * FACTOR) for ref in stats]
        whole = sum(shares[1:], shares[0])
        out = jnp.zeros((HEAD_DIM, TILE), jnp.float32)
        for value, share in zip(values, shares):
            out = out + value[tile].astype(jnp.float32) * (share / whole)
        inner, head = divmod(tile, heads)
        out_ref[
            inner * TILE : (inner + 1) * TILE, head * HEAD_DIM : (head + 1) * HEAD_DIM
        ] = out.T.astype(out_ref.dtype)


def merge(parts, rows, heads):
    flat = [array for part in parts for array in part]
    return pl.pallas_call(
        functools.partial(merge_kernel, len(parts)),
        in_specs=[VMEM] * len(flat),
        out_specs=VMEM,
        out_shape=jax.ShapeDtypeStruct((rows, heads * HEAD_DIM), flat[0].dtype),
        compiler_params=params(6),
    )(*flat)


def moved(block, axis, source):
    size = lax.axis_size(axis)
    route = [(source(i), i) for i in range(size) if 0 <= source(i) < size]
    return lax.ppermute(block, axis, route)


def body(queries, key_vectors, value_vectors, tile_lists, live_slots):
    heads = lax.axis_size("head")
    frame = lax.axis_index("frame")
    head = lax.axis_index("head")
    shard_tiles = tile_lists.shape[1]
    assert shard_tiles * PLANE == REACH and lax.axis_size("frame") % PLANE == 0

    def from_head(block, step):
        return moved(block, "head", lambda i: (i - step) % heads)

    def core_swap(block):
        return moved(block, "frame", lambda i: i ^ 1)

    own = as_tiles((key_vectors, value_vectors), (False, True))
    size = own.shape[0]
    cut = size * 9 // 16
    across = moved(own, "frame", lambda i: i ^ 2)
    chip = jnp.concatenate((core_swap(own), own))
    level = moved(chip, "frame", lambda i: i - PLANE if i % 2 == 0 else i + PLANE)

    listed, live, _ = lax.optimization_barrier((tile_lists[0], live_slots[0], chip))
    lists = work_lists(frame, head, listed, live, heads)
    q_own = as_tiles((queries,), (True,))
    blocks = [
        from_head(jnp.concatenate((q_own.reshape(-1, TILE), packed(lists[step]))), step)
        for step in range(1, heads)
    ]
    blocks, _ = lax.optimization_barrier((blocks, level))
    q_parts, by_head = [], [lists[:1]]
    for block in blocks:
        q_rows = shard_tiles * TILE
        q_parts.append(block[:q_rows].reshape(q_own.shape))
        by_head.append(unpacked(block[q_rows:], lists.shape[1])[None])
    q_rest, by_head = jnp.concatenate(q_parts), jnp.concatenate(by_head)

    far_z = moved(across[:cut], "frame", lambda i: i - PLANE if i % PLANE < 2 else i + PLANE)
    straight = moved(own[cut:], "frame", lambda i: i - 2 if i % PLANE < 2 else i + 2)
    near = [chip, level, across, core_swap(across), core_swap(level[:size])]
    state = attend(by_head, 0, q_rest, None, near, False)
    far_z, straight, state = lax.optimization_barrier((far_z, straight, state))
    far = jnp.concatenate((far_z, straight))
    far = [far, core_swap(far)]
    rest = attend(by_head, 2, q_rest, state, far, True)
    parts = [None]
    for step in range(1, heads):
        cut = slice((step - 1) * shard_tiles, step * shard_tiles)
        parts.append([from_head(array[cut], -step) for array in rest])
    q_own, _ = lax.optimization_barrier((q_own, rest))
    state = attend(by_head, 1, q_own, None, near, False)
    parts[0] = attend(by_head, 3, q_own, state, far, True)
    return merge(parts, queries.shape[0], heads)


def solution(mesh):
    placed = (
        P(("frame", "head"), None),
        P(("frame", "head"), None),
        P(("frame", "head"), None),
        P("head", "frame", None),
        P("head", "frame"),
    )
    return jax.shard_map(
        body, mesh=mesh, in_specs=placed, out_specs=P(("frame", "head"), None), check_vma=False
    )
```

```python
import functools
import math

import jax
import jax.numpy as jnp
import numpy as np
from jax import lax
from jax.experimental import pallas as pl
from jax.experimental.pallas import tpu as pltpu
from jax.sharding import PartitionSpec as P

TILE = 128
HEAD_DIM = 128
REACH = 32
PLANE = 4
GROUP = 4
LISTS = 6
FAR_OFF = 1e30
FACTOR = math.log2(math.e) / math.sqrt(HEAD_DIM)
VMEM = pl.BlockSpec(memory_space=pltpu.VMEM)
SMEM = pl.BlockSpec(memory_space=pltpu.SMEM)


def shard_table():
    table = np.zeros((PLANE, 2 * PLANE + 1), np.int32)
    for place in range(PLANE):
        x, core = divmod(place, 2)
        for distance in range(-PLANE, PLANE + 1):
            plane, there = divmod(place + distance, PLANE)
            same_x, same_core = there // 2 == x, there % 2 == core
            if plane == 0:
                phase, spot = 0, int(same_core) if same_x else (2 if same_core else 3)
            elif not same_x:
                phase, spot = 2, 0 if same_core else 1
            elif (plane < 0) == (core == 0):
                phase, spot = 1, 4 + int(same_core)
            else:
                phase, spot = 1, 6
            table[place, distance + PLANE] = phase + 4 * spot
    return table.reshape(-1)


def params(mib):
    return pltpu.CompilerParams(vmem_limit_bytes=mib * 2**20)


def cost():
    return pl.CostEstimate(flops=0, bytes_accessed=0, transcendentals=0)


def tile_kernel(heads, flip, *refs):
    out_ref = refs[-1]
    tiles = refs[0].shape[0] // TILE
    for head in range(heads):
        for which, flipped in enumerate(flip):
            for tile in range(tiles):
                block = refs[which][
                    tile * TILE : (tile + 1) * TILE, head * HEAD_DIM : (head + 1) * HEAD_DIM
                ]
                at = (tile * heads + head) * len(flip) + which
                out_ref[at] = block.T if flipped else block


def as_tiles(arrays, flip):
    rows, width = arrays[0].shape
    heads = width // HEAD_DIM
    count = len(arrays) * heads * rows // TILE
    return pl.pallas_call(
        functools.partial(tile_kernel, heads, flip),
        in_specs=[VMEM] * len(arrays),
        out_specs=VMEM,
        out_shape=jax.ShapeDtypeStruct((count, TILE, HEAD_DIM), arrays[0].dtype),
        compiler_params=params(4),
    )(*arrays)


def list_kernel(length, codes_ref, live_ref, ends, metas, places):
    tiles = live_ref.shape[0]
    lists = ends.shape[0]
    for target in range(lists):
        ends[target] = target * length
    for row in range(tiles):

        def slot_step(slot, carry, row=row):
            code = codes_ref[row, slot]
            target = (code >> 8) & 255
            at = ends[target]
            places[at] = code & 255
            metas[at >> 2] = (code >> 16) + (at & (GROUP - 1))
            ends[target] = at + 1
            return carry

        lax.fori_loop(0, live_ref[row], slot_step, 0)
        for target in range(lists):
            at = ends[target]
            up = (at + GROUP - 1) & -GROUP
            filler = places[jnp.maximum(at - 1, 0)]
            for other in range(GROUP - 1):
                places[jnp.where(at + other < up, at + other, lists * length)] = filler
            ends[target] = up
    for target in range(lists):
        ends[target] = (ends[target] - target * length) >> 2


def work_lists(frame, head, tile_lists, live_slots, heads):
    tiles, slots = tile_lists.shape
    part_tiles = tiles // heads
    assert tiles & (tiles - 1) == 0 and heads & (heads - 1) == 0 and GROUP == 4
    within = tile_lists & (tiles - 1)
    rank = within >> int(math.log2(part_tiles))
    spot = ((within & (part_tiles - 1)) * heads + head) * 2
    table = shard_table()
    key = lax.rem(frame, PLANE) * (2 * PLANE + 1) + PLANE - frame
    key = (tile_lists >> int(math.log2(tiles))) + key
    hit = key[..., None] == jnp.arange(table.size, dtype=jnp.int32)
    entry = jnp.sum(jnp.where(hit, jnp.asarray(table), 0), axis=-1, dtype=jnp.int32)
    row = jnp.arange(tiles, dtype=jnp.int32)[:, None]
    turn = (rank - (row >> int(math.log2(part_tiles)))) & (heads - 1)
    query = (turn * part_tiles + (row & (part_tiles - 1))) * heads + head
    query = jnp.where(turn == 0, query, query - heads * part_tiles)
    step = (rank - head) & (heads - 1)
    target = step * LISTS + 2 * (entry & 3) + jnp.where(turn == 0, 1, 0)
    place = (entry >> 2) * (2 * tiles) + spot
    codes = place + target * 256 + query * (8 * 65536)
    length = max(part_tiles, tiles - part_tiles) * -(-slots // GROUP) * GROUP
    total = LISTS * heads * length
    ends, metas, places = pl.pallas_call(
        functools.partial(list_kernel, length),
        in_specs=[SMEM] * 2,
        out_specs=[SMEM] * 3,
        out_shape=[
            jax.ShapeDtypeStruct((LISTS * heads,), jnp.int32),
            jax.ShapeDtypeStruct((total // GROUP,), jnp.int32),
            jax.ShapeDtypeStruct((total + 1,), jnp.int32),
        ],
        compiler_params=params(4),
        cost_estimate=cost(),
    )(codes, live_slots)
    arrays = ends, metas, places[:total]
    return jnp.concatenate([array.reshape(heads, -1) for array in arrays], axis=1)


def packed(numbers):
    rows = -(-numbers.shape[0] // TILE)
    numbers = jnp.pad(numbers, (0, rows * TILE - numbers.shape[0])).reshape(rows, TILE)
    digits = jnp.concatenate((numbers & 255, numbers >> 8)).astype(jnp.bfloat16)
    return jnp.pad(digits, ((0, -2 * rows % 16), (0, 0)))


def unpacked(block, count):
    rows = -(-count // TILE)
    digits = block.astype(jnp.int32)
    return (digits[:rows] + digits[rows : 2 * rows] * 256).reshape(-1)[:count]


def phase_kernel(whiches, shift, pieces, begins, ends, lists, q_ref, *refs):
    refs = list(refs)
    state = [refs.pop(0) for _ in range(0 if begins else 3)]
    parts = [refs.pop(0) for _ in range(pieces)]
    out_ref, stats_ref = [refs.pop(0) for _ in range(2)] if ends else [None] * 2
    top_ref, total_ref, sum_ref, window = refs[:4]
    scores, high, weights, shrinks = [None] * 4 if ends else refs[4:]
    tiles = q_ref.shape[0]
    heads, width = lists.shape
    length = (width - LISTS) // (LISTS * (GROUP + 1))

    at = 0
    for part in parts:
        window[at : at + part.shape[0]] = part[...]
        at += part.shape[0]
    if begins:
        top_ref[...] = jnp.full(top_ref.shape, -FAR_OFF, jnp.float32)
        total_ref[...] = jnp.zeros(total_ref.shape, jnp.float32)
        sum_ref[...] = jnp.zeros(sum_ref.shape, jnp.float32)
    else:
        for ref, old in zip((top_ref, total_ref, sum_ref), state):
            ref[...] = old[...]

    blocks = [(which, head) for which in whiches for head in range(heads)]
    starts = [jnp.int32(0)]
    for which, head in blocks:
        starts.append(starts[-1] + lists[head, which])

    def item_of(item):
        row, which, index = jnp.int32(0), jnp.int32(whiches[0]), item
        for number in range(1, len(blocks)):
            later = item >= starts[number]
            which = jnp.where(later, blocks[number][0], which)
            row = jnp.where(later, blocks[number][1], row)
            index = jnp.where(later, item - starts[number], index)
        real = item < starts[-1]
        index = jnp.where(real, index, 0)
        meta = lists[row, LISTS + which * length + index]
        at = LISTS * (1 + length) + (which * length + index) * GROUP
        tile = jnp.where(real, meta >> 3, 0)
        spots = [jnp.where(real, lists[row, at + slot] - shift, 0) for slot in range(GROUP)]
        return tile, jnp.where(real, meta & 7, -1), spots

    def score(entry):
        tile, _, spots = entry
        keys = jnp.concatenate([window[spot] for spot in spots])
        block = jnp.dot(keys, q_ref[tile], preferred_element_type=jnp.float32)
        top = jnp.max(block.reshape(-1, 8, TILE), axis=0)
        return block, jnp.max(top, axis=0, keepdims=True)

    def weigh(entry, block, peak):
        tile, last, _ = entry
        old = top_ref[tile]
        top = jnp.maximum(old, jnp.where(last < 0, -FAR_OFF, peak))
        shrink = jnp.exp2((old - top) * FACTOR)
        total = total_ref[tile] * shrink
        parts = []
        for slot in range(GROUP):
            level = jnp.where(slot <= last, top, FAR_OFF)
            weight = jnp.exp2((block[slot * TILE : (slot + 1) * TILE] - level) * FACTOR)
            total = total + jnp.sum(weight.reshape(-1, 8, TILE), axis=0)
            parts.append(weight.astype(jnp.bfloat16))
        top_ref[tile] = top
        total_ref[tile] = total
        return jnp.concatenate(parts), shrink

    def collect(entry, weight, shrink):
        tile, _, spots = entry
        values = jnp.concatenate([window[spot + 1] for spot in spots], axis=1)
        product = jnp.dot(values, weight, preferred_element_type=jnp.float32)
        sum_ref[tile] = sum_ref[tile] * shrink + product

    if ends:

        def whole_step(four, carry):
            entries = [item_of(4 * four + number) for number in range(4)]
            made = [score(entry) for entry in entries]
            formed = [weigh(entry, *item) for entry, item in zip(entries, made)]
            for entry, item in zip(entries, formed):
                collect(entry, *item)
            return carry

        lax.fori_loop(0, (starts[-1] + 3) >> 2, whole_step, 0)
    else:

        def store_scores(pair):
            for number, (block, peak) in enumerate(pair):
                scores[number], high[number] = block, peak

        def store_weights(pair):
            for number, (weight, shrink) in enumerate(pair):
                weights[number], shrinks[number] = weight, shrink

        ahead = [item_of(0), item_of(1)]
        second = [item_of(2), item_of(3)]
        first = [score(entry) for entry in ahead]
        store_scores([score(entry) for entry in second])
        store_weights([weigh(entry, *made) for entry, made in zip(ahead, first)])

        def step(pair, entries):
            collected, weighed = entries[:2], entries[2:]
            scored = [item_of(2 * pair + 4), item_of(2 * pair + 5)]
            made = [(scores[number], high[number]) for number in range(2)]
            formed = [(weights[number], shrinks[number]) for number in range(2)]
            blocks = [score(entry) for entry in scored]
            following = [weigh(entry, *item) for entry, item in zip(weighed, made)]
            for entry, item in zip(collected, formed):
                collect(entry, *item)
            store_scores(blocks)
            store_weights(following)
            return tuple(weighed) + tuple(scored)

        lax.fori_loop(0, (starts[-1] + 1) >> 1, step, tuple(ahead + second))

    if ends:
        for tile in range(tiles):
            total = jnp.sum(total_ref[tile], axis=0, keepdims=True)
            share = jnp.where(total > 0, 1.0 / jnp.where(total > 0, total, 1.0), 0.0)
            out_ref[tile] = (sum_ref[tile] * share).astype(out_ref.dtype)
            stats_ref[tile, 0:1] = total
            stats_ref[tile, 1:2] = top_ref[tile]


def attend(lists, whiches, shift, queries, state, pieces, ends):
    tiles = queries.shape[0]
    begins = state is None
    held = [
        jax.ShapeDtypeStruct((tiles, 1, TILE), jnp.float32),
        jax.ShapeDtypeStruct((tiles, 8, TILE), jnp.float32),
        jax.ShapeDtypeStruct((tiles, HEAD_DIM, TILE), jnp.float32),
    ]
    rows = sum(piece.shape[0] for piece in pieces)
    scratch = [pltpu.VMEM((rows, TILE, TILE), queries.dtype)]
    if not ends:
        scratch += [
            pltpu.VMEM((2, GROUP * TILE, TILE), jnp.float32),
            pltpu.VMEM((2, 1, TILE), jnp.float32),
            pltpu.VMEM((2, GROUP * TILE, TILE), queries.dtype),
            pltpu.VMEM((2, 1, TILE), jnp.float32),
        ]
    if ends:
        scratch = [pltpu.VMEM(array.shape, array.dtype) for array in held] + scratch
        held = [
            jax.ShapeDtypeStruct((tiles, HEAD_DIM, TILE), queries.dtype),
            jax.ShapeDtypeStruct((tiles, 2, TILE), jnp.float32),
        ]
    return pl.pallas_call(
        functools.partial(phase_kernel, whiches, shift, len(pieces), begins, ends),
        in_specs=[SMEM] + [VMEM] * (1 + len(pieces) + (0 if begins else 3)),
        out_specs=[VMEM] * len(held),
        out_shape=held,
        scratch_shapes=scratch,
        compiler_params=params(10),
        cost_estimate=cost(),
    )(lists, queries, *([] if begins else state), *pieces)


def merge_kernel(count, *refs):
    out_ref = refs[-1]
    values, stats = [refs[first : 2 * count : 2] for first in range(2)]
    tiles = values[0].shape[0]
    heads = out_ref.shape[1] // HEAD_DIM
    for tile in range(tiles):
        top = stats[0][tile, 1:2]
        for ref in stats[1:]:
            top = jnp.maximum(top, ref[tile, 1:2])
        shares = [ref[tile, 0:1] * jnp.exp2((ref[tile, 1:2] - top) * FACTOR) for ref in stats]
        whole = sum(shares[1:], shares[0])
        out = jnp.zeros((HEAD_DIM, TILE), jnp.float32)
        for value, share in zip(values, shares):
            out = out + value[tile].astype(jnp.float32) * (share / whole)
        inner, head = divmod(tile, heads)
        out_ref[
            inner * TILE : (inner + 1) * TILE, head * HEAD_DIM : (head + 1) * HEAD_DIM
        ] = out.T.astype(out_ref.dtype)


def merge(parts, rows, heads):
    flat = [array for part in parts for array in part]
    return pl.pallas_call(
        functools.partial(merge_kernel, len(parts)),
        in_specs=[VMEM] * len(flat),
        out_specs=VMEM,
        out_shape=jax.ShapeDtypeStruct((rows, heads * HEAD_DIM), flat[0].dtype),
        compiler_params=params(6),
    )(*flat)


def moved(block, axis, source):
    size = lax.axis_size(axis)
    route = [(source(i), i) for i in range(size) if 0 <= source(i) < size]
    return lax.ppermute(block, axis, route)


def body(queries, key_vectors, value_vectors, tile_lists, live_slots):
    heads = lax.axis_size("head")
    frame = lax.axis_index("frame")
    head = lax.axis_index("head")
    shard_tiles = tile_lists.shape[1]
    assert shard_tiles * PLANE == REACH and lax.axis_size("frame") % PLANE == 0

    def from_head(block, step):
        return moved(block, "head", lambda i: (i - step) % heads)

    def core_swap(block):
        return moved(block, "frame", lambda i: i ^ 1)

    own = as_tiles((key_vectors, value_vectors), (False, True))
    size = own.shape[0]
    cut = size * 9 // 16
    across = moved(own, "frame", lambda i: i ^ 2)
    chip = jnp.concatenate((core_swap(own), own))
    level = moved(chip, "frame", lambda i: i - PLANE if i % 2 == 0 else i + PLANE)

    listed, live, _ = lax.optimization_barrier((tile_lists[0], live_slots[0], chip))
    lists = work_lists(frame, head, listed, live, heads)
    q_own = as_tiles((queries,), (True,))
    blocks = [
        from_head(jnp.concatenate((q_own.reshape(-1, TILE), packed(lists[step]))), step)
        for step in range(1, heads)
    ]
    blocks, _ = lax.optimization_barrier((blocks, level))
    q_parts, by_head = [], [lists[:1]]
    for block in blocks:
        q_rows = shard_tiles * TILE
        q_parts.append(block[:q_rows].reshape(q_own.shape))
        by_head.append(unpacked(block[q_rows:], lists.shape[1])[None])
    q_rest, by_head = jnp.concatenate(q_parts), jnp.concatenate(by_head)

    far_z = moved(across[:cut], "frame", lambda i: i - PLANE if i % PLANE < 2 else i + PLANE)
    straight = moved(own[cut:], "frame", lambda i: i - 2 if i % PLANE < 2 else i + 2)
    plane = [chip, across, core_swap(across)]
    state = attend(by_head, (0,), 0, q_rest, None, plane, False)
    level_core, state = lax.optimization_barrier((core_swap(level[:size]), state))
    planes = [level, level_core]
    state = attend(by_head, (2,), 4 * size, q_rest, state, planes, False)
    far_z, straight, state = lax.optimization_barrier((far_z, straight, state))
    far = jnp.concatenate((far_z, straight))
    far = [far, core_swap(far)]
    rest = attend(by_head, (4,), 0, q_rest, state, far, True)
    parts = [None]
    for step in range(1, heads):
        cut = slice((step - 1) * shard_tiles, step * shard_tiles)
        parts.append([from_head(array[cut], -step) for array in rest])
    q_own, _ = lax.optimization_barrier((q_own, rest))
    state = attend(by_head, (1, 3), 0, q_own, None, plane + planes, False)
    parts[0] = attend(by_head, (5,), 0, q_own, state, far, True)
    return merge(parts, queries.shape[0], heads)


def solution(mesh):
    placed = (
        P(("frame", "head"), None),
        P(("frame", "head"), None),
        P(("frame", "head"), None),
        P("head", "frame", None),
        P("head", "frame"),
    )
    return jax.shard_map(
        body, mesh=mesh, in_specs=placed, out_specs=P(("frame", "head"), None), check_vma=False
    )
```

```python
import functools
import math

import jax
import jax.numpy as jnp
import numpy as np
from jax import lax
from jax.experimental import pallas as pl
from jax.experimental.pallas import tpu as pltpu
from jax.sharding import PartitionSpec as P

TILE = 128
HEAD_DIM = 128
REACH = 32
PLANE = 4
GROUP = 4
LISTS = 6
FAR_OFF = 1e30
FACTOR = math.log2(math.e) / math.sqrt(HEAD_DIM)
VMEM = pl.BlockSpec(memory_space=pltpu.VMEM)
SMEM = pl.BlockSpec(memory_space=pltpu.SMEM)


def shard_table():
    table = np.zeros((PLANE, 2 * PLANE + 1), np.int32)
    for place in range(PLANE):
        x, core = divmod(place, 2)
        for distance in range(-PLANE, PLANE + 1):
            plane, there = divmod(place + distance, PLANE)
            same_x, same_core = there // 2 == x, there % 2 == core
            if plane == 0:
                phase, spot = 0, int(same_core) if same_x else (2 if same_core else 3)
            elif not same_x:
                phase, spot = 2, 0 if same_core else 1
            elif (plane < 0) == (core == 0):
                phase, spot = 1, 4 + int(same_core)
            else:
                phase, spot = 1, 6
            table[place, distance + PLANE] = phase + 4 * spot
    return table.reshape(-1)


def params(mib):
    return pltpu.CompilerParams(vmem_limit_bytes=mib * 2**20)


def cost():
    return pl.CostEstimate(flops=0, bytes_accessed=0, transcendentals=0)


def tile_kernel(heads, flip, *refs):
    out_ref = refs[-1]
    tiles = refs[0].shape[0] // TILE
    for head in range(heads):
        for which, flipped in enumerate(flip):
            for tile in range(tiles):
                block = refs[which][
                    tile * TILE : (tile + 1) * TILE, head * HEAD_DIM : (head + 1) * HEAD_DIM
                ]
                at = (tile * heads + head) * len(flip) + which
                out_ref[at] = block.T if flipped else block


def as_tiles(arrays, flip):
    rows, width = arrays[0].shape
    heads = width // HEAD_DIM
    count = len(arrays) * heads * rows // TILE
    return pl.pallas_call(
        functools.partial(tile_kernel, heads, flip),
        in_specs=[VMEM] * len(arrays),
        out_specs=VMEM,
        out_shape=jax.ShapeDtypeStruct((count, TILE, HEAD_DIM), arrays[0].dtype),
        compiler_params=params(4),
    )(*arrays)


def list_kernel(length, codes_ref, live_ref, ends, metas, places):
    tiles = live_ref.shape[0]
    lists = ends.shape[0]
    for target in range(lists):
        ends[target] = target * length
    for row in range(tiles):

        def slot_step(slot, carry, row=row):
            code = codes_ref[row, slot]
            target = (code >> 8) & 255
            at = ends[target]
            places[at] = code & 255
            metas[at >> 2] = (code >> 16) + (at & (GROUP - 1))
            ends[target] = at + 1
            return carry

        lax.fori_loop(0, live_ref[row], slot_step, 0)
        for target in range(lists):
            at = ends[target]
            up = (at + GROUP - 1) & -GROUP
            filler = places[jnp.maximum(at - 1, 0)]
            for other in range(GROUP - 1):
                places[jnp.where(at + other < up, at + other, lists * length)] = filler
            ends[target] = up
    for target in range(lists):
        ends[target] = (ends[target] - target * length) >> 2


def work_lists(frame, head, tile_lists, live_slots, heads):
    tiles, slots = tile_lists.shape
    part_tiles = tiles // heads
    assert tiles & (tiles - 1) == 0 and heads & (heads - 1) == 0 and GROUP == 4
    within = tile_lists & (tiles - 1)
    rank = within >> int(math.log2(part_tiles))
    spot = ((within & (part_tiles - 1)) * heads + head) * 2
    table = shard_table()
    key = lax.rem(frame, PLANE) * (2 * PLANE + 1) + PLANE - frame
    key = (tile_lists >> int(math.log2(tiles))) + key
    hit = key[..., None] == jnp.arange(table.size, dtype=jnp.int32)
    entry = jnp.sum(jnp.where(hit, jnp.asarray(table), 0), axis=-1, dtype=jnp.int32)
    row = jnp.arange(tiles, dtype=jnp.int32)[:, None]
    turn = (rank - (row >> int(math.log2(part_tiles)))) & (heads - 1)
    query = (turn * part_tiles + (row & (part_tiles - 1))) * heads + head
    query = jnp.where(turn == 0, query, query - heads * part_tiles)
    step = (rank - head) & (heads - 1)
    target = step * LISTS + 2 * (entry & 3) + jnp.where(turn == 0, 1, 0)
    place = (entry >> 2) * (2 * tiles) + spot
    codes = place + target * 256 + query * (8 * 65536)
    length = max(part_tiles, tiles - part_tiles) * -(-slots // GROUP) * GROUP
    total = LISTS * heads * length
    ends, metas, places = pl.pallas_call(
        functools.partial(list_kernel, length),
        in_specs=[SMEM] * 2,
        out_specs=[SMEM] * 3,
        out_shape=[
            jax.ShapeDtypeStruct((LISTS * heads,), jnp.int32),
            jax.ShapeDtypeStruct((total // GROUP,), jnp.int32),
            jax.ShapeDtypeStruct((total + 1,), jnp.int32),
        ],
        compiler_params=params(4),
        cost_estimate=cost(),
    )(codes, live_slots)
    arrays = ends, metas, places[:total]
    return jnp.concatenate([array.reshape(heads, -1) for array in arrays], axis=1)


def packed(numbers):
    rows = -(-numbers.shape[0] // TILE)
    numbers = jnp.pad(numbers, (0, rows * TILE - numbers.shape[0])).reshape(rows, TILE)
    digits = jnp.concatenate((numbers & 255, numbers >> 8)).astype(jnp.bfloat16)
    return jnp.pad(digits, ((0, -2 * rows % 16), (0, 0)))


def unpacked(block, count):
    rows = -(-count // TILE)
    digits = block.astype(jnp.int32)
    return (digits[:rows] + digits[rows : 2 * rows] * 256).reshape(-1)[:count]


def phase_kernel(whiches, shifted, pieces, begins, ends, lists, q_ref, *refs):
    refs = list(refs)
    state = [refs.pop(0) for _ in range(0 if begins else 3)]
    parts = [refs.pop(0) for _ in range(pieces)]
    out_ref, stats_ref = [refs.pop(0) for _ in range(2)] if ends else [None] * 2
    top_ref, total_ref, sum_ref, window = refs[:4]
    scores, high, weights, shrinks = [None] * 4 if ends else refs[4:]
    tiles = q_ref.shape[0]
    heads, width = lists.shape
    length = (width - LISTS) // (LISTS * (GROUP + 1))

    at = 0
    for part in parts:
        window[at : at + part.shape[0]] = part[...]
        at += part.shape[0]
    if begins:
        top_ref[...] = jnp.full(top_ref.shape, -FAR_OFF, jnp.float32)
        total_ref[...] = jnp.zeros(total_ref.shape, jnp.float32)
        sum_ref[...] = jnp.zeros(sum_ref.shape, jnp.float32)
    else:
        for ref, old in zip((top_ref, total_ref, sum_ref), state):
            ref[...] = old[...]

    blocks = [(which, head) for which in whiches for head in range(heads)]
    starts = [jnp.int32(0)]
    for which, head in blocks:
        starts.append(starts[-1] + lists[head, which])

    def item_of(item):
        row, which, index = jnp.int32(0), jnp.int32(whiches[0]), item
        for number in range(1, len(blocks)):
            later = item >= starts[number]
            which = jnp.where(later, blocks[number][0], which)
            row = jnp.where(later, blocks[number][1], row)
            index = jnp.where(later, item - starts[number], index)
        real = item < starts[-1]
        index = jnp.where(real, index, 0)
        meta = lists[row, LISTS + which * length + index]
        at = LISTS * (1 + length) + (which * length + index) * GROUP
        tile = jnp.where(real, meta >> 3, 0)
        shift = jnp.where(which > 3, shifted, 0)
        spots = [jnp.where(real, lists[row, at + slot] + shift, 0) for slot in range(GROUP)]
        return tile, jnp.where(real, meta & 7, -1), spots

    def score(entry):
        tile, _, spots = entry
        keys = jnp.concatenate([window[spot] for spot in spots])
        block = jnp.dot(keys, q_ref[tile], preferred_element_type=jnp.float32)
        top = jnp.max(block.reshape(-1, 8, TILE), axis=0)
        return block, jnp.max(top, axis=0, keepdims=True)

    def weigh(entry, block, peak):
        tile, last, _ = entry
        old = top_ref[tile]
        top = jnp.maximum(old, jnp.where(last < 0, -FAR_OFF, peak))
        shrink = jnp.exp2((old - top) * FACTOR)
        total = total_ref[tile] * shrink
        parts = []
        for slot in range(GROUP):
            level = jnp.where(slot <= last, top, FAR_OFF)
            weight = jnp.exp2((block[slot * TILE : (slot + 1) * TILE] - level) * FACTOR)
            total = total + jnp.sum(weight.reshape(-1, 8, TILE), axis=0)
            parts.append(weight.astype(jnp.bfloat16))
        top_ref[tile] = top
        total_ref[tile] = total
        return jnp.concatenate(parts), shrink

    def collect(entry, weight, shrink):
        tile, _, spots = entry
        values = jnp.concatenate([window[spot + 1] for spot in spots], axis=1)
        product = jnp.dot(values, weight, preferred_element_type=jnp.float32)
        sum_ref[tile] = sum_ref[tile] * shrink + product

    if ends:

        def whole_step(four, carry):
            entries = [item_of(4 * four + number) for number in range(4)]
            made = [score(entry) for entry in entries]
            formed = [weigh(entry, *item) for entry, item in zip(entries, made)]
            for entry, item in zip(entries, formed):
                collect(entry, *item)
            return carry

        lax.fori_loop(0, (starts[-1] + 3) >> 2, whole_step, 0)
    else:

        def store_scores(pair):
            for number, (block, peak) in enumerate(pair):
                scores[number], high[number] = block, peak

        def store_weights(pair):
            for number, (weight, shrink) in enumerate(pair):
                weights[number], shrinks[number] = weight, shrink

        ahead = [item_of(0), item_of(1)]
        second = [item_of(2), item_of(3)]
        first = [score(entry) for entry in ahead]
        store_scores([score(entry) for entry in second])
        store_weights([weigh(entry, *made) for entry, made in zip(ahead, first)])

        def step(pair, entries):
            collected, weighed = entries[:2], entries[2:]
            scored = [item_of(2 * pair + 4), item_of(2 * pair + 5)]
            made = [(scores[number], high[number]) for number in range(2)]
            formed = [(weights[number], shrinks[number]) for number in range(2)]
            blocks = [score(entry) for entry in scored]
            following = [weigh(entry, *item) for entry, item in zip(weighed, made)]
            for entry, item in zip(collected, formed):
                collect(entry, *item)
            store_scores(blocks)
            store_weights(following)
            return tuple(weighed) + tuple(scored)

        lax.fori_loop(0, (starts[-1] + 1) >> 1, step, tuple(ahead + second))

    if ends:
        for tile in range(tiles):
            total = jnp.sum(total_ref[tile], axis=0, keepdims=True)
            share = jnp.where(total > 0, 1.0 / jnp.where(total > 0, total, 1.0), 0.0)
            out_ref[tile] = (sum_ref[tile] * share).astype(out_ref.dtype)
            stats_ref[tile, 0:1] = total
            stats_ref[tile, 1:2] = top_ref[tile]


def attend(lists, whiches, shifted, queries, state, pieces, ends):
    tiles = queries.shape[0]
    begins = state is None
    held = [
        jax.ShapeDtypeStruct((tiles, 1, TILE), jnp.float32),
        jax.ShapeDtypeStruct((tiles, 8, TILE), jnp.float32),
        jax.ShapeDtypeStruct((tiles, HEAD_DIM, TILE), jnp.float32),
    ]
    rows = sum(piece.shape[0] for piece in pieces)
    scratch = [pltpu.VMEM((rows, TILE, TILE), queries.dtype)]
    if not ends:
        scratch += [
            pltpu.VMEM((2, GROUP * TILE, TILE), jnp.float32),
            pltpu.VMEM((2, 1, TILE), jnp.float32),
            pltpu.VMEM((2, GROUP * TILE, TILE), queries.dtype),
            pltpu.VMEM((2, 1, TILE), jnp.float32),
        ]
    if ends:
        scratch = [pltpu.VMEM(array.shape, array.dtype) for array in held] + scratch
        held = [
            jax.ShapeDtypeStruct((tiles, HEAD_DIM, TILE), queries.dtype),
            jax.ShapeDtypeStruct((tiles, 2, TILE), jnp.float32),
        ]
    return pl.pallas_call(
        functools.partial(phase_kernel, whiches, shifted, len(pieces), begins, ends),
        in_specs=[SMEM] + [VMEM] * (1 + len(pieces) + (0 if begins else 3)),
        out_specs=[VMEM] * len(held),
        out_shape=held,
        scratch_shapes=scratch,
        compiler_params=params(10),
        cost_estimate=cost(),
    )(lists, queries, *([] if begins else state), *pieces)


def merge_kernel(count, *refs):
    out_ref = refs[-1]
    values, stats = [refs[first : 2 * count : 2] for first in range(2)]
    tiles = values[0].shape[0]
    heads = out_ref.shape[1] // HEAD_DIM
    for tile in range(tiles):
        top = stats[0][tile, 1:2]
        for ref in stats[1:]:
            top = jnp.maximum(top, ref[tile, 1:2])
        shares = [ref[tile, 0:1] * jnp.exp2((ref[tile, 1:2] - top) * FACTOR) for ref in stats]
        whole = sum(shares[1:], shares[0])
        out = jnp.zeros((HEAD_DIM, TILE), jnp.float32)
        for value, share in zip(values, shares):
            out = out + value[tile].astype(jnp.float32) * (share / whole)
        inner, head = divmod(tile, heads)
        out_ref[
            inner * TILE : (inner + 1) * TILE, head * HEAD_DIM : (head + 1) * HEAD_DIM
        ] = out.T.astype(out_ref.dtype)


def merge(parts, rows, heads):
    flat = [array for part in parts for array in part]
    return pl.pallas_call(
        functools.partial(merge_kernel, len(parts)),
        in_specs=[VMEM] * len(flat),
        out_specs=VMEM,
        out_shape=jax.ShapeDtypeStruct((rows, heads * HEAD_DIM), flat[0].dtype),
        compiler_params=params(6),
    )(*flat)


def moved(block, axis, source):
    size = lax.axis_size(axis)
    route = [(source(i), i) for i in range(size) if 0 <= source(i) < size]
    return lax.ppermute(block, axis, route)


def body(queries, key_vectors, value_vectors, tile_lists, live_slots):
    heads = lax.axis_size("head")
    frame = lax.axis_index("frame")
    head = lax.axis_index("head")
    shard_tiles = tile_lists.shape[1]
    assert shard_tiles * PLANE == REACH and lax.axis_size("frame") % PLANE == 0

    def from_head(block, step):
        return moved(block, "head", lambda i: (i - step) % heads)

    def core_swap(block):
        return moved(block, "frame", lambda i: i ^ 1)

    own = as_tiles((key_vectors, value_vectors), (False, True))
    size = own.shape[0]
    cut = size * 9 // 16
    across = moved(own, "frame", lambda i: i ^ 2)
    chip = jnp.concatenate((core_swap(own), own))
    level = moved(chip, "frame", lambda i: i - PLANE if i % 2 == 0 else i + PLANE)

    listed, live, _ = lax.optimization_barrier((tile_lists[0], live_slots[0], chip))
    lists = work_lists(frame, head, listed, live, heads)
    q_own = as_tiles((queries,), (True,))
    blocks = [
        from_head(jnp.concatenate((q_own.reshape(-1, TILE), packed(lists[step]))), step)
        for step in range(1, heads)
    ]
    blocks, _ = lax.optimization_barrier((blocks, level))
    q_parts, by_head = [], [lists[:1]]
    for block in blocks:
        q_rows = shard_tiles * TILE
        q_parts.append(block[:q_rows].reshape(q_own.shape))
        by_head.append(unpacked(block[q_rows:], lists.shape[1])[None])
    q_rest, by_head = jnp.concatenate(q_parts), jnp.concatenate(by_head)

    far_z = moved(across[:cut], "frame", lambda i: i - PLANE if i % PLANE < 2 else i + PLANE)
    straight = moved(own[cut:], "frame", lambda i: i - 2 if i % PLANE < 2 else i + 2)
    near = [chip, across, core_swap(across), level, core_swap(level[:size])]
    state = attend(by_head, (0, 2), 0, q_rest, None, near, False)
    far_z, straight, state = lax.optimization_barrier((far_z, straight, state))
    far = jnp.concatenate((far_z, straight))
    far = [far, core_swap(far)]
    rest = attend(by_head, (4,), 0, q_rest, state, far, True)
    parts = [None]
    for step in range(1, heads):
        cut = slice((step - 1) * shard_tiles, step * shard_tiles)
        parts.append([from_head(array[cut], -step) for array in rest])
    q_own, _ = lax.optimization_barrier((q_own, rest))
    parts[0] = attend(by_head, (1, 3, 5), 7 * size, q_own, None, near + far, True)
    return merge(parts, queries.shape[0], heads)


def solution(mesh):
    placed = (
        P(("frame", "head"), None),
        P(("frame", "head"), None),
        P(("frame", "head"), None),
        P("head", "frame", None),
        P("head", "frame"),
    )
    return jax.shard_map(
        body, mesh=mesh, in_specs=placed, out_specs=P(("frame", "head"), None), check_vma=False
    )
```

```python
import functools
import math

import jax
import jax.numpy as jnp
import numpy as np
from jax import lax
from jax.experimental import pallas as pl
from jax.experimental.pallas import tpu as pltpu
from jax.sharding import PartitionSpec as P

TILE = 128
HEAD_DIM = 128
REACH = 32
PLANE = 4
GROUP = 4
LISTS = 4
FAR_OFF = 1e30
FACTOR = math.log2(math.e) / math.sqrt(HEAD_DIM)
VMEM = pl.BlockSpec(memory_space=pltpu.VMEM)
SMEM = pl.BlockSpec(memory_space=pltpu.SMEM)


def shard_table():
    table = np.zeros((PLANE, 2 * PLANE + 1), np.int32)
    for place in range(PLANE):
        x, core = divmod(place, 2)
        for distance in range(-PLANE, PLANE + 1):
            plane, there = divmod(place + distance, PLANE)
            same_x, same_core = there // 2 == x, there % 2 == core
            phase = 0
            if plane == 0:
                spot = int(same_core) if same_x else (4 if same_core else 5)
            elif not same_x:
                phase, spot = 1, 0 if same_core else 1
            elif (plane < 0) == (core == 0):
                spot = 2 + int(same_core)
            else:
                spot = 6
            table[place, distance + PLANE] = phase + 4 * spot
    return table.reshape(-1)


def params(mib):
    return pltpu.CompilerParams(vmem_limit_bytes=mib * 2**20)


def cost():
    return pl.CostEstimate(flops=0, bytes_accessed=0, transcendentals=0)


def tile_kernel(heads, flip, *refs):
    out_ref = refs[-1]
    tiles = refs[0].shape[0] // TILE
    for head in range(heads):
        for which, flipped in enumerate(flip):
            for tile in range(tiles):
                block = refs[which][
                    tile * TILE : (tile + 1) * TILE, head * HEAD_DIM : (head + 1) * HEAD_DIM
                ]
                at = (tile * heads + head) * len(flip) + which
                out_ref[at] = block.T if flipped else block


def as_tiles(arrays, flip):
    rows, width = arrays[0].shape
    heads = width // HEAD_DIM
    count = len(arrays) * heads * rows // TILE
    return pl.pallas_call(
        functools.partial(tile_kernel, heads, flip),
        in_specs=[VMEM] * len(arrays),
        out_specs=VMEM,
        out_shape=jax.ShapeDtypeStruct((count, TILE, HEAD_DIM), arrays[0].dtype),
        compiler_params=params(4),
    )(*arrays)


def list_kernel(length, codes_ref, live_ref, ends, metas, places):
    tiles = live_ref.shape[0]
    lists = ends.shape[0]
    for target in range(lists):
        ends[target] = target * length
    for row in range(tiles):

        def slot_step(slot, carry, row=row):
            code = codes_ref[row, slot]
            target = (code >> 8) & 255
            at = ends[target]
            places[at] = code & 255
            metas[at >> 2] = (code >> 16) + (at & (GROUP - 1))
            ends[target] = at + 1
            return carry

        lax.fori_loop(0, live_ref[row], slot_step, 0)
        for target in range(lists):
            at = ends[target]
            up = (at + GROUP - 1) & -GROUP
            filler = places[jnp.maximum(at - 1, 0)]
            for other in range(GROUP - 1):
                places[jnp.where(at + other < up, at + other, lists * length)] = filler
            ends[target] = up
    for target in range(lists):
        ends[target] = (ends[target] - target * length) >> 2


def work_lists(frame, head, tile_lists, live_slots, heads):
    tiles, slots = tile_lists.shape
    part_tiles = tiles // heads
    assert tiles & (tiles - 1) == 0 and heads & (heads - 1) == 0 and GROUP == 4
    within = tile_lists & (tiles - 1)
    rank = within >> int(math.log2(part_tiles))
    spot = ((within & (part_tiles - 1)) * heads + head) * 2
    table = shard_table()
    key = lax.rem(frame, PLANE) * (2 * PLANE + 1) + PLANE - frame
    key = (tile_lists >> int(math.log2(tiles))) + key
    hit = key[..., None] == jnp.arange(table.size, dtype=jnp.int32)
    entry = jnp.sum(jnp.where(hit, jnp.asarray(table), 0), axis=-1, dtype=jnp.int32)
    row = jnp.arange(tiles, dtype=jnp.int32)[:, None]
    turn = (rank - (row >> int(math.log2(part_tiles)))) & (heads - 1)
    query = (turn * part_tiles + (row & (part_tiles - 1))) * heads + head
    query = jnp.where(turn == 0, query, query - heads * part_tiles)
    step = (rank - head) & (heads - 1)
    target = step * LISTS + 2 * (entry & 3) + jnp.where(turn == 0, 1, 0)
    place = (entry >> 2) * (2 * tiles) + spot
    codes = place + target * 256 + query * (8 * 65536)
    length = max(part_tiles, tiles - part_tiles) * -(-slots // GROUP) * GROUP
    total = LISTS * heads * length
    ends, metas, places = pl.pallas_call(
        functools.partial(list_kernel, length),
        in_specs=[SMEM] * 2,
        out_specs=[SMEM] * 3,
        out_shape=[
            jax.ShapeDtypeStruct((LISTS * heads,), jnp.int32),
            jax.ShapeDtypeStruct((total // GROUP,), jnp.int32),
            jax.ShapeDtypeStruct((total + 1,), jnp.int32),
        ],
        compiler_params=params(4),
        cost_estimate=cost(),
    )(codes, live_slots)
    arrays = ends, metas, places[:total]
    return jnp.concatenate([array.reshape(heads, -1) for array in arrays], axis=1)


def packed(numbers):
    rows = -(-numbers.shape[0] // TILE)
    numbers = jnp.pad(numbers, (0, rows * TILE - numbers.shape[0])).reshape(rows, TILE)
    digits = jnp.concatenate((numbers & 255, numbers >> 8)).astype(jnp.bfloat16)
    return jnp.pad(digits, ((0, -2 * rows % 16), (0, 0)))


def unpacked(block, count):
    rows = -(-count // TILE)
    digits = block.astype(jnp.int32)
    return (digits[:rows] + digits[rows : 2 * rows] * 256).reshape(-1)[:count]


def phase_kernel(whiches, shifted, pieces, begins, ends, lists, q_ref, *refs):
    refs = list(refs)
    state = [refs.pop(0) for _ in range(0 if begins else 3)]
    parts = [refs.pop(0) for _ in range(pieces)]
    out_ref, stats_ref = [refs.pop(0) for _ in range(2)] if ends else [None] * 2
    top_ref, total_ref, sum_ref, window = refs[:4]
    scores, high, weights, shrinks = [None] * 4 if ends else refs[4:]
    tiles = q_ref.shape[0]
    heads, width = lists.shape
    length = (width - LISTS) // (LISTS * (GROUP + 1))

    at = 0
    for part in parts:
        window[at : at + part.shape[0]] = part[...]
        at += part.shape[0]
    if begins:
        top_ref[...] = jnp.full(top_ref.shape, -FAR_OFF, jnp.float32)
        total_ref[...] = jnp.zeros(total_ref.shape, jnp.float32)
        sum_ref[...] = jnp.zeros(sum_ref.shape, jnp.float32)
    else:
        for ref, old in zip((top_ref, total_ref, sum_ref), state):
            ref[...] = old[...]

    blocks = [(which, head) for which in whiches for head in range(heads)]
    starts = [jnp.int32(0)]
    for which, head in blocks:
        starts.append(starts[-1] + lists[head, which])

    def item_of(item):
        row, which, index = jnp.int32(0), jnp.int32(whiches[0]), item
        for number in range(1, len(blocks)):
            later = item >= starts[number]
            which = jnp.where(later, blocks[number][0], which)
            row = jnp.where(later, blocks[number][1], row)
            index = jnp.where(later, item - starts[number], index)
        real = item < starts[-1]
        index = jnp.where(real, index, 0)
        meta = lists[row, LISTS + which * length + index]
        at = LISTS * (1 + length) + (which * length + index) * GROUP
        tile = jnp.where(real, meta >> 3, 0)
        shift = jnp.where(which > 1, shifted, 0)
        spots = [jnp.where(real, lists[row, at + slot] + shift, 0) for slot in range(GROUP)]
        return tile, jnp.where(real, meta & 7, -1), spots

    def score(entry):
        tile, _, spots = entry
        keys = jnp.concatenate([window[spot] for spot in spots])
        block = jnp.dot(keys, q_ref[tile], preferred_element_type=jnp.float32)
        top = jnp.max(block.reshape(-1, 8, TILE), axis=0)
        return block, jnp.max(top, axis=0, keepdims=True)

    def weigh(entry, block, peak):
        tile, last, _ = entry
        old = top_ref[tile]
        top = jnp.maximum(old, jnp.where(last < 0, -FAR_OFF, peak))
        shrink = jnp.exp2((old - top) * FACTOR)
        total = total_ref[tile] * shrink
        parts = []
        for slot in range(GROUP):
            shift = jnp.where(slot <= last, top, FAR_OFF)
            weight = jnp.exp2((block[slot * TILE : (slot + 1) * TILE] - shift) * FACTOR)
            total = total + jnp.sum(weight.reshape(-1, 8, TILE), axis=0)
            parts.append(weight.astype(jnp.bfloat16))
        top_ref[tile] = top
        total_ref[tile] = total
        return jnp.concatenate(parts), shrink

    def collect(entry, weight, shrink):
        tile, _, spots = entry
        values = jnp.concatenate([window[spot + 1] for spot in spots], axis=1)
        product = jnp.dot(values, weight, preferred_element_type=jnp.float32)
        sum_ref[tile] = sum_ref[tile] * shrink + product

    if ends:

        def whole_step(four, carry):
            entries = [item_of(4 * four + number) for number in range(4)]
            made = [score(entry) for entry in entries]
            formed = [weigh(entry, *item) for entry, item in zip(entries, made)]
            for entry, item in zip(entries, formed):
                collect(entry, *item)
            return carry

        lax.fori_loop(0, (starts[-1] + 3) >> 2, whole_step, 0)
    else:

        def store_scores(pair):
            for number, (block, peak) in enumerate(pair):
                scores[number], high[number] = block, peak

        def store_weights(pair):
            for number, (weight, shrink) in enumerate(pair):
                weights[number], shrinks[number] = weight, shrink

        ahead = [item_of(0), item_of(1)]
        second = [item_of(2), item_of(3)]
        first = [score(entry) for entry in ahead]
        store_scores([score(entry) for entry in second])
        store_weights([weigh(entry, *made) for entry, made in zip(ahead, first)])

        def step(pair, entries):
            collected, weighed = entries[:2], entries[2:]
            scored = [item_of(2 * pair + 4), item_of(2 * pair + 5)]
            made = [(scores[number], high[number]) for number in range(2)]
            formed = [(weights[number], shrinks[number]) for number in range(2)]
            blocks = [score(entry) for entry in scored]
            following = [weigh(entry, *item) for entry, item in zip(weighed, made)]
            for entry, item in zip(collected, formed):
                collect(entry, *item)
            store_scores(blocks)
            store_weights(following)
            return tuple(weighed) + tuple(scored)

        lax.fori_loop(0, (starts[-1] + 1) >> 1, step, tuple(ahead + second))

    if ends:
        for tile in range(tiles):
            total = jnp.sum(total_ref[tile], axis=0, keepdims=True)
            share = jnp.where(total > 0, 1.0 / jnp.where(total > 0, total, 1.0), 0.0)
            out_ref[tile] = (sum_ref[tile] * share).astype(out_ref.dtype)
            stats_ref[tile, 0:1] = total
            stats_ref[tile, 1:2] = top_ref[tile]


def attend(lists, whiches, shifted, queries, state, pieces, ends):
    tiles = queries.shape[0]
    begins = state is None
    held = [
        jax.ShapeDtypeStruct((tiles, 1, TILE), jnp.float32),
        jax.ShapeDtypeStruct((tiles, 8, TILE), jnp.float32),
        jax.ShapeDtypeStruct((tiles, HEAD_DIM, TILE), jnp.float32),
    ]
    rows = sum(piece.shape[0] for piece in pieces)
    scratch = [pltpu.VMEM((rows, TILE, TILE), queries.dtype)]
    if not ends:
        scratch += [
            pltpu.VMEM((2, GROUP * TILE, TILE), jnp.float32),
            pltpu.VMEM((2, 1, TILE), jnp.float32),
            pltpu.VMEM((2, GROUP * TILE, TILE), queries.dtype),
            pltpu.VMEM((2, 1, TILE), jnp.float32),
        ]
    if ends:
        scratch = [pltpu.VMEM(array.shape, array.dtype) for array in held] + scratch
        held = [
            jax.ShapeDtypeStruct((tiles, HEAD_DIM, TILE), queries.dtype),
            jax.ShapeDtypeStruct((tiles, 2, TILE), jnp.float32),
        ]
    return pl.pallas_call(
        functools.partial(phase_kernel, whiches, shifted, len(pieces), begins, ends),
        in_specs=[SMEM] + [VMEM] * (1 + len(pieces) + (0 if begins else 3)),
        out_specs=[VMEM] * len(held),
        out_shape=held,
        scratch_shapes=scratch,
        compiler_params=params(10),
        cost_estimate=cost(),
    )(lists, queries, *([] if begins else state), *pieces)


def merge_kernel(count, *refs):
    out_ref = refs[-1]
    values, stats = [refs[first : 2 * count : 2] for first in range(2)]
    tiles = values[0].shape[0]
    heads = out_ref.shape[1] // HEAD_DIM
    for tile in range(tiles):
        top = stats[0][tile, 1:2]
        for ref in stats[1:]:
            top = jnp.maximum(top, ref[tile, 1:2])
        shares = [ref[tile, 0:1] * jnp.exp2((ref[tile, 1:2] - top) * FACTOR) for ref in stats]
        whole = sum(shares[1:], shares[0])
        out = jnp.zeros((HEAD_DIM, TILE), jnp.float32)
        for value, share in zip(values, shares):
            out = out + value[tile].astype(jnp.float32) * (share / whole)
        inner, head = divmod(tile, heads)
        out_ref[
            inner * TILE : (inner + 1) * TILE, head * HEAD_DIM : (head + 1) * HEAD_DIM
        ] = out.T.astype(out_ref.dtype)


def merge(parts, rows, heads):
    flat = [array for part in parts for array in part]
    return pl.pallas_call(
        functools.partial(merge_kernel, len(parts)),
        in_specs=[VMEM] * len(flat),
        out_specs=VMEM,
        out_shape=jax.ShapeDtypeStruct((rows, heads * HEAD_DIM), flat[0].dtype),
        compiler_params=params(6),
    )(*flat)


def moved(block, axis, source):
    size = lax.axis_size(axis)
    route = [(source(i), i) for i in range(size) if 0 <= source(i) < size]
    return lax.ppermute(block, axis, route)


def body(queries, key_vectors, value_vectors, tile_lists, live_slots):
    heads = lax.axis_size("head")
    frame = lax.axis_index("frame")
    head = lax.axis_index("head")
    shard_tiles = tile_lists.shape[1]
    assert shard_tiles * PLANE == REACH and lax.axis_size("frame") % PLANE == 0

    def from_head(block, step):
        return moved(block, "head", lambda i: (i - step) % heads)

    def core_swap(block):
        return moved(block, "frame", lambda i: i ^ 1)

    own = as_tiles((key_vectors, value_vectors), (False, True))
    size = own.shape[0]
    cut = size * 9 // 16
    across = moved(own, "frame", lambda i: i ^ 2)
    chip = jnp.concatenate((core_swap(own), own))
    level = moved(chip, "frame", lambda i: i - PLANE if i % 2 == 0 else i + PLANE)

    listed, live, _ = lax.optimization_barrier((tile_lists[0], live_slots[0], chip))
    lists = work_lists(frame, head, listed, live, heads)
    q_own = as_tiles((queries,), (True,))
    blocks = [
        from_head(jnp.concatenate((q_own.reshape(-1, TILE), packed(lists[step]))), step)
        for step in range(1, heads)
    ]
    blocks, _ = lax.optimization_barrier((blocks, level))
    q_parts, by_head = [], [lists[:1]]
    for block in blocks:
        q_rows = shard_tiles * TILE
        q_parts.append(block[:q_rows].reshape(q_own.shape))
        by_head.append(unpacked(block[q_rows:], lists.shape[1])[None])
    q_rest, by_head = jnp.concatenate(q_parts), jnp.concatenate(by_head)

    far_z = moved(across[:cut], "frame", lambda i: i - PLANE if i % PLANE < 2 else i + PLANE)
    straight = moved(own[cut:], "frame", lambda i: i - 2 if i % PLANE < 2 else i + 2)
    near = [chip, level, across, core_swap(across), core_swap(level[:size])]
    state = attend(by_head, (0,), 0, q_rest, None, near, False)
    far_z, straight, state = lax.optimization_barrier((far_z, straight, state))
    far = jnp.concatenate((far_z, straight))
    far = [far, core_swap(far)]
    rest = attend(by_head, (2,), 0, q_rest, state, far, True)
    parts = [None]
    for step in range(1, heads):
        cut = slice((step - 1) * shard_tiles, step * shard_tiles)
        parts.append([from_head(array[cut], -step) for array in rest])
    q_own, _ = lax.optimization_barrier((q_own, rest))
    parts[0] = attend(by_head, (1, 3), 7 * size, q_own, None, near + far, True)
    return merge(parts, queries.shape[0], heads)


def solution(mesh):
    placed = (
        P(("frame", "head"), None),
        P(("frame", "head"), None),
        P(("frame", "head"), None),
        P("head", "frame", None),
        P("head", "frame"),
    )
    return jax.shard_map(
        body, mesh=mesh, in_specs=placed, out_specs=P(("frame", "head"), None), check_vma=False
    )
```

```python
import functools
import math

import jax
import jax.numpy as jnp
import numpy as np
from jax import lax
from jax.experimental import pallas as pl
from jax.experimental.pallas import tpu as pltpu
from jax.sharding import PartitionSpec as P

TILE = 128
HEAD_DIM = 128
REACH = 32
PLANE = 4
GROUP = 4
LISTS = 4
FAR_OFF = 1e30
FACTOR = math.log2(math.e) / math.sqrt(HEAD_DIM)
VMEM = pl.BlockSpec(memory_space=pltpu.VMEM)
SMEM = pl.BlockSpec(memory_space=pltpu.SMEM)


def shard_table():
    table = np.zeros((PLANE, 2 * PLANE + 1), np.int32)
    for place in range(PLANE):
        x, core = divmod(place, 2)
        for distance in range(-PLANE, PLANE + 1):
            plane, there = divmod(place + distance, PLANE)
            same_x, same_core = there // 2 == x, there % 2 == core
            phase = 0
            if plane == 0:
                spot = int(same_core) if same_x else (4 if same_core else 5)
            elif not same_x:
                phase, spot = 1, 0 if same_core else 1
            elif (plane < 0) == (core == 0):
                spot = 2 + int(same_core)
            else:
                spot = 6
            table[place, distance + PLANE] = phase + 4 * spot
    return table.reshape(-1)


def params(mib):
    return pltpu.CompilerParams(vmem_limit_bytes=mib * 2**20)


def cost():
    return pl.CostEstimate(flops=0, bytes_accessed=0, transcendentals=0)


def tile_kernel(heads, flip, *refs):
    out_ref = refs[-1]
    tiles = refs[0].shape[0] // TILE
    for head in range(heads):
        for which, flipped in enumerate(flip):
            for tile in range(tiles):
                block = refs[which][
                    tile * TILE : (tile + 1) * TILE, head * HEAD_DIM : (head + 1) * HEAD_DIM
                ]
                at = (tile * heads + head) * len(flip) + which
                out_ref[at] = block.T if flipped else block


def as_tiles(arrays, flip):
    rows, width = arrays[0].shape
    heads = width // HEAD_DIM
    count = len(arrays) * heads * rows // TILE
    return pl.pallas_call(
        functools.partial(tile_kernel, heads, flip),
        in_specs=[VMEM] * len(arrays),
        out_specs=VMEM,
        out_shape=jax.ShapeDtypeStruct((count, TILE, HEAD_DIM), arrays[0].dtype),
        compiler_params=params(4),
    )(*arrays)


def list_kernel(length, codes_ref, live_ref, ends, metas, places):
    tiles = live_ref.shape[0]
    lists = ends.shape[0]
    for target in range(lists):
        ends[target] = target * length
    for row in range(tiles):

        def slot_step(slot, carry, row=row):
            code = codes_ref[row, slot]
            target = (code >> 8) & 255
            at = ends[target]
            places[at] = code & 255
            metas[at >> 2] = (code >> 16) + (at & (GROUP - 1))
            ends[target] = at + 1
            return carry

        lax.fori_loop(0, live_ref[row], slot_step, 0)
        for target in range(lists):
            at = ends[target]
            up = (at + GROUP - 1) & -GROUP
            filler = places[jnp.maximum(at - 1, 0)]
            for other in range(GROUP - 1):
                places[jnp.where(at + other < up, at + other, lists * length)] = filler
            ends[target] = up
    for target in range(lists):
        ends[target] = (ends[target] - target * length) >> 2


def work_lists(frame, head, tile_lists, live_slots, heads):
    tiles, slots = tile_lists.shape
    part_tiles = tiles // heads
    assert tiles & (tiles - 1) == 0 and heads & (heads - 1) == 0 and GROUP == 4
    within = tile_lists & (tiles - 1)
    rank = within >> int(math.log2(part_tiles))
    spot = ((within & (part_tiles - 1)) * heads + head) * 2
    table = shard_table()
    key = lax.rem(frame, PLANE) * (2 * PLANE + 1) + PLANE - frame
    key = (tile_lists >> int(math.log2(tiles))) + key
    hit = key[..., None] == jnp.arange(table.size, dtype=jnp.int32)
    entry = jnp.sum(jnp.where(hit, jnp.asarray(table), 0), axis=-1, dtype=jnp.int32)
    row = jnp.arange(tiles, dtype=jnp.int32)[:, None]
    turn = (rank - (row >> int(math.log2(part_tiles)))) & (heads - 1)
    query = (turn * part_tiles + (row & (part_tiles - 1))) * heads + head
    query = jnp.where(turn == 0, query, query - heads * part_tiles)
    step = (rank - head) & (heads - 1)
    target = step * LISTS + 2 * (entry & 3) + jnp.where(turn == 0, 1, 0)
    place = (entry >> 2) * (2 * tiles) + spot
    codes = place + target * 256 + query * (8 * 65536)
    length = max(part_tiles, tiles - part_tiles) * -(-slots // GROUP) * GROUP
    total = LISTS * heads * length
    ends, metas, places = pl.pallas_call(
        functools.partial(list_kernel, length),
        in_specs=[SMEM] * 2,
        out_specs=[SMEM] * 3,
        out_shape=[
            jax.ShapeDtypeStruct((LISTS * heads,), jnp.int32),
            jax.ShapeDtypeStruct((total // GROUP,), jnp.int32),
            jax.ShapeDtypeStruct((total + 1,), jnp.int32),
        ],
        compiler_params=params(4),
        cost_estimate=cost(),
    )(codes, live_slots)
    arrays = ends, metas, places[:total]
    return jnp.concatenate([array.reshape(heads, -1) for array in arrays], axis=1)


def packed(numbers):
    rows = -(-numbers.shape[0] // TILE)
    numbers = jnp.pad(numbers, (0, rows * TILE - numbers.shape[0])).reshape(rows, TILE)
    digits = jnp.concatenate((numbers & 255, numbers >> 8)).astype(jnp.bfloat16)
    return jnp.pad(digits, ((0, -2 * rows % 16), (0, 0)))


def unpacked(block, count):
    rows = -(-count // TILE)
    digits = block.astype(jnp.int32)
    return (digits[:rows] + digits[rows : 2 * rows] * 256).reshape(-1)[:count]


def phase_kernel(whiches, shifted, pieces, begins, ends, lists, q_ref, *refs):
    refs = list(refs)
    state = [refs.pop(0) for _ in range(0 if begins else 3)]
    parts = [refs.pop(0) for _ in range(pieces)]
    out_ref, stats_ref = [refs.pop(0) for _ in range(2)] if ends else [None] * 2
    top_ref, total_ref, sum_ref, window = refs[:4]
    scores, high, weights, shrinks = [None] * 4 if ends else refs[4:]
    tiles = q_ref.shape[0]
    heads, width = lists.shape
    length = (width - LISTS) // (LISTS * (GROUP + 1))

    at = 0
    for part in parts:
        window[at : at + part.shape[0]] = part[...]
        at += part.shape[0]
    if begins:
        top_ref[...] = jnp.full(top_ref.shape, -FAR_OFF, jnp.float32)
        total_ref[...] = jnp.zeros(total_ref.shape, jnp.float32)
        sum_ref[...] = jnp.zeros(sum_ref.shape, jnp.float32)
    else:
        for ref, old in zip((top_ref, total_ref, sum_ref), state):
            ref[...] = old[...]

    blocks = [(which, head) for which in whiches for head in range(heads)]
    starts = [jnp.int32(0)]
    for which, head in blocks:
        starts.append(starts[-1] + lists[head, which])

    def item_of(item):
        row, which, index = jnp.int32(0), jnp.int32(whiches[0]), item
        for number in range(1, len(blocks)):
            later = item >= starts[number]
            which = jnp.where(later, blocks[number][0], which)
            row = jnp.where(later, blocks[number][1], row)
            index = jnp.where(later, item - starts[number], index)
        real = item < starts[-1]
        index = jnp.where(real, index, 0)
        meta = lists[row, LISTS + which * length + index]
        at = LISTS * (1 + length) + (which * length + index) * GROUP
        tile = jnp.where(real, meta >> 3, 0)
        shift = jnp.where(which > 1, shifted, 0)
        spots = [jnp.where(real, lists[row, at + slot] + shift, 0) for slot in range(GROUP)]
        return tile, jnp.where(real, meta & 7, -1), spots

    def score(entry):
        tile, _, spots = entry
        keys = jnp.concatenate([window[spot] for spot in spots])
        block = jnp.dot(keys, q_ref[tile], preferred_element_type=jnp.float32)
        top = jnp.max(block.reshape(-1, 8, TILE), axis=0)
        return block, jnp.max(top, axis=0, keepdims=True)

    def weigh(entry, block, peak):
        tile, last, _ = entry
        old = top_ref[tile]
        top = jnp.maximum(old, jnp.where(last < 0, -FAR_OFF, peak))
        shrink = jnp.exp2((old - top) * FACTOR)
        total = total_ref[tile] * shrink
        parts = []
        for slot in range(GROUP):
            shift = jnp.where(slot <= last, top, FAR_OFF)
            weight = jnp.exp2((block[slot * TILE : (slot + 1) * TILE] - shift) * FACTOR)
            total = total + jnp.sum(weight.reshape(-1, 8, TILE), axis=0)
            parts.append(weight.astype(jnp.bfloat16))
        top_ref[tile] = top
        total_ref[tile] = total
        return jnp.concatenate(parts), shrink

    def collect(entry, weight, shrink):
        tile, _, spots = entry
        values = jnp.concatenate([window[spot + 1] for spot in spots], axis=1)
        product = jnp.dot(values, weight, preferred_element_type=jnp.float32)
        sum_ref[tile] = sum_ref[tile] * shrink + product

    if ends:

        def whole_step(four, carry):
            entries = [item_of(4 * four + number) for number in range(4)]
            made = [score(entry) for entry in entries]
            formed = [weigh(entry, *item) for entry, item in zip(entries, made)]
            for entry, item in zip(entries, formed):
                collect(entry, *item)
            return carry

        lax.fori_loop(0, (starts[-1] + 3) >> 2, whole_step, 0)
    else:

        def store_scores(pair):
            for number, (block, peak) in enumerate(pair):
                scores[number], high[number] = block, peak

        def store_weights(pair):
            for number, (weight, shrink) in enumerate(pair):
                weights[number], shrinks[number] = weight, shrink

        ahead = [item_of(0), item_of(1)]
        second = [item_of(2), item_of(3)]
        first = [score(entry) for entry in ahead]
        store_scores([score(entry) for entry in second])
        store_weights([weigh(entry, *made) for entry, made in zip(ahead, first)])

        def step(pair, entries):
            collected, weighed = entries[:2], entries[2:]
            scored = [item_of(2 * pair + 4), item_of(2 * pair + 5)]
            made = [(scores[number], high[number]) for number in range(2)]
            formed = [(weights[number], shrinks[number]) for number in range(2)]
            blocks = [score(entry) for entry in scored]
            following = [weigh(entry, *item) for entry, item in zip(weighed, made)]
            for entry, item in zip(collected, formed):
                collect(entry, *item)
            store_scores(blocks)
            store_weights(following)
            return tuple(weighed) + tuple(scored)

        lax.fori_loop(0, (starts[-1] + 1) >> 1, step, tuple(ahead + second))

    if ends:
        for tile in range(tiles):
            total = jnp.sum(total_ref[tile], axis=0, keepdims=True)
            share = jnp.where(total > 0, 1.0 / jnp.where(total > 0, total, 1.0), 0.0)
            out_ref[tile] = (sum_ref[tile] * share).astype(out_ref.dtype)
            stats_ref[tile, 0:1] = total
            stats_ref[tile, 1:2] = top_ref[tile]


def attend(lists, whiches, shifted, queries, state, pieces, ends):
    tiles = queries.shape[0]
    begins = state is None
    held = [
        jax.ShapeDtypeStruct((tiles, 1, TILE), jnp.float32),
        jax.ShapeDtypeStruct((tiles, 8, TILE), jnp.float32),
        jax.ShapeDtypeStruct((tiles, HEAD_DIM, TILE), jnp.float32),
    ]
    rows = sum(piece.shape[0] for piece in pieces)
    scratch = [pltpu.VMEM((rows, TILE, TILE), queries.dtype)]
    if not ends:
        scratch += [
            pltpu.VMEM((2, GROUP * TILE, TILE), jnp.float32),
            pltpu.VMEM((2, 1, TILE), jnp.float32),
            pltpu.VMEM((2, GROUP * TILE, TILE), queries.dtype),
            pltpu.VMEM((2, 1, TILE), jnp.float32),
        ]
    if ends:
        scratch = [pltpu.VMEM(array.shape, array.dtype) for array in held] + scratch
        held = [
            jax.ShapeDtypeStruct((tiles, HEAD_DIM, TILE), queries.dtype),
            jax.ShapeDtypeStruct((tiles, 2, TILE), jnp.float32),
        ]
    return pl.pallas_call(
        functools.partial(phase_kernel, whiches, shifted, len(pieces), begins, ends),
        in_specs=[SMEM] + [VMEM] * (1 + len(pieces) + (0 if begins else 3)),
        out_specs=[VMEM] * len(held),
        out_shape=held,
        scratch_shapes=scratch,
        compiler_params=params(10),
        cost_estimate=cost(),
    )(lists, queries, *([] if begins else state), *pieces)


def merge_kernel(count, *refs):
    out_ref = refs[-1]
    values, stats = [refs[first : 2 * count : 2] for first in range(2)]
    tiles = values[0].shape[0]
    heads = out_ref.shape[1] // HEAD_DIM
    for tile in range(tiles):
        top = stats[0][tile, 1:2]
        for ref in stats[1:]:
            top = jnp.maximum(top, ref[tile, 1:2])
        shares = [ref[tile, 0:1] * jnp.exp2((ref[tile, 1:2] - top) * FACTOR) for ref in stats]
        whole = sum(shares[1:], shares[0])
        out = jnp.zeros((HEAD_DIM, TILE), jnp.float32)
        for value, share in zip(values, shares):
            out = out + value[tile].astype(jnp.float32) * (share / whole)
        inner, head = divmod(tile, heads)
        out_ref[
            inner * TILE : (inner + 1) * TILE, head * HEAD_DIM : (head + 1) * HEAD_DIM
        ] = out.T.astype(out_ref.dtype)


def merge(parts, rows, heads):
    flat = [array for part in parts for array in part]
    return pl.pallas_call(
        functools.partial(merge_kernel, len(parts)),
        in_specs=[VMEM] * len(flat),
        out_specs=VMEM,
        out_shape=jax.ShapeDtypeStruct((rows, heads * HEAD_DIM), flat[0].dtype),
        compiler_params=params(6),
    )(*flat)


def moved(block, axis, source):
    size = lax.axis_size(axis)
    route = [(source(i), i) for i in range(size) if 0 <= source(i) < size]
    return lax.ppermute(block, axis, route)


def body(queries, key_vectors, value_vectors, tile_lists, live_slots):
    heads = lax.axis_size("head")
    frame = lax.axis_index("frame")
    head = lax.axis_index("head")
    shard_tiles = tile_lists.shape[1]
    assert shard_tiles * PLANE == REACH and lax.axis_size("frame") % PLANE == 0

    def from_head(block, step):
        return moved(block, "head", lambda i: (i - step) % heads)

    def core_swap(block):
        return moved(block, "frame", lambda i: i ^ 1)

    own = as_tiles((key_vectors, value_vectors), (False, True))
    size = own.shape[0]
    cut = size * 5 // 8
    across = moved(own, "frame", lambda i: i ^ 2)
    chip = jnp.concatenate((core_swap(own), own))
    level = moved(chip, "frame", lambda i: i - PLANE if i % 2 == 0 else i + PLANE)

    listed, live, _ = lax.optimization_barrier((tile_lists[0], live_slots[0], chip))
    lists = work_lists(frame, head, listed, live, heads)
    q_own = as_tiles((queries,), (True,))
    blocks = [
        from_head(jnp.concatenate((q_own.reshape(-1, TILE), packed(lists[step]))), step)
        for step in range(1, heads)
    ]
    blocks, _ = lax.optimization_barrier((blocks, level))
    q_parts, by_head = [], [lists[:1]]
    for block in blocks:
        q_rows = shard_tiles * TILE
        q_parts.append(block[:q_rows].reshape(q_own.shape))
        by_head.append(unpacked(block[q_rows:], lists.shape[1])[None])
    q_rest, by_head = jnp.concatenate(q_parts), jnp.concatenate(by_head)

    far_z = moved(across[:cut], "frame", lambda i: i - PLANE if i % PLANE < 2 else i + PLANE)
    straight = moved(own[cut:], "frame", lambda i: i - 2 if i % PLANE < 2 else i + 2)
    near = [chip, level, across, core_swap(across), core_swap(level[:size])]
    state = attend(by_head, (0,), 0, q_rest, None, near, False)
    far_z, straight, state = lax.optimization_barrier((far_z, straight, state))
    far = jnp.concatenate((far_z, straight))
    far = [far, core_swap(far)]
    rest = attend(by_head, (2,), 0, q_rest, state, far, True)
    parts = [None]
    for step in range(1, heads):
        cut = slice((step - 1) * shard_tiles, step * shard_tiles)
        parts.append([from_head(array[cut], -step) for array in rest])
    q_own, _ = lax.optimization_barrier((q_own, rest))
    parts[0] = attend(by_head, (1, 3), 7 * size, q_own, None, near + far, True)
    return merge(parts, queries.shape[0], heads)


def solution(mesh):
    placed = (
        P(("frame", "head"), None),
        P(("frame", "head"), None),
        P(("frame", "head"), None),
        P("head", "frame", None),
        P("head", "frame"),
    )
    return jax.shard_map(
        body, mesh=mesh, in_specs=placed, out_specs=P(("frame", "head"), None), check_vma=False
    )
```

```python
import functools
import math

import jax
import jax.numpy as jnp
import numpy as np
from jax import lax
from jax.experimental import pallas as pl
from jax.experimental.pallas import tpu as pltpu
from jax.sharding import PartitionSpec as P

TILE = 128
HEAD_DIM = 128
REACH = 32
PLANE = 4
GROUP = 4
LISTS = 4
FAR_OFF = 1e30
FACTOR = math.log2(math.e) / math.sqrt(HEAD_DIM)
VMEM = pl.BlockSpec(memory_space=pltpu.VMEM)
SMEM = pl.BlockSpec(memory_space=pltpu.SMEM)


def shard_table():
    table = np.zeros((PLANE, 2 * PLANE + 1), np.int32)
    for place in range(PLANE):
        x, core = divmod(place, 2)
        for distance in range(-PLANE, PLANE + 1):
            plane, there = divmod(place + distance, PLANE)
            same_x, same_core = there // 2 == x, there % 2 == core
            phase = 0
            if plane == 0:
                spot = int(same_core) if same_x else (4 if same_core else 5)
            elif not same_x:
                phase, spot = 1, 0 if same_core else 1
            elif (plane < 0) == (core == 0):
                spot = 2 + int(same_core)
            else:
                spot = 6
            table[place, distance + PLANE] = phase + 4 * spot
    return table.reshape(-1)


def params(mib):
    return pltpu.CompilerParams(vmem_limit_bytes=mib * 2**20)


def cost():
    return pl.CostEstimate(flops=0, bytes_accessed=0, transcendentals=0)


def tile_kernel(heads, flip, *refs):
    out_ref = refs[-1]
    tiles = refs[0].shape[0] // TILE
    for head in range(heads):
        for which, flipped in enumerate(flip):
            for tile in range(tiles):
                block = refs[which][
                    tile * TILE : (tile + 1) * TILE, head * HEAD_DIM : (head + 1) * HEAD_DIM
                ]
                at = (tile * heads + head) * len(flip) + which
                out_ref[at] = block.T if flipped else block


def as_tiles(arrays, flip):
    rows, width = arrays[0].shape
    heads = width // HEAD_DIM
    count = len(arrays) * heads * rows // TILE
    return pl.pallas_call(
        functools.partial(tile_kernel, heads, flip),
        in_specs=[VMEM] * len(arrays),
        out_specs=VMEM,
        out_shape=jax.ShapeDtypeStruct((count, TILE, HEAD_DIM), arrays[0].dtype),
        compiler_params=params(4),
    )(*arrays)


def list_kernel(length, codes_ref, live_ref, ends, metas, places):
    tiles = live_ref.shape[0]
    lists = ends.shape[0]
    for target in range(lists):
        ends[target] = target * length
    for row in range(tiles):

        def slot_step(slot, carry, row=row):
            code = codes_ref[row, slot]
            target = (code >> 8) & 255
            at = ends[target]
            places[at] = code & 255
            metas[at >> 2] = (code >> 16) + (at & (GROUP - 1))
            ends[target] = at + 1
            return carry

        lax.fori_loop(0, live_ref[row], slot_step, 0)
        for target in range(lists):
            at = ends[target]
            up = (at + GROUP - 1) & -GROUP
            filler = places[jnp.maximum(at - 1, 0)]
            for other in range(GROUP - 1):
                places[jnp.where(at + other < up, at + other, lists * length)] = filler
            ends[target] = up
    for target in range(lists):
        ends[target] = (ends[target] - target * length) >> 2


def work_lists(frame, head, tile_lists, live_slots, heads):
    tiles, slots = tile_lists.shape
    part_tiles = tiles // heads
    assert tiles & (tiles - 1) == 0 and heads & (heads - 1) == 0 and GROUP == 4
    within = tile_lists & (tiles - 1)
    rank = within >> int(math.log2(part_tiles))
    spot = ((within & (part_tiles - 1)) * heads + head) * 2
    table = shard_table()
    key = lax.rem(frame, PLANE) * (2 * PLANE + 1) + PLANE - frame
    key = (tile_lists >> int(math.log2(tiles))) + key
    hit = key[..., None] == jnp.arange(table.size, dtype=jnp.int32)
    entry = jnp.sum(jnp.where(hit, jnp.asarray(table), 0), axis=-1, dtype=jnp.int32)
    row = jnp.arange(tiles, dtype=jnp.int32)[:, None]
    turn = (rank - (row >> int(math.log2(part_tiles)))) & (heads - 1)
    query = (turn * part_tiles + (row & (part_tiles - 1))) * heads + head
    query = jnp.where(turn == 0, query, query - heads * part_tiles)
    step = (rank - head) & (heads - 1)
    target = step * LISTS + 2 * (entry & 3) + jnp.where(turn == 0, 1, 0)
    place = (entry >> 2) * (2 * tiles) + spot
    codes = place + target * 256 + query * (8 * 65536)
    length = max(part_tiles, tiles - part_tiles) * -(-slots // GROUP) * GROUP
    total = LISTS * heads * length
    ends, metas, places = pl.pallas_call(
        functools.partial(list_kernel, length),
        in_specs=[SMEM] * 2,
        out_specs=[SMEM] * 3,
        out_shape=[
            jax.ShapeDtypeStruct((LISTS * heads,), jnp.int32),
            jax.ShapeDtypeStruct((total // GROUP,), jnp.int32),
            jax.ShapeDtypeStruct((total + 1,), jnp.int32),
        ],
        compiler_params=params(4),
        cost_estimate=cost(),
    )(codes, live_slots)
    arrays = ends, metas, places[:total]
    return jnp.concatenate([array.reshape(heads, -1) for array in arrays], axis=1)


def packed(numbers):
    rows = -(-numbers.shape[0] // TILE)
    numbers = jnp.pad(numbers, (0, rows * TILE - numbers.shape[0])).reshape(rows, TILE)
    digits = jnp.concatenate((numbers & 255, numbers >> 8)).astype(jnp.bfloat16)
    return jnp.pad(digits, ((0, -2 * rows % 16), (0, 0)))


def unpacked(block, count):
    rows = -(-count // TILE)
    digits = block.astype(jnp.int32)
    return (digits[:rows] + digits[rows : 2 * rows] * 256).reshape(-1)[:count]


def phase_kernel(whiches, shifted, pieces, begins, ends, lists, q_ref, *refs):
    refs = list(refs)
    state = [refs.pop(0) for _ in range(0 if begins else 3)]
    parts = [refs.pop(0) for _ in range(pieces)]
    out_ref, stats_ref = [refs.pop(0) for _ in range(2)] if ends else [None] * 2
    top_ref, total_ref, sum_ref, window = refs
    tiles = q_ref.shape[0]
    heads, width = lists.shape
    length = (width - LISTS) // (LISTS * (GROUP + 1))

    at = 0
    for part in parts:
        window[at : at + part.shape[0]] = part[...]
        at += part.shape[0]
    if begins:
        top_ref[...] = jnp.full(top_ref.shape, -FAR_OFF, jnp.float32)
        total_ref[...] = jnp.zeros(total_ref.shape, jnp.float32)
        sum_ref[...] = jnp.zeros(sum_ref.shape, jnp.float32)
    else:
        for ref, old in zip((top_ref, total_ref, sum_ref), state):
            ref[...] = old[...]

    blocks = [(which, head) for which in whiches for head in range(heads)]
    starts = [jnp.int32(0)]
    for which, head in blocks:
        starts.append(starts[-1] + lists[head, which])

    def item_of(item):
        row, which, index = jnp.int32(0), jnp.int32(whiches[0]), item
        for number in range(1, len(blocks)):
            later = item >= starts[number]
            which = jnp.where(later, blocks[number][0], which)
            row = jnp.where(later, blocks[number][1], row)
            index = jnp.where(later, item - starts[number], index)
        real = item < starts[-1]
        index = jnp.where(real, index, 0)
        meta = lists[row, LISTS + which * length + index]
        at = LISTS * (1 + length) + (which * length + index) * GROUP
        tile = jnp.where(real, meta >> 3, 0)
        shift = jnp.where(which > 1, shifted, 0)
        spots = [jnp.where(real, lists[row, at + slot] + shift, 0) for slot in range(GROUP)]
        return tile, jnp.where(real, meta & 7, -1), spots

    def score(entry):
        tile, _, spots = entry
        keys = jnp.concatenate([window[spot] for spot in spots])
        block = jnp.dot(keys, q_ref[tile], preferred_element_type=jnp.float32)
        top = jnp.max(block.reshape(-1, 8, TILE), axis=0)
        return block, jnp.max(top, axis=0, keepdims=True)

    def weigh(entry, block, peak):
        tile, last, _ = entry
        old = top_ref[tile]
        top = jnp.maximum(old, jnp.where(last < 0, -FAR_OFF, peak))
        shrink = jnp.exp2((old - top) * FACTOR)
        total = total_ref[tile] * shrink
        parts = []
        for slot in range(GROUP):
            shift = jnp.where(slot <= last, top, FAR_OFF)
            weight = jnp.exp2((block[slot * TILE : (slot + 1) * TILE] - shift) * FACTOR)
            total = total + jnp.sum(weight.reshape(-1, 8, TILE), axis=0)
            parts.append(weight.astype(jnp.bfloat16))
        top_ref[tile] = top
        total_ref[tile] = total
        return jnp.concatenate(parts), shrink

    def collect(entry, weight, shrink):
        tile, _, spots = entry
        values = jnp.concatenate([window[spot + 1] for spot in spots], axis=1)
        product = jnp.dot(values, weight, preferred_element_type=jnp.float32)
        sum_ref[tile] = sum_ref[tile] * shrink + product

    def step(four, carry):
        entries = [item_of(4 * four + number) for number in range(4)]
        made = [score(entry) for entry in entries]
        formed = [weigh(entry, *item) for entry, item in zip(entries, made)]
        for entry, item in zip(entries, formed):
            collect(entry, *item)
        return carry

    lax.fori_loop(0, (starts[-1] + 3) >> 2, step, 0)
    if ends:
        for tile in range(tiles):
            total = jnp.sum(total_ref[tile], axis=0, keepdims=True)
            share = jnp.where(total > 0, 1.0 / jnp.where(total > 0, total, 1.0), 0.0)
            out_ref[tile] = (sum_ref[tile] * share).astype(out_ref.dtype)
            stats_ref[tile, 0:1] = total
            stats_ref[tile, 1:2] = top_ref[tile]


def attend(lists, whiches, shifted, queries, state, pieces, ends):
    tiles = queries.shape[0]
    begins = state is None
    held = [
        jax.ShapeDtypeStruct((tiles, 1, TILE), jnp.float32),
        jax.ShapeDtypeStruct((tiles, 8, TILE), jnp.float32),
        jax.ShapeDtypeStruct((tiles, HEAD_DIM, TILE), jnp.float32),
    ]
    rows = sum(piece.shape[0] for piece in pieces)
    scratch = [pltpu.VMEM((rows, TILE, TILE), queries.dtype)]
    if ends:
        scratch = [pltpu.VMEM(array.shape, array.dtype) for array in held] + scratch
        held = [
            jax.ShapeDtypeStruct((tiles, HEAD_DIM, TILE), queries.dtype),
            jax.ShapeDtypeStruct((tiles, 2, TILE), jnp.float32),
        ]
    return pl.pallas_call(
        functools.partial(phase_kernel, whiches, shifted, len(pieces), begins, ends),
        in_specs=[SMEM] + [VMEM] * (1 + len(pieces) + (0 if begins else 3)),
        out_specs=[VMEM] * len(held),
        out_shape=held,
        scratch_shapes=scratch,
        compiler_params=params(10),
        cost_estimate=cost(),
    )(lists, queries, *([] if begins else state), *pieces)


def merge_kernel(count, *refs):
    out_ref = refs[-1]
    values, stats = [refs[first : 2 * count : 2] for first in range(2)]
    tiles = values[0].shape[0]
    heads = out_ref.shape[1] // HEAD_DIM
    for tile in range(tiles):
        top = stats[0][tile, 1:2]
        for ref in stats[1:]:
            top = jnp.maximum(top, ref[tile, 1:2])
        shares = [ref[tile, 0:1] * jnp.exp2((ref[tile, 1:2] - top) * FACTOR) for ref in stats]
        whole = sum(shares[1:], shares[0])
        out = jnp.zeros((HEAD_DIM, TILE), jnp.float32)
        for value, share in zip(values, shares):
            out = out + value[tile].astype(jnp.float32) * (share / whole)
        inner, head = divmod(tile, heads)
        out_ref[
            inner * TILE : (inner + 1) * TILE, head * HEAD_DIM : (head + 1) * HEAD_DIM
        ] = out.T.astype(out_ref.dtype)


def merge(parts, rows, heads):
    flat = [array for part in parts for array in part]
    return pl.pallas_call(
        functools.partial(merge_kernel, len(parts)),
        in_specs=[VMEM] * len(flat),
        out_specs=VMEM,
        out_shape=jax.ShapeDtypeStruct((rows, heads * HEAD_DIM), flat[0].dtype),
        compiler_params=params(6),
    )(*flat)


def moved(block, axis, source):
    size = lax.axis_size(axis)
    route = [(source(i), i) for i in range(size) if 0 <= source(i) < size]
    return lax.ppermute(block, axis, route)


def body(queries, key_vectors, value_vectors, tile_lists, live_slots):
    heads = lax.axis_size("head")
    frame = lax.axis_index("frame")
    head = lax.axis_index("head")
    shard_tiles = tile_lists.shape[1]
    assert shard_tiles * PLANE == REACH and lax.axis_size("frame") % PLANE == 0

    def from_head(block, step):
        return moved(block, "head", lambda i: (i - step) % heads)

    def core_swap(block):
        return moved(block, "frame", lambda i: i ^ 1)

    own = as_tiles((key_vectors, value_vectors), (False, True))
    size = own.shape[0]
    cut = size * 5 // 8
    across = moved(own, "frame", lambda i: i ^ 2)
    chip = jnp.concatenate((core_swap(own), own))
    level = moved(chip, "frame", lambda i: i - PLANE if i % 2 == 0 else i + PLANE)

    listed, live, _ = lax.optimization_barrier((tile_lists[0], live_slots[0], chip))
    lists = work_lists(frame, head, listed, live, heads)
    q_own = as_tiles((queries,), (True,))
    blocks = [
        from_head(jnp.concatenate((q_own.reshape(-1, TILE), packed(lists[step]))), step)
        for step in range(1, heads)
    ]
    blocks, _ = lax.optimization_barrier((blocks, level))
    q_parts, by_head = [], [lists[:1]]
    for block in blocks:
        q_rows = shard_tiles * TILE
        q_parts.append(block[:q_rows].reshape(q_own.shape))
        by_head.append(unpacked(block[q_rows:], lists.shape[1])[None])
    q_rest, by_head = jnp.concatenate(q_parts), jnp.concatenate(by_head)

    far_z = moved(across[:cut], "frame", lambda i: i - PLANE if i % PLANE < 2 else i + PLANE)
    straight = moved(own[cut:], "frame", lambda i: i - 2 if i % PLANE < 2 else i + 2)
    near = [chip, level, across, core_swap(across), core_swap(level[:size])]
    state = attend(by_head, (0,), 0, q_rest, None, near, False)
    far_z, straight, state = lax.optimization_barrier((far_z, straight, state))
    far = jnp.concatenate((far_z, straight))
    far = [far, core_swap(far)]
    rest = attend(by_head, (2,), 0, q_rest, state, far, True)
    parts = [None]
    for step in range(1, heads):
        cut = slice((step - 1) * shard_tiles, step * shard_tiles)
        parts.append([from_head(array[cut], -step) for array in rest])
    q_own, _ = lax.optimization_barrier((q_own, rest))
    parts[0] = attend(by_head, (1, 3), 7 * size, q_own, None, near + far, True)
    return merge(parts, queries.shape[0], heads)


def solution(mesh):
    placed = (
        P(("frame", "head"), None),
        P(("frame", "head"), None),
        P(("frame", "head"), None),
        P("head", "frame", None),
        P("head", "frame"),
    )
    return jax.shard_map(
        body, mesh=mesh, in_specs=placed, out_specs=P(("frame", "head"), None), check_vma=False
    )
```

```python
import functools
import math

import jax
import jax.numpy as jnp
import numpy as np
from jax import lax
from jax.experimental import pallas as pl
from jax.experimental.pallas import tpu as pltpu
from jax.sharding import PartitionSpec as P

TILE = 128
HEAD_DIM = 128
REACH = 32
PLANE = 4
GROUP = 4
LISTS = 4
FAR_OFF = 1e30
FACTOR = math.log2(math.e) / math.sqrt(HEAD_DIM)
VMEM = pl.BlockSpec(memory_space=pltpu.VMEM)
SMEM = pl.BlockSpec(memory_space=pltpu.SMEM)


def shard_table():
    table = np.zeros((PLANE, 2 * PLANE + 1), np.int32)
    for place in range(PLANE):
        x, core = divmod(place, 2)
        for distance in range(-PLANE, PLANE + 1):
            plane, there = divmod(place + distance, PLANE)
            same_x, same_core = there // 2 == x, there % 2 == core
            phase = 0
            if plane == 0:
                spot = int(same_core) if same_x else (4 if same_core else 5)
            elif not same_x:
                phase, spot = 1, 0 if same_core else 1
            elif (plane < 0) == (core == 0):
                spot = 2 + int(same_core)
            else:
                spot = 6
            table[place, distance + PLANE] = phase + 4 * spot
    return table.reshape(-1)


def params(mib):
    return pltpu.CompilerParams(vmem_limit_bytes=mib * 2**20)


def cost():
    return pl.CostEstimate(flops=0, bytes_accessed=0, transcendentals=0)


def tile_kernel(heads, flip, *refs):
    out_ref = refs[-1]
    tiles = refs[0].shape[0] // TILE
    for head in range(heads):
        for which, flipped in enumerate(flip):
            for tile in range(tiles):
                block = refs[which][
                    tile * TILE : (tile + 1) * TILE, head * HEAD_DIM : (head + 1) * HEAD_DIM
                ]
                at = (tile * heads + head) * len(flip) + which
                out_ref[at] = block.T if flipped else block


def as_tiles(arrays, flip):
    rows, width = arrays[0].shape
    heads = width // HEAD_DIM
    count = len(arrays) * heads * rows // TILE
    return pl.pallas_call(
        functools.partial(tile_kernel, heads, flip),
        in_specs=[VMEM] * len(arrays),
        out_specs=VMEM,
        out_shape=jax.ShapeDtypeStruct((count, TILE, HEAD_DIM), arrays[0].dtype),
        compiler_params=params(4),
    )(*arrays)


def list_kernel(length, codes_ref, live_ref, ends, metas, places):
    tiles = live_ref.shape[0]
    lists = ends.shape[0]
    for target in range(lists):
        ends[target] = target * length
    for row in range(tiles):

        def slot_step(slot, carry, row=row):
            code = codes_ref[row, slot]
            target = (code >> 8) & 255
            at = ends[target]
            places[at] = code & 255
            metas[at >> 2] = (code >> 16) + (at & (GROUP - 1))
            ends[target] = at + 1
            return carry

        lax.fori_loop(0, live_ref[row], slot_step, 0)
        for target in range(lists):
            at = ends[target]
            up = (at + GROUP - 1) & -GROUP
            filler = places[jnp.maximum(at - 1, 0)]
            for other in range(GROUP - 1):
                places[jnp.where(at + other < up, at + other, lists * length)] = filler
            ends[target] = up
    for target in range(lists):
        ends[target] = (ends[target] - target * length) >> 2


def work_lists(frame, head, tile_lists, live_slots, heads):
    tiles, slots = tile_lists.shape
    part_tiles = tiles // heads
    assert tiles & (tiles - 1) == 0 and heads & (heads - 1) == 0 and GROUP == 4
    within = tile_lists & (tiles - 1)
    rank = within >> int(math.log2(part_tiles))
    spot = ((within & (part_tiles - 1)) * heads + head) * 2
    table = shard_table()
    key = lax.rem(frame, PLANE) * (2 * PLANE + 1) + PLANE - frame
    key = (tile_lists >> int(math.log2(tiles))) + key
    hit = key[..., None] == jnp.arange(table.size, dtype=jnp.int32)
    entry = jnp.sum(jnp.where(hit, jnp.asarray(table), 0), axis=-1, dtype=jnp.int32)
    row = jnp.arange(tiles, dtype=jnp.int32)[:, None]
    turn = (rank - (row >> int(math.log2(part_tiles)))) & (heads - 1)
    query = (turn * part_tiles + (row & (part_tiles - 1))) * heads + head
    query = jnp.where(turn == 0, query, query - heads * part_tiles)
    step = (rank - head) & (heads - 1)
    target = step * LISTS + 2 * (entry & 3) + jnp.where(turn == 0, 1, 0)
    place = (entry >> 2) * (2 * tiles) + spot
    codes = place + target * 256 + query * (8 * 65536)
    length = max(part_tiles, tiles - part_tiles) * -(-slots // GROUP) * GROUP
    total = LISTS * heads * length
    ends, metas, places = pl.pallas_call(
        functools.partial(list_kernel, length),
        in_specs=[SMEM] * 2,
        out_specs=[SMEM] * 3,
        out_shape=[
            jax.ShapeDtypeStruct((LISTS * heads,), jnp.int32),
            jax.ShapeDtypeStruct((total // GROUP,), jnp.int32),
            jax.ShapeDtypeStruct((total + 1,), jnp.int32),
        ],
        compiler_params=params(4),
        cost_estimate=cost(),
    )(codes, live_slots)
    arrays = ends, metas, places[:total]
    return jnp.concatenate([array.reshape(heads, -1) for array in arrays], axis=1)


def packed(numbers):
    rows = -(-numbers.shape[0] // TILE)
    numbers = jnp.pad(numbers, (0, rows * TILE - numbers.shape[0])).reshape(rows, TILE)
    digits = jnp.concatenate((numbers & 255, numbers >> 8)).astype(jnp.bfloat16)
    return jnp.pad(digits, ((0, -2 * rows % 16), (0, 0)))


def unpacked(block, count):
    rows = -(-count // TILE)
    digits = block.astype(jnp.int32)
    return (digits[:rows] + digits[rows : 2 * rows] * 256).reshape(-1)[:count]


def phase_kernel(whiches, shifted, pieces, begins, ends, lists, q_ref, *refs):
    refs = list(refs)
    state = [refs.pop(0) for _ in range(0 if begins else 3)]
    parts = [refs.pop(0) for _ in range(pieces)]
    out_ref, stats_ref = [refs.pop(0) for _ in range(2)] if ends else [None] * 2
    top_ref, total_ref, sum_ref, window = refs[:4]
    scores, high, weights, shrinks = refs[4:] if begins else [None] * 4
    tiles = q_ref.shape[0]
    heads, width = lists.shape
    length = (width - LISTS) // (LISTS * (GROUP + 1))

    at = 0
    for part in parts:
        window[at : at + part.shape[0]] = part[...]
        at += part.shape[0]
    if begins:
        top_ref[...] = jnp.full(top_ref.shape, -FAR_OFF, jnp.float32)
        total_ref[...] = jnp.zeros(total_ref.shape, jnp.float32)
        sum_ref[...] = jnp.zeros(sum_ref.shape, jnp.float32)
    else:
        for ref, old in zip((top_ref, total_ref, sum_ref), state):
            ref[...] = old[...]

    blocks = [(which, head) for which in whiches for head in range(heads)]
    starts = [jnp.int32(0)]
    for which, head in blocks:
        starts.append(starts[-1] + lists[head, which])

    def item_of(item):
        row, which, index = jnp.int32(0), jnp.int32(whiches[0]), item
        for number in range(1, len(blocks)):
            later = item >= starts[number]
            which = jnp.where(later, blocks[number][0], which)
            row = jnp.where(later, blocks[number][1], row)
            index = jnp.where(later, item - starts[number], index)
        real = item < starts[-1]
        index = jnp.where(real, index, 0)
        meta = lists[row, LISTS + which * length + index]
        at = LISTS * (1 + length) + (which * length + index) * GROUP
        tile = jnp.where(real, meta >> 3, 0)
        shift = jnp.where(which > 1, shifted, 0)
        spots = [jnp.where(real, lists[row, at + slot] + shift, 0) for slot in range(GROUP)]
        return tile, jnp.where(real, meta & 7, -1), spots

    def score(entry):
        tile, _, spots = entry
        keys = jnp.concatenate([window[spot] for spot in spots])
        block = jnp.dot(keys, q_ref[tile], preferred_element_type=jnp.float32)
        top = jnp.max(block.reshape(-1, 8, TILE), axis=0)
        return block, jnp.max(top, axis=0, keepdims=True)

    def weigh(entry, block, peak):
        tile, last, _ = entry
        old = top_ref[tile]
        top = jnp.maximum(old, jnp.where(last < 0, -FAR_OFF, peak))
        shrink = jnp.exp2((old - top) * FACTOR)
        total = total_ref[tile] * shrink
        parts = []
        for slot in range(GROUP):
            shift = jnp.where(slot <= last, top, FAR_OFF)
            weight = jnp.exp2((block[slot * TILE : (slot + 1) * TILE] - shift) * FACTOR)
            total = total + jnp.sum(weight.reshape(-1, 8, TILE), axis=0)
            parts.append(weight.astype(jnp.bfloat16))
        top_ref[tile] = top
        total_ref[tile] = total
        return jnp.concatenate(parts), shrink

    def collect(entry, weight, shrink):
        tile, _, spots = entry
        values = jnp.concatenate([window[spot + 1] for spot in spots], axis=1)
        product = jnp.dot(values, weight, preferred_element_type=jnp.float32)
        sum_ref[tile] = sum_ref[tile] * shrink + product

    if not begins:

        def whole_step(four, carry):
            entries = [item_of(4 * four + number) for number in range(4)]
            made = [score(entry) for entry in entries]
            formed = [weigh(entry, *item) for entry, item in zip(entries, made)]
            for entry, item in zip(entries, formed):
                collect(entry, *item)
            return carry

        lax.fori_loop(0, (starts[-1] + 3) >> 2, whole_step, 0)
    else:

        def store_scores(pair):
            for number, (block, peak) in enumerate(pair):
                scores[number], high[number] = block, peak

        def store_weights(pair):
            for number, (weight, shrink) in enumerate(pair):
                weights[number], shrinks[number] = weight, shrink

        ahead = [item_of(0), item_of(1)]
        second = [item_of(2), item_of(3)]
        first = [score(entry) for entry in ahead]
        store_scores([score(entry) for entry in second])
        store_weights([weigh(entry, *made) for entry, made in zip(ahead, first)])

        def step(pair, entries):
            collected, weighed = entries[:2], entries[2:]
            scored = [item_of(2 * pair + 4), item_of(2 * pair + 5)]
            made = [(scores[number], high[number]) for number in range(2)]
            formed = [(weights[number], shrinks[number]) for number in range(2)]
            blocks = [score(entry) for entry in scored]
            following = [weigh(entry, *item) for entry, item in zip(weighed, made)]
            for entry, item in zip(collected, formed):
                collect(entry, *item)
            store_scores(blocks)
            store_weights(following)
            return tuple(weighed) + tuple(scored)

        lax.fori_loop(0, (starts[-1] + 1) >> 1, step, tuple(ahead + second))

    if ends:
        for tile in range(tiles):
            total = jnp.sum(total_ref[tile], axis=0, keepdims=True)
            share = jnp.where(total > 0, 1.0 / jnp.where(total > 0, total, 1.0), 0.0)
            out_ref[tile] = (sum_ref[tile] * share).astype(out_ref.dtype)
            stats_ref[tile, 0:1] = total
            stats_ref[tile, 1:2] = top_ref[tile]


def attend(lists, whiches, shifted, queries, state, pieces, ends):
    tiles = queries.shape[0]
    begins = state is None
    held = [
        jax.ShapeDtypeStruct((tiles, 1, TILE), jnp.float32),
        jax.ShapeDtypeStruct((tiles, 8, TILE), jnp.float32),
        jax.ShapeDtypeStruct((tiles, HEAD_DIM, TILE), jnp.float32),
    ]
    rows = sum(piece.shape[0] for piece in pieces)
    scratch = [pltpu.VMEM((rows, TILE, TILE), queries.dtype)]
    if begins:
        scratch += [
            pltpu.VMEM((2, GROUP * TILE, TILE), jnp.float32),
            pltpu.VMEM((2, 1, TILE), jnp.float32),
            pltpu.VMEM((2, GROUP * TILE, TILE), queries.dtype),
            pltpu.VMEM((2, 1, TILE), jnp.float32),
        ]
    if ends:
        scratch = [pltpu.VMEM(array.shape, array.dtype) for array in held] + scratch
        held = [
            jax.ShapeDtypeStruct((tiles, HEAD_DIM, TILE), queries.dtype),
            jax.ShapeDtypeStruct((tiles, 2, TILE), jnp.float32),
        ]
    return pl.pallas_call(
        functools.partial(phase_kernel, whiches, shifted, len(pieces), begins, ends),
        in_specs=[SMEM] + [VMEM] * (1 + len(pieces) + (0 if begins else 3)),
        out_specs=[VMEM] * len(held),
        out_shape=held,
        scratch_shapes=scratch,
        compiler_params=params(10),
        cost_estimate=cost(),
    )(lists, queries, *([] if begins else state), *pieces)


def merge_kernel(count, *refs):
    out_ref = refs[-1]
    values, stats = [refs[first : 2 * count : 2] for first in range(2)]
    tiles = values[0].shape[0]
    heads = out_ref.shape[1] // HEAD_DIM
    for tile in range(tiles):
        top = stats[0][tile, 1:2]
        for ref in stats[1:]:
            top = jnp.maximum(top, ref[tile, 1:2])
        shares = [ref[tile, 0:1] * jnp.exp2((ref[tile, 1:2] - top) * FACTOR) for ref in stats]
        whole = sum(shares[1:], shares[0])
        out = jnp.zeros((HEAD_DIM, TILE), jnp.float32)
        for value, share in zip(values, shares):
            out = out + value[tile].astype(jnp.float32) * (share / whole)
        inner, head = divmod(tile, heads)
        out_ref[
            inner * TILE : (inner + 1) * TILE, head * HEAD_DIM : (head + 1) * HEAD_DIM
        ] = out.T.astype(out_ref.dtype)


def merge(parts, rows, heads):
    flat = [array for part in parts for array in part]
    return pl.pallas_call(
        functools.partial(merge_kernel, len(parts)),
        in_specs=[VMEM] * len(flat),
        out_specs=VMEM,
        out_shape=jax.ShapeDtypeStruct((rows, heads * HEAD_DIM), flat[0].dtype),
        compiler_params=params(6),
    )(*flat)


def moved(block, axis, source):
    size = lax.axis_size(axis)
    route = [(source(i), i) for i in range(size) if 0 <= source(i) < size]
    return lax.ppermute(block, axis, route)


def body(queries, key_vectors, value_vectors, tile_lists, live_slots):
    heads = lax.axis_size("head")
    frame = lax.axis_index("frame")
    head = lax.axis_index("head")
    shard_tiles = tile_lists.shape[1]
    assert shard_tiles * PLANE == REACH and lax.axis_size("frame") % PLANE == 0

    def from_head(block, step):
        return moved(block, "head", lambda i: (i - step) % heads)

    def core_swap(block):
        return moved(block, "frame", lambda i: i ^ 1)

    own = as_tiles((key_vectors, value_vectors), (False, True))
    size = own.shape[0]
    cut = size * 5 // 8
    across = moved(own, "frame", lambda i: i ^ 2)
    chip = jnp.concatenate((core_swap(own), own))
    level = moved(chip, "frame", lambda i: i - PLANE if i % 2 == 0 else i + PLANE)

    listed, live, _ = lax.optimization_barrier((tile_lists[0], live_slots[0], chip))
    lists = work_lists(frame, head, listed, live, heads)
    q_own = as_tiles((queries,), (True,))
    blocks = [
        from_head(jnp.concatenate((q_own.reshape(-1, TILE), packed(lists[step]))), step)
        for step in range(1, heads)
    ]
    blocks, _ = lax.optimization_barrier((blocks, level))
    q_parts, by_head = [], [lists[:1]]
    for block in blocks:
        q_rows = shard_tiles * TILE
        q_parts.append(block[:q_rows].reshape(q_own.shape))
        by_head.append(unpacked(block[q_rows:], lists.shape[1])[None])
    q_rest, by_head = jnp.concatenate(q_parts), jnp.concatenate(by_head)

    far_z = moved(across[:cut], "frame", lambda i: i - PLANE if i % PLANE < 2 else i + PLANE)
    straight = moved(own[cut:], "frame", lambda i: i - 2 if i % PLANE < 2 else i + 2)
    near = [chip, level, across, core_swap(across), core_swap(level[:size])]
    state = attend(by_head, (0,), 0, q_rest, None, near, False)
    far_z, straight, state = lax.optimization_barrier((far_z, straight, state))
    far = jnp.concatenate((far_z, straight))
    far = [far, core_swap(far)]
    rest = attend(by_head, (2,), 0, q_rest, state, far, True)
    parts = [None]
    for step in range(1, heads):
        cut = slice((step - 1) * shard_tiles, step * shard_tiles)
        parts.append([from_head(array[cut], -step) for array in rest])
    q_own, _ = lax.optimization_barrier((q_own, rest))
    parts[0] = attend(by_head, (1, 3), 7 * size, q_own, None, near + far, True)
    return merge(parts, queries.shape[0], heads)


def solution(mesh):
    placed = (
        P(("frame", "head"), None),
        P(("frame", "head"), None),
        P(("frame", "head"), None),
        P("head", "frame", None),
        P("head", "frame"),
    )
    return jax.shard_map(
        body, mesh=mesh, in_specs=placed, out_specs=P(("frame", "head"), None), check_vma=False
    )
```
